128 devices in a mesh: rep: 16 (over y_hi, x, core), shard: 8 (over y_lo, z).
Axes of the slice: x: 4, y: 4 (y_hi: 2, y_lo: 2; y = y_hi * 2 + y_lo), z: 4, core: 2. Of those that a mesh axis runs over, the one named last changes fastest.
Arguments:
- tokens: bfloat16 [16384, 2048], P(('rep', 'shard')), may hold values from -6 to 6
- cotangent: float32 [16384, 2048], P(('rep', 'shard')), may hold values from -6 to 6
- lengths: int32 [16, 3], P('rep'), may hold values from 1 to 1022, as said below
- attn_gain: bfloat16 [2048], P('shard'), may hold values from 0.5 to 1.5
- mlp_gain: bfloat16 [2048], P('shard'), may hold values from 0.5 to 1.5
- query_gain: bfloat16 [128], replicated, may hold values from 0.796875 to 1.59375
- key_gain: bfloat16 [128], replicated, may hold values from 0.796875 to 1.59375
- w_query: bfloat16 [2048, 2048], P('shard'), may hold values from -0.125 to 0.125
- w_key: bfloat16 [2048, 1024], P('shard'), may hold values from -0.125 to 0.125
- w_value: bfloat16 [2048, 1024], P('shard'), may hold values from -0.125 to 0.125
- w_out: bfloat16 [2048, 2048], P('shard'), may hold values from -1 to 1
- w_gate: bfloat16 [6144, 2048], P('shard'), may hold values from -0.125 to 0.125
- w_up: bfloat16 [6144, 2048], P('shard'), may hold values from -0.125 to 0.125
- w_down: bfloat16 [6144, 2048], P('shard'), may hold values from -0.078125 to 0.078125
Outputs:
- result: float32 [16384, 2048], P(('rep', 'shard'))
- grad_tokens: float32 [16384, 2048], P(('rep', 'shard'))
- grad_w_query: float32 [2048, 2048], P('shard')
- grad_w_key: float32 [2048, 1024], P('shard')
- grad_w_value: float32 [2048, 1024], P('shard')
- grad_w_out: float32 [2048, 2048], P('shard')
- grad_w_gate: float32 [6144, 2048], P('shard')
- grad_w_up: float32 [6144, 2048], P('shard')
- grad_w_down: float32 [6144, 2048], P('shard')
- grad_attn_gain: float32 [2048], P('shard')
- grad_mlp_gain: float32 [2048], P('shard')
- grad_query_gain: float32 [128], P('shard')
- grad_key_gain: float32 [128], P('shard')
The draws below stay inside these ranges and needn't reach their ends.
Inputs may be any that keep to these rules, and one draw needn't show every extreme that they name: Row r holds, in order, the lengths of the three sequences of replica r; they sum to 1024, and the first and the last are each at most 127.
All inputs are finite; a program needn't handle non-finite values.
Results may differ from the reference program's by a relative error of at most 0.025.
Values may be sent and summed in bfloat16 or wider, within the bound.
A program may use at most 512 MiB of HBM per device.

```python
import math
import jax
import jax.numpy as jnp
from jax import lax

D = 2048
HEADS = 16
KV_HEADS = 8
HEAD_DIM = 128
FF = 6144
TOK_DEV = 128
REPLICAS = 16
REP_TOKENS = 1024
TOKENS = 16384
N_SHARD = 8


def draw_lengths(key, part):
    key = jax.random.fold_in(key, 11)
    first_key, last_key, pick_key = jax.random.split(key, 3)
    first_len = jax.random.randint(first_key, (REPLICAS,), 1, TOK_DEV)
    last_len = jax.random.randint(last_key, (REPLICAS,), 1, TOK_DEV)
    chosen = jax.random.randint(pick_key, (), 0, REPLICAS)
    replica_ids = jnp.arange(REPLICAS)
    first_len = jnp.where(replica_ids == chosen, 1, first_len)
    last_len = jnp.where(replica_ids == chosen, 1, last_len)
    middle_len = REP_TOKENS - first_len - last_len
    return jnp.stack([first_len, middle_len, last_len], axis=1).astype(jnp.int32)


def block_levels(key, shape, pieces, smallest, largest):
    level = 1.0
    for dim, shards_of in pieces:
        draws = jax.random.uniform(jax.random.fold_in(jax.random.fold_in(key, 6), dim), (shards_of,), jnp.float32, smallest / len(pieces), largest / len(pieces))
        level = level * jnp.repeat(jnp.exp(draws), shape[dim] // shards_of).reshape((-1,) + (1,) * (len(shape) - 1 - dim))
    return level


def gaussian(key, dims, scale, bound, cuts=(), kind=jnp.bfloat16):
    values = scale * jax.random.normal(key, dims, jnp.float32)
    if cuts:
        values = values * block_levels(key, dims, cuts, -0.22, 0.18)
    return jnp.clip(values, -bound, bound).astype(kind)


def setup_inputs(seed: int = 0) -> dict:
    seeds = jax.random.split(jax.random.key(seed), 15)
    return {
        "tokens": gaussian(seeds[0], (TOKENS, D), 1.0, 6.0, ((0, 128),)),
        "cotangent": gaussian(seeds[1], (TOKENS, D), 1.0, 6.0, ((0, 128),), jnp.float32),
        "lengths": draw_lengths(jax.random.fold_in(seeds[14], 71), 0),
        "attn_gain": jnp.clip(0.5 + 1.0 * jax.random.uniform(seeds[3], (D,), jnp.float32) ** block_levels(seeds[3], (D,), ((0, 8),), -0.2, 0.2), 0.5, 1.5).astype(jnp.bfloat16),
        "mlp_gain": jnp.clip(0.5 + 1.0 * jax.random.uniform(seeds[4], (D,), jnp.float32) ** block_levels(seeds[4], (D,), ((0, 8),), -0.2, 0.2), 0.5, 1.5).astype(jnp.bfloat16),
        "query_gain": jnp.clip(jax.random.uniform(seeds[5], (HEAD_DIM,), jnp.float32, 0.796875, 1.59375), 0.796875, 1.59375).astype(jnp.bfloat16),
        "key_gain": jnp.clip(jax.random.uniform(seeds[6], (HEAD_DIM,), jnp.float32, 0.796875, 1.59375), 0.796875, 1.59375).astype(jnp.bfloat16),
        "w_query": gaussian(seeds[7], (D, HEADS * HEAD_DIM), D ** -0.5, 0.125, ((0, 8),)),
        "w_key": gaussian(seeds[8], (D, KV_HEADS * HEAD_DIM), D ** -0.5, 0.125, ((0, 8),)),
        "w_value": gaussian(seeds[9], (D, KV_HEADS * HEAD_DIM), D ** -0.5, 0.125, ((0, 8),)),
        "w_out": gaussian(seeds[10], (D, HEADS * HEAD_DIM), (HEADS * HEAD_DIM // 64) ** -0.5, 1.0, ((0, 8),)),
        "w_gate": gaussian(seeds[11], (FF, D), D ** -0.5, 0.125, ((0, 8),)),
        "w_up": gaussian(seeds[12], (FF, D), D ** -0.5, 0.125, ((0, 8),)),
        "w_down": gaussian(seeds[13], (FF, D), FF ** -0.5, 0.078125, ((0, 8),)),
    }


@jax.custom_vjp
def low(v):
    return lax.optimization_barrier(v.astype(jnp.bfloat16)).astype(jnp.float32)

@jax.custom_vjp
def low_back(v):
    return v

def low_keep(v):
    return (low(v), None)

def low_pass(kept, grad):
    return (grad,)

def back_keep(v):
    return (v, None)

def back_low(kept, grad):
    return (low(grad),)
low.defvjp(low_keep, low_pass)
low_back.defvjp(back_keep, back_low)
epsilon = 1e-06
theta_base = 1000000.0
masked_value = -1e+30

def matmul(left, right):
    return jnp.dot(left, right, precision=lax.Precision.HIGHEST, preferred_element_type=jnp.float32)

def matmul_rows(left, right):
    return lax.dot_general(left, right, (((1,), (1,)), ((), ())), precision=lax.Precision.HIGHEST, preferred_element_type=jnp.float32)

def rms_scale(values, gain):
    return values * lax.rsqrt(lax.optimization_barrier(jnp.mean(values * values, axis=-1, keepdims=True)) + epsilon) * gain

def rotate(values, positions):
    half_dim = values.shape[-1] // 2
    frequency = theta_base ** (-jnp.arange(half_dim, dtype=jnp.float32) * (2.0 / values.shape[-1]))
    angles = positions.astype(jnp.float32)[:, None] * frequency[None, :]
    cosine = jnp.cos(angles)[:, None, :]
    sine = jnp.sin(angles)[:, None, :]
    first_half = values[..., :half_dim]
    second_half = values[..., half_dim:]
    return jnp.concatenate([first_half * cosine - second_half * sine, second_half * cosine + first_half * sine], axis=-1)

def segment_info(lengths_row, indices):
    start_one = lengths_row[0]
    start_two = lengths_row[0] + lengths_row[1]
    segment = (indices >= start_one).astype(jnp.int32) + (indices >= start_two).astype(jnp.int32)
    begin = jnp.where(segment == 0, 0, jnp.where(segment == 1, start_one, start_two)).astype(jnp.int32)
    return (segment, indices - begin)

def attend(block):
    queries, keys, values, segment = block
    count = queries.shape[0]
    indices = jnp.arange(count, dtype=jnp.int32)
    scores = jnp.einsum('tkgd,skd->kgts', queries, keys, precision=lax.Precision.HIGHEST)
    scores = low_back(scores * (1.0 / math.sqrt(HEAD_DIM)))
    visible = (segment[:, None] == segment[None, :]) & (indices[None, :] <= indices[:, None])
    masked = jnp.where(visible[None, None], scores, masked_value)
    top = lax.optimization_barrier(jnp.max(masked, axis=-1, keepdims=True))
    total = jnp.log(lax.optimization_barrier(jnp.sum(jnp.exp(masked - top), axis=-1, keepdims=True))) + top
    probs = low(jnp.exp(masked - total))
    return jnp.einsum('kgts,skd->tkgd', probs, values, precision=lax.Precision.HIGHEST)

def reference(tokens, cotangent, lengths, attn_gain, mlp_gain, query_gain, key_gain, w_query, w_key, w_value, w_out, w_gate, w_up, w_down):
    group_rows = TOK_DEV * N_SHARD
    index_row = jnp.arange(group_rows, dtype=jnp.int32)
    segment, position = jax.vmap(lambda row: segment_info(row, index_row))(lengths)
    positions = position.reshape(-1)
    group_size = HEADS // KV_HEADS

    def forward(inputs, first_gain, second_gain, q_gain, k_gain, wq, wk, wv, wo, wg, wu, wd):
        count = inputs.shape[0]
        first = low(rms_scale(inputs, first_gain))
        q_proj = low_back(matmul(first, wq))
        k_proj = low_back(matmul(first, wk))
        v_proj = low_back(matmul(first, wv))
        queries = low(rotate(rms_scale(q_proj.reshape(count, HEADS, HEAD_DIM), q_gain), positions))
        keys = low(rotate(rms_scale(k_proj.reshape(count, KV_HEADS, HEAD_DIM), k_gain), positions))
        values = low(v_proj)
        stacked = (queries.reshape(REPLICAS, group_rows, KV_HEADS, group_size, HEAD_DIM), keys.reshape(REPLICAS, group_rows, KV_HEADS, HEAD_DIM), values.reshape(REPLICAS, group_rows, KV_HEADS, HEAD_DIM), segment)
        mixed = lax.map(jax.checkpoint(attend), stacked).reshape(count, HEADS * HEAD_DIM)
        attended = low(low_back(mixed))
        resid = inputs + low_back(matmul_rows(attended, wo))
        second = low(rms_scale(resid, second_gain))
        gate = low_back(matmul_rows(second, wg))
        up = low_back(matmul_rows(second, wu))
        hidden = low(jax.nn.silu(gate) * up)
        return resid + low_back(matmul(hidden, wd))
    floats = (tokens.astype(jnp.float32), attn_gain.astype(jnp.float32), mlp_gain.astype(jnp.float32), query_gain.astype(jnp.float32), key_gain.astype(jnp.float32), w_query.astype(jnp.float32), w_key.astype(jnp.float32), w_value.astype(jnp.float32), w_out.astype(jnp.float32), w_gate.astype(jnp.float32), w_up.astype(jnp.float32), w_down.astype(jnp.float32))
    result, pullback = jax.vjp(forward, *floats)
    grads = pullback(cotangent.astype(jnp.float32))
    return (result, grads[0], grads[5], grads[6], grads[7], grads[8], grads[9], grads[10], grads[11], grads[1], grads[2], grads[3], grads[4])
```

```python
import math

import jax
import jax.numpy as jnp
from jax import lax
from jax.sharding import PartitionSpec as P

HEADS = 16
KV_HEADS = 8
HEAD_DIM = 128

epsilon = 1e-06
theta_base = 1000000.0
masked_value = -1e30


def rms_scale(values, gain):
    return values * lax.rsqrt(jnp.mean(values * values, axis=-1, keepdims=True) + epsilon) * gain


def rotate(values, positions):
    half_dim = values.shape[-1] // 2
    frequency = theta_base ** (-jnp.arange(half_dim, dtype=jnp.float32) * (2.0 / values.shape[-1]))
    angles = positions.astype(jnp.float32)[:, None] * frequency[None, :]
    cosine = jnp.cos(angles)[:, None, :]
    sine = jnp.sin(angles)[:, None, :]
    first_half = values[..., :half_dim]
    second_half = values[..., half_dim:]
    return jnp.concatenate(
        [first_half * cosine - second_half * sine, second_half * cosine + first_half * sine],
        axis=-1,
    )


def segment_info(lengths_row, indices):
    start_one = lengths_row[0]
    start_two = lengths_row[0] + lengths_row[1]
    segment = (indices >= start_one).astype(jnp.int32) + (indices >= start_two).astype(jnp.int32)
    begin = jnp.where(segment == 0, 0, jnp.where(segment == 1, start_one, start_two))
    return (segment, indices - begin)


def dot(left, right):
    return jnp.dot(left, right, preferred_element_type=jnp.float32)


def contract_rows(left, right):
    return lax.dot_general(
        left, right, (((1,), (1,)), ((), ())), preferred_element_type=jnp.float32
    )


def contract_first(left, right):
    return lax.dot_general(
        left, right, (((0,), (0,)), ((), ())), preferred_element_type=jnp.float32
    )


def gather(x):
    return lax.all_gather(x, "shard", axis=0, tiled=True)


def scatter_sum(x):
    return lax.psum_scatter(
        x.astype(jnp.bfloat16), "shard", scatter_dimension=0, tiled=True
    ).astype(jnp.float32)


def per_device(
    tokens,
    cotangent,
    lengths,
    attn_gain,
    mlp_gain,
    query_gain,
    key_gain,
    w_query,
    w_key,
    w_value,
    w_out,
    w_gate,
    w_up,
    w_down,
):
    low = jnp.bfloat16
    tok_rows, width = tokens.shape
    shards = lax.axis_size("shard")
    rows = tok_rows * shards
    group = HEADS // KV_HEADS
    feat = width // shards
    scale = 1.0 / math.sqrt(HEAD_DIM)
    my_shard = lax.axis_index("shard")
    index = jnp.arange(rows, dtype=jnp.int32)
    segment, position = segment_info(lengths[0], index)
    visible = (segment[:, None] == segment[None, :]) & (index[None, :] <= index[:, None])

    q_cols = w_query.shape[1] // shards
    k_cols = w_key.shape[1] // shards
    packed = jnp.concatenate(
        [
            w_query.reshape(feat, shards, q_cols),
            w_key.reshape(feat, shards, k_cols),
            w_value.reshape(feat, shards, k_cols),
            w_out.reshape(feat, shards, q_cols),
        ],
        axis=2,
    )
    mine = lax.all_to_all(packed, "shard", split_axis=1, concat_axis=0, tiled=True).reshape(
        width, -1
    )
    qkv_cols = q_cols + 2 * k_cols
    w_qkv = mine[:, :qkv_cols]
    w_o = mine[:, qkv_cols:]

    gains_rows = jnp.concatenate(
        [attn_gain, mlp_gain, jnp.zeros((width - 2 * feat,), low)]
    ).reshape(1, width)
    gathered = gather(
        jnp.concatenate([tokens, jnp.broadcast_to(gains_rows, (16, width))], axis=0)
    ).reshape(shards, tok_rows + 16, width)
    tokens_all = gathered[:, :tok_rows].reshape(rows, width)
    gain_one = gathered[:, tok_rows, :feat].reshape(width).astype(jnp.float32)
    gain_two = gathered[:, tok_rows, feat : 2 * feat].reshape(width).astype(jnp.float32)

    inputs = tokens.astype(jnp.float32)
    first = rms_scale(tokens_all.astype(jnp.float32), gain_one).astype(low)
    proj = dot(first, w_qkv)

    def prepare(projected, gain, count):
        return rotate(rms_scale(projected.reshape(rows, count, HEAD_DIM), gain), position)

    q_rot, query_back = jax.vjp(
        lambda p, g: prepare(p, g, group), proj[:, :q_cols], query_gain.astype(jnp.float32)
    )
    k_rot, key_back = jax.vjp(
        lambda p, g: prepare(p, g, 1), proj[:, q_cols : q_cols + k_cols], key_gain.astype(jnp.float32)
    )
    query = q_rot.astype(low)
    key = k_rot.astype(low)[:, 0]
    value = proj[:, q_cols + k_cols :].astype(low)
    scores = jnp.einsum("tgd,sd->gts", query, key, preferred_element_type=jnp.float32) * scale
    masked = jnp.where(visible[None], scores, masked_value)
    top = jnp.max(masked, axis=-1, keepdims=True)
    total = jnp.log(jnp.sum(jnp.exp(masked - top), axis=-1, keepdims=True)) + top
    weights = jnp.exp(masked - total)
    probs = weights.astype(low)
    attended = (
        jnp.einsum("gts,sd->tgd", probs, value, preferred_element_type=jnp.float32)
        .reshape(rows, q_cols)
        .astype(low)
    )
    resid = inputs + scatter_sum(contract_rows(attended, w_o))
    second_value, second_back = jax.vjp(rms_scale, resid, gain_two)
    second = gather(second_value.astype(low))
    grad_low = gather(cotangent.astype(low))
    gate = contract_rows(second, w_gate)
    up = contract_rows(second, w_up)
    sigma = jax.nn.sigmoid(gate)
    hidden = (gate * sigma * up).astype(low)
    result = resid + scatter_sum(dot(hidden, w_down))
    dhidden = contract_rows(grad_low, w_down)
    dgate = (dhidden * up * sigma * (1.0 + gate * (1.0 - sigma))).astype(low)
    dup = (dhidden * gate * sigma).astype(low)
    dsecond = scatter_sum(dot(dgate, w_gate) + dot(dup, w_up))
    ffn_grads = lax.psum(
        tuple(
            g.astype(low)
            for g in (
                contract_first(dgate, second),
                contract_first(dup, second),
                contract_first(hidden, grad_low),
            )
        ),
        "rep",
    )
    grad_resid_part, grad_second_gain = second_back(dsecond)
    grad_resid = cotangent + grad_resid_part
    branch = gather(grad_resid.astype(low))
    grad_att = dot(branch, w_o).astype(low)
    grad_heads = grad_att.reshape(rows, group, HEAD_DIM)
    dprobs = jnp.einsum("tgd,sd->gts", grad_heads, value, preferred_element_type=jnp.float32)
    inner = jnp.sum(weights * dprobs, axis=-1, keepdims=True)
    dscores = (weights * (dprobs - inner)).astype(low)
    dquery = jnp.einsum("gts,sd->tgd", dscores, key, preferred_element_type=jnp.float32) * scale
    dkey = jnp.einsum("gts,tgd->sd", dscores, query, preferred_element_type=jnp.float32) * scale
    dvalue = jnp.einsum("gts,tgd->sd", probs, grad_heads, preferred_element_type=jnp.float32)
    dq_proj, grad_query_part = query_back(dquery)
    dk_proj, grad_key_part = key_back(dkey[:, None])
    d_qkv = jnp.concatenate(
        [dq_proj.astype(low), dk_proj.astype(low), dvalue.astype(low)], axis=1
    )
    grad_first = scatter_sum(contract_rows(d_qkv, w_qkv))
    attn_grads = lax.psum(
        jnp.concatenate(
            [contract_first(first, d_qkv), contract_first(branch, attended)], axis=1
        ).astype(low),
        "rep",
    )
    attn_grads = lax.all_to_all(
        attn_grads.reshape(shards, feat, -1), "shard", split_axis=0, concat_axis=1, tiled=True
    ).reshape(shards, feat, -1).transpose(1, 0, 2).astype(jnp.float32)
    grad_query = attn_grads[:, :, :q_cols].reshape(feat, -1)
    grad_key = attn_grads[:, :, q_cols : q_cols + k_cols].reshape(feat, -1)
    grad_value = attn_grads[:, :, q_cols + k_cols : qkv_cols].reshape(feat, -1)
    grad_out = attn_grads[:, :, qkv_cols:].reshape(feat, -1)
    first_back = jax.vjp(rms_scale, inputs, gain_one)[1]
    grad_input_part, grad_first_gain = first_back(grad_first)
    grad_tokens = grad_resid + grad_input_part
    gains = lax.psum(
        jnp.concatenate([grad_first_gain, grad_second_gain, grad_query_part, grad_key_part]),
        ("rep", "shard"),
    )
    head_piece = HEAD_DIM // shards
    gains_first = lax.dynamic_slice_in_dim(gains, my_shard * feat, feat, 0)
    gains_second = lax.dynamic_slice_in_dim(gains, width + my_shard * feat, feat, 0)
    gains_query = lax.dynamic_slice_in_dim(gains, 2 * width + my_shard * head_piece, head_piece, 0)
    gains_key = lax.dynamic_slice_in_dim(
        gains, 2 * width + HEAD_DIM + my_shard * head_piece, head_piece, 0
    )
    return (
        result,
        grad_tokens,
        grad_query,
        grad_key,
        grad_value,
        grad_out,
        ffn_grads[0].astype(jnp.float32),
        ffn_grads[1].astype(jnp.float32),
        ffn_grads[2].astype(jnp.float32),
        gains_first,
        gains_second,
        gains_query,
        gains_key,
    )


def solution(mesh):
    spread = P(("rep", "shard"), None)
    rowed = P("shard", None)
    return jax.shard_map(
        per_device,
        mesh=mesh,
        in_specs=(spread, spread, P("rep", None), P("shard"), P("shard"), P(), P()) + (rowed,) * 7,
        out_specs=(spread, spread) + (rowed,) * 7 + (P("shard"),) * 4,
        check_vma=False,
    )
```

```python
import functools
import math

import jax
import jax.numpy as jnp
from jax import lax
from jax.experimental import pallas as pl
from jax.experimental.pallas import tpu as pltpu
from jax.sharding import PartitionSpec as P

HEADS = 16
KV_HEADS = 8
HEAD_DIM = 128

epsilon = 1e-06
theta_base = 1000000.0
masked_value = -1e30


MESH = pl.DeviceIdType.MESH
BLOCK = 128
HALF = 64
LINE = 512
low = jnp.bfloat16
f32 = jnp.float32


def mm(left, right):
    return lax.dot_general(left, right, (((1,), (0,)), ((), ())), preferred_element_type=f32)


def mm_nt(left, right):
    return lax.dot_general(left, right, (((1,), (1,)), ((), ())), preferred_element_type=f32)


def mm_tn(left, right):
    return lax.dot_general(left, right, (((0,), (0,)), ((), ())), preferred_element_type=f32)


class Place:
    def __init__(self):
        self.rep = lax.axis_index("rep")
        shard = lax.axis_index("shard")
        self.yl, self.z = shard // 4, shard % 4

    def block(self, dy, dz):
        return ((self.yl + dy + 2) % 2) * 4 + (self.z + dz + 8) % 4

    def dev(self, dy, dz):
        return (self.rep, self.block(dy, dz))

    def rows(self, dy, dz, start=0, count=BLOCK):
        return pl.ds(pl.multiple_of(self.block(dy, dz) * BLOCK + start, 32), count)

    def line(self, dy):
        return pl.multiple_of(((self.yl + dy + 2) % 2) * LINE, LINE)

    def greet(self):
        barrier = pltpu.get_barrier_semaphore()
        for peer in ((1, 0), (0, 1), (0, 3)):
            pl.semaphore_signal(barrier, inc=1, device_id=self.dev(*peer), device_id_type=MESH)
        pl.semaphore_wait(barrier, 3)


class Net:
    def __init__(self, send_sems, recv_sems):
        self.send_sems, self.recv_sems = send_sems, recv_sems
        self.started, self.coming = [], {}

    def send(self, tag, src, dst, dev, here):
        k = len(self.started)
        copy = pltpu.make_async_remote_copy(
            src_ref=src,
            dst_ref=dst,
            send_sem=self.send_sems.at[k],
            recv_sem=self.recv_sems.at[k],
            device_id=dev,
            device_id_type=MESH,
        )
        copy.start()
        self.started.append(copy)
        self.coming[tag] = (k, here, dev)

    def wait(self, tag):
        k, here, dev = self.coming.pop(tag)
        pltpu.make_async_remote_copy(
            src_ref=here,
            dst_ref=here,
            send_sem=self.send_sems.at[k],
            recv_sem=self.recv_sems.at[k],
            device_id=dev,
            device_id_type=MESH,
        ).wait_recv()

    def finish(self):
        for tag in list(self.coming):
            self.wait(tag)
        for copy in self.started:
            copy.wait_send()


class Gather:
    COPIES = 18

    def __init__(self, place, buf, send_sems, recv_sems):
        self.place, self.buf = place, buf
        self.net = Net(send_sems, recv_sems)

    def send(self, tag, block, start, count, to):
        rows = self.place.rows(*block, start, count)
        here = self.place.rows(block[0] - to[0], block[1] - to[1], start, count)
        self.net.send(
            tag, self.buf.at[rows], self.buf.at[rows], self.place.dev(*to), self.buf.at[here]
        )

    def start(self):
        self.send("y_up", (0, 0), 0, HALF, (1, 0))
        for d in (1, 3):
            self.send(f"z_low{d}", (0, 0), HALF, HALF, (0, d))
        self.send("y_low", (0, 0), HALF, HALF, (1, 0))

    def step_one(self):
        self.net.wait("y_up")
        for d in (1, 3):
            self.send(f"p_up{d}", (1, 0), 0, HALF, (0, d))

    def step_two(self):
        for e, d in enumerate((1, 3)):
            self.net.wait(f"z_low{d}")
            self.send(f"f_low{d}", (0, -d), HALF + 32 * e, 32, (0, d))
            self.send(f"q_low{d}", (0, -d), HALF, HALF, (1, 0))
        for d in (1, 3):
            self.send(f"z_up{d}", (0, 0), 0, HALF, (0, d))

    def step_three(self):
        for e, d in enumerate((1, 3)):
            self.net.wait(f"p_up{d}")
            self.send(f"f_p{d}", (1, -d), 32 * e, 32, (0, d))
        for e, d in enumerate((1, 3)):
            self.net.wait(f"f_low{d}")
            self.send(f"q_far{d}", (0, -2 * d), HALF + 32 * e, 32, (1, 0))

    def step_four(self):
        for e, d in enumerate((1, 3)):
            self.net.wait(f"z_up{d}")
            self.send(f"f_up{d}", (0, -d), 32 * e, 32, (0, d))

    def own_line(self):
        for d in (1, 3):
            self.net.wait(f"f_up{d}")

    def other_line(self):
        for tag in list(self.net.coming):
            self.net.wait(tag)

    def steps(self):
        return [self.start, self.step_one, self.step_two, self.step_three, self.step_four]

    def finish(self):
        self.net.finish()


class Scatter:
    COPIES = 17

    @staticmethod
    def scratch(columns):
        return [
            pltpu.VMEM((4, HALF, columns), low),
            pltpu.VMEM((3, 2, 32, columns), low),
            pltpu.VMEM((3, 2, HALF, columns), low),
            pltpu.VMEM((HALF, columns), low),
        ]

    def __init__(self, place, part, across, near, far, last, send_sems, recv_sems):
        self.place, self.part = place, part
        self.across, self.near, self.far, self.last = across, near, far, last
        self.net = Net(send_sems, recv_sems)

    def add(self, rows, *refs):
        total = self.part[rows, :].astype(f32)
        for ref in refs:
            total = total + ref[...].astype(f32)
        self.part[rows, :] = total.astype(low)

    def first(self, kind):
        dy, start = ((1, 0), (0, 0), (0, HALF))[kind]
        for e, d in enumerate((1, 3)):
            src = self.part.at[self.place.rows(dy, 2, start + 32 * e, 32)]
            dst = self.near.at[kind, e]
            self.net.send(f"near{kind}{e}", src, dst, self.place.dev(0, d), dst)

    def second(self, kind):
        dy, start = ((1, 0), (0, 0), (0, HALF))[kind]
        for e, d in enumerate((1, 3)):
            self.net.wait(f"near{kind}{e}")
            self.add(self.place.rows(dy, d, start + 32 * e, 32), self.near.at[kind, e])
            src = self.part.at[self.place.rows(dy, d, start, HALF)]
            dst = self.far.at[kind, e]
            self.net.send(f"far{kind}{e}", src, dst, self.place.dev(0, d), dst)

    def send_other(self):
        for d in (2, 1, 3, 0):
            src = self.part.at[self.place.rows(1, d, HALF, HALF)]
            dst = self.across.at[d]
            self.net.send(f"across{d}", src, dst, self.place.dev(1, 0), dst)
        self.first(0)

    def send_own(self):
        self.first(1)

    def step_one(self):
        self.net.wait("across2")
        self.add(self.place.rows(0, 2, HALF, HALF), self.across.at[2])
        self.first(2)
        self.second(0)
        self.second(1)

    def step_two(self):
        for d in (1, 3):
            self.net.wait(f"across{d}")
            self.add(self.place.rows(0, d, HALF, HALF), self.across.at[d])
        self.second(2)

    def step_three(self):
        for e in range(2):
            self.net.wait(f"far0{e}")
        rows = self.place.rows(1, 0, 0, HALF)
        self.add(rows, self.far.at[0, 0], self.far.at[0, 1])
        self.net.send("last", self.part.at[rows], self.last, self.place.dev(1, 0), self.last)

    def total(self, half):
        if half == 0:
            tags, extra, kind = ("far10", "far11", "last"), self.last, 1
        else:
            tags, extra, kind = ("far20", "far21", "across0"), self.across.at[0], 2
        for tag in tags:
            self.net.wait(tag)
        out = self.part[self.place.rows(0, 0, half * HALF, HALF), :].astype(f32)
        for ref in (self.far.at[kind, 0], self.far.at[kind, 1], extra):
            out = out + ref[...].astype(f32)
        return out

    def finish(self):
        self.net.finish()


def rms_backward(value, gain, upstream):
    root = lax.rsqrt(jnp.mean(value * value, axis=-1, keepdims=True) + epsilon)
    pulled = upstream * gain
    back = root * pulled - value * (root * root * root) * jnp.mean(
        pulled * value, axis=-1, keepdims=True
    )
    return back, upstream * (value * root)


def swap_halves(value):
    return pltpu.roll(value, HEAD_DIM // 2, 1)


def late_kernel(
    scale,
    lengths,
    resid,
    cotangent,
    tokens,
    gain_one,
    gain_two,
    query_gain,
    key_gain,
    proj,
    cosine,
    sine,
    w_attn_hbm,
    heads_hbm,
    first_hbm,
    w_gate_hbm,
    w_up_hbm,
    w_down_hbm,
    result,
    grad_tokens,
    gains,
    attn_grads,
    ffn_grads,
    second,
    cot_all,
    branch,
    w_gate,
    w_up,
    w_down,
    hidden,
    d_gate,
    d_up,
    part_out,
    part_back,
    d_att,
    d_key,
    d_value,
    d_qkv,
    staged,
    o_across,
    o_near,
    o_far,
    o_last,
    b_across,
    b_near,
    b_far,
    b_last,
    local_sems,
    stage_sems,
    send_sems,
    recv_sems,
):
    place = Place()
    rows_all = 8 * BLOCK
    hid = w_gate.shape[0]
    width = second.shape[1]

    loads = [
        pltpu.make_async_copy(src, dst, local_sems.at[i])
        for i, (src, dst) in enumerate(
            ((w_gate_hbm, w_gate), (w_up_hbm, w_up), (w_down_hbm, w_down))
        )
    ]
    for load in loads:
        load.start()

    used = [0]

    def sems(count):
        at = used[0]
        used[0] += count
        return send_sems.at[pl.ds(at, count)], recv_sems.at[pl.ds(at, count)]

    own = place.rows(0, 0)
    root = lax.rsqrt(jnp.mean(resid[...] * resid[...], axis=-1, keepdims=True) + epsilon)
    second[own, :] = (resid[...] * root * gain_two[...]).astype(low)
    cot_all[own, :] = cotangent[...].astype(low)
    place.greet()
    gather_second = Gather(place, second, *sems(Gather.COPIES))
    gather_cot = Gather(place, cot_all, *sems(Gather.COPIES))
    gather_branch = Gather(place, branch, *sems(Gather.COPIES))
    scatter_out = Scatter(
        place, part_out, o_across, o_near, o_far, o_last, *sems(Scatter.COPIES)
    )
    scatter_back = Scatter(
        place, part_back, b_across, b_near, b_far, b_last, *sems(Scatter.COPIES)
    )

    def feed_forward(dy):
        rows = pl.ds(place.line(dy), LINE)

        @pl.loop(0, hid // 256)
        def _(i):
            cols = pl.ds(pl.multiple_of(i * 256, 256), 256)
            gate = mm_nt(second[rows, :], w_gate[cols, :])
            up = mm_nt(second[rows, :], w_up[cols, :])
            sigma = 1.0 / (1.0 + jnp.exp(-gate))
            silu = gate * sigma
            hidden[rows, cols] = (silu * up).astype(low)
            d_gate[rows, cols] = (up * sigma * (1.0 + gate * (1.0 - sigma))).astype(low)
            d_up[rows, cols] = silu.astype(low)

    def project_out(dy):
        rows = pl.ds(place.line(dy), LINE)

        @pl.loop(0, width // 512)
        def _(i):
            cols = pl.ds(pl.multiple_of(i * 512, 512), 512)
            part_out[rows, cols] = mm(hidden[rows, :], w_down[:, cols]).astype(low)

    def feed_backward(dy):
        rows = pl.ds(place.line(dy), LINE)

        @pl.loop(0, hid // 256)
        def _(i):
            cols = pl.ds(pl.multiple_of(i * 256, 256), 256)
            d_hidden = mm_nt(cot_all[rows, :], w_down[cols, :])
            d_gate[rows, cols] = (d_hidden * d_gate[rows, cols].astype(f32)).astype(low)
            d_up[rows, cols] = (d_hidden * d_up[rows, cols].astype(f32)).astype(low)

        @pl.loop(0, width // 512)
        def _(i):
            cols = pl.ds(pl.multiple_of(i * 512, 512), 512)
            part_back[rows, cols] = (
                mm(d_gate[rows, :], w_gate[:, cols]) + mm(d_up[rows, :], w_up[:, cols])
            ).astype(low)

    stores = [None, None]

    def weight_grad(which, left, right):
        for i in range(hid // 256):
            slot = (which * (hid // 256) + i) % 2
            if stores[slot] is not None:
                stores[slot].wait()
            staged[slot] = mm_tn(left[:, pl.ds(i * 256, 256)], right[...]).astype(low)
            stores[slot] = pltpu.make_async_copy(
                staged.at[slot], ffn_grads.at[which, pl.ds(i * 256, 256)], stage_sems.at[slot]
            )
            stores[slot].start()

    for step in gather_second.steps():
        step()
    gather_second.own_line()
    gather_cot.start()
    for load in loads:
        load.wait()
    feed_forward(0)
    gather_cot.step_one()
    gather_cot.step_two()
    gather_second.other_line()
    feed_forward(1)
    gather_cot.step_three()
    gather_cot.step_four()
    project_out(1)
    project_out(0)
    gather_cot.own_line()
    gather_cot.other_line()
    feed_backward(1)
    scatter_back.send_other()
    feed_backward(0)
    scatter_back.send_own()
    weight_grad(0, d_gate, second)
    scatter_back.step_one()
    weight_grad(1, d_up, second)
    scatter_back.step_two()
    weight_grad(2, hidden, cot_all)
    gather_second.finish()
    gather_cot.finish()
    heads = d_up
    q_cols = 2 * HEAD_DIM
    query = heads.at[:, pl.ds(0, q_cols)]
    key = heads.at[:, pl.ds(q_cols, HEAD_DIM)]
    value = heads.at[:, pl.ds(q_cols + HEAD_DIM, HEAD_DIM)]
    attended = heads.at[:, pl.ds(q_cols + 2 * HEAD_DIM, q_cols)]
    w_attn = cot_all
    attn_cols = heads.shape[1]
    loads = [
        pltpu.make_async_copy(heads_hbm, heads, local_sems.at[0]),
        pltpu.make_async_copy(
            w_attn_hbm.at[pl.ds(0, rows_all)],
            w_attn.at[:, pl.ds(0, attn_cols)],
            local_sems.at[1],
        ),
        pltpu.make_async_copy(
            w_attn_hbm.at[pl.ds(rows_all, rows_all)],
            w_attn.at[:, pl.ds(attn_cols, attn_cols)],
            local_sems.at[2],
        ),
    ]
    for load in loads:
        load.start()
    scatter_back.step_three()
    gain_rows = None
    for half in (1, 0):
        rows = pl.ds(half * HALF, HALF)
        d_second = scatter_back.total(half)
        back, gain_part = rms_backward(resid[rows, :], gain_two[...], d_second)
        grad_tokens[rows, :] = cotangent[rows, :] + back
        gain_part = jnp.sum(gain_part, axis=0, keepdims=True)
        gain_rows = gain_part if gain_rows is None else gain_rows + gain_part
    gains[...] = jnp.zeros_like(gains)
    gains[0:1, :] = gain_rows
    branch[own, :] = grad_tokens[...].astype(low)
    gather_branch.start()
    scatter_out.send_other()
    scatter_out.send_own()
    gather_branch.step_one()
    gather_branch.step_two()
    gather_branch.step_three()
    gather_branch.step_four()
    gather_branch.own_line()
    for load in loads:
        load.wait()

    def into_attention(dy):
        rows = pl.ds(place.line(dy), LINE)
        d_att[rows, :] = (
            mm(branch[rows, 0:rows_all], w_attn[:, 4 * HEAD_DIM : attn_cols])
            + mm(branch[rows, rows_all:], w_attn[:, attn_cols + 4 * HEAD_DIM : 2 * attn_cols])
        ).astype(low)

    into_attention(0)
    gather_branch.other_line()
    into_attention(1)

    def unrotate(rows, upstream, projected, gain):
        turned = upstream * cosine[rows, :] - swap_halves(upstream) * sine[rows, :]
        return rms_backward(projected, gain, turned)

    gain_rows = jnp.zeros((1, HEAD_DIM), f32)
    start_one = lengths[0, 0]
    start_two = lengths[0, 0] + lengths[0, 1]
    d_key[...] = jnp.zeros_like(d_key)
    d_value[...] = jnp.zeros_like(d_value)
    chunk = 256
    scatter_out.step_one()
    for part in range(rows_all // chunk):
        rows = pl.ds(part * chunk, chunk)
        seen = (part + 1) * chunk
        token = part * chunk + lax.broadcasted_iota(jnp.int32, (chunk, 1), 0)
        source = lax.broadcasted_iota(jnp.int32, (1, seen), 1)
        begin = jnp.where(
            token >= start_two, start_two, jnp.where(token >= start_one, start_one, 0)
        )
        visible = (source >= begin) & (source <= token)
        for g in range(2):
            lanes = pl.ds(g * HEAD_DIM, HEAD_DIM)
            scores = mm_nt(query[rows, lanes], key[0:seen, :]) * scale
            weights = jnp.where(visible, jnp.exp(scores - proj[rows, 3 * HEAD_DIM + g : 3 * HEAD_DIM + g + 1]), 0.0)
            d_probs = mm_nt(d_att[rows, lanes], value[0:seen, :])
            inner = jnp.sum(weights * d_probs, axis=-1, keepdims=True)
            d_scores = (weights * (d_probs - inner)).astype(low)
            back, gain_part = unrotate(
                rows, mm(d_scores, key[0:seen, :]) * scale, proj[rows, lanes], query_gain[...]
            )
            d_qkv[rows, lanes] = back.astype(low)
            gain_rows = gain_rows + jnp.sum(gain_part, axis=0, keepdims=True)
            d_key[0:seen, :] += mm_tn(d_scores, query[rows, lanes])
            d_value[0:seen, :] += mm_tn(weights.astype(low), d_att[rows, lanes])
        if part == 1:
            scatter_out.step_two()
        if part == 2:
            scatter_out.step_three()
    d_qkv[:, 3 * HEAD_DIM :] = d_value[...].astype(low)

    gains[2:3, 0:HEAD_DIM] = gain_rows
    lanes = pl.ds(2 * HEAD_DIM, HEAD_DIM)
    back, gain_part = unrotate(pl.ds(0, rows_all), d_key[...] * scale, proj[:, lanes], key_gain[...])
    d_qkv[:, lanes] = back.astype(low)
    gains[2:3, HEAD_DIM : 2 * HEAD_DIM] = jnp.sum(gain_part, axis=0, keepdims=True)

    scatter_back.finish()
    scatter_first = Scatter(
        place, part_back, b_across, b_near, b_far, b_last, *sems(Scatter.COPIES)
    )
    for half in (0, 1):
        rows = pl.ds(half * HALF, HALF)
        result[rows, :] = resid[rows, :] + scatter_out.total(half)
    scatter_out.finish()
    load = pltpu.make_async_copy(first_hbm, second, local_sems.at[0])
    load.start()

    def into_first(dy):
        rows = pl.ds(place.line(dy), LINE)

        for side in range(2):

            @pl.loop(0, rows_all // 256)
            def _(i):
                feats = pl.ds(pl.multiple_of(i * 256, 256), 256)
                cols = pl.ds(pl.multiple_of(side * rows_all + i * 256, 256), 256)
                part_back[rows, cols] = mm_nt(
                    d_qkv[rows, :], w_attn[feats, pl.ds(side * attn_cols, 4 * HEAD_DIM)]
                ).astype(low)

    into_first(1)
    scatter_first.send_other()
    into_first(0)
    scatter_first.send_own()
    load.wait()

    def attention_grad(index, store):
        @pl.loop(0, 4)
        def _(i):
            cols = pl.ds(pl.multiple_of(index * rows_all + i * 256, 256), 256)
            rows = pl.ds(pl.multiple_of(i * 256, 256), 256)
            store[rows, 0 : 4 * HEAD_DIM] = mm_tn(second[:, cols], d_qkv[...]).astype(low)
            store[rows, 4 * HEAD_DIM :] = mm_tn(branch[:, cols], attended[...]).astype(low)

        copy = pltpu.make_async_copy(
            store, attn_grads.at[pl.ds(index * rows_all, rows_all)], local_sems.at[1 + index]
        )
        copy.start()
        stores.append(copy)

    attention_grad(0, hidden)
    scatter_first.step_one()
    attention_grad(1, d_gate)
    scatter_first.step_two()
    scatter_first.step_three()
    gain_rows = None
    for half in (1, 0):
        rows = pl.ds(half * HALF, HALF)
        d_first = scatter_first.total(half)
        back, gain_part = rms_backward(tokens[rows, :].astype(f32), gain_one[...], d_first)
        grad_tokens[rows, :] += back
        gain_part = jnp.sum(gain_part, axis=0, keepdims=True)
        gain_rows = gain_part if gain_rows is None else gain_rows + gain_part
    gains[1:2, :] = gain_rows

    for store in stores:
        store.wait()
    gather_branch.finish()
    scatter_first.finish()


def late_call(lengths, *args):
    width = args[0].shape[1]
    hid = args[-1].shape[0]
    rows = 8 * BLOCK
    vmem = pl.BlockSpec(memory_space=pltpu.VMEM)
    smem = pl.BlockSpec(memory_space=pltpu.SMEM)
    anywhere = pl.BlockSpec(memory_space=pl.ANY)
    copies = 3 * Gather.COPIES + 3 * Scatter.COPIES
    return pl.pallas_call(
        functools.partial(late_kernel, 1.0 / math.sqrt(HEAD_DIM)),
        name="late",
        out_shape=[
            jax.ShapeDtypeStruct((BLOCK, width), f32),
            jax.ShapeDtypeStruct((BLOCK, width), f32),
            jax.ShapeDtypeStruct((8, width), f32),
            jax.ShapeDtypeStruct((width, 6 * HEAD_DIM), low),
            jax.ShapeDtypeStruct((3, hid, width), low),
        ],
        in_specs=[smem] + [vmem] * (len(args) - 6) + [anywhere] * 6,
        out_specs=[vmem] * 3 + [anywhere] * 2,
        scratch_shapes=[
            pltpu.VMEM((rows, width), low),
            pltpu.VMEM((rows, width), low),
            pltpu.VMEM((rows, width), low),
            pltpu.VMEM((hid, width), low),
            pltpu.VMEM((hid, width), low),
            pltpu.VMEM((hid, width), low),
            pltpu.VMEM((rows, hid), low),
            pltpu.VMEM((rows, hid), low),
            pltpu.VMEM((rows, hid), low),
            pltpu.VMEM((rows, width), low),
            pltpu.VMEM((rows, width), low),
            pltpu.VMEM((rows, 2 * HEAD_DIM), low),
            pltpu.VMEM((rows, HEAD_DIM), f32),
            pltpu.VMEM((rows, HEAD_DIM), f32),
            pltpu.VMEM((rows, 4 * HEAD_DIM), low),
            pltpu.VMEM((2, 256, width), low),
        ]
        + Scatter.scratch(width)
        + Scatter.scratch(width)
        + [
            pltpu.SemaphoreType.DMA((3,)),
            pltpu.SemaphoreType.DMA((2,)),
            pltpu.SemaphoreType.DMA((copies,)),
            pltpu.SemaphoreType.DMA((copies,)),
        ],
        compiler_params=pltpu.CompilerParams(
            collective_id=1, has_side_effects=True, vmem_limit_bytes=60 << 20
        ),
        cost_estimate=pl.CostEstimate(
            flops=36_000_000_000, bytes_accessed=60_000_000, transcendentals=4_000_000
        ),
    )(lengths, *args)


def rms_scale(values, gain):
    return values * lax.rsqrt(jnp.mean(values * values, axis=-1, keepdims=True) + epsilon) * gain


def rotate(values, positions):
    half_dim = values.shape[-1] // 2
    frequency = theta_base ** (-jnp.arange(half_dim, dtype=jnp.float32) * (2.0 / values.shape[-1]))
    angles = positions.astype(jnp.float32)[:, None] * frequency[None, :]
    cosine = jnp.cos(angles)[:, None, :]
    sine = jnp.sin(angles)[:, None, :]
    first_half = values[..., :half_dim]
    second_half = values[..., half_dim:]
    return jnp.concatenate(
        [first_half * cosine - second_half * sine, second_half * cosine + first_half * sine],
        axis=-1,
    )


def segment_info(lengths_row, indices):
    start_one = lengths_row[0]
    start_two = lengths_row[0] + lengths_row[1]
    segment = (indices >= start_one).astype(jnp.int32) + (indices >= start_two).astype(jnp.int32)
    begin = jnp.where(segment == 0, 0, jnp.where(segment == 1, start_one, start_two))
    return (segment, indices - begin)


def dot(left, right):
    return jnp.dot(left, right, preferred_element_type=jnp.float32)


def contract_rows(left, right):
    return lax.dot_general(
        left, right, (((1,), (1,)), ((), ())), preferred_element_type=jnp.float32
    )


def contract_first(left, right):
    return lax.dot_general(
        left, right, (((0,), (0,)), ((), ())), preferred_element_type=jnp.float32
    )


def gather(x):
    return lax.all_gather(x, "shard", axis=0, tiled=True)


def scatter_sum(x):
    return lax.psum_scatter(
        x.astype(jnp.bfloat16), "shard", scatter_dimension=0, tiled=True
    ).astype(jnp.float32)


def per_device(
    tokens,
    cotangent,
    lengths,
    attn_gain,
    mlp_gain,
    query_gain,
    key_gain,
    w_query,
    w_key,
    w_value,
    w_out,
    w_gate,
    w_up,
    w_down,
):
    tok_rows, width = tokens.shape
    shards = lax.axis_size("shard")
    rows = tok_rows * shards
    group = HEADS // KV_HEADS
    feat = width // shards
    scale = 1.0 / math.sqrt(HEAD_DIM)
    my_shard = lax.axis_index("shard")
    index = jnp.arange(rows, dtype=jnp.int32)
    segment, position = segment_info(lengths[0], index)
    visible = (segment[:, None] == segment[None, :]) & (index[None, :] <= index[:, None])

    q_cols = w_query.shape[1] // shards
    k_cols = w_key.shape[1] // shards
    packed = jnp.concatenate(
        [
            w_query.reshape(feat, shards, q_cols),
            w_key.reshape(feat, shards, k_cols),
            w_value.reshape(feat, shards, k_cols),
            w_out.reshape(feat, shards, q_cols),
        ],
        axis=2,
    )
    mine = lax.all_to_all(packed, "shard", split_axis=1, concat_axis=0, tiled=True).reshape(
        width, -1
    )
    qkv_cols = q_cols + 2 * k_cols
    w_qkv = mine[:, :qkv_cols]
    w_o = mine[:, qkv_cols:]

    gains_rows = jnp.concatenate(
        [attn_gain, mlp_gain, jnp.zeros((width - 2 * feat,), low)]
    ).reshape(1, width)
    gathered = gather(
        jnp.concatenate([tokens, jnp.broadcast_to(gains_rows, (16, width))], axis=0)
    ).reshape(shards, tok_rows + 16, width)
    tokens_all = gathered[:, :tok_rows].reshape(rows, width)
    gain_one = gathered[:, tok_rows, :feat].reshape(width).astype(jnp.float32)
    gain_two = gathered[:, tok_rows, feat : 2 * feat].reshape(width).astype(jnp.float32)

    inputs = tokens.astype(jnp.float32)
    first = rms_scale(tokens_all.astype(jnp.float32), gain_one).astype(low)
    proj = dot(first, w_qkv)

    def prepare(projected, gain, count):
        return rotate(rms_scale(projected.reshape(rows, count, HEAD_DIM), gain), position)

    q_rot = prepare(proj[:, :q_cols], query_gain.astype(f32), group)
    k_rot = prepare(proj[:, q_cols : q_cols + k_cols], key_gain.astype(f32), 1)
    query = q_rot.astype(low)
    key = k_rot.astype(low)[:, 0]
    value = proj[:, q_cols + k_cols :].astype(low)
    scores = jnp.einsum("tgd,sd->gts", query, key, preferred_element_type=jnp.float32) * scale
    masked = jnp.where(visible[None], scores, masked_value)
    top = jnp.max(masked, axis=-1, keepdims=True)
    total = jnp.log(jnp.sum(jnp.exp(masked - top), axis=-1, keepdims=True)) + top
    weights = jnp.exp(masked - total)
    probs = weights.astype(low)
    attended = (
        jnp.einsum("gts,sd->tgd", probs, value, preferred_element_type=jnp.float32)
        .reshape(rows, q_cols)
        .astype(low)
    )
    resid = inputs + scatter_sum(contract_rows(attended, w_o))
    half = HEAD_DIM // 2
    frequency = theta_base ** (-jnp.arange(half, dtype=f32) * (2.0 / HEAD_DIM))
    angles = position.astype(f32)[:, None] * frequency[None, :]
    cosine = jnp.concatenate([jnp.cos(angles)] * 2, axis=1)
    sine = jnp.concatenate([-jnp.sin(angles), jnp.sin(angles)], axis=1)
    kept = jnp.concatenate(
        [
            proj[:, : q_cols + k_cols],
            total[0],
            total[1],
            jnp.zeros((rows, HEAD_DIM - 2), f32),
        ],
        axis=1,
    )
    result, grad_tokens, gain_parts, attn_grads, ffn_grads = late_call(
        lengths,
        resid,
        cotangent,
        tokens,
        gain_one[None],
        gain_two[None],
        query_gain.astype(f32)[None],
        key_gain.astype(f32)[None],
        kept,
        cosine,
        sine,
        mine,
        jnp.concatenate([query.reshape(rows, q_cols), key, value, attended], axis=1),
        first,
        w_gate,
        w_up,
        w_down,
    )
    ffn_grads = lax.psum(ffn_grads, "rep").astype(f32)
    attn_grads = lax.psum(attn_grads, "rep")
    attn_grads = lax.all_to_all(
        attn_grads.reshape(shards, feat, -1), "shard", split_axis=0, concat_axis=1, tiled=True
    ).reshape(shards, feat, -1).transpose(1, 0, 2).astype(f32)
    grad_query = attn_grads[:, :, :q_cols].reshape(feat, -1)
    grad_key = attn_grads[:, :, q_cols : q_cols + k_cols].reshape(feat, -1)
    grad_value = attn_grads[:, :, q_cols + k_cols : qkv_cols].reshape(feat, -1)
    grad_out = attn_grads[:, :, qkv_cols:].reshape(feat, -1)
    gains = lax.psum(
        jnp.concatenate([gain_parts[1], gain_parts[0], gain_parts[2, : 2 * HEAD_DIM]]),
        ("rep", "shard"),
    )
    head_piece = HEAD_DIM // shards
    gains_first = lax.dynamic_slice_in_dim(gains, my_shard * feat, feat, 0)
    gains_second = lax.dynamic_slice_in_dim(gains, width + my_shard * feat, feat, 0)
    gains_query = lax.dynamic_slice_in_dim(gains, 2 * width + my_shard * head_piece, head_piece, 0)
    gains_key = lax.dynamic_slice_in_dim(
        gains, 2 * width + HEAD_DIM + my_shard * head_piece, head_piece, 0
    )
    return (
        result,
        grad_tokens,
        grad_query,
        grad_key,
        grad_value,
        grad_out,
        ffn_grads[0],
        ffn_grads[1],
        ffn_grads[2],
        gains_first,
        gains_second,
        gains_query,
        gains_key,
    )


def solution(mesh):
    spread = P(("rep", "shard"), None)
    rowed = P("shard", None)
    return jax.shard_map(
        per_device,
        mesh=mesh,
        in_specs=(spread, spread, P("rep", None), P("shard"), P("shard"), P(), P()) + (rowed,) * 7,
        out_specs=(spread, spread) + (rowed,) * 7 + (P("shard"),) * 4,
        check_vma=False,
    )
```

```python
import functools
import math

import jax
import jax.numpy as jnp
from jax import lax
from jax.experimental import pallas as pl
from jax.experimental.pallas import tpu as pltpu
from jax.sharding import PartitionSpec as P

HEADS = 16
KV_HEADS = 8
HEAD_DIM = 128

epsilon = 1e-06
theta_base = 1000000.0
masked_value = -1e30


MESH = pl.DeviceIdType.MESH
BLOCK = 128
HALF = 64
LINE = 512
low = jnp.bfloat16
f32 = jnp.float32


def mm(left, right):
    return lax.dot_general(left, right, (((1,), (0,)), ((), ())), preferred_element_type=f32)


def mm_nt(left, right):
    return lax.dot_general(left, right, (((1,), (1,)), ((), ())), preferred_element_type=f32)


def mm_tn(left, right):
    return lax.dot_general(left, right, (((0,), (0,)), ((), ())), preferred_element_type=f32)


class Place:
    def __init__(self):
        self.rep = lax.axis_index("rep")
        self.shard = lax.axis_index("shard")
        self.yl, self.z = self.shard // 4, self.shard % 4
        self.yh, self.x, self.core = self.rep // 8, (self.rep // 2) % 4, self.rep % 2

    def block(self, dy, dz):
        return ((self.yl + dy + 2) % 2) * 4 + (self.z + dz + 8) % 4

    def dev(self, dy, dz):
        return (self.rep, self.block(dy, dz))

    def x_at(self, dx):
        return (self.x + dx + 8) % 4

    def rep_dev(self, dyh, dx, dcore):
        rep = ((self.yh + dyh) % 2) * 8 + self.x_at(dx) * 2 + (self.core + dcore) % 2
        return (rep, self.shard)

    def rows(self, dy, dz, start=0, count=BLOCK):
        return pl.ds(pl.multiple_of(self.block(dy, dz) * BLOCK + start, 32), count)

    def line(self, dy):
        return pl.multiple_of(((self.yl + dy + 2) % 2) * LINE, LINE)

    def shard_peers(self):
        return [self.dev(dy, dz) for dy in range(2) for dz in range(4) if dy or dz]

    def rep_peers(self):
        return [
            self.rep_dev(*by) for by in ((0, 0, 1), (0, 1, 0), (0, 2, 0), (0, 3, 0), (1, 0, 0))
        ]

    def greet(self):
        barrier = pltpu.get_barrier_semaphore()
        peers = self.shard_peers() + self.rep_peers()
        for peer in peers:
            pl.semaphore_signal(barrier, inc=1, device_id=peer, device_id_type=MESH)
        pl.semaphore_wait(barrier, len(peers))


class Net:
    def __init__(self, send_sems, recv_sems):
        self.send_sems, self.recv_sems = send_sems, recv_sems
        self.started, self.coming = [], {}

    def send(self, tag, src, dst, dev, here):
        k = len(self.started)
        copy = pltpu.make_async_remote_copy(
            src_ref=src,
            dst_ref=dst,
            send_sem=self.send_sems.at[k],
            recv_sem=self.recv_sems.at[k],
            device_id=dev,
            device_id_type=MESH,
        )
        copy.start()
        self.started.append(copy)
        self.coming[tag] = (k, here, dev)

    def wait(self, tag):
        k, here, dev = self.coming.pop(tag)
        pltpu.make_async_remote_copy(
            src_ref=here,
            dst_ref=here,
            send_sem=self.send_sems.at[k],
            recv_sem=self.recv_sems.at[k],
            device_id=dev,
            device_id_type=MESH,
        ).wait_recv()

    def finish(self):
        for tag in list(self.coming):
            self.wait(tag)
        for copy in self.started:
            copy.wait_send()


class Gather:
    COPIES = 18

    def __init__(self, place, buf, send_sems, recv_sems):
        self.place, self.buf = place, buf
        self.net = Net(send_sems, recv_sems)

    def send(self, tag, block, start, count, to):
        rows = self.place.rows(*block, start, count)
        here = self.place.rows(block[0] - to[0], block[1] - to[1], start, count)
        self.net.send(
            tag, self.buf.at[rows], self.buf.at[rows], self.place.dev(*to), self.buf.at[here]
        )

    def start(self):
        self.send("y_up", (0, 0), 0, HALF, (1, 0))
        for d in (1, 3):
            self.send(f"z_low{d}", (0, 0), HALF, HALF, (0, d))
        self.send("y_low", (0, 0), HALF, HALF, (1, 0))

    def step_one(self):
        self.net.wait("y_up")
        for d in (1, 3):
            self.send(f"p_up{d}", (1, 0), 0, HALF, (0, d))

    def step_two(self):
        for e, d in enumerate((1, 3)):
            self.net.wait(f"z_low{d}")
            self.send(f"f_low{d}", (0, -d), HALF + 32 * e, 32, (0, d))
            self.send(f"q_low{d}", (0, -d), HALF, HALF, (1, 0))
        for d in (1, 3):
            self.send(f"z_up{d}", (0, 0), 0, HALF, (0, d))

    def step_three(self):
        for e, d in enumerate((1, 3)):
            self.net.wait(f"p_up{d}")
            self.send(f"f_p{d}", (1, -d), 32 * e, 32, (0, d))
        for e, d in enumerate((1, 3)):
            self.net.wait(f"f_low{d}")
            self.send(f"q_far{d}", (0, -2 * d), HALF + 32 * e, 32, (1, 0))

    def step_four(self):
        for e, d in enumerate((1, 3)):
            self.net.wait(f"z_up{d}")
            self.send(f"f_up{d}", (0, -d), 32 * e, 32, (0, d))

    def own_line(self):
        for d in (1, 3):
            self.net.wait(f"f_up{d}")

    def other_line(self):
        for tag in list(self.net.coming):
            self.net.wait(tag)

    def steps(self):
        return [self.start, self.step_one, self.step_two, self.step_three, self.step_four]

    def finish(self):
        self.net.finish()


class Scatter:
    COPIES = 17

    @staticmethod
    def scratch(columns):
        return [
            pltpu.VMEM((4, HALF, columns), low),
            pltpu.VMEM((3, 2, 32, columns), low),
            pltpu.VMEM((3, 2, HALF, columns), low),
            pltpu.VMEM((HALF, columns), low),
        ]

    def __init__(self, place, part, across, near, far, last, send_sems, recv_sems):
        self.place, self.part = place, part
        self.across, self.near, self.far, self.last = across, near, far, last
        self.net = Net(send_sems, recv_sems)

    def add(self, rows, *refs):
        total = self.part[rows, :].astype(f32)
        for ref in refs:
            total = total + ref[...].astype(f32)
        self.part[rows, :] = total.astype(low)

    def first(self, kind):
        dy, start = ((1, 0), (0, 0), (0, HALF))[kind]
        for e, d in enumerate((1, 3)):
            src = self.part.at[self.place.rows(dy, 2, start + 32 * e, 32)]
            dst = self.near.at[kind, e]
            self.net.send(f"near{kind}{e}", src, dst, self.place.dev(0, d), dst)

    def second(self, kind):
        dy, start = ((1, 0), (0, 0), (0, HALF))[kind]
        for e, d in enumerate((1, 3)):
            self.net.wait(f"near{kind}{e}")
            self.add(self.place.rows(dy, d, start + 32 * e, 32), self.near.at[kind, e])
            src = self.part.at[self.place.rows(dy, d, start, HALF)]
            dst = self.far.at[kind, e]
            self.net.send(f"far{kind}{e}", src, dst, self.place.dev(0, d), dst)

    def send_other(self):
        for d in (2, 1, 3, 0):
            src = self.part.at[self.place.rows(1, d, HALF, HALF)]
            dst = self.across.at[d]
            self.net.send(f"across{d}", src, dst, self.place.dev(1, 0), dst)
        self.first(0)

    def send_own(self):
        self.first(1)

    def step_one(self):
        self.net.wait("across2")
        self.add(self.place.rows(0, 2, HALF, HALF), self.across.at[2])
        self.first(2)
        self.second(0)
        self.second(1)

    def step_two(self):
        for d in (1, 3):
            self.net.wait(f"across{d}")
            self.add(self.place.rows(0, d, HALF, HALF), self.across.at[d])
        self.second(2)

    def step_three(self):
        for e in range(2):
            self.net.wait(f"far0{e}")
        rows = self.place.rows(1, 0, 0, HALF)
        self.add(rows, self.far.at[0, 0], self.far.at[0, 1])
        self.net.send("last", self.part.at[rows], self.last, self.place.dev(1, 0), self.last)

    def total(self, half):
        if half == 0:
            tags, extra, kind = ("far10", "far11", "last"), self.last, 1
        else:
            tags, extra, kind = ("far20", "far21", "across0"), self.across.at[0], 2
        for tag in tags:
            self.net.wait(tag)
        out = self.part[self.place.rows(0, 0, half * HALF, HALF), :].astype(f32)
        for ref in (self.far.at[kind, 0], self.far.at[kind, 1], extra):
            out = out + ref[...].astype(f32)
        return out

    def finish(self):
        self.net.finish()


def add_rows(into, start, count, *refs):
    step = 64 if count % 64 == 0 else 48

    @pl.loop(0, count // step)
    def _(i):
        at = pl.multiple_of(i * step, 16)
        rows = pl.ds(pl.multiple_of(start + at, 16), step)
        total = into[rows, :].astype(f32)
        for ref in refs:
            total = total + ref[pl.ds(at, step), :].astype(f32)
        into[rows, :] = total.astype(low)


class RepSum:
    COPIES = 15

    def __init__(self, place, sems, own, other, landed, near, far, cross, out, unit, out_unit):
        self.place, self.net = place, Net(*sems)
        self.own, self.other, self.landed = own, other, landed
        self.near, self.far, self.cross = near, far, cross
        self.out, self.unit, self.out_unit = out, unit, out_unit

    def chunk(self, dx, start=0, count=None):
        at = self.place.x_at(dx) * 2 * self.unit + start
        return pl.ds(pl.multiple_of(at, 16), 2 * self.unit if count is None else count)

    def out_rows(self, dcore, dx, start=0, count=None):
        core = (self.place.core + dcore) % 2
        at = (core * 8 + self.place.x_at(dx) * 2 + start) * self.out_unit
        count = (2 if count is None else count) * self.out_unit
        return self.out.at[pl.ds(pl.multiple_of(at, 16), count)]

    def core_send(self):
        self.net.send("core", self.other, self.landed, self.place.rep_dev(0, 0, 1), self.landed)

    def x_first(self, load=None):
        self.net.wait("core")
        add_rows(self.own, 0, 8 * self.unit, self.landed if load is None else load())
        for e, d in enumerate((1, 3)):
            src = self.own.at[self.chunk(2, e * self.unit, self.unit)]
            dst = self.near[e]
            self.net.send(f"near{e}", src, dst, self.place.rep_dev(0, d, 0), dst)

    def x_second(self):
        for e, d in enumerate((1, 3)):
            self.net.wait(f"near{e}")
            add_rows(self.own, self.place.x_at(d) * 2 * self.unit + e * self.unit, self.unit, self.near[e])
            dst = self.far[e]
            self.net.send(
                f"far{e}", self.own.at[self.chunk(d)], dst, self.place.rep_dev(0, d, 0), dst
            )

    def y_send(self):
        for e in range(2):
            self.net.wait(f"far{e}")
        add_rows(self.own, self.place.x * 2 * self.unit, 2 * self.unit, *self.far)
        src = self.own.at[self.chunk(0, (1 - self.place.yh) * self.unit, self.unit)]
        self.net.send("cross", src, self.cross, self.place.rep_dev(1, 0, 0), self.cross)

    def piece(self):
        self.net.wait("cross")
        at = (self.place.x * 2 + self.place.yh) * self.unit
        add_rows(self.own, at, self.unit, self.cross)
        return self.own.at[pl.ds(pl.multiple_of(at, 16), self.unit)]

    def y_gather(self, piece, sem):
        mine = self.out_rows(0, 0, self.place.yh, 1)
        copy = pltpu.make_async_copy(piece, mine, sem)
        copy.start()
        self.net.send(
            "y", piece, mine, self.place.rep_dev(1, 0, 0), self.out_rows(0, 0, 1 - self.place.yh, 1)
        )
        copy.wait()

    def to_core(self, dx):
        rows = self.out_rows(0, dx)
        self.net.send(
            f"core{dx}", rows, rows, self.place.rep_dev(0, 0, 1), self.out_rows(1, dx)
        )

    def x_gather(self):
        self.net.wait("y")
        rows = self.out_rows(0, 0)
        for d in (1, 3):
            self.net.send(f"x{d}", rows, rows, self.place.rep_dev(0, d, 0), self.out_rows(0, -d))
        self.to_core(0)

    def x_forward(self):
        for e, d in enumerate((1, 3)):
            self.net.wait(f"x{d}")
            rows = self.out_rows(0, -d, e, 1)
            self.net.send(
                f"xx{d}", rows, rows, self.place.rep_dev(0, d, 0), self.out_rows(0, -2 * d, e, 1)
            )
            self.to_core(-d)

    def x_last(self):
        for d in (1, 3):
            self.net.wait(f"xx{d}")
        self.to_core(2)

    def finish(self):
        self.net.finish()


def rms_backward(value, gain, upstream):
    root = lax.rsqrt(jnp.mean(value * value, axis=-1, keepdims=True) + epsilon)
    pulled = upstream * gain
    back = root * pulled - value * (root * root * root) * jnp.mean(
        pulled * value, axis=-1, keepdims=True
    )
    return back, upstream * (value * root)


def swap_halves(value):
    return pltpu.roll(value, HEAD_DIM // 2, 1)


def late_kernel(
    scale,
    lengths,
    resid,
    cotangent,
    tokens,
    gain_one,
    gain_two,
    query_gain,
    key_gain,
    proj,
    cosine,
    sine,
    w_attn_hbm,
    heads_hbm,
    first_hbm,
    w_gate_hbm,
    w_up_hbm,
    w_down_hbm,
    result,
    grad_tokens,
    gains,
    attn_grads,
    ffn_grads,
    core_landed,
    second,
    cot_all,
    branch,
    w_gate,
    w_up,
    w_down,
    pair,
    d_up,
    part_out,
    part_back,
    d_att,
    d_key,
    d_value,
    d_qkv,
    staged,
    across,
    near,
    far,
    last,
    swapped,
    assembled,
    gain_sums,
    gain_landed,
    free_sem,
    core_free_sem,
    landing_free,
    heads_free,
    local_sems,
    send_sems,
    recv_sems,
):
    place = Place()
    hidden = pair.at[pl.ds(0, 8 * BLOCK)]
    d_gate = pair.at[pl.ds(8 * BLOCK, 8 * BLOCK)]
    rows_all = 8 * BLOCK
    hid = w_gate.shape[0]
    width = second.shape[1]

    loads = [
        pltpu.make_async_copy(src, dst, local_sems.at[i])
        for i, (src, dst) in enumerate(
            ((w_gate_hbm, w_gate), (w_up_hbm, w_up), (w_down_hbm, w_down))
        )
    ]
    for load in loads:
        load.start()

    used = [0]

    def sems(count):
        at = used[0]
        used[0] += count
        return send_sems.at[pl.ds(at, count)], recv_sems.at[pl.ds(at, count)]

    own = place.rows(0, 0)
    root = lax.rsqrt(jnp.mean(resid[...] * resid[...], axis=-1, keepdims=True) + epsilon)
    second[own, :] = (resid[...] * root * gain_two[...]).astype(low)
    cot_all[own, :] = cotangent[...].astype(low)
    place.greet()
    gather_second = Gather(place, second, *sems(Gather.COPIES))
    gather_cot = Gather(place, cot_all, *sems(Gather.COPIES))
    gather_branch = Gather(place, branch, *sems(Gather.COPIES))
    landing = (across, near, far, last)
    scatter_out = Scatter(place, part_out, *landing, *sems(Scatter.COPIES))
    scatter_back = Scatter(place, part_back, *landing, *sems(Scatter.COPIES))

    def feed_forward(dy):
        rows = pl.ds(place.line(dy), LINE)

        @pl.loop(0, hid // 256)
        def _(i):
            cols = pl.ds(pl.multiple_of(i * 256, 256), 256)
            gate = mm_nt(second[rows, :], w_gate[cols, :])
            up = mm_nt(second[rows, :], w_up[cols, :])
            sigma = 1.0 / (1.0 + jnp.exp(-gate))
            silu = gate * sigma
            hidden[rows, cols] = (silu * up).astype(low)
            d_gate[rows, cols] = (up * sigma * (1.0 + gate * (1.0 - sigma))).astype(low)
            d_up[rows, cols] = silu.astype(low)

    def project_out(dy):
        rows = pl.ds(place.line(dy), LINE)

        @pl.loop(0, width // 512)
        def _(i):
            cols = pl.ds(pl.multiple_of(i * 512, 512), 512)
            part_out[rows, cols] = mm(hidden[rows, :], w_down[:, cols]).astype(low)

    def feed_backward(dy):
        rows = pl.ds(place.line(dy), LINE)

        @pl.loop(0, hid // 256)
        def _(i):
            cols = pl.ds(pl.multiple_of(i * 256, 256), 256)
            d_hidden = mm_nt(cot_all[rows, :], w_down[cols, :])
            d_gate[rows, cols] = (d_hidden * d_gate[rows, cols].astype(f32)).astype(low)
            d_up[rows, cols] = (d_hidden * d_up[rows, cols].astype(f32)).astype(low)

        @pl.loop(0, width // 512)
        def _(i):
            cols = pl.ds(pl.multiple_of(i * 512, 512), 512)
            part_back[rows, cols] = (
                mm(d_gate[rows, :], w_gate[:, cols]) + mm(d_up[rows, :], w_up[:, cols])
            ).astype(low)

    def weight_grad(into, left, right):
        @pl.loop(0, hid // 256)
        def _(i):
            cols = pl.ds(pl.multiple_of(i * 256, 256), 256)
            into[cols, :] = mm_tn(left[:, cols], right[...]).astype(low)

    unit = hid // 16
    sums = []
    for i, whole in enumerate((w_gate, w_up, w_down)):
        base = i * 7 * unit

        def view(start, count, base=base):
            return second.at[pl.ds(base + start * unit, count * unit)]

        sums.append(
            RepSum(
                place,
                sems(RepSum.COPIES),
                whole.at[pl.ds(pl.multiple_of(place.core * 8 * unit, 16), 8 * unit)],
                whole.at[pl.ds(pl.multiple_of((1 - place.core) * 8 * unit, 16), 8 * unit)],
                core_landed.at[i],
                [view(0, 1), view(1, 1)],
                [view(2, 2), view(4, 2)],
                view(6, 1),
                ffn_grads.at[i],
                unit,
                unit,
            )
        )
    sum_gate, sum_up, sum_down = sums

    def load_landed(i):
        def load():
            here = staged.at[pl.ds(0, 8 * unit)]
            copy = pltpu.make_async_copy(core_landed.at[i], here, local_sems.at[3])
            copy.start()
            copy.wait()
            return here

        return load

    for step in gather_second.steps():
        step()
    gather_second.own_line()
    gather_cot.start()
    for load in loads:
        load.wait()
    feed_forward(0)
    gather_cot.step_one()
    gather_cot.step_two()
    gather_second.other_line()
    feed_forward(1)
    gather_cot.step_three()
    gather_cot.step_four()
    project_out(1)
    project_out(0)
    gather_cot.own_line()
    gather_cot.other_line()
    feed_backward(1)
    scatter_back.send_other()
    feed_backward(0)
    scatter_back.send_own()
    weight_grad(w_gate, d_gate, second)
    sum_gate.core_send()
    scatter_back.step_one()
    weight_grad(w_up, d_up, second)
    sum_up.core_send()
    gather_second.finish()
    for by in ((0, 1, 0), (0, 3, 0), (1, 0, 0)):
        pl.semaphore_signal(
            free_sem, inc=1, device_id=place.rep_dev(*by), device_id_type=MESH
        )
    scatter_back.step_two()
    weight_grad(w_down, hidden, cot_all)
    sum_down.core_send()
    pl.semaphore_wait(free_sem, 3)
    sum_gate.x_first(load_landed(0))
    sum_up.x_first(load_landed(1))
    gather_cot.finish()
    heads = d_up
    q_cols = 2 * HEAD_DIM
    query = heads.at[:, pl.ds(0, q_cols)]
    key = heads.at[:, pl.ds(q_cols, HEAD_DIM)]
    value = heads.at[:, pl.ds(q_cols + HEAD_DIM, HEAD_DIM)]
    attended = heads.at[:, pl.ds(q_cols + 2 * HEAD_DIM, q_cols)]
    w_attn = cot_all
    attn_cols = heads.shape[1]
    loads = [
        pltpu.make_async_copy(heads_hbm, heads, local_sems.at[0]),
        pltpu.make_async_copy(
            w_attn_hbm.at[pl.ds(0, rows_all)],
            w_attn.at[:, pl.ds(0, attn_cols)],
            local_sems.at[1],
        ),
        pltpu.make_async_copy(
            w_attn_hbm.at[pl.ds(rows_all, rows_all)],
            w_attn.at[:, pl.ds(attn_cols, attn_cols)],
            local_sems.at[2],
        ),
    ]
    for load in loads:
        load.start()
    scatter_back.step_three()
    gain_rows = None
    for half in (1, 0):
        rows = pl.ds(half * HALF, HALF)
        d_second = scatter_back.total(half)
        back, gain_part = rms_backward(resid[rows, :], gain_two[...], d_second)
        grad_tokens[rows, :] = cotangent[rows, :] + back
        gain_part = jnp.sum(gain_part, axis=0, keepdims=True)
        gain_rows = gain_part if gain_rows is None else gain_rows + gain_part
    gain_sums[0] = jnp.zeros_like(gain_sums[0])

    def keep_gain(first_row, value):
        for i in range(value.shape[1] // HEAD_DIM):
            gain_sums[0, first_row + i : first_row + i + 1, :] = value[
                :, i * HEAD_DIM : (i + 1) * HEAD_DIM
            ]

    gain_slots = width // HEAD_DIM
    keep_gain(gain_slots, gain_rows)
    branch[own, :] = grad_tokens[...].astype(low)
    gather_branch.start()
    sum_down.x_first(load_landed(2))
    gather_branch.step_one()
    sum_gate.x_second()
    gather_branch.step_two()
    scatter_out.send_other()
    scatter_out.send_own()
    sum_up.x_second()
    gather_branch.step_three()
    gather_branch.step_four()
    sum_down.x_second()
    gather_branch.own_line()
    for load in loads:
        load.wait()

    def into_attention(dy):
        rows = pl.ds(place.line(dy), LINE)
        d_att[rows, :] = (
            mm(branch[rows, 0:rows_all], w_attn[:, 4 * HEAD_DIM : attn_cols])
            + mm(branch[rows, rows_all:], w_attn[:, attn_cols + 4 * HEAD_DIM : 2 * attn_cols])
        ).astype(low)

    into_attention(0)
    gather_branch.other_line()
    into_attention(1)

    def unrotate(rows, upstream, projected, gain):
        turned = upstream * cosine[rows, :] - swap_halves(upstream) * sine[rows, :]
        return rms_backward(projected, gain, turned)

    gain_rows = jnp.zeros((1, HEAD_DIM), f32)
    start_one = lengths[0, 0]
    start_two = lengths[0, 0] + lengths[0, 1]
    d_key[...] = jnp.zeros_like(d_key)
    d_value[...] = jnp.zeros_like(d_value)
    chunk = 256
    scatter_out.step_one()
    for part in range(rows_all // chunk):
        rows = pl.ds(part * chunk, chunk)
        seen = (part + 1) * chunk
        token = part * chunk + lax.broadcasted_iota(jnp.int32, (chunk, 1), 0)
        source = lax.broadcasted_iota(jnp.int32, (1, seen), 1)
        begin = jnp.where(
            token >= start_two, start_two, jnp.where(token >= start_one, start_one, 0)
        )
        visible = (source >= begin) & (source <= token)
        for g in range(2):
            lanes = pl.ds(g * HEAD_DIM, HEAD_DIM)
            scores = mm_nt(query[rows, lanes], key[0:seen, :]) * scale
            weights = jnp.where(visible, jnp.exp(scores - proj[rows, 3 * HEAD_DIM + g : 3 * HEAD_DIM + g + 1]), 0.0)
            d_probs = mm_nt(d_att[rows, lanes], value[0:seen, :])
            inner = jnp.sum(weights * d_probs, axis=-1, keepdims=True)
            d_scores = (weights * (d_probs - inner)).astype(low)
            back, gain_part = unrotate(
                rows, mm(d_scores, key[0:seen, :]) * scale, proj[rows, lanes], query_gain[...]
            )
            d_qkv[rows, lanes] = back.astype(low)
            gain_rows = gain_rows + jnp.sum(gain_part, axis=0, keepdims=True)
            d_key[0:seen, :] += mm_tn(d_scores, query[rows, lanes])
            d_value[0:seen, :] += mm_tn(weights.astype(low), d_att[rows, lanes])
        if part == 0:
            sum_gate.y_send()
        if part == 1:
            scatter_out.step_two()
            sum_up.y_send()
            sum_gate.y_gather(sum_gate.piece(), local_sems.at[3])
        if part == 2:
            scatter_out.step_three()
            sum_down.y_send()
            sum_up.y_gather(sum_up.piece(), local_sems.at[3])
            sum_gate.x_gather()
    d_qkv[:, 3 * HEAD_DIM :] = d_value[...].astype(low)

    keep_gain(2 * gain_slots, gain_rows)
    lanes = pl.ds(2 * HEAD_DIM, HEAD_DIM)
    back, gain_part = unrotate(pl.ds(0, rows_all), d_key[...] * scale, proj[:, lanes], key_gain[...])
    d_qkv[:, lanes] = back.astype(low)
    keep_gain(2 * gain_slots + 1, jnp.sum(gain_part, axis=0, keepdims=True))

    scatter_back.finish()
    scatter_first = Scatter(place, part_back, *landing, *sems(Scatter.COPIES))
    for half in (0, 1):
        rows = pl.ds(half * HALF, HALF)
        result[rows, :] = resid[rows, :] + scatter_out.total(half)
    scatter_out.finish()
    for by in ((1, 0), (0, 1), (0, 3)):
        pl.semaphore_signal(landing_free, inc=1, device_id=place.dev(*by), device_id_type=MESH)
    load = pltpu.make_async_copy(first_hbm, part_out, local_sems.at[0])
    load.start()
    sum_down.y_gather(sum_down.piece(), local_sems.at[3])
    sum_up.x_gather()

    def into_first(dy):
        rows = pl.ds(place.line(dy), LINE)

        for side in range(2):

            @pl.loop(0, rows_all // 256)
            def _(i):
                feats = pl.ds(pl.multiple_of(i * 256, 256), 256)
                cols = pl.ds(pl.multiple_of(side * rows_all + i * 256, 256), 256)
                part_back[rows, cols] = mm_nt(
                    d_qkv[rows, :], w_attn[feats, pl.ds(side * attn_cols, 4 * HEAD_DIM)]
                ).astype(low)

    into_first(1)
    pl.semaphore_wait(landing_free, 3)
    scatter_first.send_other()
    into_first(0)
    scatter_first.send_own()
    for by in ((0, 1, 0), (0, 3, 0), (1, 0, 0)):
        pl.semaphore_signal(
            heads_free, inc=1, device_id=place.rep_dev(*by), device_id_type=MESH
        )
    head_landed = cot_all.at[:, pl.ds(0, 6 * HEAD_DIM)]
    load.wait()

    sum_attn = RepSum(
        place,
        sems(RepSum.COPIES),
        pair.at[pl.ds(pl.multiple_of(place.core * rows_all, BLOCK), rows_all)],
        pair.at[pl.ds(pl.multiple_of((1 - place.core) * rows_all, BLOCK), rows_all)],
        d_up,
        [head_landed.at[pl.ds(e * BLOCK, BLOCK)] for e in range(2)],
        [head_landed.at[pl.ds((1 + e) * 2 * BLOCK, 2 * BLOCK)] for e in range(2)],
        head_landed.at[pl.ds(6 * BLOCK, BLOCK)],
        attn_grads,
        BLOCK,
        16,
    )

    @pl.loop(0, width // 256)
    def _(i):
        cols = pl.ds(pl.multiple_of(i * 256, 256), 256)
        from_first = mm_tn(part_out[:, cols], d_qkv[...]).astype(low)
        from_branch = mm_tn(branch[:, cols], attended[...]).astype(low)
        for piece in range(16):
            rows = pl.ds(pl.multiple_of(piece * BLOCK + i * 16, 16), 16)
            pair[rows, 0 : 4 * HEAD_DIM] = from_first[piece * 16 : piece * 16 + 16, :]
            pair[rows, 4 * HEAD_DIM :] = from_branch[piece * 16 : piece * 16 + 16, :]

    pl.semaphore_signal(
        core_free_sem, inc=1, device_id=place.rep_dev(0, 0, 1), device_id_type=MESH
    )
    pl.semaphore_wait(core_free_sem, 1)
    sum_attn.core_send()
    scatter_first.step_one()
    sum_gate.x_forward()
    pl.semaphore_wait(heads_free, 3)
    sum_attn.x_first()
    scatter_first.step_two()
    sum_down.x_gather()
    sum_up.x_forward()
    scatter_first.step_three()
    sum_gate.x_last()
    sum_attn.x_second()
    gain_rows = None
    for half in (1, 0):
        rows = pl.ds(half * HALF, HALF)
        d_first = scatter_first.total(half)
        back, gain_part = rms_backward(tokens[rows, :].astype(f32), gain_one[...], d_first)
        grad_tokens[rows, :] += back
        gain_part = jnp.sum(gain_part, axis=0, keepdims=True)
        gain_rows = gain_part if gain_rows is None else gain_rows + gain_part
    keep_gain(0, gain_rows)

    gain_net = Net(*sems(9))
    stages = (
        [place.dev(0, d) for d in (1, 2, 3)],
        [place.dev(1, 0)],
        [place.rep_dev(0, 0, 1)],
        [place.rep_dev(0, d, 0) for d in (1, 2, 3)],
        [place.rep_dev(1, 0, 0)],
    )

    def gain_send(stage):
        for i, dev in enumerate(stages[stage]):
            dst = gain_landed.at[3 * stage + i]
            gain_net.send(f"{stage}.{i}", gain_sums.at[stage], dst, dev, dst)

    def gain_add(stage):
        total = gain_sums[stage]
        for i in range(len(stages[stage])):
            gain_net.wait(f"{stage}.{i}")
            total = total + gain_landed[3 * stage + i]
        gain_sums[stage + 1] = total

    gain_send(0)
    sum_attn.y_send()
    sum_down.x_forward()
    gain_add(0)
    gain_send(1)
    sum_up.x_last()
    piece = sum_attn.piece()
    swap_net = Net(*sems(7))
    for dy in range(2):
        for dz in range(4):
            if dy or dz:
                to = place.block(dy, dz)
                src = piece.at[pl.ds(pl.multiple_of(to * 16, 16), 16)]
                dst = swapped.at[pl.ds(pl.multiple_of(place.shard * 16, 16), 16)]
                here = place.block(-dy, -dz)
                here = swapped.at[pl.ds(pl.multiple_of(here * 16, 16), 16)]
                swap_net.send(f"{dy}{dz}", src, dst, place.dev(dy, dz), here)
    own_rows = pl.ds(pl.multiple_of(place.shard * 16, 16), 16)
    swapped[own_rows, :] = piece[own_rows, :]
    gain_add(1)
    gain_send(2)
    sum_down.x_last()
    swap_net.finish()
    kv = 8 * HEAD_DIM
    for j in range(8):
        rows = pl.ds(j * 16, 16)
        at = 0
        for begin, size in ((0, 2), (2, 1), (3, 1), (4, 2)):
            assembled[:, at + j * size * HEAD_DIM : at + (j + 1) * size * HEAD_DIM] = swapped[
                rows, begin * HEAD_DIM : (begin + size) * HEAD_DIM
            ]
            at += size * kv
    sum_attn.y_gather(assembled, local_sems.at[3])
    gain_add(2)
    gain_send(3)
    sum_attn.x_gather()
    gain_add(3)
    gain_send(4)
    sum_attn.x_forward()
    sum_attn.x_last()
    gain_add(4)
    gains[...] = gain_sums[5]

    gather_branch.finish()
    scatter_first.finish()
    for one in sums:
        one.finish()
    sum_attn.finish()
    gain_net.finish()


def late_call(lengths, *args):
    width = args[0].shape[1]
    hid = args[-1].shape[0]
    rows = 8 * BLOCK
    vmem = pl.BlockSpec(memory_space=pltpu.VMEM)
    smem = pl.BlockSpec(memory_space=pltpu.SMEM)
    anywhere = pl.BlockSpec(memory_space=pl.ANY)
    copies = 3 * Gather.COPIES + 3 * Scatter.COPIES + 4 * RepSum.COPIES + 9 + 7
    gain_shape = (2 * width // HEAD_DIM + 8, HEAD_DIM)
    return pl.pallas_call(
        functools.partial(late_kernel, 1.0 / math.sqrt(HEAD_DIM)),
        name="late",
        out_shape=[
            jax.ShapeDtypeStruct((BLOCK, width), f32),
            jax.ShapeDtypeStruct((BLOCK, width), f32),
            jax.ShapeDtypeStruct(gain_shape, f32),
            jax.ShapeDtypeStruct((256, 3 * width), low),
            jax.ShapeDtypeStruct((3, hid, width), low),
            jax.ShapeDtypeStruct((3, hid // 2, width), low),
        ],
        in_specs=[smem] + [vmem] * (len(args) - 6) + [anywhere] * 6,
        out_specs=[vmem] * 3 + [pl.BlockSpec(memory_space=pltpu.HBM)] * 3,
        scratch_shapes=[
            pltpu.VMEM((rows, width), low),
            pltpu.VMEM((rows, width), low),
            pltpu.VMEM((rows, width), low),
            pltpu.VMEM((hid, width), low),
            pltpu.VMEM((hid, width), low),
            pltpu.VMEM((hid, width), low),
            pltpu.VMEM((2 * rows, hid), low),
            pltpu.VMEM((rows, hid), low),
            pltpu.VMEM((rows, width), low),
            pltpu.VMEM((rows, width), low),
            pltpu.VMEM((rows, 2 * HEAD_DIM), low),
            pltpu.VMEM((rows, HEAD_DIM), f32),
            pltpu.VMEM((rows, HEAD_DIM), f32),
            pltpu.VMEM((rows, 4 * HEAD_DIM), low),
            pltpu.VMEM((hid // 2, width), low),
        ]
        + Scatter.scratch(width)
        + [
            pltpu.VMEM((BLOCK, 6 * HEAD_DIM), low),
            pltpu.VMEM((16, 3 * width), low),
            pltpu.VMEM((6,) + gain_shape, f32),
            pltpu.VMEM((15,) + gain_shape, f32),
            pltpu.SemaphoreType.REGULAR,
            pltpu.SemaphoreType.REGULAR,
            pltpu.SemaphoreType.REGULAR,
            pltpu.SemaphoreType.REGULAR,
            pltpu.SemaphoreType.DMA((4,)),
            pltpu.SemaphoreType.DMA((copies,)),
            pltpu.SemaphoreType.DMA((copies,)),
        ],
        compiler_params=pltpu.CompilerParams(
            collective_id=1, has_side_effects=True, vmem_limit_bytes=60 << 20
        ),
        cost_estimate=pl.CostEstimate(
            flops=36_000_000_000, bytes_accessed=60_000_000, transcendentals=4_000_000
        ),
    )(lengths, *args)


def rms_scale(values, gain):
    return values * lax.rsqrt(jnp.mean(values * values, axis=-1, keepdims=True) + epsilon) * gain


def rotate(values, positions):
    half_dim = values.shape[-1] // 2
    frequency = theta_base ** (-jnp.arange(half_dim, dtype=jnp.float32) * (2.0 / values.shape[-1]))
    angles = positions.astype(jnp.float32)[:, None] * frequency[None, :]
    cosine = jnp.cos(angles)[:, None, :]
    sine = jnp.sin(angles)[:, None, :]
    first_half = values[..., :half_dim]
    second_half = values[..., half_dim:]
    return jnp.concatenate(
        [first_half * cosine - second_half * sine, second_half * cosine + first_half * sine],
        axis=-1,
    )


def segment_info(lengths_row, indices):
    start_one = lengths_row[0]
    start_two = lengths_row[0] + lengths_row[1]
    segment = (indices >= start_one).astype(jnp.int32) + (indices >= start_two).astype(jnp.int32)
    begin = jnp.where(segment == 0, 0, jnp.where(segment == 1, start_one, start_two))
    return (segment, indices - begin)


def dot(left, right):
    return jnp.dot(left, right, preferred_element_type=jnp.float32)


def contract_rows(left, right):
    return lax.dot_general(
        left, right, (((1,), (1,)), ((), ())), preferred_element_type=jnp.float32
    )


def contract_first(left, right):
    return lax.dot_general(
        left, right, (((0,), (0,)), ((), ())), preferred_element_type=jnp.float32
    )


def gather(x):
    return lax.all_gather(x, "shard", axis=0, tiled=True)


def scatter_sum(x):
    return lax.psum_scatter(
        x.astype(jnp.bfloat16), "shard", scatter_dimension=0, tiled=True
    ).astype(jnp.float32)


def per_device(
    tokens,
    cotangent,
    lengths,
    attn_gain,
    mlp_gain,
    query_gain,
    key_gain,
    w_query,
    w_key,
    w_value,
    w_out,
    w_gate,
    w_up,
    w_down,
):
    tok_rows, width = tokens.shape
    shards = lax.axis_size("shard")
    rows = tok_rows * shards
    group = HEADS // KV_HEADS
    feat = width // shards
    scale = 1.0 / math.sqrt(HEAD_DIM)
    my_shard = lax.axis_index("shard")
    index = jnp.arange(rows, dtype=jnp.int32)
    segment, position = segment_info(lengths[0], index)
    visible = (segment[:, None] == segment[None, :]) & (index[None, :] <= index[:, None])

    q_cols = w_query.shape[1] // shards
    k_cols = w_key.shape[1] // shards
    packed = jnp.concatenate(
        [
            w_query.reshape(feat, shards, q_cols),
            w_key.reshape(feat, shards, k_cols),
            w_value.reshape(feat, shards, k_cols),
            w_out.reshape(feat, shards, q_cols),
        ],
        axis=2,
    )
    mine = lax.all_to_all(packed, "shard", split_axis=1, concat_axis=0, tiled=True).reshape(
        width, -1
    )
    qkv_cols = q_cols + 2 * k_cols
    w_qkv = mine[:, :qkv_cols]
    w_o = mine[:, qkv_cols:]

    gains_rows = jnp.concatenate(
        [attn_gain, mlp_gain, jnp.zeros((width - 2 * feat,), low)]
    ).reshape(1, width)
    gathered = gather(
        jnp.concatenate([tokens, jnp.broadcast_to(gains_rows, (16, width))], axis=0)
    ).reshape(shards, tok_rows + 16, width)
    tokens_all = gathered[:, :tok_rows].reshape(rows, width)
    gain_one = gathered[:, tok_rows, :feat].reshape(width).astype(jnp.float32)
    gain_two = gathered[:, tok_rows, feat : 2 * feat].reshape(width).astype(jnp.float32)

    inputs = tokens.astype(jnp.float32)
    first = rms_scale(tokens_all.astype(jnp.float32), gain_one).astype(low)
    proj = dot(first, w_qkv)

    def prepare(projected, gain, count):
        return rotate(rms_scale(projected.reshape(rows, count, HEAD_DIM), gain), position)

    q_rot = prepare(proj[:, :q_cols], query_gain.astype(f32), group)
    k_rot = prepare(proj[:, q_cols : q_cols + k_cols], key_gain.astype(f32), 1)
    query = q_rot.astype(low)
    key = k_rot.astype(low)[:, 0]
    value = proj[:, q_cols + k_cols :].astype(low)
    scores = jnp.einsum("tgd,sd->gts", query, key, preferred_element_type=jnp.float32) * scale
    masked = jnp.where(visible[None], scores, masked_value)
    top = jnp.max(masked, axis=-1, keepdims=True)
    total = jnp.log(jnp.sum(jnp.exp(masked - top), axis=-1, keepdims=True)) + top
    weights = jnp.exp(masked - total)
    probs = weights.astype(low)
    attended = (
        jnp.einsum("gts,sd->tgd", probs, value, preferred_element_type=jnp.float32)
        .reshape(rows, q_cols)
        .astype(low)
    )
    resid = inputs + scatter_sum(contract_rows(attended, w_o))
    half = HEAD_DIM // 2
    frequency = theta_base ** (-jnp.arange(half, dtype=f32) * (2.0 / HEAD_DIM))
    angles = position.astype(f32)[:, None] * frequency[None, :]
    cosine = jnp.concatenate([jnp.cos(angles)] * 2, axis=1)
    sine = jnp.concatenate([-jnp.sin(angles), jnp.sin(angles)], axis=1)
    kept = jnp.concatenate(
        [
            proj[:, : q_cols + k_cols],
            total[0],
            total[1],
            jnp.zeros((rows, HEAD_DIM - 2), f32),
        ],
        axis=1,
    )
    result, grad_tokens, gains, attn_grads, ffn_grads, _ = late_call(
        lengths,
        resid,
        cotangent,
        tokens,
        gain_one[None],
        gain_two[None],
        query_gain.astype(f32)[None],
        key_gain.astype(f32)[None],
        kept,
        cosine,
        sine,
        mine,
        jnp.concatenate([query.reshape(rows, q_cols), key, value, attended], axis=1),
        first,
        w_gate,
        w_up,
        w_down,
    )
    ffn_grads = ffn_grads.astype(f32)
    attn_grads = attn_grads.astype(f32)
    grad_query = attn_grads[:, :width]
    grad_key = attn_grads[:, width : width + width // 2]
    grad_value = attn_grads[:, width + width // 2 : 2 * width]
    grad_out = attn_grads[:, 2 * width :]
    gains = gains.reshape(-1)
    head_piece = HEAD_DIM // shards
    gains_first = lax.dynamic_slice_in_dim(gains, my_shard * feat, feat, 0)
    gains_second = lax.dynamic_slice_in_dim(gains, width + my_shard * feat, feat, 0)
    gains_query = lax.dynamic_slice_in_dim(gains, 2 * width + my_shard * head_piece, head_piece, 0)
    gains_key = lax.dynamic_slice_in_dim(
        gains, 2 * width + HEAD_DIM + my_shard * head_piece, head_piece, 0
    )
    return (
        result,
        grad_tokens,
        grad_query,
        grad_key,
        grad_value,
        grad_out,
        ffn_grads[0],
        ffn_grads[1],
        ffn_grads[2],
        gains_first,
        gains_second,
        gains_query,
        gains_key,
    )


def solution(mesh):
    spread = P(("rep", "shard"), None)
    rowed = P("shard", None)
    return jax.shard_map(
        per_device,
        mesh=mesh,
        in_specs=(spread, spread, P("rep", None), P("shard"), P("shard"), P(), P()) + (rowed,) * 7,
        out_specs=(spread, spread) + (rowed,) * 7 + (P("shard"),) * 4,
        check_vma=False,
    )
```

```python
import functools
import math

import jax
import jax.numpy as jnp
from jax import lax
from jax.experimental import pallas as pl
from jax.experimental.pallas import tpu as pltpu
from jax.sharding import PartitionSpec as P

HEADS = 16
KV_HEADS = 8
HEAD_DIM = 128

epsilon = 1e-06
theta_base = 1000000.0
masked_value = -1e30


MESH = pl.DeviceIdType.MESH
BLOCK = 128
HALF = 64
LINE = 512
low = jnp.bfloat16
f32 = jnp.float32


def mm(left, right):
    return lax.dot_general(left, right, (((1,), (0,)), ((), ())), preferred_element_type=f32)


def mm_nt(left, right):
    return lax.dot_general(left, right, (((1,), (1,)), ((), ())), preferred_element_type=f32)


def mm_tn(left, right):
    return lax.dot_general(left, right, (((0,), (0,)), ((), ())), preferred_element_type=f32)


class Place:
    def __init__(self):
        self.rep = lax.axis_index("rep")
        self.shard = lax.axis_index("shard")
        self.yl, self.z = self.shard // 4, self.shard % 4
        self.yh, self.x, self.core = self.rep // 8, (self.rep // 2) % 4, self.rep % 2

    def block(self, dy, dz):
        return ((self.yl + dy + 2) % 2) * 4 + (self.z + dz + 8) % 4

    def dev(self, dy, dz):
        return (self.rep, self.block(dy, dz))

    def x_at(self, dx):
        return (self.x + dx + 8) % 4

    def rep_dev(self, dyh, dx, dcore):
        rep = ((self.yh + dyh) % 2) * 8 + self.x_at(dx) * 2 + (self.core + dcore) % 2
        return (rep, self.shard)

    def rows(self, dy, dz, start=0, count=BLOCK):
        return pl.ds(pl.multiple_of(self.block(dy, dz) * BLOCK + start, 32), count)

    def line(self, dy):
        return pl.multiple_of(((self.yl + dy + 2) % 2) * LINE, LINE)

    def shard_peers(self):
        return [self.dev(dy, dz) for dy in range(2) for dz in range(4) if dy or dz]

    def rep_peers(self):
        return [
            self.rep_dev(*by) for by in ((0, 0, 1), (0, 1, 0), (0, 2, 0), (0, 3, 0), (1, 0, 0))
        ]

    def greet(self):
        barrier = pltpu.get_barrier_semaphore()
        peers = self.shard_peers() + self.rep_peers()
        for peer in peers:
            pl.semaphore_signal(barrier, inc=1, device_id=peer, device_id_type=MESH)
        pl.semaphore_wait(barrier, len(peers))


class Net:
    def __init__(self, send_sems, recv_sems):
        self.send_sems, self.recv_sems = send_sems, recv_sems
        self.started, self.coming = [], {}

    def send(self, tag, src, dst, dev, here):
        k = len(self.started)
        copy = pltpu.make_async_remote_copy(
            src_ref=src,
            dst_ref=dst,
            send_sem=self.send_sems.at[k],
            recv_sem=self.recv_sems.at[k],
            device_id=dev,
            device_id_type=MESH,
        )
        copy.start()
        self.started.append(copy)
        self.coming[tag] = (k, here, dev)

    def wait(self, tag):
        k, here, dev = self.coming.pop(tag)
        pltpu.make_async_remote_copy(
            src_ref=here,
            dst_ref=here,
            send_sem=self.send_sems.at[k],
            recv_sem=self.recv_sems.at[k],
            device_id=dev,
            device_id_type=MESH,
        ).wait_recv()

    def finish(self):
        for tag in list(self.coming):
            self.wait(tag)
        for copy in self.started:
            copy.wait_send()


class Gather:
    COPIES = 18

    def __init__(self, place, buf, send_sems, recv_sems):
        self.place, self.buf = place, buf
        self.net = Net(send_sems, recv_sems)

    def send(self, tag, block, start, count, to):
        rows = self.place.rows(*block, start, count)
        here = self.place.rows(block[0] - to[0], block[1] - to[1], start, count)
        self.net.send(
            tag, self.buf.at[rows], self.buf.at[rows], self.place.dev(*to), self.buf.at[here]
        )

    def start(self):
        self.send("y_up", (0, 0), 0, HALF, (1, 0))
        for d in (1, 3):
            self.send(f"z_low{d}", (0, 0), HALF, HALF, (0, d))
        self.send("y_low", (0, 0), HALF, HALF, (1, 0))

    def step_one(self):
        self.net.wait("y_up")
        for d in (1, 3):
            self.send(f"p_up{d}", (1, 0), 0, HALF, (0, d))

    def step_two(self):
        for e, d in enumerate((1, 3)):
            self.net.wait(f"z_low{d}")
            self.send(f"f_low{d}", (0, -d), HALF + 32 * e, 32, (0, d))
            self.send(f"q_low{d}", (0, -d), HALF, HALF, (1, 0))
        for d in (1, 3):
            self.send(f"z_up{d}", (0, 0), 0, HALF, (0, d))

    def step_three(self):
        for e, d in enumerate((1, 3)):
            self.net.wait(f"p_up{d}")
            self.send(f"f_p{d}", (1, -d), 32 * e, 32, (0, d))
        for e, d in enumerate((1, 3)):
            self.net.wait(f"f_low{d}")
            self.send(f"q_far{d}", (0, -2 * d), HALF + 32 * e, 32, (1, 0))

    def step_four(self):
        for e, d in enumerate((1, 3)):
            self.net.wait(f"z_up{d}")
            self.send(f"f_up{d}", (0, -d), 32 * e, 32, (0, d))

    def own_line(self):
        for d in (1, 3):
            self.net.wait(f"f_up{d}")

    def other_line(self):
        for tag in list(self.net.coming):
            self.net.wait(tag)

    def steps(self):
        return [self.start, self.step_one, self.step_two, self.step_three, self.step_four]

    def finish(self):
        self.net.finish()


class Scatter:
    COPIES = 17

    @staticmethod
    def scratch(columns):
        return [
            pltpu.VMEM((4, HALF, columns), low),
            pltpu.VMEM((3, 2, 32, columns), low),
            pltpu.VMEM((3, 2, HALF, columns), low),
            pltpu.VMEM((HALF, columns), low),
        ]

    def __init__(self, place, part, across, near, far, last, send_sems, recv_sems):
        self.place, self.part = place, part
        self.across, self.near, self.far, self.last = across, near, far, last
        self.net = Net(send_sems, recv_sems)

    def add(self, rows, *refs):
        total = self.part[rows, :].astype(f32)
        for ref in refs:
            total = total + ref[...].astype(f32)
        self.part[rows, :] = total.astype(low)

    def first(self, kind):
        dy, start = ((1, 0), (0, 0), (0, HALF))[kind]
        for e, d in enumerate((1, 3)):
            src = self.part.at[self.place.rows(dy, 2, start + 32 * e, 32)]
            dst = self.near.at[kind, e]
            self.net.send(f"near{kind}{e}", src, dst, self.place.dev(0, d), dst)

    def second(self, kind):
        dy, start = ((1, 0), (0, 0), (0, HALF))[kind]
        for e, d in enumerate((1, 3)):
            self.net.wait(f"near{kind}{e}")
            self.add(self.place.rows(dy, d, start + 32 * e, 32), self.near.at[kind, e])
            src = self.part.at[self.place.rows(dy, d, start, HALF)]
            dst = self.far.at[kind, e]
            self.net.send(f"far{kind}{e}", src, dst, self.place.dev(0, d), dst)

    def send_other(self):
        for d in (2, 1, 3, 0):
            src = self.part.at[self.place.rows(1, d, HALF, HALF)]
            dst = self.across.at[d]
            self.net.send(f"across{d}", src, dst, self.place.dev(1, 0), dst)
        self.first(0)

    def send_own(self):
        self.first(1)

    def step_one(self):
        self.net.wait("across2")
        self.add(self.place.rows(0, 2, HALF, HALF), self.across.at[2])
        self.first(2)
        self.second(0)
        self.second(1)

    def step_two(self):
        for d in (1, 3):
            self.net.wait(f"across{d}")
            self.add(self.place.rows(0, d, HALF, HALF), self.across.at[d])
        self.second(2)

    def step_three(self):
        for e in range(2):
            self.net.wait(f"far0{e}")
        rows = self.place.rows(1, 0, 0, HALF)
        self.add(rows, self.far.at[0, 0], self.far.at[0, 1])
        self.net.send("last", self.part.at[rows], self.last, self.place.dev(1, 0), self.last)

    def total(self, half):
        if half == 0:
            tags, extra, kind = ("far10", "far11", "last"), self.last, 1
        else:
            tags, extra, kind = ("far20", "far21", "across0"), self.across.at[0], 2
        for tag in tags:
            self.net.wait(tag)
        out = self.part[self.place.rows(0, 0, half * HALF, HALF), :].astype(f32)
        for ref in (self.far.at[kind, 0], self.far.at[kind, 1], extra):
            out = out + ref[...].astype(f32)
        return out

    def finish(self):
        self.net.finish()


def add_rows(into, start, count, *refs):
    step = 64 if count % 64 == 0 else 48

    @pl.loop(0, count // step)
    def _(i):
        at = pl.multiple_of(i * step, 16)
        rows = pl.ds(pl.multiple_of(start + at, 16), step)
        total = into[rows, :].astype(f32)
        for ref in refs:
            total = total + ref[pl.ds(at, step), :].astype(f32)
        into[rows, :] = total.astype(low)


class RepSum:
    COPIES = 15

    def __init__(self, place, sems, own, other, landed, near, far, cross, out, unit, out_unit):
        self.place, self.net = place, Net(*sems)
        self.own, self.other, self.landed = own, other, landed
        self.near, self.far, self.cross = near, far, cross
        self.out, self.unit, self.out_unit = out, unit, out_unit

    def chunk(self, dx, start=0, count=None):
        at = self.place.x_at(dx) * 2 * self.unit + start
        return pl.ds(pl.multiple_of(at, 16), 2 * self.unit if count is None else count)

    def out_rows(self, dcore, dx, start=0, count=None):
        core = (self.place.core + dcore) % 2
        at = (core * 8 + self.place.x_at(dx) * 2 + start) * self.out_unit
        count = (2 if count is None else count) * self.out_unit
        return self.out.at[pl.ds(pl.multiple_of(at, 16), count)]

    def core_send(self):
        self.net.send("core", self.other, self.landed, self.place.rep_dev(0, 0, 1), self.landed)

    def x_first(self, load=None):
        self.net.wait("core")
        add_rows(self.own, 0, 8 * self.unit, self.landed if load is None else load())
        for e, d in enumerate((1, 3)):
            src = self.own.at[self.chunk(2, e * self.unit, self.unit)]
            dst = self.near[e]
            self.net.send(f"near{e}", src, dst, self.place.rep_dev(0, d, 0), dst)

    def x_second(self):
        for e, d in enumerate((1, 3)):
            self.net.wait(f"near{e}")
            add_rows(self.own, self.place.x_at(d) * 2 * self.unit + e * self.unit, self.unit, self.near[e])
            dst = self.far[e]
            self.net.send(
                f"far{e}", self.own.at[self.chunk(d)], dst, self.place.rep_dev(0, d, 0), dst
            )

    def y_send(self):
        for e in range(2):
            self.net.wait(f"far{e}")
        add_rows(self.own, self.place.x * 2 * self.unit, 2 * self.unit, *self.far)
        src = self.own.at[self.chunk(0, (1 - self.place.yh) * self.unit, self.unit)]
        self.net.send("cross", src, self.cross, self.place.rep_dev(1, 0, 0), self.cross)

    def piece(self):
        self.net.wait("cross")
        at = (self.place.x * 2 + self.place.yh) * self.unit
        add_rows(self.own, at, self.unit, self.cross)
        return self.own.at[pl.ds(pl.multiple_of(at, 16), self.unit)]

    def y_gather(self, piece, sem):
        mine = self.out_rows(0, 0, self.place.yh, 1)
        copy = pltpu.make_async_copy(piece, mine, sem)
        copy.start()
        self.net.send(
            "y", piece, mine, self.place.rep_dev(1, 0, 0), self.out_rows(0, 0, 1 - self.place.yh, 1)
        )
        copy.wait()

    def to_core(self, dx):
        rows = self.out_rows(0, dx)
        self.net.send(
            f"core{dx}", rows, rows, self.place.rep_dev(0, 0, 1), self.out_rows(1, dx)
        )

    def x_gather(self):
        self.net.wait("y")
        rows = self.out_rows(0, 0)
        for d in (1, 3):
            self.net.send(f"x{d}", rows, rows, self.place.rep_dev(0, d, 0), self.out_rows(0, -d))
        self.to_core(0)

    def x_forward(self):
        for e, d in enumerate((1, 3)):
            self.net.wait(f"x{d}")
            rows = self.out_rows(0, -d, e, 1)
            self.net.send(
                f"xx{d}", rows, rows, self.place.rep_dev(0, d, 0), self.out_rows(0, -2 * d, e, 1)
            )
            self.to_core(-d)

    def x_last(self):
        for d in (1, 3):
            self.net.wait(f"xx{d}")
        self.to_core(2)

    def finish(self):
        self.net.finish()


def rms_backward(value, gain, upstream):
    root = lax.rsqrt(jnp.mean(value * value, axis=-1, keepdims=True) + epsilon)
    pulled = upstream * gain
    back = root * pulled - value * (root * root * root) * jnp.mean(
        pulled * value, axis=-1, keepdims=True
    )
    return back, upstream * (value * root)


def swap_halves(value):
    return pltpu.roll(value, HEAD_DIM // 2, 1)


def layer_kernel(
    scale,
    lengths,
    tokens,
    cotangent,
    gain_shard,
    query_gain,
    key_gain,
    frequency,
    w_query_hbm,
    w_key_hbm,
    w_value_hbm,
    w_out_hbm,
    w_gate_hbm,
    w_up_hbm,
    w_down_hbm,
    result,
    grad_tokens,
    gains,
    attn_grads,
    ffn_grads,
    core_landed,
    first_hbm,
    w_attn_hbm,
    heads_hbm,
    resid,
    gain_rows_all,
    gain_blocks,
    proj,
    cosine,
    sine,
    second,
    cot_all,
    branch,
    w_gate,
    w_up,
    w_down,
    pair,
    d_up,
    part_out,
    part_back,
    d_att,
    d_key,
    d_value,
    d_qkv,
    staged,
    across,
    near,
    far,
    last,
    swapped,
    assembled,
    gain_sums,
    gain_landed,
    swap_sems,
    sibling_sems,
    free_sem,
    core_free_sem,
    landing_free,
    heads_free,
    local_sems,
    send_sems,
    recv_sems,
):
    place = Place()
    hidden = pair.at[pl.ds(0, 8 * BLOCK)]
    d_gate = pair.at[pl.ds(8 * BLOCK, 8 * BLOCK)]
    rows_all = 8 * BLOCK
    hid = w_gate.shape[0]
    width = second.shape[1]

    loads = [
        pltpu.make_async_copy(src, dst, local_sems.at[i])
        for i, (src, dst) in enumerate(
            ((w_gate_hbm, w_gate), (w_up_hbm, w_up), (w_down_hbm, w_down))
        )
    ]
    for load in loads:
        load.start()

    used = [0]

    def sems(count):
        at = used[0]
        used[0] += count
        return send_sems.at[pl.ds(at, count)], recv_sems.at[pl.ds(at, count)]

    own = place.rows(0, 0)
    gain_one = gain_rows_all.at[pl.ds(0, 1)]
    gain_two = gain_rows_all.at[pl.ds(1, 1)]
    cot_all[own, :] = cotangent[...].astype(low)
    branch[own, :] = tokens[...]
    feat = w_query_hbm.shape[0]
    gain_blocks[place.shard] = gain_shard[...]
    place.greet()

    gain_share = Net(*sems(7))
    peers = [(dy, dz) for dy in range(2) for dz in range(4) if dy or dz]
    for by in peers:
        gain_share.send(
            str(by),
            gain_blocks.at[place.shard],
            gain_blocks.at[place.shard],
            place.dev(*by),
            gain_blocks.at[place.block(-by[0], -by[1])],
        )
    qkv_parts = (
        (w_query_hbm, 0, 2 * HEAD_DIM),
        (w_key_hbm, 2 * HEAD_DIM, HEAD_DIM),
        (w_value_hbm, 3 * HEAD_DIM, HEAD_DIM),
    )
    out_parts = ((w_out_hbm, 4 * HEAD_DIM, 2 * HEAD_DIM),)
    half_rows = feat // 2
    qkv_span = pl.ds(0, 4 * HEAD_DIM)
    out_span = pl.ds(4 * HEAD_DIM, 2 * HEAD_DIM)

    def swap_rows(block):
        at = block * feat + place.core * half_rows
        return pl.ds(pl.multiple_of(at, half_rows), half_rows)

    def swap_copy(src, dst, kind, i, dev):
        return pltpu.make_async_remote_copy(
            src_ref=src,
            dst_ref=dst,
            send_sem=swap_sems.at[0, kind, i],
            recv_sem=swap_sems.at[1, kind, i],
            device_id=dev,
            device_id_type=MESH,
        )

    def swap_send(parts, kind):
        for i, by in enumerate(peers):
            to = place.block(*by)
            for whole, begin, size in parts:
                cols = pl.ds(pl.multiple_of(to * size, HEAD_DIM), size)
                src = whole.at[pl.ds(pl.multiple_of(place.core * half_rows, half_rows), half_rows), cols]
                dst = pair.at[swap_rows(place.shard), pl.ds(begin, size)]
                swap_copy(src, dst, kind, i, place.dev(*by)).start()
        for whole, begin, size in parts:
            cols = pl.ds(pl.multiple_of(place.shard * size, HEAD_DIM), size)
            rows = pl.ds(pl.multiple_of(place.shard * feat, feat), feat)
            copy = pltpu.make_async_copy(
                whole.at[:, cols], pair.at[rows, pl.ds(begin, size)], sibling_sems.at[2, kind]
            )
            copy.start()

    def sibling_copy(ref, kind):
        return pltpu.make_async_remote_copy(
            src_ref=ref,
            dst_ref=ref,
            send_sem=sibling_sems.at[0, kind],
            recv_sem=sibling_sems.at[1, kind],
            device_id=place.rep_dev(0, 0, 1),
            device_id_type=MESH,
        )

    def swap_relay(span, kind):
        for i, by in enumerate(peers):
            here = pair.at[swap_rows(place.block(-by[0], -by[1])), span]
            swap_copy(here, here, kind, i, place.dev(*by)).wait_recv()
            sibling_copy(here, kind).start()

    def swap_done(span, kind):
        rows = pl.ds(pl.multiple_of(place.shard * feat, feat), feat)
        mine = pair.at[rows, span]
        pltpu.make_async_copy(mine, mine, sibling_sems.at[2, kind]).wait()
        others = pair.at[pl.ds(0, 7 * half_rows), span]
        sibling_copy(others, kind).wait()
        for i, by in enumerate(peers):
            here = pair.at[swap_rows(place.block(-by[0], -by[1])), span]
            swap_copy(here, here, kind, i, place.dev(*by)).wait_send()

    swap_send(qkv_parts, 0)
    gather_tokens = Gather(place, branch, *sems(Gather.COPIES))
    gather_tokens.start()

    start_one = lengths[0, 0]
    start_two = lengths[0, 0] + lengths[0, 1]

    def begin_of(token):
        return jnp.where(
            token >= start_two, start_two, jnp.where(token >= start_one, start_one, 0)
        )

    token = lax.broadcasted_iota(jnp.int32, (rows_all, 1), 0)
    angles = (token - begin_of(token)).astype(f32) * frequency[...]
    lane = lax.broadcasted_iota(jnp.int32, (1, HEAD_DIM), 1)
    cosine[...] = jnp.cos(angles)
    sine[...] = jnp.sin(angles) * jnp.where(lane < HEAD_DIM // 2, -1.0, 1.0)

    gather_tokens.step_one()
    gather_tokens.step_two()
    gain_share.finish()
    for j in range(8):
        span = slice(j * feat, (j + 1) * feat)
        gain_rows_all[0:2, span] = gain_blocks[j, 0:2, :].astype(f32)
    swap_relay(qkv_span, 0)
    swap_send(out_parts, 1)
    gather_tokens.step_three()
    gather_tokens.step_four()

    def normalise(dy):
        line = place.line(dy)

        @pl.loop(0, LINE // BLOCK)
        def _(i):
            rows = pl.ds(pl.multiple_of(line + i * BLOCK, BLOCK), BLOCK)
            x = branch[rows, :].astype(f32)
            root = lax.rsqrt(jnp.mean(x * x, axis=-1, keepdims=True) + epsilon)
            second[rows, :] = (x * root * gain_one[...]).astype(low)

    gather_tokens.own_line()
    normalise(0)
    gather_tokens.other_line()
    normalise(1)
    gather_tokens.finish()
    keep_first = pltpu.make_async_copy(second, first_hbm, local_sems.at[3])
    keep_first.start()
    swap_done(qkv_span, 0)
    heads = d_up
    gains_of_head = (query_gain, query_gain, key_gain)

    @pl.loop(0, rows_all // 256)
    def _(i):
        rows = pl.ds(pl.multiple_of(i * 256, 256), 256)
        proj[rows, :] = mm(second[rows, :], pair[:, 0 : 4 * HEAD_DIM])
        for g in range(3):
            lanes = pl.ds(g * HEAD_DIM, HEAD_DIM)
            u = proj[rows, lanes]
            root = lax.rsqrt(jnp.mean(u * u, axis=-1, keepdims=True) + epsilon)
            u = u * root * gains_of_head[g][...]
            heads[rows, lanes] = (u * cosine[rows, :] + swap_halves(u) * sine[rows, :]).astype(low)
        lanes = pl.ds(3 * HEAD_DIM, HEAD_DIM)
        heads[rows, lanes] = proj[rows, lanes].astype(low)

    swap_relay(out_span, 1)
    chunk = 256
    for part in range(rows_all // chunk):
        rows = pl.ds(part * chunk, chunk)
        seen = (part + 1) * chunk
        token = part * chunk + lax.broadcasted_iota(jnp.int32, (chunk, 1), 0)
        source = lax.broadcasted_iota(jnp.int32, (1, seen), 1)
        visible = (source >= begin_of(token)) & (source <= token)
        for g in range(2):
            lanes = pl.ds(g * HEAD_DIM, HEAD_DIM)
            scores = mm_nt(heads[rows, lanes], heads[0:seen, 2 * HEAD_DIM : 3 * HEAD_DIM]) * scale
            scores = jnp.where(visible, scores, masked_value)
            top = jnp.max(scores, axis=-1, keepdims=True)
            raised = jnp.exp(scores - top)
            total = jnp.sum(raised, axis=-1, keepdims=True)
            probs = (raised * (1.0 / total)).astype(low)
            proj[rows, 3 * HEAD_DIM + g : 3 * HEAD_DIM + g + 1] = jnp.log(total) + top
            heads[rows, pl.ds((4 + g) * HEAD_DIM, HEAD_DIM)] = mm(
                probs, heads[0:seen, 3 * HEAD_DIM : 4 * HEAD_DIM]
            ).astype(low)
    keep_heads = pltpu.make_async_copy(heads, heads_hbm, local_sems.at[4])
    keep_heads.start()
    swap_done(out_span, 1)
    keep_weights = pltpu.make_async_copy(pair, w_attn_hbm, local_sems.at[5])
    keep_weights.start()
    landing = (across, near, far, last)
    scatter_attn = Scatter(place, part_back, *landing, *sems(Scatter.COPIES))

    def attention_out(dy):
        rows = pl.ds(place.line(dy), LINE)

        @pl.loop(0, width // 256)
        def _(i):
            cols = pl.ds(pl.multiple_of(i * 256, 256), 256)
            part_back[rows, cols] = mm_nt(
                heads[rows, 4 * HEAD_DIM :], pair[cols, 4 * HEAD_DIM :]
            ).astype(low)

    attention_out(1)
    keep_first.wait()
    scatter_attn.send_other()
    attention_out(0)
    scatter_attn.send_own()
    scatter_attn.step_one()
    scatter_attn.step_two()
    scatter_attn.step_three()
    keep_heads.wait()
    keep_weights.wait()
    for half in (1, 0):
        rows = pl.ds(half * HALF, HALF)
        x = tokens[rows, :].astype(f32) + scatter_attn.total(half)
        resid[rows, :] = x
        root = lax.rsqrt(jnp.mean(x * x, axis=-1, keepdims=True) + epsilon)
        at = place.rows(0, 0, half * HALF, HALF)
        second[at, :] = (x * root * gain_two[...]).astype(low)
    scatter_attn.finish()
    gather_second = Gather(place, second, *sems(Gather.COPIES))
    gather_cot = Gather(place, cot_all, *sems(Gather.COPIES))
    gather_branch = Gather(place, branch, *sems(Gather.COPIES))
    scatter_out = Scatter(place, part_out, *landing, *sems(Scatter.COPIES))
    scatter_back = Scatter(place, part_back, *landing, *sems(Scatter.COPIES))

    def feed_forward(dy):
        rows = pl.ds(place.line(dy), LINE)

        @pl.loop(0, hid // 256)
        def _(i):
            cols = pl.ds(pl.multiple_of(i * 256, 256), 256)
            gate = mm_nt(second[rows, :], w_gate[cols, :])
            up = mm_nt(second[rows, :], w_up[cols, :])
            sigma = 1.0 / (1.0 + jnp.exp(-gate))
            silu = gate * sigma
            hidden[rows, cols] = (silu * up).astype(low)
            d_gate[rows, cols] = (up * sigma * (1.0 + gate * (1.0 - sigma))).astype(low)
            d_up[rows, cols] = silu.astype(low)

    def project_out(dy):
        rows = pl.ds(place.line(dy), LINE)

        @pl.loop(0, width // 512)
        def _(i):
            cols = pl.ds(pl.multiple_of(i * 512, 512), 512)
            part_out[rows, cols] = mm(hidden[rows, :], w_down[:, cols]).astype(low)

    def feed_backward(dy):
        rows = pl.ds(place.line(dy), LINE)

        @pl.loop(0, hid // 256)
        def _(i):
            cols = pl.ds(pl.multiple_of(i * 256, 256), 256)
            d_hidden = mm_nt(cot_all[rows, :], w_down[cols, :])
            d_gate[rows, cols] = (d_hidden * d_gate[rows, cols].astype(f32)).astype(low)
            d_up[rows, cols] = (d_hidden * d_up[rows, cols].astype(f32)).astype(low)

        @pl.loop(0, width // 512)
        def _(i):
            cols = pl.ds(pl.multiple_of(i * 512, 512), 512)
            part_back[rows, cols] = (
                mm(d_gate[rows, :], w_gate[:, cols]) + mm(d_up[rows, :], w_up[:, cols])
            ).astype(low)

    def weight_grad(into, left, right):
        @pl.loop(0, hid // 256)
        def _(i):
            cols = pl.ds(pl.multiple_of(i * 256, 256), 256)
            into[cols, :] = mm_tn(left[:, cols], right[...]).astype(low)

    unit = hid // 16
    sums = []
    for i, whole in enumerate((w_gate, w_up, w_down)):
        base = i * 7 * unit

        def view(start, count, base=base):
            return second.at[pl.ds(base + start * unit, count * unit)]

        sums.append(
            RepSum(
                place,
                sems(RepSum.COPIES),
                whole.at[pl.ds(pl.multiple_of(place.core * 8 * unit, 16), 8 * unit)],
                whole.at[pl.ds(pl.multiple_of((1 - place.core) * 8 * unit, 16), 8 * unit)],
                core_landed.at[i],
                [view(0, 1), view(1, 1)],
                [view(2, 2), view(4, 2)],
                view(6, 1),
                ffn_grads.at[i],
                unit,
                unit,
            )
        )
    sum_gate, sum_up, sum_down = sums

    def load_landed(i):
        def load():
            here = staged.at[pl.ds(0, 8 * unit)]
            copy = pltpu.make_async_copy(core_landed.at[i], here, local_sems.at[3])
            copy.start()
            copy.wait()
            return here

        return load

    for step in gather_second.steps():
        step()
    gather_second.own_line()
    gather_cot.start()
    for load in loads:
        load.wait()
    feed_forward(0)
    gather_cot.step_one()
    gather_cot.step_two()
    gather_second.other_line()
    feed_forward(1)
    gather_cot.step_three()
    gather_cot.step_four()
    project_out(1)
    project_out(0)
    gather_cot.own_line()
    gather_cot.other_line()
    feed_backward(1)
    scatter_back.send_other()
    feed_backward(0)
    scatter_back.send_own()
    weight_grad(w_gate, d_gate, second)
    sum_gate.core_send()
    scatter_back.step_one()
    weight_grad(w_up, d_up, second)
    sum_up.core_send()
    gather_second.finish()
    for by in ((0, 1, 0), (0, 3, 0), (1, 0, 0)):
        pl.semaphore_signal(
            free_sem, inc=1, device_id=place.rep_dev(*by), device_id_type=MESH
        )
    scatter_back.step_two()
    weight_grad(w_down, hidden, cot_all)
    sum_down.core_send()
    pl.semaphore_wait(free_sem, 3)
    sum_gate.x_first(load_landed(0))
    sum_up.x_first(load_landed(1))
    gather_cot.finish()
    q_cols = 2 * HEAD_DIM
    query = heads.at[:, pl.ds(0, q_cols)]
    key = heads.at[:, pl.ds(q_cols, HEAD_DIM)]
    value = heads.at[:, pl.ds(q_cols + HEAD_DIM, HEAD_DIM)]
    attended = heads.at[:, pl.ds(q_cols + 2 * HEAD_DIM, q_cols)]
    w_attn = cot_all
    attn_cols = heads.shape[1]
    loads = [
        pltpu.make_async_copy(heads_hbm, heads, local_sems.at[0]),
        pltpu.make_async_copy(
            w_attn_hbm.at[pl.ds(0, rows_all)],
            w_attn.at[:, pl.ds(0, attn_cols)],
            local_sems.at[1],
        ),
        pltpu.make_async_copy(
            w_attn_hbm.at[pl.ds(rows_all, rows_all)],
            w_attn.at[:, pl.ds(attn_cols, attn_cols)],
            local_sems.at[2],
        ),
    ]
    for load in loads:
        load.start()
    scatter_back.step_three()
    gain_rows = None
    for half in (1, 0):
        rows = pl.ds(half * HALF, HALF)
        d_second = scatter_back.total(half)
        back, gain_part = rms_backward(resid[rows, :], gain_two[...], d_second)
        grad_tokens[rows, :] = cotangent[rows, :] + back
        gain_part = jnp.sum(gain_part, axis=0, keepdims=True)
        gain_rows = gain_part if gain_rows is None else gain_rows + gain_part
    gain_sums[0] = jnp.zeros_like(gain_sums[0])

    def keep_gain(first_row, value):
        for i in range(value.shape[1] // HEAD_DIM):
            gain_sums[0, first_row + i : first_row + i + 1, :] = value[
                :, i * HEAD_DIM : (i + 1) * HEAD_DIM
            ]

    gain_slots = width // HEAD_DIM
    keep_gain(gain_slots, gain_rows)
    branch[own, :] = grad_tokens[...].astype(low)
    gather_branch.start()
    sum_down.x_first(load_landed(2))
    gather_branch.step_one()
    sum_gate.x_second()
    gather_branch.step_two()
    scatter_out.send_other()
    scatter_out.send_own()
    sum_up.x_second()
    gather_branch.step_three()
    gather_branch.step_four()
    sum_down.x_second()
    gather_branch.own_line()
    for load in loads:
        load.wait()

    def into_attention(dy):
        rows = pl.ds(place.line(dy), LINE)
        d_att[rows, :] = (
            mm(branch[rows, 0:rows_all], w_attn[:, 4 * HEAD_DIM : attn_cols])
            + mm(branch[rows, rows_all:], w_attn[:, attn_cols + 4 * HEAD_DIM : 2 * attn_cols])
        ).astype(low)

    into_attention(0)
    gather_branch.other_line()
    into_attention(1)

    def unrotate(rows, upstream, projected, gain):
        turned = upstream * cosine[rows, :] - swap_halves(upstream) * sine[rows, :]
        return rms_backward(projected, gain, turned)

    gain_rows = jnp.zeros((1, HEAD_DIM), f32)
    d_key[...] = jnp.zeros_like(d_key)
    d_value[...] = jnp.zeros_like(d_value)
    scatter_out.step_one()
    for part in range(rows_all // chunk):
        rows = pl.ds(part * chunk, chunk)
        seen = (part + 1) * chunk
        token = part * chunk + lax.broadcasted_iota(jnp.int32, (chunk, 1), 0)
        source = lax.broadcasted_iota(jnp.int32, (1, seen), 1)
        visible = (source >= begin_of(token)) & (source <= token)
        for g in range(2):
            lanes = pl.ds(g * HEAD_DIM, HEAD_DIM)
            scores = mm_nt(query[rows, lanes], key[0:seen, :]) * scale
            weights = jnp.where(visible, jnp.exp(scores - proj[rows, 3 * HEAD_DIM + g : 3 * HEAD_DIM + g + 1]), 0.0)
            d_probs = mm_nt(d_att[rows, lanes], value[0:seen, :])
            inner = jnp.sum(weights * d_probs, axis=-1, keepdims=True)
            d_scores = (weights * (d_probs - inner)).astype(low)
            back, gain_part = unrotate(
                rows, mm(d_scores, key[0:seen, :]) * scale, proj[rows, lanes], query_gain[...]
            )
            d_qkv[rows, lanes] = back.astype(low)
            gain_rows = gain_rows + jnp.sum(gain_part, axis=0, keepdims=True)
            d_key[0:seen, :] += mm_tn(d_scores, query[rows, lanes])
            d_value[0:seen, :] += mm_tn(weights.astype(low), d_att[rows, lanes])
        if part == 0:
            sum_gate.y_send()
        if part == 1:
            scatter_out.step_two()
            sum_up.y_send()
            sum_gate.y_gather(sum_gate.piece(), local_sems.at[3])
        if part == 2:
            scatter_out.step_three()
            sum_down.y_send()
            sum_up.y_gather(sum_up.piece(), local_sems.at[3])
            sum_gate.x_gather()
    d_qkv[:, 3 * HEAD_DIM :] = d_value[...].astype(low)

    keep_gain(2 * gain_slots, gain_rows)
    lanes = pl.ds(2 * HEAD_DIM, HEAD_DIM)
    back, gain_part = unrotate(pl.ds(0, rows_all), d_key[...] * scale, proj[:, lanes], key_gain[...])
    d_qkv[:, lanes] = back.astype(low)
    keep_gain(2 * gain_slots + 1, jnp.sum(gain_part, axis=0, keepdims=True))

    scatter_back.finish()
    scatter_first = Scatter(place, part_back, *landing, *sems(Scatter.COPIES))
    for half in (0, 1):
        rows = pl.ds(half * HALF, HALF)
        result[rows, :] = resid[rows, :] + scatter_out.total(half)
    scatter_out.finish()
    for by in ((1, 0), (0, 1), (0, 3)):
        pl.semaphore_signal(landing_free, inc=1, device_id=place.dev(*by), device_id_type=MESH)
    load = pltpu.make_async_copy(first_hbm, part_out, local_sems.at[0])
    load.start()
    sum_down.y_gather(sum_down.piece(), local_sems.at[3])
    sum_up.x_gather()

    def into_first(dy):
        rows = pl.ds(place.line(dy), LINE)

        for side in range(2):

            @pl.loop(0, rows_all // 256)
            def _(i):
                feats = pl.ds(pl.multiple_of(i * 256, 256), 256)
                cols = pl.ds(pl.multiple_of(side * rows_all + i * 256, 256), 256)
                part_back[rows, cols] = mm_nt(
                    d_qkv[rows, :], w_attn[feats, pl.ds(side * attn_cols, 4 * HEAD_DIM)]
                ).astype(low)

    into_first(1)
    pl.semaphore_wait(landing_free, 3)
    scatter_first.send_other()
    into_first(0)
    scatter_first.send_own()
    for by in ((0, 1, 0), (0, 3, 0), (1, 0, 0)):
        pl.semaphore_signal(
            heads_free, inc=1, device_id=place.rep_dev(*by), device_id_type=MESH
        )
    head_landed = cot_all.at[:, pl.ds(0, 6 * HEAD_DIM)]
    load.wait()

    sum_attn = RepSum(
        place,
        sems(RepSum.COPIES),
        pair.at[pl.ds(pl.multiple_of(place.core * rows_all, BLOCK), rows_all)],
        pair.at[pl.ds(pl.multiple_of((1 - place.core) * rows_all, BLOCK), rows_all)],
        d_up,
        [head_landed.at[pl.ds(e * BLOCK, BLOCK)] for e in range(2)],
        [head_landed.at[pl.ds((1 + e) * 2 * BLOCK, 2 * BLOCK)] for e in range(2)],
        head_landed.at[pl.ds(6 * BLOCK, BLOCK)],
        attn_grads,
        BLOCK,
        16,
    )

    @pl.loop(0, width // 256)
    def _(i):
        cols = pl.ds(pl.multiple_of(i * 256, 256), 256)
        from_first = mm_tn(part_out[:, cols], d_qkv[...]).astype(low)
        from_branch = mm_tn(branch[:, cols], attended[...]).astype(low)
        for piece in range(16):
            rows = pl.ds(pl.multiple_of(piece * BLOCK + i * 16, 16), 16)
            pair[rows, 0 : 4 * HEAD_DIM] = from_first[piece * 16 : piece * 16 + 16, :]
            pair[rows, 4 * HEAD_DIM :] = from_branch[piece * 16 : piece * 16 + 16, :]

    pl.semaphore_signal(
        core_free_sem, inc=1, device_id=place.rep_dev(0, 0, 1), device_id_type=MESH
    )
    pl.semaphore_wait(core_free_sem, 1)
    sum_attn.core_send()
    scatter_first.step_one()
    sum_gate.x_forward()
    pl.semaphore_wait(heads_free, 3)
    sum_attn.x_first()
    scatter_first.step_two()
    sum_down.x_gather()
    sum_up.x_forward()
    scatter_first.step_three()
    sum_gate.x_last()
    sum_attn.x_second()
    gain_rows = None
    for half in (1, 0):
        rows = pl.ds(half * HALF, HALF)
        d_first = scatter_first.total(half)
        back, gain_part = rms_backward(tokens[rows, :].astype(f32), gain_one[...], d_first)
        grad_tokens[rows, :] += back
        gain_part = jnp.sum(gain_part, axis=0, keepdims=True)
        gain_rows = gain_part if gain_rows is None else gain_rows + gain_part
    keep_gain(0, gain_rows)

    gain_net = Net(*sems(9))
    stages = (
        [place.dev(0, d) for d in (1, 2, 3)],
        [place.dev(1, 0)],
        [place.rep_dev(0, 0, 1)],
        [place.rep_dev(0, d, 0) for d in (1, 2, 3)],
        [place.rep_dev(1, 0, 0)],
    )

    def gain_send(stage):
        for i, dev in enumerate(stages[stage]):
            dst = gain_landed.at[3 * stage + i]
            gain_net.send(f"{stage}.{i}", gain_sums.at[stage], dst, dev, dst)

    def gain_add(stage):
        total = gain_sums[stage]
        for i in range(len(stages[stage])):
            gain_net.wait(f"{stage}.{i}")
            total = total + gain_landed[3 * stage + i]
        gain_sums[stage + 1] = total

    gain_send(0)
    sum_attn.y_send()
    sum_down.x_forward()
    gain_add(0)
    gain_send(1)
    sum_up.x_last()
    piece = sum_attn.piece()
    swap_net = Net(*sems(7))
    for dy in range(2):
        for dz in range(4):
            if dy or dz:
                to = place.block(dy, dz)
                src = piece.at[pl.ds(pl.multiple_of(to * 16, 16), 16)]
                dst = swapped.at[pl.ds(pl.multiple_of(place.shard * 16, 16), 16)]
                here = place.block(-dy, -dz)
                here = swapped.at[pl.ds(pl.multiple_of(here * 16, 16), 16)]
                swap_net.send(f"{dy}{dz}", src, dst, place.dev(dy, dz), here)
    own_rows = pl.ds(pl.multiple_of(place.shard * 16, 16), 16)
    swapped[own_rows, :] = piece[own_rows, :]
    gain_add(1)
    gain_send(2)
    sum_down.x_last()
    swap_net.finish()
    kv = 8 * HEAD_DIM
    for j in range(8):
        rows = pl.ds(j * 16, 16)
        at = 0
        for begin, size in ((0, 2), (2, 1), (3, 1), (4, 2)):
            assembled[:, at + j * size * HEAD_DIM : at + (j + 1) * size * HEAD_DIM] = swapped[
                rows, begin * HEAD_DIM : (begin + size) * HEAD_DIM
            ]
            at += size * kv
    sum_attn.y_gather(assembled, local_sems.at[3])
    gain_add(2)
    gain_send(3)
    sum_attn.x_gather()
    gain_add(3)
    gain_send(4)
    sum_attn.x_forward()
    sum_attn.x_last()
    gain_add(4)
    gains[...] = gain_sums[5]

    gather_branch.finish()
    scatter_first.finish()
    for one in sums:
        one.finish()
    sum_attn.finish()
    gain_net.finish()


def layer_call(lengths, *args):
    tokens, cotangent = args[:2]
    width = tokens.shape[1]
    hid = args[-1].shape[0]
    rows = 8 * BLOCK
    vmem = pl.BlockSpec(memory_space=pltpu.VMEM)
    smem = pl.BlockSpec(memory_space=pltpu.SMEM)
    hbm = pl.BlockSpec(memory_space=pltpu.HBM)
    copies = 4 * Gather.COPIES + 4 * Scatter.COPIES + 4 * RepSum.COPIES + 9 + 7 + 7
    gain_shape = (2 * width // HEAD_DIM + 8, HEAD_DIM)
    return pl.pallas_call(
        functools.partial(layer_kernel, 1.0 / math.sqrt(HEAD_DIM)),
        name="layer",
        out_shape=[
            jax.ShapeDtypeStruct((BLOCK, width), f32),
            jax.ShapeDtypeStruct((BLOCK, width), f32),
            jax.ShapeDtypeStruct(gain_shape, f32),
            jax.ShapeDtypeStruct((256, 3 * width), low),
            jax.ShapeDtypeStruct((3, hid, width), low),
            jax.ShapeDtypeStruct((3, hid // 2, width), low),
            jax.ShapeDtypeStruct((rows, width), low),
            jax.ShapeDtypeStruct((2 * rows, 6 * HEAD_DIM), low),
            jax.ShapeDtypeStruct((rows, 6 * HEAD_DIM), low),
        ],
        in_specs=[smem] + [vmem] * 6 + [hbm] * 7,
        out_specs=[vmem] * 3 + [hbm] * 6,
        scratch_shapes=[
            pltpu.VMEM((BLOCK, width), f32),
            pltpu.VMEM((2, width), f32),
            pltpu.VMEM((8, 16, 256), low),
            pltpu.VMEM((rows, 4 * HEAD_DIM), f32),
            pltpu.VMEM((rows, HEAD_DIM), f32),
            pltpu.VMEM((rows, HEAD_DIM), f32),
            pltpu.VMEM((rows, width), low),
            pltpu.VMEM((rows, width), low),
            pltpu.VMEM((rows, width), low),
            pltpu.VMEM((hid, width), low),
            pltpu.VMEM((hid, width), low),
            pltpu.VMEM((hid, width), low),
            pltpu.VMEM((2 * rows, hid), low),
            pltpu.VMEM((rows, hid), low),
            pltpu.VMEM((rows, width), low),
            pltpu.VMEM((rows, width), low),
            pltpu.VMEM((rows, 2 * HEAD_DIM), low),
            pltpu.VMEM((rows, HEAD_DIM), f32),
            pltpu.VMEM((rows, HEAD_DIM), f32),
            pltpu.VMEM((rows, 4 * HEAD_DIM), low),
            pltpu.VMEM((hid // 2, width), low),
        ]
        + Scatter.scratch(width)
        + [
            pltpu.VMEM((BLOCK, 6 * HEAD_DIM), low),
            pltpu.VMEM((16, 3 * width), low),
            pltpu.VMEM((6,) + gain_shape, f32),
            pltpu.VMEM((15,) + gain_shape, f32),
            pltpu.SemaphoreType.DMA((2, 2, 7)),
            pltpu.SemaphoreType.DMA((3, 2)),
            pltpu.SemaphoreType.REGULAR,
            pltpu.SemaphoreType.REGULAR,
            pltpu.SemaphoreType.REGULAR,
            pltpu.SemaphoreType.REGULAR,
            pltpu.SemaphoreType.DMA((6,)),
            pltpu.SemaphoreType.DMA((copies,)),
            pltpu.SemaphoreType.DMA((copies,)),
        ],
        compiler_params=pltpu.CompilerParams(
            collective_id=1, has_side_effects=True, vmem_limit_bytes=60 << 20
        ),
        cost_estimate=pl.CostEstimate(
            flops=36_000_000_000, bytes_accessed=60_000_000, transcendentals=4_000_000
        ),
    )(lengths, *args)


def per_device(
    tokens,
    cotangent,
    lengths,
    attn_gain,
    mlp_gain,
    query_gain,
    key_gain,
    w_query,
    w_key,
    w_value,
    w_out,
    w_gate,
    w_up,
    w_down,
):
    width = tokens.shape[1]
    shards = lax.axis_size("shard")
    feat = width // shards
    my_shard = lax.axis_index("shard")
    half = HEAD_DIM // 2
    frequency = theta_base ** (-jnp.arange(half, dtype=f32) * (2.0 / HEAD_DIM))
    frequency = jnp.concatenate([frequency, frequency])[None]
    gain_shard = jnp.concatenate([attn_gain[None], mlp_gain[None], jnp.zeros((14, feat), low)])
    result, grad_tokens, gains, attn_grads, ffn_grads, *_ = layer_call(
        lengths,
        tokens,
        cotangent,
        gain_shard,
        query_gain.astype(f32)[None],
        key_gain.astype(f32)[None],
        frequency,
        w_query,
        w_key,
        w_value,
        w_out,
        w_gate,
        w_up,
        w_down,
    )
    ffn_grads = ffn_grads.astype(f32)
    attn_grads = attn_grads.astype(f32)
    grad_query = attn_grads[:, :width]
    grad_key = attn_grads[:, width : width + width // 2]
    grad_value = attn_grads[:, width + width // 2 : 2 * width]
    grad_out = attn_grads[:, 2 * width :]
    gains = gains.reshape(-1)
    head_piece = HEAD_DIM // shards
    gains_first = lax.dynamic_slice_in_dim(gains, my_shard * feat, feat, 0)
    gains_second = lax.dynamic_slice_in_dim(gains, width + my_shard * feat, feat, 0)
    gains_query = lax.dynamic_slice_in_dim(gains, 2 * width + my_shard * head_piece, head_piece, 0)
    gains_key = lax.dynamic_slice_in_dim(
        gains, 2 * width + HEAD_DIM + my_shard * head_piece, head_piece, 0
    )
    return (
        result,
        grad_tokens,
        grad_query,
        grad_key,
        grad_value,
        grad_out,
        ffn_grads[0],
        ffn_grads[1],
        ffn_grads[2],
        gains_first,
        gains_second,
        gains_query,
        gains_key,
    )


def solution(mesh):
    spread = P(("rep", "shard"), None)
    rowed = P("shard", None)
    return jax.shard_map(
        per_device,
        mesh=mesh,
        in_specs=(spread, spread, P("rep", None), P("shard"), P("shard"), P(), P()) + (rowed,) * 7,
        out_specs=(spread, spread) + (rowed,) * 7 + (P("shard"),) * 4,
        check_vma=False,
    )
```

```python
import functools
import math

import jax
import jax.numpy as jnp
from jax import lax
from jax.experimental import pallas as pl
from jax.experimental.pallas import tpu as pltpu
from jax.sharding import PartitionSpec as P

HEADS = 16
KV_HEADS = 8
HEAD_DIM = 128

epsilon = 1e-06
theta_base = 1000000.0
masked_value = -1e30


MESH = pl.DeviceIdType.MESH
BLOCK = 128
HALF = 64
LINE = 512
low = jnp.bfloat16
f32 = jnp.float32


def mm(left, right):
    return lax.dot_general(left, right, (((1,), (0,)), ((), ())), preferred_element_type=f32)


def mm_nt(left, right):
    return lax.dot_general(left, right, (((1,), (1,)), ((), ())), preferred_element_type=f32)


def mm_tn(left, right):
    return lax.dot_general(left, right, (((0,), (0,)), ((), ())), preferred_element_type=f32)


class Place:
    def __init__(self):
        self.rep = lax.axis_index("rep")
        self.shard = lax.axis_index("shard")
        self.yl, self.z = self.shard // 4, self.shard % 4
        self.yh, self.x, self.core = self.rep // 8, (self.rep // 2) % 4, self.rep % 2

    def block(self, dy, dz):
        return ((self.yl + dy + 2) % 2) * 4 + (self.z + dz + 8) % 4

    def dev(self, dy, dz):
        return (self.rep, self.block(dy, dz))

    def x_at(self, dx):
        return (self.x + dx + 8) % 4

    def rep_dev(self, dyh, dx, dcore):
        rep = ((self.yh + dyh) % 2) * 8 + self.x_at(dx) * 2 + (self.core + dcore) % 2
        return (rep, self.shard)

    def rows(self, dy, dz, start=0, count=BLOCK):
        return pl.ds(pl.multiple_of(self.block(dy, dz) * BLOCK + start, 32), count)

    def line(self, dy):
        return pl.multiple_of(((self.yl + dy + 2) % 2) * LINE, LINE)

    def shard_peers(self):
        return [self.dev(dy, dz) for dy in range(2) for dz in range(4) if dy or dz]

    def rep_peers(self):
        return [
            self.rep_dev(*by) for by in ((0, 0, 1), (0, 1, 0), (0, 2, 0), (0, 3, 0), (1, 0, 0))
        ]

    def greet(self):
        barrier = pltpu.get_barrier_semaphore()
        peers = self.shard_peers() + self.rep_peers()
        for peer in peers:
            pl.semaphore_signal(barrier, inc=1, device_id=peer, device_id_type=MESH)
        pl.semaphore_wait(barrier, len(peers))


class Net:
    def __init__(self, send_sems, recv_sems):
        self.send_sems, self.recv_sems = send_sems, recv_sems
        self.started, self.coming = [], {}

    def send(self, tag, src, dst, dev, here):
        k = len(self.started)
        copy = pltpu.make_async_remote_copy(
            src_ref=src,
            dst_ref=dst,
            send_sem=self.send_sems.at[k],
            recv_sem=self.recv_sems.at[k],
            device_id=dev,
            device_id_type=MESH,
        )
        copy.start()
        self.started.append(copy)
        self.coming[tag] = (k, here, dev)

    def wait(self, tag):
        k, here, dev = self.coming.pop(tag)
        pltpu.make_async_remote_copy(
            src_ref=here,
            dst_ref=here,
            send_sem=self.send_sems.at[k],
            recv_sem=self.recv_sems.at[k],
            device_id=dev,
            device_id_type=MESH,
        ).wait_recv()

    def finish(self):
        for tag in list(self.coming):
            self.wait(tag)
        for copy in self.started:
            copy.wait_send()


class Gather:
    COPIES = 18

    def __init__(self, place, buf, send_sems, recv_sems):
        self.place, self.buf = place, buf
        self.net = Net(send_sems, recv_sems)

    def send(self, tag, block, start, count, to):
        rows = self.place.rows(*block, start, count)
        here = self.place.rows(block[0] - to[0], block[1] - to[1], start, count)
        self.net.send(
            tag, self.buf.at[rows], self.buf.at[rows], self.place.dev(*to), self.buf.at[here]
        )

    def start(self):
        self.send("y_up", (0, 0), 0, HALF, (1, 0))
        for d in (1, 3):
            self.send(f"z_low{d}", (0, 0), HALF, HALF, (0, d))
        self.send("y_low", (0, 0), HALF, HALF, (1, 0))

    def step_one(self):
        self.net.wait("y_up")
        for d in (1, 3):
            self.send(f"p_up{d}", (1, 0), 0, HALF, (0, d))

    def step_two(self):
        for e, d in enumerate((1, 3)):
            self.net.wait(f"z_low{d}")
            self.send(f"f_low{d}", (0, -d), HALF + 32 * e, 32, (0, d))
            self.send(f"q_low{d}", (0, -d), HALF, HALF, (1, 0))
        for d in (1, 3):
            self.send(f"z_up{d}", (0, 0), 0, HALF, (0, d))

    def step_three(self):
        for e, d in enumerate((1, 3)):
            self.net.wait(f"p_up{d}")
            self.send(f"f_p{d}", (1, -d), 32 * e, 32, (0, d))
        for e, d in enumerate((1, 3)):
            self.net.wait(f"f_low{d}")
            self.send(f"q_far{d}", (0, -2 * d), HALF + 32 * e, 32, (1, 0))

    def step_four(self):
        for e, d in enumerate((1, 3)):
            self.net.wait(f"z_up{d}")
            self.send(f"f_up{d}", (0, -d), 32 * e, 32, (0, d))

    def own_line(self):
        for d in (1, 3):
            self.net.wait(f"f_up{d}")

    def other_line(self):
        for tag in list(self.net.coming):
            self.net.wait(tag)

    def steps(self):
        return [self.start, self.step_one, self.step_two, self.step_three, self.step_four]

    def finish(self):
        self.net.finish()


class Scatter:
    COPIES = 17

    @staticmethod
    def scratch(columns):
        return [
            pltpu.VMEM((4, HALF, columns), low),
            pltpu.VMEM((3, 2, 32, columns), low),
            pltpu.VMEM((3, 2, HALF, columns), low),
            pltpu.VMEM((HALF, columns), low),
        ]

    def __init__(self, place, part, across, near, far, last, send_sems, recv_sems):
        self.place, self.part = place, part
        self.across, self.near, self.far, self.last = across, near, far, last
        self.net = Net(send_sems, recv_sems)

    def add(self, rows, *refs):
        total = self.part[rows, :].astype(f32)
        for ref in refs:
            total = total + ref[...].astype(f32)
        self.part[rows, :] = total.astype(low)

    def first(self, kind):
        dy, start = ((1, 0), (0, 0), (0, HALF))[kind]
        for e, d in enumerate((1, 3)):
            src = self.part.at[self.place.rows(dy, 2, start + 32 * e, 32)]
            dst = self.near.at[kind, e]
            self.net.send(f"near{kind}{e}", src, dst, self.place.dev(0, d), dst)

    def second(self, kind):
        dy, start = ((1, 0), (0, 0), (0, HALF))[kind]
        for e, d in enumerate((1, 3)):
            self.net.wait(f"near{kind}{e}")
            self.add(self.place.rows(dy, d, start + 32 * e, 32), self.near.at[kind, e])
            src = self.part.at[self.place.rows(dy, d, start, HALF)]
            dst = self.far.at[kind, e]
            self.net.send(f"far{kind}{e}", src, dst, self.place.dev(0, d), dst)

    def send_other(self):
        for d in (2, 1, 3, 0):
            src = self.part.at[self.place.rows(1, d, HALF, HALF)]
            dst = self.across.at[d]
            self.net.send(f"across{d}", src, dst, self.place.dev(1, 0), dst)
        self.first(0)

    def send_own(self):
        self.first(1)

    def step_one(self):
        self.net.wait("across2")
        self.add(self.place.rows(0, 2, HALF, HALF), self.across.at[2])
        self.first(2)
        self.second(0)
        self.second(1)

    def step_two(self):
        for d in (1, 3):
            self.net.wait(f"across{d}")
            self.add(self.place.rows(0, d, HALF, HALF), self.across.at[d])
        self.second(2)

    def step_three(self):
        for e in range(2):
            self.net.wait(f"far0{e}")
        rows = self.place.rows(1, 0, 0, HALF)
        self.add(rows, self.far.at[0, 0], self.far.at[0, 1])
        self.net.send("last", self.part.at[rows], self.last, self.place.dev(1, 0), self.last)

    def total(self, half):
        if half == 0:
            tags, extra, kind = ("far10", "far11", "last"), self.last, 1
        else:
            tags, extra, kind = ("far20", "far21", "across0"), self.across.at[0], 2
        for tag in tags:
            self.net.wait(tag)
        out = self.part[self.place.rows(0, 0, half * HALF, HALF), :].astype(f32)
        for ref in (self.far.at[kind, 0], self.far.at[kind, 1], extra):
            out = out + ref[...].astype(f32)
        return out

    def finish(self):
        self.net.finish()


def add_rows(into, start, count, *refs):
    step = 64 if count % 64 == 0 else 48

    @pl.loop(0, count // step)
    def _(i):
        at = pl.multiple_of(i * step, 16)
        rows = pl.ds(pl.multiple_of(start + at, 16), step)
        total = into[rows, :].astype(f32)
        for ref in refs:
            total = total + ref[pl.ds(at, step), :].astype(f32)
        into[rows, :] = total.astype(low)


class RepSum:
    COPIES = 15

    def __init__(self, place, sems, own, other, landed, near, far, cross, out, unit, out_unit):
        self.place, self.net = place, Net(*sems)
        self.own, self.other, self.landed = own, other, landed
        self.near, self.far, self.cross = near, far, cross
        self.out, self.unit, self.out_unit = out, unit, out_unit

    def chunk(self, dx, start=0, count=None):
        at = self.place.x_at(dx) * 2 * self.unit + start
        return pl.ds(pl.multiple_of(at, 16), 2 * self.unit if count is None else count)

    def out_rows(self, dcore, dx, start=0, count=None):
        core = (self.place.core + dcore) % 2
        at = (core * 8 + self.place.x_at(dx) * 2 + start) * self.out_unit
        count = (2 if count is None else count) * self.out_unit
        return self.out.at[pl.ds(pl.multiple_of(at, 16), count)]

    def core_send(self):
        self.net.send("core", self.other, self.landed, self.place.rep_dev(0, 0, 1), self.landed)

    def x_first(self, load=None):
        self.net.wait("core")
        add_rows(self.own, 0, 8 * self.unit, self.landed if load is None else load())
        for e, d in enumerate((1, 3)):
            src = self.own.at[self.chunk(2, e * self.unit, self.unit)]
            dst = self.near[e]
            self.net.send(f"near{e}", src, dst, self.place.rep_dev(0, d, 0), dst)

    def x_second(self):
        for e, d in enumerate((1, 3)):
            self.net.wait(f"near{e}")
            add_rows(self.own, self.place.x_at(d) * 2 * self.unit + e * self.unit, self.unit, self.near[e])
            dst = self.far[e]
            self.net.send(
                f"far{e}", self.own.at[self.chunk(d)], dst, self.place.rep_dev(0, d, 0), dst
            )

    def y_send(self):
        for e in range(2):
            self.net.wait(f"far{e}")
        add_rows(self.own, self.place.x * 2 * self.unit, 2 * self.unit, *self.far)
        src = self.own.at[self.chunk(0, (1 - self.place.yh) * self.unit, self.unit)]
        self.net.send("cross", src, self.cross, self.place.rep_dev(1, 0, 0), self.cross)

    def piece(self):
        self.net.wait("cross")
        at = (self.place.x * 2 + self.place.yh) * self.unit
        add_rows(self.own, at, self.unit, self.cross)
        return self.own.at[pl.ds(pl.multiple_of(at, 16), self.unit)]

    def y_gather(self, piece, sem):
        mine = self.out_rows(0, 0, self.place.yh, 1)
        copy = pltpu.make_async_copy(piece, mine, sem)
        copy.start()
        self.net.send(
            "y", piece, mine, self.place.rep_dev(1, 0, 0), self.out_rows(0, 0, 1 - self.place.yh, 1)
        )
        copy.wait()

    def to_core(self, dx):
        rows = self.out_rows(0, dx)
        self.net.send(
            f"core{dx}", rows, rows, self.place.rep_dev(0, 0, 1), self.out_rows(1, dx)
        )

    def x_gather(self):
        self.net.wait("y")
        rows = self.out_rows(0, 0)
        for d in (1, 3):
            self.net.send(f"x{d}", rows, rows, self.place.rep_dev(0, d, 0), self.out_rows(0, -d))
        self.to_core(0)

    def x_forward(self):
        for e, d in enumerate((1, 3)):
            self.net.wait(f"x{d}")
            rows = self.out_rows(0, -d, e, 1)
            self.net.send(
                f"xx{d}", rows, rows, self.place.rep_dev(0, d, 0), self.out_rows(0, -2 * d, e, 1)
            )
            self.to_core(-d)

    def x_last(self):
        for d in (1, 3):
            self.net.wait(f"xx{d}")
        self.to_core(2)

    def finish(self):
        self.net.finish()


def rms_backward(value, gain, upstream):
    root = lax.rsqrt(jnp.mean(value * value, axis=-1, keepdims=True) + epsilon)
    pulled = upstream * gain
    back = root * pulled - value * (root * root * root) * jnp.mean(
        pulled * value, axis=-1, keepdims=True
    )
    return back, upstream * (value * root)


def swap_halves(value):
    return pltpu.roll(value, HEAD_DIM // 2, 1)


def layer_kernel(
    scale,
    lengths,
    tokens,
    cotangent,
    gain_shard,
    query_gain,
    key_gain,
    frequency,
    w_query_hbm,
    w_key_hbm,
    w_value_hbm,
    w_out_hbm,
    w_gate_hbm,
    w_up_hbm,
    w_down_hbm,
    result,
    grad_tokens,
    gains,
    attn_grads,
    ffn_grads,
    core_landed,
    first_hbm,
    w_attn_hbm,
    heads_hbm,
    resid,
    gain_rows_all,
    gain_blocks,
    proj,
    cosine,
    sine,
    second,
    cot_all,
    branch,
    w_gate,
    w_up,
    w_down,
    pair,
    d_up,
    part_out,
    part_back,
    d_att,
    d_key,
    d_value,
    d_qkv,
    staged,
    across,
    near,
    far,
    last,
    swapped,
    assembled,
    gain_sums,
    gain_landed,
    swap_sems,
    sibling_sems,
    free_sem,
    core_free_sem,
    landing_free,
    heads_free,
    local_sems,
    send_sems,
    recv_sems,
):
    place = Place()
    hidden = pair.at[pl.ds(0, 8 * BLOCK)]
    d_gate = pair.at[pl.ds(8 * BLOCK, 8 * BLOCK)]
    rows_all = 8 * BLOCK
    hid = w_gate.shape[0]
    width = second.shape[1]

    loads = [
        pltpu.make_async_copy(src, dst, local_sems.at[i])
        for i, (src, dst) in enumerate(
            ((w_gate_hbm, w_gate), (w_up_hbm, w_up), (w_down_hbm, w_down))
        )
    ]
    for load in loads:
        load.start()

    used = [0]

    def sems(count):
        at = used[0]
        used[0] += count
        return send_sems.at[pl.ds(at, count)], recv_sems.at[pl.ds(at, count)]

    own = place.rows(0, 0)
    gain_one = gain_rows_all.at[pl.ds(0, 1)]
    gain_two = gain_rows_all.at[pl.ds(1, 1)]
    cot_all[own, :] = cotangent[...].astype(low)
    branch[own, :] = tokens[...]
    feat = w_query_hbm.shape[0]
    gain_blocks[place.shard] = gain_shard[...]
    place.greet()

    gain_share = Net(*sems(7))
    peers = [(dy, dz) for dy in range(2) for dz in range(4) if dy or dz]
    for by in peers:
        gain_share.send(
            str(by),
            gain_blocks.at[place.shard],
            gain_blocks.at[place.shard],
            place.dev(*by),
            gain_blocks.at[place.block(-by[0], -by[1])],
        )
    qkv_parts = (
        (w_query_hbm, 0, 2 * HEAD_DIM),
        (w_key_hbm, 2 * HEAD_DIM, HEAD_DIM),
        (w_value_hbm, 3 * HEAD_DIM, HEAD_DIM),
    )
    out_parts = ((w_out_hbm, 4 * HEAD_DIM, 2 * HEAD_DIM),)
    half_rows = feat // 2
    qkv_span = pl.ds(0, 4 * HEAD_DIM)
    out_span = pl.ds(4 * HEAD_DIM, 2 * HEAD_DIM)

    def swap_rows(block):
        at = block * feat + place.core * half_rows
        return pl.ds(pl.multiple_of(at, half_rows), half_rows)

    def swap_copy(src, dst, kind, i, dev):
        return pltpu.make_async_remote_copy(
            src_ref=src,
            dst_ref=dst,
            send_sem=swap_sems.at[0, kind, i],
            recv_sem=swap_sems.at[1, kind, i],
            device_id=dev,
            device_id_type=MESH,
        )

    def swap_send(parts, kind):
        for i, by in enumerate(peers):
            to = place.block(*by)
            for whole, begin, size in parts:
                cols = pl.ds(pl.multiple_of(to * size, HEAD_DIM), size)
                src = whole.at[pl.ds(pl.multiple_of(place.core * half_rows, half_rows), half_rows), cols]
                dst = pair.at[swap_rows(place.shard), pl.ds(begin, size)]
                swap_copy(src, dst, kind, i, place.dev(*by)).start()
        for whole, begin, size in parts:
            cols = pl.ds(pl.multiple_of(place.shard * size, HEAD_DIM), size)
            rows = pl.ds(pl.multiple_of(place.shard * feat, feat), feat)
            copy = pltpu.make_async_copy(
                whole.at[:, cols], pair.at[rows, pl.ds(begin, size)], sibling_sems.at[2, kind]
            )
            copy.start()

    def sibling_copy(ref, kind):
        return pltpu.make_async_remote_copy(
            src_ref=ref,
            dst_ref=ref,
            send_sem=sibling_sems.at[0, kind],
            recv_sem=sibling_sems.at[1, kind],
            device_id=place.rep_dev(0, 0, 1),
            device_id_type=MESH,
        )

    def swap_relay(span, kind):
        for i, by in enumerate(peers):
            here = pair.at[swap_rows(place.block(-by[0], -by[1])), span]
            swap_copy(here, here, kind, i, place.dev(*by)).wait_recv()
            sibling_copy(here, kind).start()

    def swap_done(span, kind):
        rows = pl.ds(pl.multiple_of(place.shard * feat, feat), feat)
        mine = pair.at[rows, span]
        pltpu.make_async_copy(mine, mine, sibling_sems.at[2, kind]).wait()
        others = pair.at[pl.ds(0, 7 * half_rows), span]
        sibling_copy(others, kind).wait()
        for i, by in enumerate(peers):
            here = pair.at[swap_rows(place.block(-by[0], -by[1])), span]
            swap_copy(here, here, kind, i, place.dev(*by)).wait_send()

    swap_send(qkv_parts, 0)
    gather_tokens = Gather(place, branch, *sems(Gather.COPIES))
    gather_tokens.start()

    start_one = lengths[0, 0]
    start_two = lengths[0, 0] + lengths[0, 1]

    def begin_of(token):
        return jnp.where(
            token >= start_two, start_two, jnp.where(token >= start_one, start_one, 0)
        )

    token = lax.broadcasted_iota(jnp.int32, (rows_all, 1), 0)
    angles = (token - begin_of(token)).astype(f32) * frequency[...]
    lane = lax.broadcasted_iota(jnp.int32, (1, HEAD_DIM), 1)
    cosine[...] = jnp.cos(angles)
    sine[...] = jnp.sin(angles) * jnp.where(lane < HEAD_DIM // 2, -1.0, 1.0)

    gather_tokens.step_one()
    gather_tokens.step_two()
    gain_share.finish()
    for j in range(8):
        span = slice(j * feat, (j + 1) * feat)
        gain_rows_all[0:2, span] = gain_blocks[j, 0:2, :].astype(f32)
    swap_relay(qkv_span, 0)
    swap_send(out_parts, 1)
    gather_tokens.step_three()
    gather_tokens.step_four()

    def normalise(dy):
        line = place.line(dy)

        @pl.loop(0, LINE // BLOCK)
        def _(i):
            rows = pl.ds(pl.multiple_of(line + i * BLOCK, BLOCK), BLOCK)
            x = branch[rows, :].astype(f32)
            root = lax.rsqrt(jnp.mean(x * x, axis=-1, keepdims=True) + epsilon)
            second[rows, :] = (x * root * gain_one[...]).astype(low)

    gather_tokens.own_line()
    normalise(0)
    gather_tokens.other_line()
    normalise(1)
    gather_tokens.finish()
    keep_first = pltpu.make_async_copy(second, first_hbm, local_sems.at[3])
    keep_first.start()
    swap_done(qkv_span, 0)
    heads = d_up
    gains_of_head = (query_gain, query_gain, key_gain)

    @pl.loop(0, rows_all // 256)
    def _(i):
        rows = pl.ds(pl.multiple_of(i * 256, 256), 256)
        proj[rows, :] = mm(second[rows, :], pair[:, 0 : 4 * HEAD_DIM])
        for g in range(3):
            lanes = pl.ds(g * HEAD_DIM, HEAD_DIM)
            u = proj[rows, lanes]
            root = lax.rsqrt(jnp.mean(u * u, axis=-1, keepdims=True) + epsilon)
            u = u * root * gains_of_head[g][...]
            heads[rows, lanes] = (u * cosine[rows, :] + swap_halves(u) * sine[rows, :]).astype(low)
        lanes = pl.ds(3 * HEAD_DIM, HEAD_DIM)
        heads[rows, lanes] = proj[rows, lanes].astype(low)

    swap_relay(out_span, 1)
    gather_cot = Gather(place, cot_all, *sems(Gather.COPIES))
    gather_cot.start()
    chunk = 256
    for part in range(rows_all // chunk):
        rows = pl.ds(part * chunk, chunk)
        seen = (part + 1) * chunk
        token = part * chunk + lax.broadcasted_iota(jnp.int32, (chunk, 1), 0)
        source = lax.broadcasted_iota(jnp.int32, (1, seen), 1)
        visible = (source >= begin_of(token)) & (source <= token)
        for g in range(2):
            lanes = pl.ds(g * HEAD_DIM, HEAD_DIM)
            scores = mm_nt(heads[rows, lanes], heads[0:seen, 2 * HEAD_DIM : 3 * HEAD_DIM]) * scale
            scores = jnp.where(visible, scores, masked_value)
            top = jnp.max(scores, axis=-1, keepdims=True)
            raised = jnp.exp(scores - top)
            total = jnp.sum(raised, axis=-1, keepdims=True)
            probs = (raised * (1.0 / total)).astype(low)
            proj[rows, 3 * HEAD_DIM + g : 3 * HEAD_DIM + g + 1] = jnp.log(total) + top
            heads[rows, pl.ds((4 + g) * HEAD_DIM, HEAD_DIM)] = mm(
                probs, heads[0:seen, 3 * HEAD_DIM : 4 * HEAD_DIM]
            ).astype(low)
        if part == 1:
            gather_cot.step_one()
    keep_heads = pltpu.make_async_copy(heads, heads_hbm, local_sems.at[4])
    keep_heads.start()
    swap_done(out_span, 1)
    keep_weights = pltpu.make_async_copy(pair, w_attn_hbm, local_sems.at[5])
    keep_weights.start()
    landing = (across, near, far, last)
    scatter_attn = Scatter(place, part_back, *landing, *sems(Scatter.COPIES))

    def attention_out(dy):
        rows = pl.ds(place.line(dy), LINE)

        @pl.loop(0, width // 256)
        def _(i):
            cols = pl.ds(pl.multiple_of(i * 256, 256), 256)
            part_back[rows, cols] = mm_nt(
                heads[rows, 4 * HEAD_DIM :], pair[cols, 4 * HEAD_DIM :]
            ).astype(low)

    attention_out(1)
    keep_first.wait()
    scatter_attn.send_other()
    attention_out(0)
    scatter_attn.send_own()
    scatter_attn.step_one()
    scatter_attn.step_two()
    scatter_attn.step_three()
    keep_heads.wait()
    keep_weights.wait()
    for half in (1, 0):
        rows = pl.ds(half * HALF, HALF)
        x = tokens[rows, :].astype(f32) + scatter_attn.total(half)
        resid[rows, :] = x
        root = lax.rsqrt(jnp.mean(x * x, axis=-1, keepdims=True) + epsilon)
        at = place.rows(0, 0, half * HALF, HALF)
        second[at, :] = (x * root * gain_two[...]).astype(low)
    scatter_attn.finish()
    gather_second = Gather(place, second, *sems(Gather.COPIES))
    gather_branch = Gather(place, branch, *sems(Gather.COPIES))
    scatter_out = Scatter(place, part_out, *landing, *sems(Scatter.COPIES))
    scatter_back = Scatter(place, part_back, *landing, *sems(Scatter.COPIES))

    def feed_forward(rows):
        @pl.loop(0, hid // 256)
        def _(i):
            cols = pl.ds(pl.multiple_of(i * 256, 256), 256)
            gate = mm_nt(second[rows, :], w_gate[cols, :])
            up = mm_nt(second[rows, :], w_up[cols, :])
            sigma = 1.0 / (1.0 + jnp.exp(-gate))
            silu = gate * sigma
            hidden[rows, cols] = (silu * up).astype(low)
            d_gate[rows, cols] = (up * sigma * (1.0 + gate * (1.0 - sigma))).astype(low)
            d_up[rows, cols] = silu.astype(low)

    def project_out(dy):
        rows = pl.ds(place.line(dy), LINE)

        @pl.loop(0, width // 512)
        def _(i):
            cols = pl.ds(pl.multiple_of(i * 512, 512), 512)
            part_out[rows, cols] = mm(hidden[rows, :], w_down[:, cols]).astype(low)

    def feed_backward(dy):
        rows = pl.ds(place.line(dy), LINE)

        @pl.loop(0, hid // 256)
        def _(i):
            cols = pl.ds(pl.multiple_of(i * 256, 256), 256)
            d_hidden = mm_nt(cot_all[rows, :], w_down[cols, :])
            d_gate[rows, cols] = (d_hidden * d_gate[rows, cols].astype(f32)).astype(low)
            d_up[rows, cols] = (d_hidden * d_up[rows, cols].astype(f32)).astype(low)

        @pl.loop(0, width // 512)
        def _(i):
            cols = pl.ds(pl.multiple_of(i * 512, 512), 512)
            part_back[rows, cols] = (
                mm(d_gate[rows, :], w_gate[:, cols]) + mm(d_up[rows, :], w_up[:, cols])
            ).astype(low)

    def weight_grad(into, left, right):
        @pl.loop(0, hid // 256)
        def _(i):
            cols = pl.ds(pl.multiple_of(i * 256, 256), 256)
            into[cols, :] = mm_tn(left[:, cols], right[...]).astype(low)

    unit = hid // 16
    sums = []
    for i, whole in enumerate((w_gate, w_up, w_down)):
        base = i * 7 * unit

        def view(start, count, base=base):
            return second.at[pl.ds(base + start * unit, count * unit)]

        sums.append(
            RepSum(
                place,
                sems(RepSum.COPIES),
                whole.at[pl.ds(pl.multiple_of(place.core * 8 * unit, 16), 8 * unit)],
                whole.at[pl.ds(pl.multiple_of((1 - place.core) * 8 * unit, 16), 8 * unit)],
                core_landed.at[i],
                [view(0, 1), view(1, 1)],
                [view(2, 2), view(4, 2)],
                view(6, 1),
                ffn_grads.at[i],
                unit,
                unit,
            )
        )
    sum_gate, sum_up, sum_down = sums

    def load_landed(i):
        def load():
            here = staged.at[pl.ds(0, 8 * unit)]
            copy = pltpu.make_async_copy(core_landed.at[i], here, local_sems.at[3])
            copy.start()
            copy.wait()
            return here

        return load

    gather_second.start()
    for load in loads:
        load.wait()
    feed_forward(own)
    gather_second.step_one()
    gather_second.step_two()
    gather_second.step_three()
    gather_second.step_four()
    gather_cot.step_two()
    feed_forward(place.rows(0, 1))
    feed_forward(place.rows(0, 3))
    gather_second.own_line()
    gather_cot.step_three()
    feed_forward(place.rows(0, 2))
    gather_second.other_line()
    gather_cot.step_four()
    feed_forward(pl.ds(place.line(1), LINE))
    project_out(1)
    project_out(0)
    gather_cot.own_line()
    gather_cot.other_line()
    feed_backward(1)
    scatter_back.send_other()
    feed_backward(0)
    scatter_back.send_own()
    weight_grad(w_gate, d_gate, second)
    sum_gate.core_send()
    scatter_back.step_one()
    weight_grad(w_up, d_up, second)
    sum_up.core_send()
    gather_second.finish()
    for by in ((0, 1, 0), (0, 3, 0), (1, 0, 0)):
        pl.semaphore_signal(
            free_sem, inc=1, device_id=place.rep_dev(*by), device_id_type=MESH
        )
    scatter_back.step_two()
    weight_grad(w_down, hidden, cot_all)
    sum_down.core_send()
    pl.semaphore_wait(free_sem, 3)
    sum_gate.x_first(load_landed(0))
    sum_up.x_first(load_landed(1))
    gather_cot.finish()
    q_cols = 2 * HEAD_DIM
    query = heads.at[:, pl.ds(0, q_cols)]
    key = heads.at[:, pl.ds(q_cols, HEAD_DIM)]
    value = heads.at[:, pl.ds(q_cols + HEAD_DIM, HEAD_DIM)]
    attended = heads.at[:, pl.ds(q_cols + 2 * HEAD_DIM, q_cols)]
    w_attn = cot_all
    attn_cols = heads.shape[1]
    loads = [
        pltpu.make_async_copy(heads_hbm, heads, local_sems.at[0]),
        pltpu.make_async_copy(
            w_attn_hbm.at[pl.ds(0, rows_all)],
            w_attn.at[:, pl.ds(0, attn_cols)],
            local_sems.at[1],
        ),
        pltpu.make_async_copy(
            w_attn_hbm.at[pl.ds(rows_all, rows_all)],
            w_attn.at[:, pl.ds(attn_cols, attn_cols)],
            local_sems.at[2],
        ),
    ]
    for load in loads:
        load.start()
    scatter_back.step_three()
    gain_rows = None
    for half in (1, 0):
        rows = pl.ds(half * HALF, HALF)
        d_second = scatter_back.total(half)
        back, gain_part = rms_backward(resid[rows, :], gain_two[...], d_second)
        grad_tokens[rows, :] = cotangent[rows, :] + back
        gain_part = jnp.sum(gain_part, axis=0, keepdims=True)
        gain_rows = gain_part if gain_rows is None else gain_rows + gain_part
    gain_sums[0] = jnp.zeros_like(gain_sums[0])

    def keep_gain(first_row, value):
        for i in range(value.shape[1] // HEAD_DIM):
            gain_sums[0, first_row + i : first_row + i + 1, :] = value[
                :, i * HEAD_DIM : (i + 1) * HEAD_DIM
            ]

    gain_slots = width // HEAD_DIM
    keep_gain(gain_slots, gain_rows)
    branch[own, :] = grad_tokens[...].astype(low)
    gather_branch.start()
    sum_down.x_first(load_landed(2))
    gather_branch.step_one()
    sum_gate.x_second()
    gather_branch.step_two()
    sum_up.x_second()
    gather_branch.step_three()
    gather_branch.step_four()
    gather_branch.own_line()
    for load in loads:
        load.wait()

    def into_attention(dy):
        rows = pl.ds(place.line(dy), LINE)
        d_att[rows, :] = (
            mm(branch[rows, 0:rows_all], w_attn[:, 4 * HEAD_DIM : attn_cols])
            + mm(branch[rows, rows_all:], w_attn[:, attn_cols + 4 * HEAD_DIM : 2 * attn_cols])
        ).astype(low)

    into_attention(0)
    gather_branch.other_line()
    scatter_out.send_other()
    scatter_out.send_own()
    into_attention(1)
    sum_down.x_second()
    scatter_back.finish()
    load = pltpu.make_async_copy(first_hbm, part_back, local_sems.at[0])
    load.start()

    def unrotate(rows, upstream, projected, gain):
        turned = upstream * cosine[rows, :] - swap_halves(upstream) * sine[rows, :]
        return rms_backward(projected, gain, turned)

    gain_rows = jnp.zeros((1, HEAD_DIM), f32)
    d_key[...] = jnp.zeros_like(d_key)
    d_value[...] = jnp.zeros_like(d_value)
    for part in range(rows_all // chunk):
        rows = pl.ds(part * chunk, chunk)
        seen = (part + 1) * chunk
        token = part * chunk + lax.broadcasted_iota(jnp.int32, (chunk, 1), 0)
        source = lax.broadcasted_iota(jnp.int32, (1, seen), 1)
        visible = (source >= begin_of(token)) & (source <= token)
        for g in range(2):
            lanes = pl.ds(g * HEAD_DIM, HEAD_DIM)
            scores = mm_nt(query[rows, lanes], key[0:seen, :]) * scale
            weights = jnp.where(visible, jnp.exp(scores - proj[rows, 3 * HEAD_DIM + g : 3 * HEAD_DIM + g + 1]), 0.0)
            d_probs = mm_nt(d_att[rows, lanes], value[0:seen, :])
            inner = jnp.sum(weights * d_probs, axis=-1, keepdims=True)
            d_scores = (weights * (d_probs - inner)).astype(low)
            back, gain_part = unrotate(
                rows, mm(d_scores, key[0:seen, :]) * scale, proj[rows, lanes], query_gain[...]
            )
            d_qkv[rows, lanes] = back.astype(low)
            gain_rows = gain_rows + jnp.sum(gain_part, axis=0, keepdims=True)
            d_key[0:seen, :] += mm_tn(d_scores, query[rows, lanes])
            d_value[0:seen, :] += mm_tn(weights.astype(low), d_att[rows, lanes])
        if part == 0:
            sum_gate.y_send()
        if part == 1:
            scatter_out.step_one()
            sum_up.y_send()
            sum_gate.y_gather(sum_gate.piece(), local_sems.at[3])
        if part == 2:
            scatter_out.step_two()
            sum_down.y_send()
            sum_up.y_gather(sum_up.piece(), local_sems.at[3])
            sum_gate.x_gather()
    d_qkv[:, 3 * HEAD_DIM :] = d_value[...].astype(low)

    keep_gain(2 * gain_slots, gain_rows)
    lanes = pl.ds(2 * HEAD_DIM, HEAD_DIM)
    back, gain_part = unrotate(pl.ds(0, rows_all), d_key[...] * scale, proj[:, lanes], key_gain[...])
    d_qkv[:, lanes] = back.astype(low)
    keep_gain(2 * gain_slots + 1, jnp.sum(gain_part, axis=0, keepdims=True))

    head_landed = cot_all.at[:, pl.ds(0, 6 * HEAD_DIM)]
    sum_attn = RepSum(
        place,
        sems(RepSum.COPIES),
        pair.at[pl.ds(pl.multiple_of(place.core * rows_all, BLOCK), rows_all)],
        pair.at[pl.ds(pl.multiple_of((1 - place.core) * rows_all, BLOCK), rows_all)],
        d_up,
        [head_landed.at[pl.ds(e * BLOCK, BLOCK)] for e in range(2)],
        [head_landed.at[pl.ds((1 + e) * 2 * BLOCK, 2 * BLOCK)] for e in range(2)],
        head_landed.at[pl.ds(6 * BLOCK, BLOCK)],
        attn_grads,
        BLOCK,
        16,
    )

    load.wait()

    @pl.loop(0, width // 256)
    def _(i):
        cols = pl.ds(pl.multiple_of(i * 256, 256), 256)
        from_first = mm_tn(part_back[:, cols], d_qkv[...]).astype(low)
        from_branch = mm_tn(branch[:, cols], attended[...]).astype(low)
        for piece in range(16):
            rows = pl.ds(pl.multiple_of(piece * BLOCK + i * 16, 16), 16)
            pair[rows, 0 : 4 * HEAD_DIM] = from_first[piece * 16 : piece * 16 + 16, :]
            pair[rows, 4 * HEAD_DIM :] = from_branch[piece * 16 : piece * 16 + 16, :]

    pl.semaphore_signal(
        core_free_sem, inc=1, device_id=place.rep_dev(0, 0, 1), device_id_type=MESH
    )
    pl.semaphore_wait(core_free_sem, 1)
    sum_attn.core_send()
    scatter_out.step_three()
    for half in (0, 1):
        rows = pl.ds(half * HALF, HALF)
        result[rows, :] = resid[rows, :] + scatter_out.total(half)
    scatter_out.finish()
    for by in ((1, 0), (0, 1), (0, 3)):
        pl.semaphore_signal(landing_free, inc=1, device_id=place.dev(*by), device_id_type=MESH)
    scatter_first = Scatter(place, part_back, *landing, *sems(Scatter.COPIES))

    def into_first(dy):
        rows = pl.ds(place.line(dy), LINE)

        for side in range(2):

            @pl.loop(0, rows_all // 256)
            def _(i):
                feats = pl.ds(pl.multiple_of(i * 256, 256), 256)
                cols = pl.ds(pl.multiple_of(side * rows_all + i * 256, 256), 256)
                part_back[rows, cols] = mm_nt(
                    d_qkv[rows, :], w_attn[feats, pl.ds(side * attn_cols, 4 * HEAD_DIM)]
                ).astype(low)

    into_first(1)
    pl.semaphore_wait(landing_free, 3)
    scatter_first.send_other()
    into_first(0)
    scatter_first.send_own()
    for by in ((0, 1, 0), (0, 3, 0), (1, 0, 0)):
        pl.semaphore_signal(
            heads_free, inc=1, device_id=place.rep_dev(*by), device_id_type=MESH
        )
    sum_down.y_gather(sum_down.piece(), local_sems.at[3])
    sum_up.x_gather()
    pl.semaphore_wait(heads_free, 3)
    sum_attn.x_first()
    scatter_first.step_one()
    sum_gate.x_forward()
    scatter_first.step_two()
    sum_attn.x_second()
    sum_down.x_gather()
    sum_up.x_forward()
    scatter_first.step_three()
    sum_gate.x_last()
    gain_rows = None
    for half in (1, 0):
        rows = pl.ds(half * HALF, HALF)
        d_first = scatter_first.total(half)
        back, gain_part = rms_backward(tokens[rows, :].astype(f32), gain_one[...], d_first)
        grad_tokens[rows, :] += back
        gain_part = jnp.sum(gain_part, axis=0, keepdims=True)
        gain_rows = gain_part if gain_rows is None else gain_rows + gain_part
    keep_gain(0, gain_rows)

    gain_net = Net(*sems(9))
    stages = (
        [place.dev(0, d) for d in (1, 2, 3)],
        [place.dev(1, 0)],
        [place.rep_dev(0, 0, 1)],
        [place.rep_dev(0, d, 0) for d in (1, 2, 3)],
        [place.rep_dev(1, 0, 0)],
    )

    def gain_send(stage):
        for i, dev in enumerate(stages[stage]):
            dst = gain_landed.at[3 * stage + i]
            gain_net.send(f"{stage}.{i}", gain_sums.at[stage], dst, dev, dst)

    def gain_add(stage):
        total = gain_sums[stage]
        for i in range(len(stages[stage])):
            gain_net.wait(f"{stage}.{i}")
            total = total + gain_landed[3 * stage + i]
        gain_sums[stage + 1] = total

    gain_send(0)
    sum_attn.y_send()
    sum_down.x_forward()
    gain_add(0)
    gain_send(1)
    sum_up.x_last()
    piece = sum_attn.piece()
    swap_net = Net(*sems(7))
    for dy in range(2):
        for dz in range(4):
            if dy or dz:
                to = place.block(dy, dz)
                src = piece.at[pl.ds(pl.multiple_of(to * 16, 16), 16)]
                dst = swapped.at[pl.ds(pl.multiple_of(place.shard * 16, 16), 16)]
                here = place.block(-dy, -dz)
                here = swapped.at[pl.ds(pl.multiple_of(here * 16, 16), 16)]
                swap_net.send(f"{dy}{dz}", src, dst, place.dev(dy, dz), here)
    own_rows = pl.ds(pl.multiple_of(place.shard * 16, 16), 16)
    swapped[own_rows, :] = piece[own_rows, :]
    gain_add(1)
    gain_send(2)
    sum_down.x_last()
    swap_net.finish()
    kv = 8 * HEAD_DIM
    for j in range(8):
        rows = pl.ds(j * 16, 16)
        at = 0
        for begin, size in ((0, 2), (2, 1), (3, 1), (4, 2)):
            assembled[:, at + j * size * HEAD_DIM : at + (j + 1) * size * HEAD_DIM] = swapped[
                rows, begin * HEAD_DIM : (begin + size) * HEAD_DIM
            ]
            at += size * kv
    sum_attn.y_gather(assembled, local_sems.at[3])
    gain_add(2)
    gain_send(3)
    sum_attn.x_gather()
    gain_add(3)
    gain_send(4)
    sum_attn.x_forward()
    sum_attn.x_last()
    gain_add(4)
    gains[...] = gain_sums[5]

    gather_branch.finish()
    scatter_first.finish()
    for one in sums:
        one.finish()
    sum_attn.finish()
    gain_net.finish()


def layer_call(lengths, *args):
    tokens, cotangent = args[:2]
    width = tokens.shape[1]
    hid = args[-1].shape[0]
    rows = 8 * BLOCK
    vmem = pl.BlockSpec(memory_space=pltpu.VMEM)
    smem = pl.BlockSpec(memory_space=pltpu.SMEM)
    hbm = pl.BlockSpec(memory_space=pltpu.HBM)
    copies = 4 * Gather.COPIES + 4 * Scatter.COPIES + 4 * RepSum.COPIES + 9 + 7 + 7
    gain_shape = (2 * width // HEAD_DIM + 8, HEAD_DIM)
    return pl.pallas_call(
        functools.partial(layer_kernel, 1.0 / math.sqrt(HEAD_DIM)),
        name="layer",
        out_shape=[
            jax.ShapeDtypeStruct((BLOCK, width), f32),
            jax.ShapeDtypeStruct((BLOCK, width), f32),
            jax.ShapeDtypeStruct(gain_shape, f32),
            jax.ShapeDtypeStruct((256, 3 * width), low),
            jax.ShapeDtypeStruct((3, hid, width), low),
            jax.ShapeDtypeStruct((3, hid // 2, width), low),
            jax.ShapeDtypeStruct((rows, width), low),
            jax.ShapeDtypeStruct((2 * rows, 6 * HEAD_DIM), low),
            jax.ShapeDtypeStruct((rows, 6 * HEAD_DIM), low),
        ],
        in_specs=[smem] + [vmem] * 6 + [hbm] * 7,
        out_specs=[vmem] * 3 + [hbm] * 6,
        scratch_shapes=[
            pltpu.VMEM((BLOCK, width), f32),
            pltpu.VMEM((2, width), f32),
            pltpu.VMEM((8, 16, 256), low),
            pltpu.VMEM((rows, 4 * HEAD_DIM), f32),
            pltpu.VMEM((rows, HEAD_DIM), f32),
            pltpu.VMEM((rows, HEAD_DIM), f32),
            pltpu.VMEM((rows, width), low),
            pltpu.VMEM((rows, width), low),
            pltpu.VMEM((rows, width), low),
            pltpu.VMEM((hid, width), low),
            pltpu.VMEM((hid, width), low),
            pltpu.VMEM((hid, width), low),
            pltpu.VMEM((2 * rows, hid), low),
            pltpu.VMEM((rows, hid), low),
            pltpu.VMEM((rows, width), low),
            pltpu.VMEM((rows, width), low),
            pltpu.VMEM((rows, 2 * HEAD_DIM), low),
            pltpu.VMEM((rows, HEAD_DIM), f32),
            pltpu.VMEM((rows, HEAD_DIM), f32),
            pltpu.VMEM((rows, 4 * HEAD_DIM), low),
            pltpu.VMEM((hid // 2, width), low),
        ]
        + Scatter.scratch(width)
        + [
            pltpu.VMEM((BLOCK, 6 * HEAD_DIM), low),
            pltpu.VMEM((16, 3 * width), low),
            pltpu.VMEM((6,) + gain_shape, f32),
            pltpu.VMEM((15,) + gain_shape, f32),
            pltpu.SemaphoreType.DMA((2, 2, 7)),
            pltpu.SemaphoreType.DMA((3, 2)),
            pltpu.SemaphoreType.REGULAR,
            pltpu.SemaphoreType.REGULAR,
            pltpu.SemaphoreType.REGULAR,
            pltpu.SemaphoreType.REGULAR,
            pltpu.SemaphoreType.DMA((6,)),
            pltpu.SemaphoreType.DMA((copies,)),
            pltpu.SemaphoreType.DMA((copies,)),
        ],
        compiler_params=pltpu.CompilerParams(
            collective_id=1, has_side_effects=True, vmem_limit_bytes=60 << 20
        ),
        cost_estimate=pl.CostEstimate(
            flops=36_000_000_000, bytes_accessed=60_000_000, transcendentals=4_000_000
        ),
    )(lengths, *args)


def widen_kernel(ffn, attn, gate, up, down, query, key, value, out):
    step = pl.program_id(0)
    per = pl.num_programs(0) // 3
    wide = ffn[0].astype(f32)
    for which, ref in enumerate((gate, up, down)):

        @pl.when(step // per == which)
        def _(ref=ref):
            ref[...] = wide

    at = 0
    for ref in (query, key, value, out):
        ref[...] = attn[:, at : at + ref.shape[1]].astype(f32)
        at += ref.shape[1]


def widen(ffn, attn):
    _, hid, width = ffn.shape
    rows = attn.shape[0]
    per, tall, some = 3, hid // 3, rows // 8

    def block_of(which):
        return lambda i: (jnp.clip(i - which * per, 0, per - 1), 0)

    def attn_block(i):
        return (jnp.minimum(i, 7), 0)

    sizes = (width, width // 2, width // 2, width)
    return pl.pallas_call(
        widen_kernel,
        name="widen",
        grid=(3 * per,),
        out_shape=[jax.ShapeDtypeStruct((hid, width), f32)] * 3
        + [jax.ShapeDtypeStruct((rows, size), f32) for size in sizes],
        in_specs=[
            pl.BlockSpec((1, tall, width), lambda i: (i // per, i % per, 0)),
            pl.BlockSpec((some, 3 * width), attn_block),
        ],
        out_specs=[pl.BlockSpec((tall, width), block_of(which)) for which in range(3)]
        + [pl.BlockSpec((some, size), attn_block) for size in sizes],
        compiler_params=pltpu.CompilerParams(vmem_limit_bytes=40 << 20),
    )(ffn, attn)


def per_device(
    tokens,
    cotangent,
    lengths,
    attn_gain,
    mlp_gain,
    query_gain,
    key_gain,
    w_query,
    w_key,
    w_value,
    w_out,
    w_gate,
    w_up,
    w_down,
):
    width = tokens.shape[1]
    shards = lax.axis_size("shard")
    feat = width // shards
    my_shard = lax.axis_index("shard")
    half = HEAD_DIM // 2
    frequency = theta_base ** (-jnp.arange(half, dtype=f32) * (2.0 / HEAD_DIM))
    frequency = jnp.concatenate([frequency, frequency])[None]
    gain_shard = jnp.concatenate([attn_gain[None], mlp_gain[None], jnp.zeros((14, feat), low)])
    result, grad_tokens, gains, attn_grads, ffn_grads, *_ = layer_call(
        lengths,
        tokens,
        cotangent,
        gain_shard,
        query_gain.astype(f32)[None],
        key_gain.astype(f32)[None],
        frequency,
        w_query,
        w_key,
        w_value,
        w_out,
        w_gate,
        w_up,
        w_down,
    )
    grad_gate, grad_up, grad_down, grad_query, grad_key, grad_value, grad_out = widen(
        ffn_grads, attn_grads
    )
    gains = gains.reshape(-1)
    head_piece = HEAD_DIM // shards
    gains_first = lax.dynamic_slice_in_dim(gains, my_shard * feat, feat, 0)
    gains_second = lax.dynamic_slice_in_dim(gains, width + my_shard * feat, feat, 0)
    gains_query = lax.dynamic_slice_in_dim(gains, 2 * width + my_shard * head_piece, head_piece, 0)
    gains_key = lax.dynamic_slice_in_dim(
        gains, 2 * width + HEAD_DIM + my_shard * head_piece, head_piece, 0
    )
    return (
        result,
        grad_tokens,
        grad_query,
        grad_key,
        grad_value,
        grad_out,
        grad_gate,
        grad_up,
        grad_down,
        gains_first,
        gains_second,
        gains_query,
        gains_key,
    )


def solution(mesh):
    spread = P(("rep", "shard"), None)
    rowed = P("shard", None)
    return jax.shard_map(
        per_device,
        mesh=mesh,
        in_specs=(spread, spread, P("rep", None), P("shard"), P("shard"), P(), P()) + (rowed,) * 7,
        out_specs=(spread, spread) + (rowed,) * 7 + (P("shard"),) * 4,
        check_vma=False,
    )
```

```python
import functools
import math

import jax
import jax.numpy as jnp
import numpy as np
from jax import lax
from jax.experimental import pallas as pl
from jax.experimental.pallas import tpu as pltpu
from jax.sharding import PartitionSpec as P

HEADS = 16
KV_HEADS = 8
HEAD_DIM = 128

epsilon = 1e-06
theta_base = 1000000.0
masked_value = -1e30


MESH = pl.DeviceIdType.MESH
BLOCK = 128
HALF = 64
LINE = 512
low = jnp.bfloat16
f32 = jnp.float32


def mm(left, right):
    return lax.dot_general(left, right, (((1,), (0,)), ((), ())), preferred_element_type=f32)


def mm_nt(left, right):
    return lax.dot_general(left, right, (((1,), (1,)), ((), ())), preferred_element_type=f32)


def mm_tn(left, right):
    return lax.dot_general(left, right, (((0,), (0,)), ((), ())), preferred_element_type=f32)


class Place:
    def __init__(self):
        self.rep = lax.axis_index("rep")
        self.shard = lax.axis_index("shard")
        self.yl, self.z = self.shard // 4, self.shard % 4
        self.yh, self.x, self.core = self.rep // 8, (self.rep // 2) % 4, self.rep % 2

    def block(self, dy, dz):
        return ((self.yl + dy + 2) % 2) * 4 + (self.z + dz + 8) % 4

    def dev(self, dy, dz):
        return (self.rep, self.block(dy, dz))

    def x_at(self, dx):
        return (self.x + dx + 8) % 4

    def rep_dev(self, dyh, dx, dcore):
        rep = ((self.yh + dyh) % 2) * 8 + self.x_at(dx) * 2 + (self.core + dcore) % 2
        return (rep, self.shard)

    def rows(self, dy, dz, start=0, count=BLOCK):
        return pl.ds(pl.multiple_of(self.block(dy, dz) * BLOCK + start, 32), count)

    def line(self, dy):
        return pl.multiple_of(((self.yl + dy + 2) % 2) * LINE, LINE)

    def shard_peers(self):
        return [self.dev(dy, dz) for dy in range(2) for dz in range(4) if dy or dz]

    def rep_peers(self):
        return [
            self.rep_dev(*by) for by in ((0, 0, 1), (0, 1, 0), (0, 2, 0), (0, 3, 0), (1, 0, 0))
        ]

    def greet(self):
        barrier = pltpu.get_barrier_semaphore()
        peers = self.shard_peers() + self.rep_peers()
        for peer in peers:
            pl.semaphore_signal(barrier, inc=1, device_id=peer, device_id_type=MESH)
        pl.semaphore_wait(barrier, len(peers))


class Net:
    def __init__(self, send_sems, recv_sems):
        self.send_sems, self.recv_sems = send_sems, recv_sems
        self.started, self.coming = [], {}

    def send(self, tag, src, dst, dev, here):
        k = len(self.started)
        copy = pltpu.make_async_remote_copy(
            src_ref=src,
            dst_ref=dst,
            send_sem=self.send_sems.at[k],
            recv_sem=self.recv_sems.at[k],
            device_id=dev,
            device_id_type=MESH,
        )
        copy.start()
        self.started.append(copy)
        self.coming[tag] = (k, here, dev)

    def wait(self, tag):
        k, here, dev = self.coming.pop(tag)
        pltpu.make_async_remote_copy(
            src_ref=here,
            dst_ref=here,
            send_sem=self.send_sems.at[k],
            recv_sem=self.recv_sems.at[k],
            device_id=dev,
            device_id_type=MESH,
        ).wait_recv()

    def finish(self):
        for tag in list(self.coming):
            self.wait(tag)
        for copy in self.started:
            copy.wait_send()


class Gather:
    COPIES = 18

    def __init__(self, place, buf, send_sems, recv_sems):
        self.place, self.buf = place, buf
        self.net = Net(send_sems, recv_sems)

    def send(self, tag, block, start, count, to):
        rows = self.place.rows(*block, start, count)
        here = self.place.rows(block[0] - to[0], block[1] - to[1], start, count)
        self.net.send(
            tag, self.buf.at[rows], self.buf.at[rows], self.place.dev(*to), self.buf.at[here]
        )

    def start(self):
        self.send("y_up", (0, 0), 0, HALF, (1, 0))
        for d in (1, 3):
            self.send(f"z_low{d}", (0, 0), HALF, HALF, (0, d))
        self.send("y_low", (0, 0), HALF, HALF, (1, 0))

    def step_one(self):
        self.net.wait("y_up")
        for d in (1, 3):
            self.send(f"p_up{d}", (1, 0), 0, HALF, (0, d))

    def step_two(self):
        for e, d in enumerate((1, 3)):
            self.net.wait(f"z_low{d}")
            self.send(f"f_low{d}", (0, -d), HALF + 32 * e, 32, (0, d))
            self.send(f"q_low{d}", (0, -d), HALF, HALF, (1, 0))
        for d in (1, 3):
            self.send(f"z_up{d}", (0, 0), 0, HALF, (0, d))

    def step_three(self):
        for e, d in enumerate((1, 3)):
            self.net.wait(f"p_up{d}")
            self.send(f"f_p{d}", (1, -d), 32 * e, 32, (0, d))
        for e, d in enumerate((1, 3)):
            self.net.wait(f"f_low{d}")
            self.send(f"q_far{d}", (0, -2 * d), HALF + 32 * e, 32, (1, 0))

    def step_four(self):
        for e, d in enumerate((1, 3)):
            self.net.wait(f"z_up{d}")
            self.send(f"f_up{d}", (0, -d), 32 * e, 32, (0, d))

    def own_line(self):
        for d in (1, 3):
            self.net.wait(f"f_up{d}")

    def other_line(self):
        for tag in list(self.net.coming):
            self.net.wait(tag)

    def steps(self):
        return [self.start, self.step_one, self.step_two, self.step_three, self.step_four]

    def finish(self):
        self.net.finish()


class Slots:
    def __init__(self, ref, base, size):
        self.ref, self.base, self.size = ref, base, size

    @property
    def at(self):
        return self

    def __getitem__(self, i):
        i = i if isinstance(i, int) else 2 * i[0] + i[1]
        return self.ref.at[pl.ds(self.base + i * self.size, self.size)]


class Scatter:
    COPIES = 17

    @staticmethod
    def scratch(columns):
        return [
            pltpu.VMEM((4, HALF, columns), low),
            pltpu.VMEM((3, 2, 32, columns), low),
            pltpu.VMEM((3, 2, HALF, columns), low),
            pltpu.VMEM((HALF, columns), low),
        ]

    def __init__(self, place, part, across, near, far, last, send_sems, recv_sems):
        self.place, self.part = place, part
        self.across, self.near, self.far, self.last = across, near, far, last
        self.net = Net(send_sems, recv_sems)

    def add(self, rows, *refs):
        total = self.part[rows, :].astype(f32)
        for ref in refs:
            total = total + ref[...].astype(f32)
        self.part[rows, :] = total.astype(low)

    def first(self, kind):
        dy, start = ((1, 0), (0, 0), (0, HALF))[kind]
        for e, d in enumerate((1, 3)):
            src = self.part.at[self.place.rows(dy, 2, start + 32 * e, 32)]
            dst = self.near.at[kind, e]
            self.net.send(f"near{kind}{e}", src, dst, self.place.dev(0, d), dst)

    def second(self, kind):
        dy, start = ((1, 0), (0, 0), (0, HALF))[kind]
        for e, d in enumerate((1, 3)):
            self.net.wait(f"near{kind}{e}")
            self.add(self.place.rows(dy, d, start + 32 * e, 32), self.near.at[kind, e])
            src = self.part.at[self.place.rows(dy, d, start, HALF)]
            dst = self.far.at[kind, e]
            self.net.send(f"far{kind}{e}", src, dst, self.place.dev(0, d), dst)

    def send_other(self):
        for d in (2, 1, 3, 0):
            src = self.part.at[self.place.rows(1, d, HALF, HALF)]
            dst = self.across.at[d]
            self.net.send(f"across{d}", src, dst, self.place.dev(1, 0), dst)
        self.first(0)

    def send_own(self):
        self.first(1)

    def step_one(self):
        self.net.wait("across2")
        self.add(self.place.rows(0, 2, HALF, HALF), self.across.at[2])
        self.first(2)
        self.second(0)
        self.second(1)

    def step_two(self):
        for d in (1, 3):
            self.net.wait(f"across{d}")
            self.add(self.place.rows(0, d, HALF, HALF), self.across.at[d])
        self.second(2)

    def step_three(self):
        for e in range(2):
            self.net.wait(f"far0{e}")
        rows = self.place.rows(1, 0, 0, HALF)
        self.add(rows, self.far.at[0, 0], self.far.at[0, 1])
        self.net.send("last", self.part.at[rows], self.last, self.place.dev(1, 0), self.last)

    def total(self, half):
        if half == 0:
            tags, extra, kind = ("far10", "far11", "last"), self.last, 1
        else:
            tags, extra, kind = ("far20", "far21", "across0"), self.across.at[0], 2
        for tag in tags:
            self.net.wait(tag)
        out = self.part[self.place.rows(0, 0, half * HALF, HALF), :].astype(f32)
        for ref in (self.far.at[kind, 0], self.far.at[kind, 1], extra):
            out = out + ref[...].astype(f32)
        return out

    def finish(self):
        self.net.finish()


def add_rows(into, start, count, *refs):
    step = 64 if count % 64 == 0 else 48

    @pl.loop(0, count // step)
    def _(i):
        at = pl.multiple_of(i * step, 16)
        rows = pl.ds(pl.multiple_of(start + at, 16), step)
        total = into[rows, :].astype(f32)
        for ref in refs:
            total = total + ref[pl.ds(at, step), :].astype(f32)
        into[rows, :] = total.astype(low)


class RepSum:
    COPIES = 15

    def __init__(self, place, sems, own, other, landed, near, far, cross, out, unit, out_unit):
        self.place, self.net = place, Net(*sems)
        self.own, self.other, self.landed = own, other, landed
        self.near, self.far, self.cross = near, far, cross
        self.out, self.unit, self.out_unit = out, unit, out_unit

    def chunk(self, dx, start=0, count=None):
        at = self.place.x_at(dx) * 2 * self.unit + start
        return pl.ds(pl.multiple_of(at, 16), 2 * self.unit if count is None else count)

    def out_rows(self, dcore, dx, start=0, count=None):
        core = (self.place.core + dcore) % 2
        at = (core * 8 + self.place.x_at(dx) * 2 + start) * self.out_unit
        count = (2 if count is None else count) * self.out_unit
        return self.out.at[pl.ds(pl.multiple_of(at, 16), count)]

    def core_send(self):
        self.net.send("core", self.other, self.landed, self.place.rep_dev(0, 0, 1), self.landed)

    def x_first(self, load=None):
        self.net.wait("core")
        add_rows(self.own, 0, 8 * self.unit, self.landed if load is None else load())
        for e, d in enumerate((1, 3)):
            src = self.own.at[self.chunk(2, e * self.unit, self.unit)]
            dst = self.near[e]
            self.net.send(f"near{e}", src, dst, self.place.rep_dev(0, d, 0), dst)

    def x_second(self):
        for e, d in enumerate((1, 3)):
            self.net.wait(f"near{e}")
            add_rows(self.own, self.place.x_at(d) * 2 * self.unit + e * self.unit, self.unit, self.near[e])
            dst = self.far[e]
            self.net.send(
                f"far{e}", self.own.at[self.chunk(d)], dst, self.place.rep_dev(0, d, 0), dst
            )

    def y_send(self):
        for e in range(2):
            self.net.wait(f"far{e}")
        add_rows(self.own, self.place.x * 2 * self.unit, 2 * self.unit, *self.far)
        src = self.own.at[self.chunk(0, (1 - self.place.yh) * self.unit, self.unit)]
        self.net.send("cross", src, self.cross, self.place.rep_dev(1, 0, 0), self.cross)

    def piece(self):
        self.net.wait("cross")
        at = (self.place.x * 2 + self.place.yh) * self.unit
        add_rows(self.own, at, self.unit, self.cross)
        return self.own.at[pl.ds(pl.multiple_of(at, 16), self.unit)]

    def y_gather(self, piece, sem):
        mine = self.out_rows(0, 0, self.place.yh, 1)
        copy = pltpu.make_async_copy(piece, mine, sem)
        copy.start()
        self.net.send(
            "y", piece, mine, self.place.rep_dev(1, 0, 0), self.out_rows(0, 0, 1 - self.place.yh, 1)
        )
        copy.wait()

    def to_core(self, dx):
        rows = self.out_rows(0, dx)
        self.net.send(
            f"core{dx}", rows, rows, self.place.rep_dev(0, 0, 1), self.out_rows(1, dx)
        )

    def x_gather(self):
        self.net.wait("y")
        rows = self.out_rows(0, 0)
        for d in (1, 3):
            self.net.send(f"x{d}", rows, rows, self.place.rep_dev(0, d, 0), self.out_rows(0, -d))
        self.to_core(0)

    def x_forward(self):
        for e, d in enumerate((1, 3)):
            self.net.wait(f"x{d}")
            rows = self.out_rows(0, -d, e, 1)
            self.net.send(
                f"xx{d}", rows, rows, self.place.rep_dev(0, d, 0), self.out_rows(0, -2 * d, e, 1)
            )
            self.to_core(-d)

    def x_last(self):
        for d in (1, 3):
            self.net.wait(f"xx{d}")
        self.to_core(2)

    def finish(self):
        self.net.finish()


def rms_backward(value, gain, upstream):
    root = lax.rsqrt(jnp.mean(value * value, axis=-1, keepdims=True) + epsilon)
    pulled = upstream * gain
    back = root * pulled - value * (root * root * root) * jnp.mean(
        pulled * value, axis=-1, keepdims=True
    )
    return back, upstream * (value * root)


def swap_halves(value):
    return pltpu.roll(value, HEAD_DIM // 2, 1)


def layer_kernel(
    scale,
    lengths,
    tokens,
    cotangent,
    attn_gain,
    mlp_gain,
    query_gain,
    key_gain,
    frequency,
    w_query_hbm,
    w_key_hbm,
    w_value_hbm,
    w_out_hbm,
    w_gate_hbm,
    w_up_hbm,
    w_down_hbm,
    result,
    grad_tokens,
    gains,
    attn_grads,
    ffn_grads,
    core_landed,
    head_core_landed,
    first_hbm,
    w_attn_hbm,
    heads_hbm,
    resid,
    gain_rows_all,
    gain_blocks,
    proj,
    cosine,
    sine,
    second,
    cot_all,
    branch,
    w_gate,
    w_up,
    w_down,
    pair,
    d_up,
    part_out,
    part_back,
    d_att,
    d_key,
    d_value,
    d_qkv,
    staged,
    across,
    near,
    far,
    last,
    swapped,
    assembled,
    gain_sums,
    gain_landed,
    swap_sems,
    sibling_sems,
    free_sem,
    landing_free,
    heads_free,
    local_sems,
    send_sems,
    recv_sems,
):
    place = Place()
    hidden = pair.at[pl.ds(0, 8 * BLOCK)]
    d_gate = pair.at[pl.ds(8 * BLOCK, 8 * BLOCK)]
    rows_all = 8 * BLOCK
    hid = w_gate.shape[0]
    width = second.shape[1]

    loads = [
        pltpu.make_async_copy(src, dst, local_sems.at[i])
        for i, (src, dst) in enumerate(
            ((w_gate_hbm, w_gate), (w_up_hbm, w_up), (w_down_hbm, w_down))
        )
    ]
    for load in loads:
        load.start()

    used = [0]

    def sems(count):
        at = used[0]
        used[0] += count
        return send_sems.at[pl.ds(at, count)], recv_sems.at[pl.ds(at, count)]

    own = place.rows(0, 0)
    gain_one = gain_rows_all.at[pl.ds(0, 1)]
    gain_two = gain_rows_all.at[pl.ds(1, 1)]
    cot_all[own, :] = cotangent[...].astype(low)
    branch[own, :] = tokens[...]
    feat = w_query_hbm.shape[0]
    at = lax.broadcasted_iota(jnp.int32, (16, attn_gain.shape[1]), 0)
    gain_blocks[place.shard] = jnp.where(
        at == 0, attn_gain[...].astype(f32), mlp_gain[...].astype(f32)
    ).astype(low)
    place.greet()

    gain_share = Net(*sems(7))
    peers = [(dy, dz) for dy in range(2) for dz in range(4) if dy or dz]
    for by in peers:
        gain_share.send(
            str(by),
            gain_blocks.at[place.shard],
            gain_blocks.at[place.shard],
            place.dev(*by),
            gain_blocks.at[place.block(-by[0], -by[1])],
        )
    qkv_parts = (
        (w_query_hbm, 0, 2 * HEAD_DIM),
        (w_key_hbm, 2 * HEAD_DIM, HEAD_DIM),
        (w_value_hbm, 3 * HEAD_DIM, HEAD_DIM),
    )
    out_parts = ((w_out_hbm, 4 * HEAD_DIM, 2 * HEAD_DIM),)
    few = feat // 8
    qkv_span = pl.ds(0, 4 * HEAD_DIM)
    out_span = pl.ds(4 * HEAD_DIM, 2 * HEAD_DIM)

    def swap_rows(block, dx=0, count=1):
        first = place.x_at(dx) if count == 1 else 0
        at = block * feat + (place.core * 4 + first) * few
        return pl.ds(pl.multiple_of(at, few), count * few)

    def swap_copy(src, dst, kind, i, dev):
        return pltpu.make_async_remote_copy(
            src_ref=src,
            dst_ref=dst,
            send_sem=swap_sems.at[0, kind, i],
            recv_sem=swap_sems.at[1, kind, i],
            device_id=dev,
            device_id_type=MESH,
        )

    def swap_send(parts, kind):
        own_rows = pl.ds(pl.multiple_of((place.core * 4 + place.x) * few, few), few)
        for i, by in enumerate(peers):
            to = place.block(*by)
            for whole, begin, size in parts:
                cols = pl.ds(pl.multiple_of(to * size, HEAD_DIM), size)
                src = whole.at[own_rows, cols]
                dst = pair.at[swap_rows(place.shard), pl.ds(begin, size)]
                swap_copy(src, dst, kind, i, place.dev(*by)).start()
        for whole, begin, size in parts:
            cols = pl.ds(pl.multiple_of(place.shard * size, HEAD_DIM), size)
            rows = pl.ds(pl.multiple_of(place.shard * feat, feat), feat)
            copy = pltpu.make_async_copy(
                whole.at[:, cols], pair.at[rows, pl.ds(begin, size)], sibling_sems.at[2, kind]
            )
            copy.start()

    def share_copy(ref, kind, i):
        return swap_copy(
            ref, ref, kind, 7 + i, place.rep_dev(0, i + 1, 0) if i < 3 else place.rep_dev(0, 0, 1)
        )

    def swap_relay(span, kind):
        for i, by in enumerate(peers):
            here = pair.at[swap_rows(place.block(-by[0], -by[1])), span]
            swap_copy(here, here, kind, i, place.dev(*by)).wait_recv()
            for d in range(3):
                share_copy(here, kind, d).start()

    def swap_share(span, kind):
        for d in range(3):
            share_copy(pair.at[pl.ds(0, 7 * few), span], kind, d).wait_recv()
        for by in peers:
            here = pair.at[swap_rows(place.block(-by[0], -by[1]), 0, 4), span]
            share_copy(here, kind, 3).start()

    def swap_done(span, kind):
        rows = pl.ds(pl.multiple_of(place.shard * feat, feat), feat)
        mine = pair.at[rows, span]
        pltpu.make_async_copy(mine, mine, sibling_sems.at[2, kind]).wait()
        share_copy(pair.at[pl.ds(0, 7 * 4 * few), span], kind, 3).wait()
        for d in range(3):
            share_copy(pair.at[pl.ds(0, 7 * few), span], kind, d).wait_send()
        for i, by in enumerate(peers):
            here = pair.at[swap_rows(place.block(-by[0], -by[1])), span]
            swap_copy(here, here, kind, i, place.dev(*by)).wait_send()

    swap_send(qkv_parts, 0)
    gather_tokens = Gather(place, branch, *sems(Gather.COPIES))
    gather_tokens.start()

    start_one = lengths[0, 0]
    start_two = lengths[0, 0] + lengths[0, 1]

    def begin_of(token):
        return jnp.where(
            token >= start_two, start_two, jnp.where(token >= start_one, start_one, 0)
        )

    token = lax.broadcasted_iota(jnp.int32, (rows_all, 1), 0)
    angles = (token - begin_of(token)).astype(f32) * frequency[...]
    lane = lax.broadcasted_iota(jnp.int32, (1, HEAD_DIM), 1)
    cosine[...] = jnp.cos(angles)
    sine[...] = jnp.sin(angles) * jnp.where(lane < HEAD_DIM // 2, -1.0, 1.0)

    gather_tokens.step_one()
    swap_relay(qkv_span, 0)
    gather_tokens.step_two()
    gain_share.finish()
    for j in range(8):
        span = slice(j * feat, (j + 1) * feat)
        gain_rows_all[0:2, span] = gain_blocks[j, 0:2, :].astype(f32)
    gather_tokens.step_three()
    swap_share(qkv_span, 0)
    swap_send(out_parts, 1)
    gather_tokens.step_four()

    def normalise(dy):
        line = place.line(dy)

        @pl.loop(0, LINE // BLOCK)
        def _(i):
            rows = pl.ds(pl.multiple_of(line + i * BLOCK, BLOCK), BLOCK)
            x = branch[rows, :].astype(f32)
            root = lax.rsqrt(jnp.mean(x * x, axis=-1, keepdims=True) + epsilon)
            second[rows, :] = (x * root * gain_one[...]).astype(low)

    gather_tokens.own_line()
    normalise(0)
    gather_tokens.other_line()
    normalise(1)
    gather_tokens.finish()
    keep_first = pltpu.make_async_copy(second, first_hbm, local_sems.at[3])
    keep_first.start()
    gather_cot = Gather(place, cot_all, *sems(Gather.COPIES))
    gather_cot.start()
    swap_relay(out_span, 1)
    swap_done(qkv_span, 0)
    heads = d_up
    gains_of_head = (query_gain, query_gain, key_gain)

    @pl.loop(0, rows_all // 256)
    def _(i):
        rows = pl.ds(pl.multiple_of(i * 256, 256), 256)
        proj[rows, :] = mm(second[rows, :], pair[:, 0 : 4 * HEAD_DIM])
        for g in range(3):
            lanes = pl.ds(g * HEAD_DIM, HEAD_DIM)
            u = proj[rows, lanes]
            root = lax.rsqrt(jnp.mean(u * u, axis=-1, keepdims=True) + epsilon)
            u = u * root * gains_of_head[g][...].astype(f32)
            heads[rows, lanes] = (u * cosine[rows, :] + swap_halves(u) * sine[rows, :]).astype(low)
        lanes = pl.ds(3 * HEAD_DIM, HEAD_DIM)
        heads[rows, lanes] = proj[rows, lanes].astype(low)

    swap_share(out_span, 1)
    chunk = 256
    for part in range(rows_all // chunk):
        rows = pl.ds(part * chunk, chunk)
        seen = (part + 1) * chunk
        token = part * chunk + lax.broadcasted_iota(jnp.int32, (chunk, 1), 0)
        source = lax.broadcasted_iota(jnp.int32, (1, seen), 1)
        visible = (source >= begin_of(token)) & (source <= token)
        for g in range(2):
            lanes = pl.ds(g * HEAD_DIM, HEAD_DIM)
            scores = mm_nt(heads[rows, lanes], heads[0:seen, 2 * HEAD_DIM : 3 * HEAD_DIM]) * scale
            scores = jnp.where(visible, scores, masked_value)
            top = jnp.max(scores, axis=-1, keepdims=True)
            raised = jnp.exp(scores - top)
            total = jnp.sum(raised, axis=-1, keepdims=True)
            probs = (raised * (1.0 / total)).astype(low)
            proj[rows, 3 * HEAD_DIM + g : 3 * HEAD_DIM + g + 1] = jnp.log(total) + top
            heads[rows, pl.ds((4 + g) * HEAD_DIM, HEAD_DIM)] = mm(
                probs, heads[0:seen, 3 * HEAD_DIM : 4 * HEAD_DIM]
            ).astype(low)
        if part == 2:
            gather_cot.step_one()
    keep_heads = pltpu.make_async_copy(heads, heads_hbm, local_sems.at[4])
    keep_heads.start()
    swap_done(out_span, 1)
    keep_weights = pltpu.make_async_copy(pair, w_attn_hbm, local_sems.at[5])
    keep_weights.start()
    landing = (across, near, far, last)
    scatter_attn = Scatter(place, part_back, *landing, *sems(Scatter.COPIES))

    def attention_out(dy):
        rows = pl.ds(place.line(dy), LINE)

        @pl.loop(0, width // 256)
        def _(i):
            cols = pl.ds(pl.multiple_of(i * 256, 256), 256)
            part_back[rows, cols] = mm_nt(
                heads[rows, 4 * HEAD_DIM :], pair[cols, 4 * HEAD_DIM :]
            ).astype(low)

    attention_out(1)
    keep_first.wait()
    scatter_attn.send_other()
    attention_out(0)
    scatter_attn.send_own()
    scatter_attn.step_one()
    scatter_attn.step_two()
    scatter_attn.step_three()
    keep_heads.wait()
    keep_weights.wait()
    for half in (1, 0):
        rows = pl.ds(half * HALF, HALF)
        x = tokens[rows, :].astype(f32) + scatter_attn.total(half)
        resid[rows, :] = x
        root = lax.rsqrt(jnp.mean(x * x, axis=-1, keepdims=True) + epsilon)
        at = place.rows(0, 0, half * HALF, HALF)
        second[at, :] = (x * root * gain_two[...]).astype(low)
    scatter_attn.finish()
    gather_second = Gather(place, second, *sems(Gather.COPIES))
    gather_branch = Gather(place, branch, *sems(Gather.COPIES))
    scatter_out = Scatter(place, part_out, *landing, *sems(Scatter.COPIES))
    scatter_back = Scatter(place, part_back, *landing, *sems(Scatter.COPIES))

    def feed_forward(rows):
        @pl.loop(0, hid // 256)
        def _(i):
            cols = pl.ds(pl.multiple_of(i * 256, 256), 256)
            gate = mm_nt(second[rows, :], w_gate[cols, :])
            up = mm_nt(second[rows, :], w_up[cols, :])
            sigma = 1.0 / (1.0 + jnp.exp(-gate))
            silu = gate * sigma
            hidden[rows, cols] = (silu * up).astype(low)
            d_gate[rows, cols] = (up * sigma * (1.0 + gate * (1.0 - sigma))).astype(low)
            d_up[rows, cols] = silu.astype(low)

    def project_out(dy):
        rows = pl.ds(place.line(dy), LINE)

        @pl.loop(0, width // 512)
        def _(i):
            cols = pl.ds(pl.multiple_of(i * 512, 512), 512)
            part_out[rows, cols] = mm(hidden[rows, :], w_down[:, cols]).astype(low)

    def feed_backward(dy):
        rows = pl.ds(place.line(dy), LINE)

        @pl.loop(0, hid // 256)
        def _(i):
            cols = pl.ds(pl.multiple_of(i * 256, 256), 256)
            d_hidden = mm_nt(cot_all[rows, :], w_down[cols, :])
            d_gate[rows, cols] = (d_hidden * d_gate[rows, cols].astype(f32)).astype(low)
            d_up[rows, cols] = (d_hidden * d_up[rows, cols].astype(f32)).astype(low)

        @pl.loop(0, width // 512)
        def _(i):
            cols = pl.ds(pl.multiple_of(i * 512, 512), 512)
            part_back[rows, cols] = (
                mm(d_gate[rows, :], w_gate[:, cols]) + mm(d_up[rows, :], w_up[:, cols])
            ).astype(low)

    def weight_grad(into, left, right):
        @pl.loop(0, hid // 256)
        def _(i):
            cols = pl.ds(pl.multiple_of(i * 256, 256), 256)
            into[cols, :] = mm_tn(left[:, cols], right[...]).astype(low)

    unit = hid // 16
    sums = []
    for i, whole in enumerate((w_gate, w_up, w_down)):
        base = i * 7 * unit

        def view(start, count, base=base):
            return second.at[pl.ds(base + start * unit, count * unit)]

        sums.append(
            RepSum(
                place,
                sems(RepSum.COPIES),
                whole.at[pl.ds(pl.multiple_of(place.core * 8 * unit, 16), 8 * unit)],
                whole.at[pl.ds(pl.multiple_of((1 - place.core) * 8 * unit, 16), 8 * unit)],
                core_landed.at[i],
                [view(0, 1), view(1, 1)],
                [view(2, 2), view(4, 2)],
                view(6, 1),
                ffn_grads.at[i],
                unit,
                unit,
            )
        )
    sum_gate, sum_up, sum_down = sums

    def load_landed(i):
        def load():
            here = staged.at[pl.ds(0, 8 * unit)]
            copy = pltpu.make_async_copy(core_landed.at[i], here, local_sems.at[3])
            copy.start()
            copy.wait()
            return here

        return load

    for step in gather_second.steps():
        step()
    gather_cot.step_two()
    for load in loads:
        load.wait()
    gather_second.own_line()
    gather_cot.step_three()
    feed_forward(pl.ds(place.line(0), LINE))
    gather_second.other_line()
    gather_cot.step_four()
    feed_forward(pl.ds(place.line(1), LINE))
    gather_cot.own_line()
    gather_cot.other_line()
    feed_backward(1)
    scatter_back.send_other()
    feed_backward(0)
    scatter_back.send_own()
    project_out(1)
    project_out(0)
    weight_grad(w_gate, d_gate, second)
    sum_gate.core_send()
    scatter_back.step_one()
    weight_grad(w_up, d_up, second)
    sum_up.core_send()
    gather_second.finish()
    for by in ((0, 1, 0), (0, 3, 0), (1, 0, 0)):
        pl.semaphore_signal(
            free_sem, inc=1, device_id=place.rep_dev(*by), device_id_type=MESH
        )
    scatter_back.step_two()
    weight_grad(w_down, hidden, cot_all)
    sum_down.core_send()
    pl.semaphore_wait(free_sem, 3)
    sum_gate.x_first(load_landed(0))
    sum_up.x_first(load_landed(1))
    gather_cot.finish()
    q_cols = 2 * HEAD_DIM
    query = heads.at[:, pl.ds(0, q_cols)]
    key = heads.at[:, pl.ds(q_cols, HEAD_DIM)]
    value = heads.at[:, pl.ds(q_cols + HEAD_DIM, HEAD_DIM)]
    attended = heads.at[:, pl.ds(q_cols + 2 * HEAD_DIM, q_cols)]
    w_attn = cot_all
    attn_cols = heads.shape[1]
    loads = [
        pltpu.make_async_copy(heads_hbm, heads, local_sems.at[0]),
        pltpu.make_async_copy(
            w_attn_hbm.at[pl.ds(0, rows_all)],
            w_attn.at[:, pl.ds(0, attn_cols)],
            local_sems.at[1],
        ),
        pltpu.make_async_copy(
            w_attn_hbm.at[pl.ds(rows_all, rows_all)],
            w_attn.at[:, pl.ds(attn_cols, attn_cols)],
            local_sems.at[2],
        ),
    ]
    for load in loads:
        load.start()
    scatter_back.step_three()
    gain_rows = None
    for half in (1, 0):
        rows = pl.ds(half * HALF, HALF)
        d_second = scatter_back.total(half)
        back, gain_part = rms_backward(resid[rows, :], gain_two[...], d_second)
        grad_tokens[rows, :] = cotangent[rows, :] + back
        gain_part = jnp.sum(gain_part, axis=0, keepdims=True)
        gain_rows = gain_part if gain_rows is None else gain_rows + gain_part
    gain_sums[0] = jnp.zeros_like(gain_sums[0])

    def keep_gain(first_row, value):
        for i in range(value.shape[1] // HEAD_DIM):
            gain_sums[0, first_row + i : first_row + i + 1, :] = value[
                :, i * HEAD_DIM : (i + 1) * HEAD_DIM
            ]

    gain_slots = width // HEAD_DIM
    keep_gain(gain_slots, gain_rows)
    branch[own, :] = grad_tokens[...].astype(low)
    gather_branch.start()
    sum_down.x_first(load_landed(2))
    gather_branch.step_one()
    sum_gate.x_second()
    gather_branch.step_two()
    sum_up.x_second()
    gather_branch.step_three()
    sum_down.x_second()
    sum_gate.y_send()
    gather_branch.step_four()
    sum_up.y_send()
    gather_branch.own_line()
    for load in loads:
        load.wait()

    def into_attention(dy):
        rows = pl.ds(place.line(dy), LINE)
        d_att[rows, :] = (
            mm(branch[rows, 0:rows_all], w_attn[:, 4 * HEAD_DIM : attn_cols])
            + mm(branch[rows, rows_all:], w_attn[:, attn_cols + 4 * HEAD_DIM : 2 * attn_cols])
        ).astype(low)

    into_attention(0)
    gather_branch.other_line()
    into_attention(1)
    sum_down.y_send()
    scatter_back.finish()
    load = pltpu.make_async_copy(first_hbm, part_back, local_sems.at[0])
    load.start()

    def unrotate(rows, upstream, projected, gain):
        turned = upstream * cosine[rows, :] - swap_halves(upstream) * sine[rows, :]
        return rms_backward(projected, gain, turned)

    gain_rows = jnp.zeros((1, HEAD_DIM), f32)
    d_key[...] = jnp.zeros_like(d_key)
    d_value[...] = jnp.zeros_like(d_value)
    for part in range(rows_all // chunk):
        rows = pl.ds(part * chunk, chunk)
        seen = (part + 1) * chunk
        token = part * chunk + lax.broadcasted_iota(jnp.int32, (chunk, 1), 0)
        source = lax.broadcasted_iota(jnp.int32, (1, seen), 1)
        visible = (source >= begin_of(token)) & (source <= token)
        for g in range(2):
            lanes = pl.ds(g * HEAD_DIM, HEAD_DIM)
            scores = mm_nt(query[rows, lanes], key[0:seen, :]) * scale
            weights = jnp.where(visible, jnp.exp(scores - proj[rows, 3 * HEAD_DIM + g : 3 * HEAD_DIM + g + 1]), 0.0)
            d_probs = mm_nt(d_att[rows, lanes], value[0:seen, :])
            inner = jnp.sum(weights * d_probs, axis=-1, keepdims=True)
            d_scores = (weights * (d_probs - inner)).astype(low)
            back, gain_part = unrotate(
                rows, mm(d_scores, key[0:seen, :]) * scale, proj[rows, lanes], query_gain[...].astype(f32)
            )
            d_qkv[rows, lanes] = back.astype(low)
            gain_rows = gain_rows + jnp.sum(gain_part, axis=0, keepdims=True)
            d_key[0:seen, :] += mm_tn(d_scores, query[rows, lanes])
            d_value[0:seen, :] += mm_tn(weights.astype(low), d_att[rows, lanes])
        if part == 0:
            sum_gate.y_gather(sum_gate.piece(), local_sems.at[3])
        if part == 1:
            sum_up.y_gather(sum_up.piece(), local_sems.at[3])
        if part == 2:
            sum_down.y_gather(sum_down.piece(), local_sems.at[3])
            scatter_out.send_other()
            scatter_out.send_own()
    d_qkv[:, 3 * HEAD_DIM :] = d_value[...].astype(low)

    keep_gain(2 * gain_slots, gain_rows)
    lanes = pl.ds(2 * HEAD_DIM, HEAD_DIM)
    back, gain_part = unrotate(pl.ds(0, rows_all), d_key[...] * scale, proj[:, lanes], key_gain[...].astype(f32))
    d_qkv[:, lanes] = back.astype(low)
    keep_gain(2 * gain_slots + 1, jnp.sum(gain_part, axis=0, keepdims=True))

    head_landed = cot_all.at[:, pl.ds(0, 6 * HEAD_DIM)]
    sum_attn = RepSum(
        place,
        sems(RepSum.COPIES),
        pair.at[pl.ds(pl.multiple_of(place.core * rows_all, BLOCK), rows_all)],
        pair.at[pl.ds(pl.multiple_of((1 - place.core) * rows_all, BLOCK), rows_all)],
        head_core_landed,
        [head_landed.at[pl.ds(e * BLOCK, BLOCK)] for e in range(2)],
        [head_landed.at[pl.ds((1 + e) * 2 * BLOCK, 2 * BLOCK)] for e in range(2)],
        head_landed.at[pl.ds(6 * BLOCK, BLOCK)],
        attn_grads,
        BLOCK,
        16,
    )

    load.wait()

    @pl.loop(0, width // 256)
    def _(i):
        cols = pl.ds(pl.multiple_of(i * 256, 256), 256)
        from_first = mm_tn(part_back[:, cols], d_qkv[...]).astype(low)
        from_branch = mm_tn(branch[:, cols], attended[...]).astype(low)
        for piece in range(16):
            rows = pl.ds(pl.multiple_of(piece * BLOCK + i * 16, 16), 16)
            pair[rows, 0 : 4 * HEAD_DIM] = from_first[piece * 16 : piece * 16 + 16, :]
            pair[rows, 4 * HEAD_DIM :] = from_branch[piece * 16 : piece * 16 + 16, :]

    gather_branch.finish()
    for by in ((1, 0), (0, 1), (0, 3)):
        pl.semaphore_signal(landing_free, inc=1, device_id=place.dev(*by), device_id_type=MESH)
    sum_attn.core_send()
    sum_gate.x_gather()
    sum_up.x_gather()
    scatter_first = Scatter(
        place,
        part_back,
        Slots(branch, 0, HALF),
        Slots(branch, 4 * HALF, 32),
        Slots(branch, 7 * HALF, HALF),
        branch.at[pl.ds(13 * HALF, HALF)],
        *sems(Scatter.COPIES),
    )

    def load_heads():
        copy = pltpu.make_async_copy(head_core_landed, d_up, local_sems.at[3])
        copy.start()
        copy.wait()
        return d_up

    def into_first(dy):
        rows = pl.ds(place.line(dy), LINE)

        for side in range(2):

            @pl.loop(0, rows_all // 256)
            def _(i):
                feats = pl.ds(pl.multiple_of(i * 256, 256), 256)
                cols = pl.ds(pl.multiple_of(side * rows_all + i * 256, 256), 256)
                part_back[rows, cols] = mm_nt(
                    d_qkv[rows, :], w_attn[feats, pl.ds(side * attn_cols, 4 * HEAD_DIM)]
                ).astype(low)

    into_first(1)
    pl.semaphore_wait(landing_free, 3)
    scatter_first.send_other()
    into_first(0)
    scatter_first.send_own()
    for by in ((0, 1, 0), (0, 3, 0), (1, 0, 0)):
        pl.semaphore_signal(
            heads_free, inc=1, device_id=place.rep_dev(*by), device_id_type=MESH
        )
    pl.semaphore_wait(heads_free, 3)
    sum_attn.x_first(load_heads)
    scatter_out.step_one()
    scatter_first.step_one()
    sum_attn.x_second()
    sum_gate.x_forward()
    scatter_out.step_two()
    sum_attn.y_send()
    sum_down.x_gather()
    scatter_first.step_two()
    scatter_out.step_three()
    scatter_first.step_three()
    sum_up.x_forward()
    piece = sum_attn.piece()
    swap_net = Net(*sems(7))
    for dy in range(2):
        for dz in range(4):
            if dy or dz:
                to = place.block(dy, dz)
                src = piece.at[pl.ds(pl.multiple_of(to * 16, 16), 16)]
                dst = swapped.at[pl.ds(pl.multiple_of(place.shard * 16, 16), 16)]
                here = place.block(-dy, -dz)
                here = swapped.at[pl.ds(pl.multiple_of(here * 16, 16), 16)]
                swap_net.send(f"{dy}{dz}", src, dst, place.dev(dy, dz), here)
    own_rows = pl.ds(pl.multiple_of(place.shard * 16, 16), 16)
    swapped[own_rows, :] = piece[own_rows, :]
    gain_rows = None
    for half in (1, 0):
        rows = pl.ds(half * HALF, HALF)
        d_first = scatter_first.total(half)
        back, gain_part = rms_backward(tokens[rows, :].astype(f32), gain_one[...], d_first)
        grad_tokens[rows, :] += back
        gain_part = jnp.sum(gain_part, axis=0, keepdims=True)
        gain_rows = gain_part if gain_rows is None else gain_rows + gain_part
    keep_gain(0, gain_rows)

    gain_net = Net(*sems(9))
    stages = (
        [place.dev(0, d) for d in (1, 2, 3)],
        [place.dev(1, 0)],
        [place.rep_dev(0, 0, 1)],
        [place.rep_dev(0, d, 0) for d in (1, 2, 3)],
        [place.rep_dev(1, 0, 0)],
    )

    def gain_send(stage):
        for i, dev in enumerate(stages[stage]):
            dst = gain_landed.at[3 * stage + i]
            gain_net.send(f"{stage}.{i}", gain_sums.at[stage], dst, dev, dst)

    def gain_add(stage):
        total = gain_sums[stage]
        for i in range(len(stages[stage])):
            gain_net.wait(f"{stage}.{i}")
            total = total + gain_landed[3 * stage + i]
        gain_sums[stage + 1] = total

    gain_send(0)
    swap_net.finish()
    kv = 8 * HEAD_DIM
    for j in range(8):
        rows = pl.ds(j * 16, 16)
        at = 0
        for begin, size in ((0, 2), (2, 1), (3, 1), (4, 2)):
            assembled[:, at + j * size * HEAD_DIM : at + (j + 1) * size * HEAD_DIM] = swapped[
                rows, begin * HEAD_DIM : (begin + size) * HEAD_DIM
            ]
            at += size * kv
    sum_attn.y_gather(assembled, local_sems.at[3])
    gain_add(0)
    gain_send(1)
    for half in (0, 1):
        rows = pl.ds(half * HALF, HALF)
        result[rows, :] = resid[rows, :] + scatter_out.total(half)
    sum_down.x_forward()
    sum_attn.x_gather()
    gain_add(1)
    gain_send(2)
    sum_gate.x_last()
    gain_add(2)
    gain_send(3)
    sum_up.x_last()
    sum_attn.x_forward()
    gain_add(3)
    gain_send(4)
    sum_down.x_last()
    sum_attn.x_last()
    gain_add(4)
    gains[...] = gain_sums[5]

    scatter_first.finish()
    scatter_out.finish()
    for one in sums:
        one.finish()
    sum_attn.finish()
    gain_net.finish()


def layer_call(lengths, *args):
    tokens, cotangent = args[:2]
    width = tokens.shape[1]
    hid = args[-1].shape[0]
    rows = 8 * BLOCK
    vmem = pl.BlockSpec(memory_space=pltpu.VMEM)
    smem = pl.BlockSpec(memory_space=pltpu.SMEM)
    hbm = pl.BlockSpec(memory_space=pltpu.HBM)
    copies = 4 * Gather.COPIES + 4 * Scatter.COPIES + 4 * RepSum.COPIES + 9 + 7 + 7
    gain_shape = (2 * width // HEAD_DIM + 8, HEAD_DIM)
    return pl.pallas_call(
        functools.partial(layer_kernel, 1.0 / math.sqrt(HEAD_DIM)),
        name="layer",
        out_shape=[
            jax.ShapeDtypeStruct((BLOCK, width), f32),
            jax.ShapeDtypeStruct((BLOCK, width), f32),
            jax.ShapeDtypeStruct(gain_shape, f32),
            jax.ShapeDtypeStruct((256, 3 * width), low),
            jax.ShapeDtypeStruct((3, hid, width), low),
            jax.ShapeDtypeStruct((3, hid // 2, width), low),
            jax.ShapeDtypeStruct((rows, 6 * HEAD_DIM), low),
            jax.ShapeDtypeStruct((rows, width), low),
            jax.ShapeDtypeStruct((2 * rows, 6 * HEAD_DIM), low),
            jax.ShapeDtypeStruct((rows, 6 * HEAD_DIM), low),
        ],
        in_specs=[smem] + [vmem] * 7 + [hbm] * 7,
        out_specs=[vmem] * 3 + [hbm] * 7,
        scratch_shapes=[
            pltpu.VMEM((BLOCK, width), f32),
            pltpu.VMEM((2, width), f32),
            pltpu.VMEM((8, 16, 256), low),
            pltpu.VMEM((rows, 4 * HEAD_DIM), f32),
            pltpu.VMEM((rows, HEAD_DIM), f32),
            pltpu.VMEM((rows, HEAD_DIM), f32),
            pltpu.VMEM((rows, width), low),
            pltpu.VMEM((rows, width), low),
            pltpu.VMEM((rows, width), low),
            pltpu.VMEM((hid, width), low),
            pltpu.VMEM((hid, width), low),
            pltpu.VMEM((hid, width), low),
            pltpu.VMEM((2 * rows, hid), low),
            pltpu.VMEM((rows, hid), low),
            pltpu.VMEM((rows, width), low),
            pltpu.VMEM((rows, width), low),
            pltpu.VMEM((rows, 2 * HEAD_DIM), low),
            pltpu.VMEM((rows, HEAD_DIM), f32),
            pltpu.VMEM((rows, HEAD_DIM), f32),
            pltpu.VMEM((rows, 4 * HEAD_DIM), low),
            pltpu.VMEM((hid // 2, width), low),
        ]
        + Scatter.scratch(width)
        + [
            pltpu.VMEM((BLOCK, 6 * HEAD_DIM), low),
            pltpu.VMEM((16, 3 * width), low),
            pltpu.VMEM((6,) + gain_shape, f32),
            pltpu.VMEM((15,) + gain_shape, f32),
            pltpu.SemaphoreType.DMA((2, 2, 11)),
            pltpu.SemaphoreType.DMA((3, 2)),
            pltpu.SemaphoreType.REGULAR,
            pltpu.SemaphoreType.REGULAR,
            pltpu.SemaphoreType.REGULAR,
            pltpu.SemaphoreType.DMA((6,)),
            pltpu.SemaphoreType.DMA((copies,)),
            pltpu.SemaphoreType.DMA((copies,)),
        ],
        compiler_params=pltpu.CompilerParams(
            collective_id=1, has_side_effects=True, vmem_limit_bytes=60 << 20
        ),
        cost_estimate=pl.CostEstimate(
            flops=36_000_000_000, bytes_accessed=60_000_000, transcendentals=4_000_000
        ),
    )(lengths, *args)


def widen_kernel(ffn, attn, gate, up, down, query, key, value, out):
    step = pl.program_id(0)
    per = pl.num_programs(0) // 3
    wide = ffn[0].astype(f32)
    for which, ref in enumerate((gate, up, down)):

        @pl.when(step // per == which)
        def _(ref=ref):
            ref[...] = wide

    at = 0
    for ref in (query, key, value, out):
        ref[...] = attn[:, at : at + ref.shape[1]].astype(f32)
        at += ref.shape[1]


def widen(ffn, attn):
    _, hid, width = ffn.shape
    rows = attn.shape[0]
    per, tall, some = 3, hid // 3, rows // 8

    def block_of(which):
        return lambda i: (jnp.clip(i - which * per, 0, per - 1), 0)

    def attn_block(i):
        return (jnp.minimum(i, 7), 0)

    sizes = (width, width // 2, width // 2, width)
    return pl.pallas_call(
        widen_kernel,
        name="widen",
        grid=(3 * per,),
        out_shape=[jax.ShapeDtypeStruct((hid, width), f32)] * 3
        + [jax.ShapeDtypeStruct((rows, size), f32) for size in sizes],
        in_specs=[
            pl.BlockSpec((1, tall, width), lambda i: (i // per, i % per, 0)),
            pl.BlockSpec((some, 3 * width), attn_block),
        ],
        out_specs=[pl.BlockSpec((tall, width), block_of(which)) for which in range(3)]
        + [pl.BlockSpec((some, size), attn_block) for size in sizes],
        compiler_params=pltpu.CompilerParams(vmem_limit_bytes=60 << 20),
    )(ffn, attn)


def per_device(
    tokens,
    cotangent,
    lengths,
    attn_gain,
    mlp_gain,
    query_gain,
    key_gain,
    w_query,
    w_key,
    w_value,
    w_out,
    w_gate,
    w_up,
    w_down,
):
    width = tokens.shape[1]
    shards = lax.axis_size("shard")
    feat = width // shards
    my_shard = lax.axis_index("shard")
    half = np.arange(HEAD_DIM, dtype=np.float64) % (HEAD_DIM // 2)
    frequency = jnp.asarray(theta_base ** (-half * (2.0 / HEAD_DIM)), f32)[None]
    result, grad_tokens, gains, attn_grads, ffn_grads, *_ = layer_call(
        lengths,
        tokens,
        cotangent,
        attn_gain[None],
        mlp_gain[None],
        query_gain[None],
        key_gain[None],
        frequency,
        w_query,
        w_key,
        w_value,
        w_out,
        w_gate,
        w_up,
        w_down,
    )
    grad_gate, grad_up, grad_down, grad_query, grad_key, grad_value, grad_out = widen(
        ffn_grads, attn_grads
    )
    gains = gains.reshape(-1)
    head_piece = HEAD_DIM // shards
    gains_first = lax.dynamic_slice_in_dim(gains, my_shard * feat, feat, 0)
    gains_second = lax.dynamic_slice_in_dim(gains, width + my_shard * feat, feat, 0)
    gains_query = lax.dynamic_slice_in_dim(gains, 2 * width + my_shard * head_piece, head_piece, 0)
    gains_key = lax.dynamic_slice_in_dim(
        gains, 2 * width + HEAD_DIM + my_shard * head_piece, head_piece, 0
    )
    return (
        result,
        grad_tokens,
        grad_query,
        grad_key,
        grad_value,
        grad_out,
        grad_gate,
        grad_up,
        grad_down,
        gains_first,
        gains_second,
        gains_query,
        gains_key,
    )


def solution(mesh):
    spread = P(("rep", "shard"), None)
    rowed = P("shard", None)
    return jax.shard_map(
        per_device,
        mesh=mesh,
        in_specs=(spread, spread, P("rep", None), P("shard"), P("shard"), P(), P()) + (rowed,) * 7,
        out_specs=(spread, spread) + (rowed,) * 7 + (P("shard"),) * 4,
        check_vma=False,
    )
```

```python
import functools
import math

import jax
import jax.numpy as jnp
import numpy as np
from jax import lax
from jax.experimental import pallas as pl
from jax.experimental.pallas import tpu as pltpu
from jax.sharding import PartitionSpec as P

HEADS = 16
KV_HEADS = 8
HEAD_DIM = 128

epsilon = 1e-06
theta_base = 1000000.0
masked_value = -1e30


MESH = pl.DeviceIdType.MESH
BLOCK = 128
HALF = 64
LINE = 512
low = jnp.bfloat16
f32 = jnp.float32


def mm(left, right):
    return lax.dot_general(left, right, (((1,), (0,)), ((), ())), preferred_element_type=f32)


def mm_nt(left, right):
    return lax.dot_general(left, right, (((1,), (1,)), ((), ())), preferred_element_type=f32)


def mm_tn(left, right):
    return lax.dot_general(left, right, (((0,), (0,)), ((), ())), preferred_element_type=f32)


class Place:
    def __init__(self):
        self.rep = lax.axis_index("rep")
        self.shard = lax.axis_index("shard")
        self.yl, self.z = self.shard // 4, self.shard % 4
        self.yh, self.x, self.core = self.rep // 8, (self.rep // 2) % 4, self.rep % 2

    def block(self, dy, dz):
        return ((self.yl + dy + 2) % 2) * 4 + (self.z + dz + 8) % 4

    def dev(self, dy, dz):
        return (self.rep, self.block(dy, dz))

    def x_at(self, dx):
        return (self.x + dx + 8) % 4

    def rep_dev(self, dyh, dx, dcore):
        rep = ((self.yh + dyh) % 2) * 8 + self.x_at(dx) * 2 + (self.core + dcore) % 2
        return (rep, self.shard)

    def rows(self, dy, dz, start=0, count=BLOCK):
        return pl.ds(pl.multiple_of(self.block(dy, dz) * BLOCK + start, 32), count)

    def line(self, dy):
        return pl.multiple_of(((self.yl + dy + 2) % 2) * LINE, LINE)

    def shard_peers(self):
        return [self.dev(dy, dz) for dy in range(2) for dz in range(4) if dy or dz]

    def rep_peers(self):
        return [
            self.rep_dev(*by) for by in ((0, 0, 1), (0, 1, 0), (0, 2, 0), (0, 3, 0), (1, 0, 0))
        ]

    def greet(self):
        barrier = pltpu.get_barrier_semaphore()
        peers = self.shard_peers() + self.rep_peers()
        for peer in peers:
            pl.semaphore_signal(barrier, inc=1, device_id=peer, device_id_type=MESH)
        pl.semaphore_wait(barrier, len(peers))


class Net:
    def __init__(self, send_sems, recv_sems):
        self.send_sems, self.recv_sems = send_sems, recv_sems
        self.started, self.coming = [], {}

    def send(self, tag, src, dst, dev, here):
        k = len(self.started)
        copy = pltpu.make_async_remote_copy(
            src_ref=src,
            dst_ref=dst,
            send_sem=self.send_sems.at[k],
            recv_sem=self.recv_sems.at[k],
            device_id=dev,
            device_id_type=MESH,
        )
        copy.start()
        self.started.append(copy)
        self.coming[tag] = (k, here, dev)

    def wait(self, tag):
        k, here, dev = self.coming.pop(tag)
        pltpu.make_async_remote_copy(
            src_ref=here,
            dst_ref=here,
            send_sem=self.send_sems.at[k],
            recv_sem=self.recv_sems.at[k],
            device_id=dev,
            device_id_type=MESH,
        ).wait_recv()

    def finish(self):
        for tag in list(self.coming):
            self.wait(tag)
        for copy in self.started:
            copy.wait_send()


class Gather:
    COPIES = 18

    def __init__(self, place, buf, send_sems, recv_sems):
        self.place, self.buf = place, buf
        self.net = Net(send_sems, recv_sems)

    def send(self, tag, block, start, count, to):
        rows = self.place.rows(*block, start, count)
        here = self.place.rows(block[0] - to[0], block[1] - to[1], start, count)
        self.net.send(
            tag, self.buf.at[rows], self.buf.at[rows], self.place.dev(*to), self.buf.at[here]
        )

    def start(self):
        self.send("y_up", (0, 0), 0, HALF, (1, 0))
        for d in (1, 3):
            self.send(f"z_low{d}", (0, 0), HALF, HALF, (0, d))
        self.send("y_low", (0, 0), HALF, HALF, (1, 0))

    def step_one(self):
        self.net.wait("y_up")
        for d in (1, 3):
            self.send(f"p_up{d}", (1, 0), 0, HALF, (0, d))

    def step_two(self):
        for e, d in enumerate((1, 3)):
            self.net.wait(f"z_low{d}")
            self.send(f"f_low{d}", (0, -d), HALF + 32 * e, 32, (0, d))
            self.send(f"q_low{d}", (0, -d), HALF, HALF, (1, 0))
        for d in (1, 3):
            self.send(f"z_up{d}", (0, 0), 0, HALF, (0, d))

    def step_three(self):
        for e, d in enumerate((1, 3)):
            self.net.wait(f"p_up{d}")
            self.send(f"f_p{d}", (1, -d), 32 * e, 32, (0, d))
        for e, d in enumerate((1, 3)):
            self.net.wait(f"f_low{d}")
            self.send(f"q_far{d}", (0, -2 * d), HALF + 32 * e, 32, (1, 0))

    def step_four(self):
        for e, d in enumerate((1, 3)):
            self.net.wait(f"z_up{d}")
            self.send(f"f_up{d}", (0, -d), 32 * e, 32, (0, d))

    def own_line(self):
        for d in (1, 3):
            self.net.wait(f"f_up{d}")

    def other_line(self):
        for tag in list(self.net.coming):
            self.net.wait(tag)

    def steps(self):
        return [self.start, self.step_one, self.step_two, self.step_three, self.step_four]

    def finish(self):
        self.net.finish()


class Slots:
    def __init__(self, ref, base, size):
        self.ref, self.base, self.size = ref, base, size

    @property
    def at(self):
        return self

    def __getitem__(self, i):
        i = i if isinstance(i, int) else 2 * i[0] + i[1]
        return self.ref.at[pl.ds(self.base + i * self.size, self.size)]


class Scatter:
    COPIES = 17

    @staticmethod
    def scratch(columns):
        return [
            pltpu.VMEM((4, HALF, columns), low),
            pltpu.VMEM((3, 2, 32, columns), low),
            pltpu.VMEM((3, 2, HALF, columns), low),
            pltpu.VMEM((HALF, columns), low),
        ]

    def __init__(self, place, part, across, near, far, last, send_sems, recv_sems):
        self.place, self.part = place, part
        self.across, self.near, self.far, self.last = across, near, far, last
        self.net = Net(send_sems, recv_sems)

    def add(self, rows, *refs):
        total = self.part[rows, :].astype(f32)
        for ref in refs:
            total = total + ref[...].astype(f32)
        self.part[rows, :] = total.astype(low)

    def first(self, kind):
        dy, start = ((1, 0), (0, 0), (0, HALF))[kind]
        for e, d in enumerate((1, 3)):
            src = self.part.at[self.place.rows(dy, 2, start + 32 * e, 32)]
            dst = self.near.at[kind, e]
            self.net.send(f"near{kind}{e}", src, dst, self.place.dev(0, d), dst)

    def second(self, kind):
        dy, start = ((1, 0), (0, 0), (0, HALF))[kind]
        for e, d in enumerate((1, 3)):
            self.net.wait(f"near{kind}{e}")
            self.add(self.place.rows(dy, d, start + 32 * e, 32), self.near.at[kind, e])
            src = self.part.at[self.place.rows(dy, d, start, HALF)]
            dst = self.far.at[kind, e]
            self.net.send(f"far{kind}{e}", src, dst, self.place.dev(0, d), dst)

    def send_other(self):
        for d in (2, 1, 3, 0):
            src = self.part.at[self.place.rows(1, d, HALF, HALF)]
            dst = self.across.at[d]
            self.net.send(f"across{d}", src, dst, self.place.dev(1, 0), dst)
        self.first(0)

    def send_own(self):
        self.first(1)

    def step_one(self):
        self.net.wait("across2")
        self.add(self.place.rows(0, 2, HALF, HALF), self.across.at[2])
        self.first(2)
        self.second(0)
        self.second(1)

    def step_two(self):
        for d in (1, 3):
            self.net.wait(f"across{d}")
            self.add(self.place.rows(0, d, HALF, HALF), self.across.at[d])
        self.second(2)

    def step_three(self):
        for e in range(2):
            self.net.wait(f"far0{e}")
        rows = self.place.rows(1, 0, 0, HALF)
        self.add(rows, self.far.at[0, 0], self.far.at[0, 1])
        self.net.send("last", self.part.at[rows], self.last, self.place.dev(1, 0), self.last)

    def total(self, half):
        if half == 0:
            tags, extra, kind = ("far10", "far11", "last"), self.last, 1
        else:
            tags, extra, kind = ("far20", "far21", "across0"), self.across.at[0], 2
        for tag in tags:
            self.net.wait(tag)
        out = self.part[self.place.rows(0, 0, half * HALF, HALF), :].astype(f32)
        for ref in (self.far.at[kind, 0], self.far.at[kind, 1], extra):
            out = out + ref[...].astype(f32)
        return out

    def finish(self):
        self.net.finish()


def add_rows(into, start, count, *refs):
    step = 64 if count % 64 == 0 else 48

    @pl.loop(0, count // step)
    def _(i):
        at = pl.multiple_of(i * step, 16)
        rows = pl.ds(pl.multiple_of(start + at, 16), step)
        total = into[rows, :].astype(f32)
        for ref in refs:
            total = total + ref[pl.ds(at, step), :].astype(f32)
        into[rows, :] = total.astype(low)


class RepSum:
    COPIES = 15

    def __init__(self, place, sems, own, other, landed, near, far, cross, out, unit, out_unit):
        self.place, self.net = place, Net(*sems)
        self.own, self.other, self.landed = own, other, landed
        self.near, self.far, self.cross = near, far, cross
        self.out, self.unit, self.out_unit = out, unit, out_unit

    def chunk(self, dx, start=0, count=None):
        at = self.place.x_at(dx) * 2 * self.unit + start
        return pl.ds(pl.multiple_of(at, 16), 2 * self.unit if count is None else count)

    def out_rows(self, dcore, dx, start=0, count=None):
        core = (self.place.core + dcore) % 2
        at = (core * 8 + self.place.x_at(dx) * 2 + start) * self.out_unit
        count = (2 if count is None else count) * self.out_unit
        return self.out.at[pl.ds(pl.multiple_of(at, 16), count)]

    def core_send(self):
        self.net.send("core", self.other, self.landed, self.place.rep_dev(0, 0, 1), self.landed)

    def x_first(self, load=None):
        self.net.wait("core")
        add_rows(self.own, 0, 8 * self.unit, self.landed if load is None else load())
        for e, d in enumerate((1, 3)):
            src = self.own.at[self.chunk(2, e * self.unit, self.unit)]
            dst = self.near[e]
            self.net.send(f"near{e}", src, dst, self.place.rep_dev(0, d, 0), dst)

    def x_second(self):
        for e, d in enumerate((1, 3)):
            self.net.wait(f"near{e}")
            add_rows(self.own, self.place.x_at(d) * 2 * self.unit + e * self.unit, self.unit, self.near[e])
            dst = self.far[e]
            self.net.send(
                f"far{e}", self.own.at[self.chunk(d)], dst, self.place.rep_dev(0, d, 0), dst
            )

    def y_send(self):
        for e in range(2):
            self.net.wait(f"far{e}")
        add_rows(self.own, self.place.x * 2 * self.unit, 2 * self.unit, *self.far)
        src = self.own.at[self.chunk(0, (1 - self.place.yh) * self.unit, self.unit)]
        self.net.send("cross", src, self.cross, self.place.rep_dev(1, 0, 0), self.cross)

    def piece(self):
        self.net.wait("cross")
        at = (self.place.x * 2 + self.place.yh) * self.unit
        add_rows(self.own, at, self.unit, self.cross)
        return self.own.at[pl.ds(pl.multiple_of(at, 16), self.unit)]

    def y_gather(self, piece, sem):
        mine = self.out_rows(0, 0, self.place.yh, 1)
        copy = pltpu.make_async_copy(piece, mine, sem)
        copy.start()
        self.net.send(
            "y", piece, mine, self.place.rep_dev(1, 0, 0), self.out_rows(0, 0, 1 - self.place.yh, 1)
        )
        copy.wait()

    def to_core(self, dx):
        rows = self.out_rows(0, dx)
        self.net.send(
            f"core{dx}", rows, rows, self.place.rep_dev(0, 0, 1), self.out_rows(1, dx)
        )

    def x_gather(self):
        self.net.wait("y")
        rows = self.out_rows(0, 0)
        for d in (1, 3):
            self.net.send(f"x{d}", rows, rows, self.place.rep_dev(0, d, 0), self.out_rows(0, -d))
        self.to_core(0)

    def x_forward(self):
        for e, d in enumerate((1, 3)):
            self.net.wait(f"x{d}")
            rows = self.out_rows(0, -d, e, 1)
            self.net.send(
                f"xx{d}", rows, rows, self.place.rep_dev(0, d, 0), self.out_rows(0, -2 * d, e, 1)
            )
            self.to_core(-d)

    def x_last(self):
        for d in (1, 3):
            self.net.wait(f"xx{d}")
        self.to_core(2)

    def finish(self):
        self.net.finish()


def rms_backward(value, gain, upstream):
    root = lax.rsqrt(jnp.mean(value * value, axis=-1, keepdims=True) + epsilon)
    pulled = upstream * gain
    back = root * pulled - value * (root * root * root) * jnp.mean(
        pulled * value, axis=-1, keepdims=True
    )
    return back, upstream * (value * root)


def swap_halves(value):
    return pltpu.roll(value, HEAD_DIM // 2, 1)


def layer_kernel(
    scale,
    lengths,
    tokens,
    cotangent,
    gain_shard,
    query_gain,
    key_gain,
    frequency,
    w_query_hbm,
    w_key_hbm,
    w_value_hbm,
    w_out_hbm,
    w_gate_hbm,
    w_up_hbm,
    w_down_hbm,
    result,
    grad_tokens,
    gains,
    attn_grads,
    ffn_grads,
    core_landed,
    head_core_landed,
    first_hbm,
    w_attn_hbm,
    heads_hbm,
    resid,
    gain_rows_all,
    gain_blocks,
    proj,
    cosine,
    sine,
    second,
    cot_all,
    branch,
    w_gate,
    w_up,
    w_down,
    pair,
    d_up,
    part_out,
    part_back,
    d_att,
    d_key,
    d_value,
    d_qkv,
    staged,
    across,
    near,
    far,
    last,
    swapped,
    assembled,
    gain_sums,
    gain_landed,
    swap_sems,
    sibling_sems,
    free_sem,
    landing_free,
    heads_free,
    local_sems,
    send_sems,
    recv_sems,
):
    place = Place()
    hidden = pair.at[pl.ds(0, 8 * BLOCK)]
    d_gate = pair.at[pl.ds(8 * BLOCK, 8 * BLOCK)]
    rows_all = 8 * BLOCK
    hid = w_gate.shape[0]
    width = second.shape[1]

    loads = [
        pltpu.make_async_copy(src, dst, local_sems.at[i])
        for i, (src, dst) in enumerate(
            ((w_gate_hbm, w_gate), (w_up_hbm, w_up), (w_down_hbm, w_down))
        )
    ]
    for load in loads:
        load.start()

    used = [0]

    def sems(count):
        at = used[0]
        used[0] += count
        return send_sems.at[pl.ds(at, count)], recv_sems.at[pl.ds(at, count)]

    own = place.rows(0, 0)
    gain_one = gain_rows_all.at[pl.ds(0, 1)]
    gain_two = gain_rows_all.at[pl.ds(1, 1)]
    cot_all[own, :] = cotangent[...].astype(low)
    branch[own, :] = tokens[...]
    feat = w_query_hbm.shape[0]
    gain_blocks[place.shard] = gain_shard[...]
    place.greet()

    gain_share = Net(*sems(7))
    peers = [(dy, dz) for dy in range(2) for dz in range(4) if dy or dz]
    for by in peers:
        gain_share.send(
            str(by),
            gain_blocks.at[place.shard],
            gain_blocks.at[place.shard],
            place.dev(*by),
            gain_blocks.at[place.block(-by[0], -by[1])],
        )
    qkv_parts = (
        (w_query_hbm, 0, 2 * HEAD_DIM),
        (w_key_hbm, 2 * HEAD_DIM, HEAD_DIM),
        (w_value_hbm, 3 * HEAD_DIM, HEAD_DIM),
    )
    out_parts = ((w_out_hbm, 4 * HEAD_DIM, 2 * HEAD_DIM),)
    few = feat // 8
    qkv_span = pl.ds(0, 4 * HEAD_DIM)
    out_span = pl.ds(4 * HEAD_DIM, 2 * HEAD_DIM)

    def swap_rows(block, dx=0, count=1):
        first = place.x_at(dx) if count == 1 else 0
        at = block * feat + (place.core * 4 + first) * few
        return pl.ds(pl.multiple_of(at, few), count * few)

    def swap_copy(src, dst, kind, i, dev):
        return pltpu.make_async_remote_copy(
            src_ref=src,
            dst_ref=dst,
            send_sem=swap_sems.at[0, kind, i],
            recv_sem=swap_sems.at[1, kind, i],
            device_id=dev,
            device_id_type=MESH,
        )

    def swap_send(parts, kind):
        own_rows = pl.ds(pl.multiple_of((place.core * 4 + place.x) * few, few), few)
        for i, by in enumerate(peers):
            to = place.block(*by)
            for whole, begin, size in parts:
                cols = pl.ds(pl.multiple_of(to * size, HEAD_DIM), size)
                src = whole.at[own_rows, cols]
                dst = pair.at[swap_rows(place.shard), pl.ds(begin, size)]
                swap_copy(src, dst, kind, i, place.dev(*by)).start()
        for whole, begin, size in parts:
            cols = pl.ds(pl.multiple_of(place.shard * size, HEAD_DIM), size)
            rows = pl.ds(pl.multiple_of(place.shard * feat, feat), feat)
            copy = pltpu.make_async_copy(
                whole.at[:, cols], pair.at[rows, pl.ds(begin, size)], sibling_sems.at[2, kind]
            )
            copy.start()

    def share_copy(ref, kind, i):
        return swap_copy(
            ref, ref, kind, 7 + i, place.rep_dev(0, i + 1, 0) if i < 3 else place.rep_dev(0, 0, 1)
        )

    def swap_relay(span, kind):
        for i, by in enumerate(peers):
            here = pair.at[swap_rows(place.block(-by[0], -by[1])), span]
            swap_copy(here, here, kind, i, place.dev(*by)).wait_recv()
            for d in range(3):
                share_copy(here, kind, d).start()

    def swap_share(span, kind):
        for d in range(3):
            share_copy(pair.at[pl.ds(0, 7 * few), span], kind, d).wait_recv()
        for by in peers:
            here = pair.at[swap_rows(place.block(-by[0], -by[1]), 0, 4), span]
            share_copy(here, kind, 3).start()

    def swap_done(span, kind):
        rows = pl.ds(pl.multiple_of(place.shard * feat, feat), feat)
        mine = pair.at[rows, span]
        pltpu.make_async_copy(mine, mine, sibling_sems.at[2, kind]).wait()
        share_copy(pair.at[pl.ds(0, 7 * 4 * few), span], kind, 3).wait()
        for d in range(3):
            share_copy(pair.at[pl.ds(0, 7 * few), span], kind, d).wait_send()
        for i, by in enumerate(peers):
            here = pair.at[swap_rows(place.block(-by[0], -by[1])), span]
            swap_copy(here, here, kind, i, place.dev(*by)).wait_send()

    swap_send(qkv_parts, 0)
    gather_tokens = Gather(place, branch, *sems(Gather.COPIES))
    gather_tokens.start()

    start_one = lengths[0, 0]
    start_two = lengths[0, 0] + lengths[0, 1]

    def begin_of(token):
        return jnp.where(
            token >= start_two, start_two, jnp.where(token >= start_one, start_one, 0)
        )

    token = lax.broadcasted_iota(jnp.int32, (rows_all, 1), 0)
    angles = (token - begin_of(token)).astype(f32) * frequency[...]
    lane = lax.broadcasted_iota(jnp.int32, (1, HEAD_DIM), 1)
    cosine[...] = jnp.cos(angles)
    sine[...] = jnp.sin(angles) * jnp.where(lane < HEAD_DIM // 2, -1.0, 1.0)

    gather_tokens.step_one()
    swap_relay(qkv_span, 0)
    gather_tokens.step_two()
    gain_share.finish()
    for j in range(8):
        span = slice(j * feat, (j + 1) * feat)
        gain_rows_all[0:2, span] = gain_blocks[j, 0:2, :].astype(f32)
    gather_tokens.step_three()
    swap_share(qkv_span, 0)
    swap_send(out_parts, 1)
    gather_tokens.step_four()

    def normalise(dy):
        line = place.line(dy)

        @pl.loop(0, LINE // BLOCK)
        def _(i):
            rows = pl.ds(pl.multiple_of(line + i * BLOCK, BLOCK), BLOCK)
            x = branch[rows, :].astype(f32)
            root = lax.rsqrt(jnp.mean(x * x, axis=-1, keepdims=True) + epsilon)
            second[rows, :] = (x * root * gain_one[...]).astype(low)

    gather_tokens.own_line()
    normalise(0)
    gather_tokens.other_line()
    normalise(1)
    gather_tokens.finish()
    keep_first = pltpu.make_async_copy(second, first_hbm, local_sems.at[3])
    keep_first.start()
    gather_cot = Gather(place, cot_all, *sems(Gather.COPIES))
    gather_cot.start()
    swap_relay(out_span, 1)
    swap_done(qkv_span, 0)
    heads = d_up
    gains_of_head = (query_gain, query_gain, key_gain)

    @pl.loop(0, rows_all // 256)
    def _(i):
        rows = pl.ds(pl.multiple_of(i * 256, 256), 256)
        proj[rows, :] = mm(second[rows, :], pair[:, 0 : 4 * HEAD_DIM])
        for g in range(3):
            lanes = pl.ds(g * HEAD_DIM, HEAD_DIM)
            u = proj[rows, lanes]
            root = lax.rsqrt(jnp.mean(u * u, axis=-1, keepdims=True) + epsilon)
            u = u * root * gains_of_head[g][...].astype(f32)
            heads[rows, lanes] = (u * cosine[rows, :] + swap_halves(u) * sine[rows, :]).astype(low)
        lanes = pl.ds(3 * HEAD_DIM, HEAD_DIM)
        heads[rows, lanes] = proj[rows, lanes].astype(low)

    swap_share(out_span, 1)
    chunk = 256
    for part in range(rows_all // chunk):
        rows = pl.ds(part * chunk, chunk)
        seen = (part + 1) * chunk
        token = part * chunk + lax.broadcasted_iota(jnp.int32, (chunk, 1), 0)
        source = lax.broadcasted_iota(jnp.int32, (1, seen), 1)
        visible = (source >= begin_of(token)) & (source <= token)
        for g in range(2):
            lanes = pl.ds(g * HEAD_DIM, HEAD_DIM)
            scores = mm_nt(heads[rows, lanes], heads[0:seen, 2 * HEAD_DIM : 3 * HEAD_DIM]) * scale
            scores = jnp.where(visible, scores, masked_value)
            top = jnp.max(scores, axis=-1, keepdims=True)
            raised = jnp.exp(scores - top)
            total = jnp.sum(raised, axis=-1, keepdims=True)
            probs = (raised * (1.0 / total)).astype(low)
            proj[rows, 3 * HEAD_DIM + g : 3 * HEAD_DIM + g + 1] = jnp.log(total) + top
            heads[rows, pl.ds((4 + g) * HEAD_DIM, HEAD_DIM)] = mm(
                probs, heads[0:seen, 3 * HEAD_DIM : 4 * HEAD_DIM]
            ).astype(low)
        if part == 2:
            gather_cot.step_one()
    keep_heads = pltpu.make_async_copy(heads, heads_hbm, local_sems.at[4])
    keep_heads.start()
    swap_done(out_span, 1)
    keep_weights = pltpu.make_async_copy(pair, w_attn_hbm, local_sems.at[5])
    keep_weights.start()
    landing = (across, near, far, last)
    scatter_attn = Scatter(place, part_back, *landing, *sems(Scatter.COPIES))

    def attention_out(dy):
        rows = pl.ds(place.line(dy), LINE)

        @pl.loop(0, width // 256)
        def _(i):
            cols = pl.ds(pl.multiple_of(i * 256, 256), 256)
            part_back[rows, cols] = mm_nt(
                heads[rows, 4 * HEAD_DIM :], pair[cols, 4 * HEAD_DIM :]
            ).astype(low)

    attention_out(1)
    keep_first.wait()
    scatter_attn.send_other()
    attention_out(0)
    scatter_attn.send_own()
    scatter_attn.step_one()
    scatter_attn.step_two()
    scatter_attn.step_three()
    keep_heads.wait()
    keep_weights.wait()
    for half in (1, 0):
        rows = pl.ds(half * HALF, HALF)
        x = tokens[rows, :].astype(f32) + scatter_attn.total(half)
        resid[rows, :] = x
        root = lax.rsqrt(jnp.mean(x * x, axis=-1, keepdims=True) + epsilon)
        at = place.rows(0, 0, half * HALF, HALF)
        second[at, :] = (x * root * gain_two[...]).astype(low)
    scatter_attn.finish()
    gather_second = Gather(place, second, *sems(Gather.COPIES))
    gather_branch = Gather(place, branch, *sems(Gather.COPIES))
    left, right = (pl.ds(side * (width // 2), width // 2) for side in range(2))
    scatter_left, scatter_right = (
        Scatter(
            place,
            part_out.at[:, cols],
            across.at[:, :, cols],
            near.at[:, :, :, cols],
            far.at[:, :, :, cols],
            last.at[:, cols],
            *sems(Scatter.COPIES),
        )
        for cols in (left, right)
    )
    scatter_back = Scatter(place, part_back, *landing, *sems(Scatter.COPIES))

    def feed_forward(rows):
        @pl.loop(0, hid // 256)
        def _(i):
            cols = pl.ds(pl.multiple_of(i * 256, 256), 256)
            gate = mm_nt(second[rows, :], w_gate[cols, :])
            up = mm_nt(second[rows, :], w_up[cols, :])
            sigma = 1.0 / (1.0 + jnp.exp(-gate))
            silu = gate * sigma
            hidden[rows, cols] = (silu * up).astype(low)
            d_gate[rows, cols] = (up * sigma * (1.0 + gate * (1.0 - sigma))).astype(low)
            d_up[rows, cols] = silu.astype(low)

    def project_out(dy):
        rows = pl.ds(place.line(dy), LINE)

        @pl.loop(0, width // 512)
        def _(i):
            cols = pl.ds(pl.multiple_of(i * 512, 512), 512)
            part_out[rows, cols] = mm(hidden[rows, :], w_down[:, cols]).astype(low)

    def feed_backward(dy):
        rows = pl.ds(place.line(dy), LINE)

        @pl.loop(0, hid // 256)
        def _(i):
            cols = pl.ds(pl.multiple_of(i * 256, 256), 256)
            d_hidden = mm_nt(cot_all[rows, :], w_down[cols, :])
            d_gate[rows, cols] = (d_hidden * d_gate[rows, cols].astype(f32)).astype(low)
            d_up[rows, cols] = (d_hidden * d_up[rows, cols].astype(f32)).astype(low)

        @pl.loop(0, width // 512)
        def _(i):
            cols = pl.ds(pl.multiple_of(i * 512, 512), 512)
            part_back[rows, cols] = (
                mm(d_gate[rows, :], w_gate[:, cols]) + mm(d_up[rows, :], w_up[:, cols])
            ).astype(low)

    def weight_grad(into, left, right):
        @pl.loop(0, hid // 256)
        def _(i):
            cols = pl.ds(pl.multiple_of(i * 256, 256), 256)
            into[cols, :] = mm_tn(left[:, cols], right[...]).astype(low)

    unit = hid // 16
    sums = []
    for i, whole in enumerate((w_gate, w_up, w_down)):
        base = i * 7 * unit

        def view(start, count, base=base):
            return second.at[pl.ds(base + start * unit, count * unit)]

        sums.append(
            RepSum(
                place,
                sems(RepSum.COPIES),
                whole.at[pl.ds(pl.multiple_of(place.core * 8 * unit, 16), 8 * unit)],
                whole.at[pl.ds(pl.multiple_of((1 - place.core) * 8 * unit, 16), 8 * unit)],
                core_landed.at[i],
                [view(0, 1), view(1, 1)],
                [view(2, 2), view(4, 2)],
                view(6, 1),
                ffn_grads.at[i],
                unit,
                unit,
            )
        )
    sum_gate, sum_up, sum_down = sums

    def load_landed(i):
        def load():
            here = staged.at[pl.ds(0, 8 * unit)]
            copy = pltpu.make_async_copy(core_landed.at[i], here, local_sems.at[3])
            copy.start()
            copy.wait()
            return here

        return load

    for step in gather_second.steps():
        step()
    gather_cot.step_two()
    for load in loads:
        load.wait()
    gather_second.own_line()
    gather_cot.step_three()
    feed_forward(pl.ds(place.line(0), LINE))
    gather_second.other_line()
    gather_cot.step_four()
    feed_forward(pl.ds(place.line(1), LINE))
    gather_cot.own_line()
    gather_cot.other_line()
    feed_backward(1)
    scatter_back.send_other()
    feed_backward(0)
    scatter_back.send_own()
    project_out(1)
    project_out(0)
    weight_grad(w_gate, d_gate, second)
    sum_gate.core_send()
    scatter_back.step_one()
    weight_grad(w_up, d_up, second)
    sum_up.core_send()
    gather_second.finish()
    for by in ((0, 1, 0), (0, 3, 0), (1, 0, 0)):
        pl.semaphore_signal(
            free_sem, inc=1, device_id=place.rep_dev(*by), device_id_type=MESH
        )
    scatter_back.step_two()
    weight_grad(w_down, hidden, cot_all)
    sum_down.core_send()
    pl.semaphore_wait(free_sem, 3)
    sum_gate.x_first(load_landed(0))
    sum_up.x_first(load_landed(1))
    gather_cot.finish()
    q_cols = 2 * HEAD_DIM
    query = heads.at[:, pl.ds(0, q_cols)]
    key = heads.at[:, pl.ds(q_cols, HEAD_DIM)]
    value = heads.at[:, pl.ds(q_cols + HEAD_DIM, HEAD_DIM)]
    attended = heads.at[:, pl.ds(q_cols + 2 * HEAD_DIM, q_cols)]
    w_attn = cot_all
    attn_cols = heads.shape[1]
    loads = [
        pltpu.make_async_copy(heads_hbm, heads, local_sems.at[0]),
        pltpu.make_async_copy(
            w_attn_hbm.at[pl.ds(0, rows_all)],
            w_attn.at[:, pl.ds(0, attn_cols)],
            local_sems.at[1],
        ),
        pltpu.make_async_copy(
            w_attn_hbm.at[pl.ds(rows_all, rows_all)],
            w_attn.at[:, pl.ds(attn_cols, attn_cols)],
            local_sems.at[2],
        ),
    ]
    for load in loads:
        load.start()
    scatter_back.step_three()
    gain_rows = None
    for half in (1, 0):
        rows = pl.ds(half * HALF, HALF)
        d_second = scatter_back.total(half)
        back, gain_part = rms_backward(resid[rows, :], gain_two[...], d_second)
        grad_tokens[rows, :] = cotangent[rows, :] + back
        gain_part = jnp.sum(gain_part, axis=0, keepdims=True)
        gain_rows = gain_part if gain_rows is None else gain_rows + gain_part
    gain_sums[0] = jnp.zeros_like(gain_sums[0])

    def keep_gain(first_row, value):
        for i in range(value.shape[1] // HEAD_DIM):
            gain_sums[0, first_row + i : first_row + i + 1, :] = value[
                :, i * HEAD_DIM : (i + 1) * HEAD_DIM
            ]

    gain_slots = width // HEAD_DIM
    keep_gain(gain_slots, gain_rows)
    branch[own, :] = grad_tokens[...].astype(low)
    gather_branch.start()
    sum_down.x_first(load_landed(2))
    gather_branch.step_one()
    sum_gate.x_second()
    gather_branch.step_two()
    sum_up.x_second()
    gather_branch.step_three()
    sum_down.x_second()
    sum_gate.y_send()
    gather_branch.step_four()
    sum_up.y_send()
    gather_branch.own_line()
    for load in loads:
        load.wait()

    def into_attention(dy):
        rows = pl.ds(place.line(dy), LINE)
        d_att[rows, :] = (
            mm(branch[rows, 0:rows_all], w_attn[:, 4 * HEAD_DIM : attn_cols])
            + mm(branch[rows, rows_all:], w_attn[:, attn_cols + 4 * HEAD_DIM : 2 * attn_cols])
        ).astype(low)

    into_attention(0)
    gather_branch.other_line()
    into_attention(1)
    sum_down.y_send()
    scatter_left.send_other()
    scatter_left.send_own()
    scatter_back.finish()
    load = pltpu.make_async_copy(first_hbm, part_back, local_sems.at[0])
    load.start()

    def unrotate(rows, upstream, projected, gain):
        turned = upstream * cosine[rows, :] - swap_halves(upstream) * sine[rows, :]
        return rms_backward(projected, gain, turned)

    gain_rows = jnp.zeros((1, HEAD_DIM), f32)
    d_key[...] = jnp.zeros_like(d_key)
    d_value[...] = jnp.zeros_like(d_value)
    for part in range(rows_all // chunk):
        rows = pl.ds(part * chunk, chunk)
        seen = (part + 1) * chunk
        token = part * chunk + lax.broadcasted_iota(jnp.int32, (chunk, 1), 0)
        source = lax.broadcasted_iota(jnp.int32, (1, seen), 1)
        visible = (source >= begin_of(token)) & (source <= token)
        for g in range(2):
            lanes = pl.ds(g * HEAD_DIM, HEAD_DIM)
            scores = mm_nt(query[rows, lanes], key[0:seen, :]) * scale
            weights = jnp.where(visible, jnp.exp(scores - proj[rows, 3 * HEAD_DIM + g : 3 * HEAD_DIM + g + 1]), 0.0)
            d_probs = mm_nt(d_att[rows, lanes], value[0:seen, :])
            inner = jnp.sum(weights * d_probs, axis=-1, keepdims=True)
            d_scores = (weights * (d_probs - inner)).astype(low)
            back, gain_part = unrotate(
                rows, mm(d_scores, key[0:seen, :]) * scale, proj[rows, lanes], query_gain[...].astype(f32)
            )
            d_qkv[rows, lanes] = back.astype(low)
            gain_rows = gain_rows + jnp.sum(gain_part, axis=0, keepdims=True)
            d_key[0:seen, :] += mm_tn(d_scores, query[rows, lanes])
            d_value[0:seen, :] += mm_tn(weights.astype(low), d_att[rows, lanes])
        if part == 1:
            sum_gate.y_gather(sum_gate.piece(), local_sems.at[3])
        if part == 3:
            sum_up.y_gather(sum_up.piece(), local_sems.at[3])
    d_qkv[:, 3 * HEAD_DIM :] = d_value[...].astype(low)

    keep_gain(2 * gain_slots, gain_rows)
    lanes = pl.ds(2 * HEAD_DIM, HEAD_DIM)
    back, gain_part = unrotate(pl.ds(0, rows_all), d_key[...] * scale, proj[:, lanes], key_gain[...].astype(f32))
    d_qkv[:, lanes] = back.astype(low)
    keep_gain(2 * gain_slots + 1, jnp.sum(gain_part, axis=0, keepdims=True))

    head_landed = cot_all.at[:, pl.ds(0, 6 * HEAD_DIM)]
    sum_attn = RepSum(
        place,
        sems(RepSum.COPIES),
        pair.at[pl.ds(pl.multiple_of(place.core * rows_all, BLOCK), rows_all)],
        pair.at[pl.ds(pl.multiple_of((1 - place.core) * rows_all, BLOCK), rows_all)],
        head_core_landed,
        [head_landed.at[pl.ds(e * BLOCK, BLOCK)] for e in range(2)],
        [head_landed.at[pl.ds((1 + e) * 2 * BLOCK, 2 * BLOCK)] for e in range(2)],
        head_landed.at[pl.ds(6 * BLOCK, BLOCK)],
        attn_grads,
        BLOCK,
        16,
    )

    load.wait()

    @pl.loop(0, width // 256)
    def _(i):
        cols = pl.ds(pl.multiple_of(i * 256, 256), 256)
        from_first = mm_tn(part_back[:, cols], d_qkv[...]).astype(low)
        from_branch = mm_tn(branch[:, cols], attended[...]).astype(low)
        for piece in range(16):
            rows = pl.ds(pl.multiple_of(piece * BLOCK + i * 16, 16), 16)
            pair[rows, 0 : 4 * HEAD_DIM] = from_first[piece * 16 : piece * 16 + 16, :]
            pair[rows, 4 * HEAD_DIM :] = from_branch[piece * 16 : piece * 16 + 16, :]

    gather_branch.finish()
    for by in ((1, 0), (0, 1), (0, 3)):
        pl.semaphore_signal(landing_free, inc=1, device_id=place.dev(*by), device_id_type=MESH)
    sum_attn.core_send()
    scatter_first = Scatter(
        place,
        part_back,
        Slots(branch, 0, HALF),
        Slots(branch, 4 * HALF, 32),
        Slots(branch, 7 * HALF, HALF),
        branch.at[pl.ds(13 * HALF, HALF)],
        *sems(Scatter.COPIES),
    )

    def load_heads():
        copy = pltpu.make_async_copy(head_core_landed, d_up, local_sems.at[3])
        copy.start()
        copy.wait()
        return d_up

    def into_first(dy):
        rows = pl.ds(place.line(dy), LINE)

        for side in range(2):

            @pl.loop(0, rows_all // 256)
            def _(i):
                feats = pl.ds(pl.multiple_of(i * 256, 256), 256)
                cols = pl.ds(pl.multiple_of(side * rows_all + i * 256, 256), 256)
                part_back[rows, cols] = mm_nt(
                    d_qkv[rows, :], w_attn[feats, pl.ds(side * attn_cols, 4 * HEAD_DIM)]
                ).astype(low)

    into_first(1)
    pl.semaphore_wait(landing_free, 3)
    scatter_first.send_other()
    into_first(0)
    scatter_first.send_own()
    for by in ((0, 1, 0), (0, 3, 0), (1, 0, 0)):
        pl.semaphore_signal(
            heads_free, inc=1, device_id=place.rep_dev(*by), device_id_type=MESH
        )
    sum_down.y_gather(sum_down.piece(), local_sems.at[3])
    sum_gate.x_gather()
    pl.semaphore_wait(heads_free, 3)
    sum_attn.x_first(load_heads)
    scatter_left.step_one()
    sum_attn.x_second()
    scatter_left.step_two()
    scatter_first.step_one()
    sum_up.x_gather()
    sum_gate.x_forward()
    sum_attn.y_send()
    scatter_left.step_three()
    scatter_first.step_two()
    piece = sum_attn.piece()
    swap_net = Net(*sems(7))
    for dy in range(2):
        for dz in range(4):
            if dy or dz:
                to = place.block(dy, dz)
                src = piece.at[pl.ds(pl.multiple_of(to * 16, 16), 16)]
                dst = swapped.at[pl.ds(pl.multiple_of(place.shard * 16, 16), 16)]
                here = place.block(-dy, -dz)
                here = swapped.at[pl.ds(pl.multiple_of(here * 16, 16), 16)]
                swap_net.send(f"{dy}{dz}", src, dst, place.dev(dy, dz), here)
    own_rows = pl.ds(pl.multiple_of(place.shard * 16, 16), 16)
    swapped[own_rows, :] = piece[own_rows, :]
    scatter_first.step_three()
    sum_down.x_gather()
    gain_rows = None
    for half in (1, 0):
        rows = pl.ds(half * HALF, HALF)
        d_first = scatter_first.total(half)
        back, gain_part = rms_backward(tokens[rows, :].astype(f32), gain_one[...], d_first)
        grad_tokens[rows, :] += back
        gain_part = jnp.sum(gain_part, axis=0, keepdims=True)
        gain_rows = gain_part if gain_rows is None else gain_rows + gain_part
    keep_gain(0, gain_rows)

    gain_net = Net(*sems(9))
    stages = (
        [place.dev(0, d) for d in (1, 2, 3)],
        [place.dev(1, 0)],
        [place.rep_dev(1, 0, 0)],
        [place.rep_dev(0, 0, 1)],
        [place.rep_dev(0, d, 0) for d in (1, 2, 3)],
    )

    def gain_send(stage):
        for i, dev in enumerate(stages[stage]):
            dst = gain_landed.at[3 * stage + i]
            gain_net.send(f"{stage}.{i}", gain_sums.at[stage], dst, dev, dst)

    def gain_add(stage):
        total = gain_sums[stage]
        for i in range(len(stages[stage])):
            gain_net.wait(f"{stage}.{i}")
            total = total + gain_landed[3 * stage + i]
        gain_sums[stage + 1] = total

    gain_send(0)
    swap_net.finish()
    kv = 8 * HEAD_DIM
    for j in range(8):
        rows = pl.ds(j * 16, 16)
        at = 0
        for begin, size in ((0, 2), (2, 1), (3, 1), (4, 2)):
            assembled[:, at + j * size * HEAD_DIM : at + (j + 1) * size * HEAD_DIM] = swapped[
                rows, begin * HEAD_DIM : (begin + size) * HEAD_DIM
            ]
            at += size * kv
    sum_attn.y_gather(assembled, local_sems.at[3])
    gain_add(0)
    gain_send(1)
    for half in (0, 1):
        rows = pl.ds(half * HALF, HALF)
        result[rows, left] = resid[rows, left] + scatter_left.total(half)
    sum_up.x_forward()
    gain_add(1)
    gain_send(2)
    scatter_right.send_other()
    scatter_right.send_own()
    sum_attn.x_gather()
    sum_gate.x_last()
    gain_add(2)
    gain_send(3)
    sum_down.x_forward()
    scatter_right.step_one()
    sum_attn.x_forward()
    gain_add(3)
    gain_send(4)
    sum_up.x_last()
    scatter_right.step_two()
    sum_down.x_last()
    sum_attn.x_last()
    scatter_right.step_three()
    gain_add(4)
    for half in (0, 1):
        rows = pl.ds(half * HALF, HALF)
        result[rows, right] = resid[rows, right] + scatter_right.total(half)
    gains[...] = gain_sums[5]

    for one in (scatter_first, scatter_left, scatter_right):
        one.finish()
    for one in sums:
        one.finish()
    sum_attn.finish()
    gain_net.finish()


def layer_call(lengths, *args):
    tokens, cotangent = args[:2]
    width = tokens.shape[1]
    hid = args[-1].shape[0]
    rows = 8 * BLOCK
    vmem = pl.BlockSpec(memory_space=pltpu.VMEM)
    smem = pl.BlockSpec(memory_space=pltpu.SMEM)
    hbm = pl.BlockSpec(memory_space=pltpu.HBM)
    copies = 4 * Gather.COPIES + 5 * Scatter.COPIES + 4 * RepSum.COPIES + 9 + 7 + 7
    gain_shape = (2 * width // HEAD_DIM + 8, HEAD_DIM)
    return pl.pallas_call(
        functools.partial(layer_kernel, 1.0 / math.sqrt(HEAD_DIM)),
        name="layer",
        out_shape=[
            jax.ShapeDtypeStruct((BLOCK, width), f32),
            jax.ShapeDtypeStruct((BLOCK, width), f32),
            jax.ShapeDtypeStruct(gain_shape, f32),
            jax.ShapeDtypeStruct((256, 3 * width), low),
            jax.ShapeDtypeStruct((3, hid, width), low),
            jax.ShapeDtypeStruct((3, hid // 2, width), low),
            jax.ShapeDtypeStruct((rows, 6 * HEAD_DIM), low),
            jax.ShapeDtypeStruct((rows, width), low),
            jax.ShapeDtypeStruct((2 * rows, 6 * HEAD_DIM), low),
            jax.ShapeDtypeStruct((rows, 6 * HEAD_DIM), low),
        ],
        in_specs=[smem] + [vmem] * 6 + [hbm] * 7,
        out_specs=[vmem] * 3 + [hbm] * 7,
        scratch_shapes=[
            pltpu.VMEM((BLOCK, width), f32),
            pltpu.VMEM((2, width), f32),
            pltpu.VMEM((8, 16, 256), low),
            pltpu.VMEM((rows, 4 * HEAD_DIM), f32),
            pltpu.VMEM((rows, HEAD_DIM), f32),
            pltpu.VMEM((rows, HEAD_DIM), f32),
            pltpu.VMEM((rows, width), low),
            pltpu.VMEM((rows, width), low),
            pltpu.VMEM((rows, width), low),
            pltpu.VMEM((hid, width), low),
            pltpu.VMEM((hid, width), low),
            pltpu.VMEM((hid, width), low),
            pltpu.VMEM((2 * rows, hid), low),
            pltpu.VMEM((rows, hid), low),
            pltpu.VMEM((rows, width), low),
            pltpu.VMEM((rows, width), low),
            pltpu.VMEM((rows, 2 * HEAD_DIM), low),
            pltpu.VMEM((rows, HEAD_DIM), f32),
            pltpu.VMEM((rows, HEAD_DIM), f32),
            pltpu.VMEM((rows, 4 * HEAD_DIM), low),
            pltpu.VMEM((hid // 2, width), low),
        ]
        + Scatter.scratch(width)
        + [
            pltpu.VMEM((BLOCK, 6 * HEAD_DIM), low),
            pltpu.VMEM((16, 3 * width), low),
            pltpu.VMEM((6,) + gain_shape, f32),
            pltpu.VMEM((15,) + gain_shape, f32),
            pltpu.SemaphoreType.DMA((2, 2, 11)),
            pltpu.SemaphoreType.DMA((3, 2)),
            pltpu.SemaphoreType.REGULAR,
            pltpu.SemaphoreType.REGULAR,
            pltpu.SemaphoreType.REGULAR,
            pltpu.SemaphoreType.DMA((6,)),
            pltpu.SemaphoreType.DMA((copies,)),
            pltpu.SemaphoreType.DMA((copies,)),
        ],
        compiler_params=pltpu.CompilerParams(
            collective_id=1, has_side_effects=True, vmem_limit_bytes=60 << 20
        ),
        cost_estimate=pl.CostEstimate(
            flops=36_000_000_000, bytes_accessed=60_000_000, transcendentals=4_000_000
        ),
    )(lengths, *args)


def widen_kernel(ffn, attn, *refs):
    outs, (narrow, narrow_attn, wide, wide_attn, load_sems, store_sems, attn_sems) = refs[:7], refs[7:]
    slots, tall, _ = wide.shape
    count = narrow.shape[0] // tall
    per = count // 3
    loads = []
    for i in range(count):
        rows = pl.ds(i % per * tall, tall)
        loads.append(
            pltpu.make_async_copy(
                ffn.at[i // per, rows], narrow.at[pl.ds(i * tall, tall)], load_sems.at[i]
            )
        )
    first = pltpu.make_async_copy(attn, narrow_attn, load_sems.at[count])
    first.start()
    for load in loads:
        load.start()
    first.wait()
    wide_attn[...] = narrow_attn[...].astype(f32)
    stores, at = [], 0
    for j, ref in enumerate(outs[3:]):
        size = ref.shape[1]
        stores.append(
            pltpu.make_async_copy(wide_attn.at[:, pl.ds(at, size)], ref, attn_sems.at[j])
        )
        stores[-1].start()
        at += size
    busy = [None] * slots
    for i in range(count):
        loads[i].wait()
        slot = i % slots
        if busy[slot] is not None:
            busy[slot].wait()
        wide[slot] = narrow[pl.ds(i * tall, tall), :].astype(f32)
        rows = pl.ds(i % per * tall, tall)
        busy[slot] = pltpu.make_async_copy(wide.at[slot], outs[i // per].at[rows], store_sems.at[slot])
        busy[slot].start()
    for copy in busy + stores:
        copy.wait()


def widen(ffn, attn):
    _, hid, width = ffn.shape
    rows = attn.shape[0]
    tall, slots = hid // 3, 6
    sizes = (width, width // 2, width // 2, width)
    hbm = pl.BlockSpec(memory_space=pltpu.HBM)
    return pl.pallas_call(
        widen_kernel,
        name="widen",
        out_shape=[jax.ShapeDtypeStruct((hid, width), f32)] * 3
        + [jax.ShapeDtypeStruct((rows, size), f32) for size in sizes],
        in_specs=[hbm, hbm],
        out_specs=[hbm] * 7,
        scratch_shapes=[
            pltpu.VMEM((3 * hid, width), low),
            pltpu.VMEM((rows, 3 * width), low),
            pltpu.VMEM((slots, tall, width), f32),
            pltpu.VMEM((rows, 3 * width), f32),
            pltpu.SemaphoreType.DMA((10,)),
            pltpu.SemaphoreType.DMA((slots,)),
            pltpu.SemaphoreType.DMA((4,)),
        ],
        compiler_params=pltpu.CompilerParams(vmem_limit_bytes=60 << 20),
    )(ffn, attn)


def per_device(
    tokens,
    cotangent,
    lengths,
    attn_gain,
    mlp_gain,
    query_gain,
    key_gain,
    w_query,
    w_key,
    w_value,
    w_out,
    w_gate,
    w_up,
    w_down,
):
    width = tokens.shape[1]
    shards = lax.axis_size("shard")
    feat = width // shards
    my_shard = lax.axis_index("shard")
    half = np.arange(HEAD_DIM, dtype=np.float64) % (HEAD_DIM // 2)
    frequency = jnp.asarray(theta_base ** (-half * (2.0 / HEAD_DIM)), f32)[None]
    result, grad_tokens, gains, attn_grads, ffn_grads, *_ = layer_call(
        lengths,
        tokens,
        cotangent,
        jnp.concatenate([attn_gain[None], mlp_gain[None], jnp.zeros((14, feat), low)]),
        query_gain[None],
        key_gain[None],
        frequency,
        w_query,
        w_key,
        w_value,
        w_out,
        w_gate,
        w_up,
        w_down,
    )
    grad_gate, grad_up, grad_down, grad_query, grad_key, grad_value, grad_out = widen(
        ffn_grads, attn_grads
    )
    gains = gains.reshape(-1)
    head_piece = HEAD_DIM // shards
    gains_first = lax.dynamic_slice_in_dim(gains, my_shard * feat, feat, 0)
    gains_second = lax.dynamic_slice_in_dim(gains, width + my_shard * feat, feat, 0)
    gains_query = lax.dynamic_slice_in_dim(gains, 2 * width + my_shard * head_piece, head_piece, 0)
    gains_key = lax.dynamic_slice_in_dim(
        gains, 2 * width + HEAD_DIM + my_shard * head_piece, head_piece, 0
    )
    return (
        result,
        grad_tokens,
        grad_query,
        grad_key,
        grad_value,
        grad_out,
        grad_gate,
        grad_up,
        grad_down,
        gains_first,
        gains_second,
        gains_query,
        gains_key,
    )


def solution(mesh):
    spread = P(("rep", "shard"), None)
    rowed = P("shard", None)
    return jax.shard_map(
        per_device,
        mesh=mesh,
        in_specs=(spread, spread, P("rep", None), P("shard"), P("shard"), P(), P()) + (rowed,) * 7,
        out_specs=(spread, spread) + (rowed,) * 7 + (P("shard"),) * 4,
        check_vma=False,
    )
```

```python
import functools
import math

import jax
import jax.numpy as jnp
import numpy as np
from jax import lax
from jax.experimental import pallas as pl
from jax.experimental.pallas import tpu as pltpu
from jax.sharding import PartitionSpec as P

HEADS = 16
KV_HEADS = 8
HEAD_DIM = 128

epsilon = 1e-06
theta_base = 1000000.0
masked_value = -1e30


MESH = pl.DeviceIdType.MESH
BLOCK = 128
HALF = 64
LINE = 512
low = jnp.bfloat16
f32 = jnp.float32


def mm(left, right):
    return lax.dot_general(left, right, (((1,), (0,)), ((), ())), preferred_element_type=f32)


def mm_nt(left, right):
    return lax.dot_general(left, right, (((1,), (1,)), ((), ())), preferred_element_type=f32)


def mm_tn(left, right):
    return lax.dot_general(left, right, (((0,), (0,)), ((), ())), preferred_element_type=f32)


class Place:
    def __init__(self):
        self.rep = lax.axis_index("rep")
        self.shard = lax.axis_index("shard")
        self.yl, self.z = self.shard // 4, self.shard % 4
        self.yh, self.x, self.core = self.rep // 8, (self.rep // 2) % 4, self.rep % 2

    def block(self, dy, dz):
        return ((self.yl + dy + 2) % 2) * 4 + (self.z + dz + 8) % 4

    def dev(self, dy, dz):
        return (self.rep, self.block(dy, dz))

    def x_at(self, dx):
        return (self.x + dx + 8) % 4

    def rep_dev(self, dyh, dx, dcore):
        rep = ((self.yh + dyh) % 2) * 8 + self.x_at(dx) * 2 + (self.core + dcore) % 2
        return (rep, self.shard)

    def rows(self, dy, dz, start=0, count=BLOCK):
        return pl.ds(pl.multiple_of(self.block(dy, dz) * BLOCK + start, 32), count)

    def line(self, dy):
        return pl.multiple_of(((self.yl + dy + 2) % 2) * LINE, LINE)

    def shard_peers(self):
        return [self.dev(dy, dz) for dy in range(2) for dz in range(4) if dy or dz]

    def rep_peers(self):
        return [
            self.rep_dev(*by) for by in ((0, 0, 1), (0, 1, 0), (0, 2, 0), (0, 3, 0), (1, 0, 0))
        ]

    def greet(self):
        barrier = pltpu.get_barrier_semaphore()
        peers = self.shard_peers() + self.rep_peers()
        for peer in peers:
            pl.semaphore_signal(barrier, inc=1, device_id=peer, device_id_type=MESH)
        pl.semaphore_wait(barrier, len(peers))


class Net:
    def __init__(self, send_sems, recv_sems):
        self.send_sems, self.recv_sems = send_sems, recv_sems
        self.started, self.coming = [], {}

    def send(self, tag, src, dst, dev, here):
        k = len(self.started)
        copy = pltpu.make_async_remote_copy(
            src_ref=src,
            dst_ref=dst,
            send_sem=self.send_sems.at[k],
            recv_sem=self.recv_sems.at[k],
            device_id=dev,
            device_id_type=MESH,
        )
        copy.start()
        self.started.append(copy)
        self.coming[tag] = (k, here, dev)

    def wait(self, tag):
        k, here, dev = self.coming.pop(tag)
        pltpu.make_async_remote_copy(
            src_ref=here,
            dst_ref=here,
            send_sem=self.send_sems.at[k],
            recv_sem=self.recv_sems.at[k],
            device_id=dev,
            device_id_type=MESH,
        ).wait_recv()

    def finish(self):
        for tag in list(self.coming):
            self.wait(tag)
        for copy in self.started:
            copy.wait_send()


class Gather:
    COPIES = 18

    def __init__(self, place, buf, send_sems, recv_sems):
        self.place, self.buf = place, buf
        self.net = Net(send_sems, recv_sems)

    def send(self, tag, block, start, count, to):
        rows = self.place.rows(*block, start, count)
        here = self.place.rows(block[0] - to[0], block[1] - to[1], start, count)
        self.net.send(
            tag, self.buf.at[rows], self.buf.at[rows], self.place.dev(*to), self.buf.at[here]
        )

    def start(self):
        self.send("y_up", (0, 0), 0, HALF, (1, 0))
        for d in (1, 3):
            self.send(f"z_low{d}", (0, 0), HALF, HALF, (0, d))
        self.send("y_low", (0, 0), HALF, HALF, (1, 0))

    def step_one(self):
        self.net.wait("y_up")
        for d in (1, 3):
            self.send(f"p_up{d}", (1, 0), 0, HALF, (0, d))

    def step_two(self):
        for e, d in enumerate((1, 3)):
            self.net.wait(f"z_low{d}")
            self.send(f"f_low{d}", (0, -d), HALF + 32 * e, 32, (0, d))
            self.send(f"q_low{d}", (0, -d), HALF, HALF, (1, 0))
        for d in (1, 3):
            self.send(f"z_up{d}", (0, 0), 0, HALF, (0, d))

    def step_three(self):
        for e, d in enumerate((1, 3)):
            self.net.wait(f"p_up{d}")
            self.send(f"f_p{d}", (1, -d), 32 * e, 32, (0, d))
        for e, d in enumerate((1, 3)):
            self.net.wait(f"f_low{d}")
            self.send(f"q_far{d}", (0, -2 * d), HALF + 32 * e, 32, (1, 0))

    def step_four(self):
        for e, d in enumerate((1, 3)):
            self.net.wait(f"z_up{d}")
            self.send(f"f_up{d}", (0, -d), 32 * e, 32, (0, d))

    def own_line(self):
        for d in (1, 3):
            self.net.wait(f"f_up{d}")

    def other_line(self):
        for tag in list(self.net.coming):
            self.net.wait(tag)

    def steps(self):
        return [self.start, self.step_one, self.step_two, self.step_three, self.step_four]

    def finish(self):
        self.net.finish()


class Slots:
    def __init__(self, ref, base, size):
        self.ref, self.base, self.size = ref, base, size

    @property
    def at(self):
        return self

    def __getitem__(self, i):
        i = i if isinstance(i, int) else 2 * i[0] + i[1]
        return self.ref.at[pl.ds(self.base + i * self.size, self.size)]


class Scatter:
    COPIES = 17

    @staticmethod
    def scratch(columns):
        return [
            pltpu.VMEM((4, HALF, columns), low),
            pltpu.VMEM((3, 2, 32, columns), low),
            pltpu.VMEM((3, 2, HALF, columns), low),
            pltpu.VMEM((HALF, columns), low),
        ]

    def __init__(self, place, part, across, near, far, last, send_sems, recv_sems):
        self.place, self.part = place, part
        self.across, self.near, self.far, self.last = across, near, far, last
        self.net = Net(send_sems, recv_sems)

    def add(self, rows, *refs):
        total = self.part[rows, :].astype(f32)
        for ref in refs:
            total = total + ref[...].astype(f32)
        self.part[rows, :] = total.astype(low)

    def first(self, kind):
        dy, start = ((1, 0), (0, 0), (0, HALF))[kind]
        for e, d in enumerate((1, 3)):
            src = self.part.at[self.place.rows(dy, 2, start + 32 * e, 32)]
            dst = self.near.at[kind, e]
            self.net.send(f"near{kind}{e}", src, dst, self.place.dev(0, d), dst)

    def second(self, kind):
        dy, start = ((1, 0), (0, 0), (0, HALF))[kind]
        for e, d in enumerate((1, 3)):
            self.net.wait(f"near{kind}{e}")
            self.add(self.place.rows(dy, d, start + 32 * e, 32), self.near.at[kind, e])
            src = self.part.at[self.place.rows(dy, d, start, HALF)]
            dst = self.far.at[kind, e]
            self.net.send(f"far{kind}{e}", src, dst, self.place.dev(0, d), dst)

    def send_other(self):
        for d in (2, 1, 3, 0):
            src = self.part.at[self.place.rows(1, d, HALF, HALF)]
            dst = self.across.at[d]
            self.net.send(f"across{d}", src, dst, self.place.dev(1, 0), dst)
        self.first(0)

    def send_own(self):
        self.first(1)

    def step_one(self):
        self.net.wait("across2")
        self.add(self.place.rows(0, 2, HALF, HALF), self.across.at[2])
        self.first(2)
        self.second(0)
        self.second(1)

    def step_two(self):
        for d in (1, 3):
            self.net.wait(f"across{d}")
            self.add(self.place.rows(0, d, HALF, HALF), self.across.at[d])
        self.second(2)

    def step_three(self):
        for e in range(2):
            self.net.wait(f"far0{e}")
        rows = self.place.rows(1, 0, 0, HALF)
        self.add(rows, self.far.at[0, 0], self.far.at[0, 1])
        self.net.send("last", self.part.at[rows], self.last, self.place.dev(1, 0), self.last)

    def total(self, half):
        if half == 0:
            tags, extra, kind = ("far10", "far11", "last"), self.last, 1
        else:
            tags, extra, kind = ("far20", "far21", "across0"), self.across.at[0], 2
        for tag in tags:
            self.net.wait(tag)
        out = self.part[self.place.rows(0, 0, half * HALF, HALF), :].astype(f32)
        for ref in (self.far.at[kind, 0], self.far.at[kind, 1], extra):
            out = out + ref[...].astype(f32)
        return out

    def finish(self):
        self.net.finish()


def add_rows(into, start, count, *refs):
    step = 64 if count % 64 == 0 else 48

    @pl.loop(0, count // step)
    def _(i):
        at = pl.multiple_of(i * step, 16)
        rows = pl.ds(pl.multiple_of(start + at, 16), step)
        total = into[rows, :].astype(f32)
        for ref in refs:
            total = total + ref[pl.ds(at, step), :].astype(f32)
        into[rows, :] = total.astype(low)


class RepSum:
    COPIES = 15

    def __init__(self, place, sems, own, other, landed, near, far, cross, out, unit, out_unit):
        self.place, self.net = place, Net(*sems)
        self.own, self.other, self.landed = own, other, landed
        self.near, self.far, self.cross = near, far, cross
        self.out, self.unit, self.out_unit = out, unit, out_unit

    def chunk(self, dx, start=0, count=None):
        at = self.place.x_at(dx) * 2 * self.unit + start
        return pl.ds(pl.multiple_of(at, 16), 2 * self.unit if count is None else count)

    def out_rows(self, dcore, dx, start=0, count=None):
        core = (self.place.core + dcore) % 2
        at = (core * 8 + self.place.x_at(dx) * 2 + start) * self.out_unit
        count = (2 if count is None else count) * self.out_unit
        return self.out.at[pl.ds(pl.multiple_of(at, 16), count)]

    def core_send(self):
        self.net.send("core", self.other, self.landed, self.place.rep_dev(0, 0, 1), self.landed)

    def x_first(self, load=None):
        self.net.wait("core")
        add_rows(self.own, 0, 8 * self.unit, self.landed if load is None else load())
        for e, d in enumerate((1, 3)):
            src = self.own.at[self.chunk(2, e * self.unit, self.unit)]
            dst = self.near[e]
            self.net.send(f"near{e}", src, dst, self.place.rep_dev(0, d, 0), dst)

    def x_second(self):
        for e, d in enumerate((1, 3)):
            self.net.wait(f"near{e}")
            add_rows(self.own, self.place.x_at(d) * 2 * self.unit + e * self.unit, self.unit, self.near[e])
            dst = self.far[e]
            self.net.send(
                f"far{e}", self.own.at[self.chunk(d)], dst, self.place.rep_dev(0, d, 0), dst
            )

    def y_send(self):
        for e in range(2):
            self.net.wait(f"far{e}")
        add_rows(self.own, self.place.x * 2 * self.unit, 2 * self.unit, *self.far)
        src = self.own.at[self.chunk(0, (1 - self.place.yh) * self.unit, self.unit)]
        self.net.send("cross", src, self.cross, self.place.rep_dev(1, 0, 0), self.cross)

    def piece(self):
        self.net.wait("cross")
        at = (self.place.x * 2 + self.place.yh) * self.unit
        add_rows(self.own, at, self.unit, self.cross)
        return self.own.at[pl.ds(pl.multiple_of(at, 16), self.unit)]

    def y_gather(self, piece, sem):
        mine = self.out_rows(0, 0, self.place.yh, 1)
        copy = pltpu.make_async_copy(piece, mine, sem)
        copy.start()
        self.net.send(
            "y", piece, mine, self.place.rep_dev(1, 0, 0), self.out_rows(0, 0, 1 - self.place.yh, 1)
        )
        copy.wait()

    def to_core(self, dx):
        rows = self.out_rows(0, dx)
        self.net.send(
            f"core{dx}", rows, rows, self.place.rep_dev(0, 0, 1), self.out_rows(1, dx)
        )

    def x_gather(self):
        self.net.wait("y")
        rows = self.out_rows(0, 0)
        for d in (1, 3):
            self.net.send(f"x{d}", rows, rows, self.place.rep_dev(0, d, 0), self.out_rows(0, -d))
        self.to_core(0)

    def x_forward(self):
        for e, d in enumerate((1, 3)):
            self.net.wait(f"x{d}")
            rows = self.out_rows(0, -d, e, 1)
            self.net.send(
                f"xx{d}", rows, rows, self.place.rep_dev(0, d, 0), self.out_rows(0, -2 * d, e, 1)
            )
            self.to_core(-d)

    def x_last(self):
        for d in (1, 3):
            self.net.wait(f"xx{d}")
        self.to_core(2)

    def finish(self):
        self.net.finish()


def rms_backward(value, gain, upstream):
    root = lax.rsqrt(jnp.mean(value * value, axis=-1, keepdims=True) + epsilon)
    pulled = upstream * gain
    back = root * pulled - value * (root * root * root) * jnp.mean(
        pulled * value, axis=-1, keepdims=True
    )
    return back, upstream * (value * root)


def swap_halves(value):
    return pltpu.roll(value, HEAD_DIM // 2, 1)


def layer_kernel(
    scale,
    lengths,
    tokens,
    cotangent,
    gain_shard,
    query_gain,
    key_gain,
    frequency,
    w_query_hbm,
    w_key_hbm,
    w_value_hbm,
    w_out_hbm,
    w_gate_hbm,
    w_up_hbm,
    w_down_hbm,
    result,
    grad_tokens,
    gains,
    attn_grads,
    ffn_grads,
    core_landed,
    head_core_landed,
    first_hbm,
    w_attn_hbm,
    heads_hbm,
    resid,
    gain_rows_all,
    gain_blocks,
    proj,
    cosine,
    sine,
    second,
    cot_all,
    branch,
    w_gate,
    w_up,
    w_down,
    pair,
    d_up,
    part_out,
    part_back,
    d_att,
    d_key,
    d_value,
    d_qkv,
    staged,
    across,
    near,
    far,
    last,
    swapped,
    assembled,
    gain_sums,
    gain_landed,
    swap_sems,
    sibling_sems,
    free_sem,
    landing_free,
    heads_free,
    local_sems,
    send_sems,
    recv_sems,
):
    place = Place()
    hidden = pair.at[pl.ds(0, 8 * BLOCK)]
    d_gate = pair.at[pl.ds(8 * BLOCK, 8 * BLOCK)]
    rows_all = 8 * BLOCK
    hid = w_gate.shape[0]
    width = second.shape[1]

    loads = [
        pltpu.make_async_copy(src, dst, local_sems.at[i])
        for i, (src, dst) in enumerate(
            ((w_gate_hbm, w_gate), (w_up_hbm, w_up), (w_down_hbm, w_down))
        )
    ]
    for load in loads:
        load.start()

    used = [0]

    def sems(count):
        at = used[0]
        used[0] += count
        return send_sems.at[pl.ds(at, count)], recv_sems.at[pl.ds(at, count)]

    own = place.rows(0, 0)
    gain_one = gain_rows_all.at[pl.ds(0, 1)]
    gain_two = gain_rows_all.at[pl.ds(1, 1)]
    cot_all[own, :] = cotangent[...].astype(low)
    branch[own, :] = tokens[...]
    feat = w_query_hbm.shape[0]
    gain_blocks[place.shard] = gain_shard[...]
    place.greet()

    gain_share = Net(*sems(7))
    peers = [(dy, dz) for dy in range(2) for dz in range(4) if dy or dz]
    for by in peers:
        gain_share.send(
            str(by),
            gain_blocks.at[place.shard],
            gain_blocks.at[place.shard],
            place.dev(*by),
            gain_blocks.at[place.block(-by[0], -by[1])],
        )
    qkv_parts = (
        (w_query_hbm, 0, 2 * HEAD_DIM),
        (w_key_hbm, 2 * HEAD_DIM, HEAD_DIM),
        (w_value_hbm, 3 * HEAD_DIM, HEAD_DIM),
    )
    out_parts = ((w_out_hbm, 4 * HEAD_DIM, 2 * HEAD_DIM),)
    few = feat // 8
    qkv_span = pl.ds(0, 4 * HEAD_DIM)
    out_span = pl.ds(4 * HEAD_DIM, 2 * HEAD_DIM)

    def swap_rows(block, dx=0, count=1):
        first = place.x_at(dx) if count == 1 else 0
        at = block * feat + (place.core * 4 + first) * few
        return pl.ds(pl.multiple_of(at, few), count * few)

    def swap_copy(src, dst, kind, i, dev):
        return pltpu.make_async_remote_copy(
            src_ref=src,
            dst_ref=dst,
            send_sem=swap_sems.at[0, kind, i],
            recv_sem=swap_sems.at[1, kind, i],
            device_id=dev,
            device_id_type=MESH,
        )

    def swap_send(parts, kind):
        own_rows = pl.ds(pl.multiple_of((place.core * 4 + place.x) * few, few), few)
        for i, by in enumerate(peers):
            to = place.block(*by)
            for whole, begin, size in parts:
                cols = pl.ds(pl.multiple_of(to * size, HEAD_DIM), size)
                src = whole.at[own_rows, cols]
                dst = pair.at[swap_rows(place.shard), pl.ds(begin, size)]
                swap_copy(src, dst, kind, i, place.dev(*by)).start()
        for whole, begin, size in parts:
            cols = pl.ds(pl.multiple_of(place.shard * size, HEAD_DIM), size)
            rows = pl.ds(pl.multiple_of(place.shard * feat, feat), feat)
            copy = pltpu.make_async_copy(
                whole.at[:, cols], pair.at[rows, pl.ds(begin, size)], sibling_sems.at[2, kind]
            )
            copy.start()

    def share_copy(ref, kind, i):
        return swap_copy(
            ref, ref, kind, 7 + i, place.rep_dev(0, i + 1, 0) if i < 3 else place.rep_dev(0, 0, 1)
        )

    def swap_relay(span, kind):
        for i, by in enumerate(peers):
            here = pair.at[swap_rows(place.block(-by[0], -by[1])), span]
            swap_copy(here, here, kind, i, place.dev(*by)).wait_recv()
            for d in range(3):
                share_copy(here, kind, d).start()

    def swap_share(span, kind):
        for d in range(3):
            share_copy(pair.at[pl.ds(0, 7 * few), span], kind, d).wait_recv()
        for by in peers:
            here = pair.at[swap_rows(place.block(-by[0], -by[1]), 0, 4), span]
            share_copy(here, kind, 3).start()

    def swap_done(span, kind):
        rows = pl.ds(pl.multiple_of(place.shard * feat, feat), feat)
        mine = pair.at[rows, span]
        pltpu.make_async_copy(mine, mine, sibling_sems.at[2, kind]).wait()
        share_copy(pair.at[pl.ds(0, 7 * 4 * few), span], kind, 3).wait()
        for d in range(3):
            share_copy(pair.at[pl.ds(0, 7 * few), span], kind, d).wait_send()
        for i, by in enumerate(peers):
            here = pair.at[swap_rows(place.block(-by[0], -by[1])), span]
            swap_copy(here, here, kind, i, place.dev(*by)).wait_send()

    swap_send(qkv_parts, 0)
    gather_tokens = Gather(place, branch, *sems(Gather.COPIES))
    gather_tokens.start()

    start_one = lengths[0, 0]
    start_two = lengths[0, 0] + lengths[0, 1]

    def begin_of(token):
        return jnp.where(
            token >= start_two, start_two, jnp.where(token >= start_one, start_one, 0)
        )

    token = lax.broadcasted_iota(jnp.int32, (rows_all, 1), 0)
    angles = (token - begin_of(token)).astype(f32) * frequency[...]
    lane = lax.broadcasted_iota(jnp.int32, (1, HEAD_DIM), 1)
    cosine[...] = jnp.cos(angles)
    sine[...] = jnp.sin(angles) * jnp.where(lane < HEAD_DIM // 2, -1.0, 1.0)

    gather_tokens.step_one()
    swap_relay(qkv_span, 0)
    gather_tokens.step_two()
    gain_share.finish()
    for j in range(8):
        span = slice(j * feat, (j + 1) * feat)
        gain_rows_all[0:2, span] = gain_blocks[j, 0:2, :].astype(f32)
    gather_tokens.step_three()
    swap_share(qkv_span, 0)
    swap_send(out_parts, 1)
    gather_tokens.step_four()

    def normalise(dy):
        line = place.line(dy)

        @pl.loop(0, LINE // BLOCK)
        def _(i):
            rows = pl.ds(pl.multiple_of(line + i * BLOCK, BLOCK), BLOCK)
            x = branch[rows, :].astype(f32)
            root = lax.rsqrt(jnp.mean(x * x, axis=-1, keepdims=True) + epsilon)
            second[rows, :] = (x * root * gain_one[...]).astype(low)

    gather_tokens.own_line()
    normalise(0)
    gather_tokens.other_line()
    normalise(1)
    gather_tokens.finish()
    keep_first = pltpu.make_async_copy(second, first_hbm, local_sems.at[3])
    keep_first.start()
    gather_cot = Gather(place, cot_all, *sems(Gather.COPIES))
    gather_cot.start()
    swap_relay(out_span, 1)
    swap_done(qkv_span, 0)
    heads = d_up
    gains_of_head = (query_gain, query_gain, key_gain)

    @pl.loop(0, rows_all // 256)
    def _(i):
        rows = pl.ds(pl.multiple_of(i * 256, 256), 256)
        proj[rows, :] = mm(second[rows, :], pair[:, 0 : 4 * HEAD_DIM])
        for g in range(3):
            lanes = pl.ds(g * HEAD_DIM, HEAD_DIM)
            u = proj[rows, lanes]
            root = lax.rsqrt(jnp.mean(u * u, axis=-1, keepdims=True) + epsilon)
            u = u * root * gains_of_head[g][...].astype(f32)
            heads[rows, lanes] = (u * cosine[rows, :] + swap_halves(u) * sine[rows, :]).astype(low)
        lanes = pl.ds(3 * HEAD_DIM, HEAD_DIM)
        heads[rows, lanes] = proj[rows, lanes].astype(low)

    swap_share(out_span, 1)
    chunk = 256
    for part in range(rows_all // chunk):
        rows = pl.ds(part * chunk, chunk)
        seen = (part + 1) * chunk
        token = part * chunk + lax.broadcasted_iota(jnp.int32, (chunk, 1), 0)
        source = lax.broadcasted_iota(jnp.int32, (1, seen), 1)
        visible = (source >= begin_of(token)) & (source <= token)
        for g in range(2):
            lanes = pl.ds(g * HEAD_DIM, HEAD_DIM)
            scores = mm_nt(heads[rows, lanes], heads[0:seen, 2 * HEAD_DIM : 3 * HEAD_DIM]) * scale
            scores = jnp.where(visible, scores, masked_value)
            top = jnp.max(scores, axis=-1, keepdims=True)
            raised = jnp.exp(scores - top)
            total = jnp.sum(raised, axis=-1, keepdims=True)
            probs = (raised * (1.0 / total)).astype(low)
            proj[rows, 3 * HEAD_DIM + g : 3 * HEAD_DIM + g + 1] = jnp.log(total) + top
            heads[rows, pl.ds((4 + g) * HEAD_DIM, HEAD_DIM)] = mm(
                probs, heads[0:seen, 3 * HEAD_DIM : 4 * HEAD_DIM]
            ).astype(low)
        if part == 2:
            gather_cot.step_one()
    keep_heads = pltpu.make_async_copy(heads, heads_hbm, local_sems.at[4])
    keep_heads.start()
    swap_done(out_span, 1)
    keep_weights = pltpu.make_async_copy(pair, w_attn_hbm, local_sems.at[5])
    keep_weights.start()
    landing = (across, near, far, last)
    scatter_attn = Scatter(place, part_back, *landing, *sems(Scatter.COPIES))

    def attention_out(dy):
        rows = pl.ds(place.line(dy), LINE)

        @pl.loop(0, width // 256)
        def _(i):
            cols = pl.ds(pl.multiple_of(i * 256, 256), 256)
            part_back[rows, cols] = mm_nt(
                heads[rows, 4 * HEAD_DIM :], pair[cols, 4 * HEAD_DIM :]
            ).astype(low)

    attention_out(1)
    keep_first.wait()
    scatter_attn.send_other()
    attention_out(0)
    scatter_attn.send_own()
    scatter_attn.step_one()
    scatter_attn.step_two()
    scatter_attn.step_three()
    keep_heads.wait()
    keep_weights.wait()
    for half in (1, 0):
        rows = pl.ds(half * HALF, HALF)
        x = tokens[rows, :].astype(f32) + scatter_attn.total(half)
        resid[rows, :] = x
        root = lax.rsqrt(jnp.mean(x * x, axis=-1, keepdims=True) + epsilon)
        at = place.rows(0, 0, half * HALF, HALF)
        second[at, :] = (x * root * gain_two[...]).astype(low)
    scatter_attn.finish()
    gather_second = Gather(place, second, *sems(Gather.COPIES))
    gather_branch = Gather(place, branch, *sems(Gather.COPIES))
    left, right = (pl.ds(side * (width // 2), width // 2) for side in range(2))
    scatter_left, scatter_right = (
        Scatter(
            place,
            part_out.at[:, cols],
            across.at[:, :, cols],
            near.at[:, :, :, cols],
            far.at[:, :, :, cols],
            last.at[:, cols],
            *sems(Scatter.COPIES),
        )
        for cols in (left, right)
    )
    scatter_back = Scatter(place, part_back, *landing, *sems(Scatter.COPIES))

    def feed_forward(rows):
        @pl.loop(0, hid // 256)
        def _(i):
            cols = pl.ds(pl.multiple_of(i * 256, 256), 256)
            gate = mm_nt(second[rows, :], w_gate[cols, :])
            up = mm_nt(second[rows, :], w_up[cols, :])
            sigma = 1.0 / (1.0 + jnp.exp(-gate))
            silu = gate * sigma
            hidden[rows, cols] = (silu * up).astype(low)
            d_gate[rows, cols] = (up * sigma * (1.0 + gate * (1.0 - sigma))).astype(low)
            d_up[rows, cols] = silu.astype(low)

    def project_out(dy):
        rows = pl.ds(place.line(dy), LINE)

        @pl.loop(0, width // 512)
        def _(i):
            cols = pl.ds(pl.multiple_of(i * 512, 512), 512)
            part_out[rows, cols] = mm(hidden[rows, :], w_down[:, cols]).astype(low)

    def feed_backward(dy):
        rows = pl.ds(place.line(dy), LINE)

        @pl.loop(0, hid // 256)
        def _(i):
            cols = pl.ds(pl.multiple_of(i * 256, 256), 256)
            d_hidden = mm_nt(cot_all[rows, :], w_down[cols, :])
            d_gate[rows, cols] = (d_hidden * d_gate[rows, cols].astype(f32)).astype(low)
            d_up[rows, cols] = (d_hidden * d_up[rows, cols].astype(f32)).astype(low)

        @pl.loop(0, width // 512)
        def _(i):
            cols = pl.ds(pl.multiple_of(i * 512, 512), 512)
            part_back[rows, cols] = (
                mm(d_gate[rows, :], w_gate[:, cols]) + mm(d_up[rows, :], w_up[:, cols])
            ).astype(low)

    def weight_grad(into, left, right):
        @pl.loop(0, hid // 256)
        def _(i):
            cols = pl.ds(pl.multiple_of(i * 256, 256), 256)
            into[cols, :] = mm_tn(left[:, cols], right[...]).astype(low)

    unit = hid // 16
    sums = []
    for i, whole in enumerate((w_gate, w_up, w_down)):
        base = i * 7 * unit

        def view(start, count, base=base):
            return second.at[pl.ds(base + start * unit, count * unit)]

        sums.append(
            RepSum(
                place,
                sems(RepSum.COPIES),
                whole.at[pl.ds(pl.multiple_of(place.core * 8 * unit, 16), 8 * unit)],
                whole.at[pl.ds(pl.multiple_of((1 - place.core) * 8 * unit, 16), 8 * unit)],
                core_landed.at[i],
                [view(0, 1), view(1, 1)],
                [view(2, 2), view(4, 2)],
                view(6, 1),
                ffn_grads.at[i],
                unit,
                unit,
            )
        )
    sum_gate, sum_up, sum_down = sums

    def load_landed(i):
        def load():
            here = staged.at[pl.ds(0, 8 * unit)]
            copy = pltpu.make_async_copy(core_landed.at[i], here, local_sems.at[3])
            copy.start()
            copy.wait()
            return here

        return load

    for step in gather_second.steps():
        step()
    gather_cot.step_two()
    for load in loads:
        load.wait()
    gather_second.own_line()
    gather_cot.step_three()
    feed_forward(pl.ds(place.line(0), LINE))
    gather_second.other_line()
    gather_cot.step_four()
    feed_forward(pl.ds(place.line(1), LINE))
    gather_cot.own_line()
    gather_cot.other_line()
    feed_backward(1)
    scatter_back.send_other()
    feed_backward(0)
    scatter_back.send_own()
    project_out(1)
    project_out(0)
    weight_grad(w_gate, d_gate, second)
    sum_gate.core_send()
    scatter_back.step_one()
    weight_grad(w_up, d_up, second)
    sum_up.core_send()
    gather_second.finish()
    for by in ((0, 1, 0), (0, 3, 0), (1, 0, 0)):
        pl.semaphore_signal(
            free_sem, inc=1, device_id=place.rep_dev(*by), device_id_type=MESH
        )
    scatter_back.step_two()
    weight_grad(w_down, hidden, cot_all)
    sum_down.core_send()
    pl.semaphore_wait(free_sem, 3)
    sum_gate.x_first(load_landed(0))
    sum_up.x_first(load_landed(1))
    gather_cot.finish()
    q_cols = 2 * HEAD_DIM
    query = heads.at[:, pl.ds(0, q_cols)]
    key = heads.at[:, pl.ds(q_cols, HEAD_DIM)]
    value = heads.at[:, pl.ds(q_cols + HEAD_DIM, HEAD_DIM)]
    attended = heads.at[:, pl.ds(q_cols + 2 * HEAD_DIM, q_cols)]
    w_attn = cot_all
    attn_cols = heads.shape[1]
    loads = [
        pltpu.make_async_copy(heads_hbm, heads, local_sems.at[0]),
        pltpu.make_async_copy(
            w_attn_hbm.at[pl.ds(0, rows_all)],
            w_attn.at[:, pl.ds(0, attn_cols)],
            local_sems.at[1],
        ),
        pltpu.make_async_copy(
            w_attn_hbm.at[pl.ds(rows_all, rows_all)],
            w_attn.at[:, pl.ds(attn_cols, attn_cols)],
            local_sems.at[2],
        ),
    ]
    for load in loads:
        load.start()
    scatter_back.step_three()
    gain_rows = None
    for half in (1, 0):
        rows = pl.ds(half * HALF, HALF)
        d_second = scatter_back.total(half)
        back, gain_part = rms_backward(resid[rows, :], gain_two[...], d_second)
        grad_tokens[rows, :] = cotangent[rows, :] + back
        gain_part = jnp.sum(gain_part, axis=0, keepdims=True)
        gain_rows = gain_part if gain_rows is None else gain_rows + gain_part
    gain_sums[0] = jnp.zeros_like(gain_sums[0])

    def keep_gain(first_row, value):
        for i in range(value.shape[1] // HEAD_DIM):
            gain_sums[0, first_row + i : first_row + i + 1, :] = value[
                :, i * HEAD_DIM : (i + 1) * HEAD_DIM
            ]

    gain_slots = width // HEAD_DIM
    keep_gain(gain_slots, gain_rows)
    branch[own, :] = grad_tokens[...].astype(low)
    gather_branch.start()
    sum_down.x_first(load_landed(2))
    gather_branch.step_one()
    sum_gate.x_second()
    gather_branch.step_two()
    sum_up.x_second()
    gather_branch.step_three()
    sum_down.x_second()
    sum_gate.y_send()
    gather_branch.step_four()
    sum_up.y_send()
    gather_branch.own_line()
    for load in loads:
        load.wait()

    def into_attention(dy):
        rows = pl.ds(place.line(dy), LINE)
        d_att[rows, :] = (
            mm(branch[rows, 0:rows_all], w_attn[:, 4 * HEAD_DIM : attn_cols])
            + mm(branch[rows, rows_all:], w_attn[:, attn_cols + 4 * HEAD_DIM : 2 * attn_cols])
        ).astype(low)

    into_attention(0)
    gather_branch.other_line()
    into_attention(1)
    sum_down.y_send()
    scatter_back.finish()
    load = pltpu.make_async_copy(first_hbm, part_back, local_sems.at[0])
    load.start()

    def unrotate(rows, upstream, projected, gain):
        turned = upstream * cosine[rows, :] - swap_halves(upstream) * sine[rows, :]
        return rms_backward(projected, gain, turned)

    gain_rows = jnp.zeros((1, HEAD_DIM), f32)
    d_key[...] = jnp.zeros_like(d_key)
    d_value[...] = jnp.zeros_like(d_value)
    for part in range(rows_all // chunk):
        rows = pl.ds(part * chunk, chunk)
        seen = (part + 1) * chunk
        token = part * chunk + lax.broadcasted_iota(jnp.int32, (chunk, 1), 0)
        source = lax.broadcasted_iota(jnp.int32, (1, seen), 1)
        visible = (source >= begin_of(token)) & (source <= token)
        for g in range(2):
            lanes = pl.ds(g * HEAD_DIM, HEAD_DIM)
            scores = mm_nt(query[rows, lanes], key[0:seen, :]) * scale
            weights = jnp.where(visible, jnp.exp(scores - proj[rows, 3 * HEAD_DIM + g : 3 * HEAD_DIM + g + 1]), 0.0)
            d_probs = mm_nt(d_att[rows, lanes], value[0:seen, :])
            inner = jnp.sum(weights * d_probs, axis=-1, keepdims=True)
            d_scores = (weights * (d_probs - inner)).astype(low)
            back, gain_part = unrotate(
                rows, mm(d_scores, key[0:seen, :]) * scale, proj[rows, lanes], query_gain[...].astype(f32)
            )
            d_qkv[rows, lanes] = back.astype(low)
            gain_rows = gain_rows + jnp.sum(gain_part, axis=0, keepdims=True)
            d_key[0:seen, :] += mm_tn(d_scores, query[rows, lanes])
            d_value[0:seen, :] += mm_tn(weights.astype(low), d_att[rows, lanes])
        if part == 1:
            sum_gate.y_gather(sum_gate.piece(), local_sems.at[3])
            scatter_left.send_other()
            scatter_left.send_own()
        if part == 3:
            sum_up.y_gather(sum_up.piece(), local_sems.at[3])
    d_qkv[:, 3 * HEAD_DIM :] = d_value[...].astype(low)

    keep_gain(2 * gain_slots, gain_rows)
    lanes = pl.ds(2 * HEAD_DIM, HEAD_DIM)
    back, gain_part = unrotate(pl.ds(0, rows_all), d_key[...] * scale, proj[:, lanes], key_gain[...].astype(f32))
    d_qkv[:, lanes] = back.astype(low)
    keep_gain(2 * gain_slots + 1, jnp.sum(gain_part, axis=0, keepdims=True))

    head_landed = cot_all.at[:, pl.ds(0, 6 * HEAD_DIM)]
    sum_attn = RepSum(
        place,
        sems(RepSum.COPIES),
        pair.at[pl.ds(pl.multiple_of(place.core * rows_all, BLOCK), rows_all)],
        pair.at[pl.ds(pl.multiple_of((1 - place.core) * rows_all, BLOCK), rows_all)],
        head_core_landed,
        [head_landed.at[pl.ds(e * BLOCK, BLOCK)] for e in range(2)],
        [head_landed.at[pl.ds((1 + e) * 2 * BLOCK, 2 * BLOCK)] for e in range(2)],
        head_landed.at[pl.ds(6 * BLOCK, BLOCK)],
        attn_grads,
        BLOCK,
        16,
    )

    load.wait()

    @pl.loop(0, width // 256)
    def _(i):
        cols = pl.ds(pl.multiple_of(i * 256, 256), 256)
        from_first = mm_tn(part_back[:, cols], d_qkv[...]).astype(low)
        from_branch = mm_tn(branch[:, cols], attended[...]).astype(low)
        for piece in range(16):
            rows = pl.ds(pl.multiple_of(piece * BLOCK + i * 16, 16), 16)
            pair[rows, 0 : 4 * HEAD_DIM] = from_first[piece * 16 : piece * 16 + 16, :]
            pair[rows, 4 * HEAD_DIM :] = from_branch[piece * 16 : piece * 16 + 16, :]

    gather_branch.finish()
    for by in ((1, 0), (0, 1), (0, 3)):
        pl.semaphore_signal(landing_free, inc=1, device_id=place.dev(*by), device_id_type=MESH)
    sum_attn.core_send()
    sum_gate.x_gather()
    scatter_left.step_one()
    scatter_first = Scatter(
        place,
        part_back,
        Slots(branch, 0, HALF),
        Slots(branch, 4 * HALF, 32),
        Slots(branch, 7 * HALF, HALF),
        branch.at[pl.ds(13 * HALF, HALF)],
        *sems(Scatter.COPIES),
    )

    def load_heads():
        copy = pltpu.make_async_copy(head_core_landed, d_up, local_sems.at[3])
        copy.start()
        copy.wait()
        return d_up

    def into_first(dy):
        rows = pl.ds(place.line(dy), LINE)

        for side in range(2):

            @pl.loop(0, rows_all // 256)
            def _(i):
                feats = pl.ds(pl.multiple_of(i * 256, 256), 256)
                cols = pl.ds(pl.multiple_of(side * rows_all + i * 256, 256), 256)
                part_back[rows, cols] = mm_nt(
                    d_qkv[rows, :], w_attn[feats, pl.ds(side * attn_cols, 4 * HEAD_DIM)]
                ).astype(low)

    into_first(1)
    pl.semaphore_wait(landing_free, 3)
    scatter_first.send_other()
    into_first(0)
    scatter_first.send_own()
    for by in ((0, 1, 0), (0, 3, 0), (1, 0, 0)):
        pl.semaphore_signal(
            heads_free, inc=1, device_id=place.rep_dev(*by), device_id_type=MESH
        )
    sum_down.y_gather(sum_down.piece(), local_sems.at[3])
    pl.semaphore_wait(heads_free, 3)
    sum_attn.x_first(load_heads)
    scatter_first.step_one()
    scatter_left.step_two()
    sum_attn.x_second()
    sum_gate.x_forward()
    sum_up.x_gather()
    scatter_left.step_three()
    scatter_first.step_two()
    scatter_first.step_three()
    sum_attn.y_send()
    gain_rows = None
    for half in (1, 0):
        rows = pl.ds(half * HALF, HALF)
        d_first = scatter_first.total(half)
        back, gain_part = rms_backward(tokens[rows, :].astype(f32), gain_one[...], d_first)
        grad_tokens[rows, :] += back
        gain_part = jnp.sum(gain_part, axis=0, keepdims=True)
        gain_rows = gain_part if gain_rows is None else gain_rows + gain_part
    keep_gain(0, gain_rows)

    gain_net = Net(*sems(9))
    stages = (
        [place.dev(0, d) for d in (1, 2, 3)],
        [place.dev(1, 0)],
        [place.rep_dev(1, 0, 0)],
        [place.rep_dev(0, 0, 1)],
        [place.rep_dev(0, d, 0) for d in (1, 2, 3)],
    )

    def gain_send(stage):
        for i, dev in enumerate(stages[stage]):
            dst = gain_landed.at[3 * stage + i]
            gain_net.send(f"{stage}.{i}", gain_sums.at[stage], dst, dev, dst)

    def gain_add(stage):
        total = gain_sums[stage]
        for i in range(len(stages[stage])):
            gain_net.wait(f"{stage}.{i}")
            total = total + gain_landed[3 * stage + i]
        gain_sums[stage + 1] = total

    gain_send(0)
    piece = sum_attn.piece()
    swap_net = Net(*sems(7))
    for dy in range(2):
        for dz in range(4):
            if dy or dz:
                to = place.block(dy, dz)
                src = piece.at[pl.ds(pl.multiple_of(to * 16, 16), 16)]
                dst = swapped.at[pl.ds(pl.multiple_of(place.shard * 16, 16), 16)]
                here = place.block(-dy, -dz)
                here = swapped.at[pl.ds(pl.multiple_of(here * 16, 16), 16)]
                swap_net.send(f"{dy}{dz}", src, dst, place.dev(dy, dz), here)
    own_rows = pl.ds(pl.multiple_of(place.shard * 16, 16), 16)
    swapped[own_rows, :] = piece[own_rows, :]
    sum_up.x_forward()
    sum_down.x_gather()
    gain_add(0)
    gain_send(1)
    swap_net.finish()
    kv = 8 * HEAD_DIM
    for j in range(8):
        rows = pl.ds(j * 16, 16)
        at = 0
        for begin, size in ((0, 2), (2, 1), (3, 1), (4, 2)):
            assembled[:, at + j * size * HEAD_DIM : at + (j + 1) * size * HEAD_DIM] = swapped[
                rows, begin * HEAD_DIM : (begin + size) * HEAD_DIM
            ]
            at += size * kv
    sum_attn.y_gather(assembled, local_sems.at[3])
    gain_add(1)
    gain_send(2)
    scatter_right.send_other()
    scatter_right.send_own()
    for half in (0, 1):
        rows = pl.ds(half * HALF, HALF)
        result[rows, left] = resid[rows, left] + scatter_left.total(half)
    sum_gate.x_last()
    sum_attn.x_gather()
    gain_add(2)
    gain_send(3)
    sum_down.x_forward()
    scatter_right.step_one()
    sum_up.x_last()
    sum_attn.x_forward()
    gain_add(3)
    gain_send(4)
    scatter_right.step_two()
    sum_down.x_last()
    scatter_right.step_three()
    sum_attn.x_last()
    gain_add(4)
    for half in (0, 1):
        rows = pl.ds(half * HALF, HALF)
        result[rows, right] = resid[rows, right] + scatter_right.total(half)
    gains[...] = gain_sums[5]

    for one in (scatter_first, scatter_left, scatter_right):
        one.finish()
    for one in sums:
        one.finish()
    sum_attn.finish()
    gain_net.finish()


def layer_call(lengths, *args):
    tokens, cotangent = args[:2]
    width = tokens.shape[1]
    hid = args[-1].shape[0]
    rows = 8 * BLOCK
    vmem = pl.BlockSpec(memory_space=pltpu.VMEM)
    smem = pl.BlockSpec(memory_space=pltpu.SMEM)
    hbm = pl.BlockSpec(memory_space=pltpu.HBM)
    copies = 4 * Gather.COPIES + 5 * Scatter.COPIES + 4 * RepSum.COPIES + 9 + 7 + 7
    gain_shape = (2 * width // HEAD_DIM + 8, HEAD_DIM)
    return pl.pallas_call(
        functools.partial(layer_kernel, 1.0 / math.sqrt(HEAD_DIM)),
        name="layer",
        out_shape=[
            jax.ShapeDtypeStruct((BLOCK, width), f32),
            jax.ShapeDtypeStruct((BLOCK, width), f32),
            jax.ShapeDtypeStruct(gain_shape, f32),
            jax.ShapeDtypeStruct((256, 3 * width), low),
            jax.ShapeDtypeStruct((3, hid, width), low),
            jax.ShapeDtypeStruct((3, hid // 2, width), low),
            jax.ShapeDtypeStruct((rows, 6 * HEAD_DIM), low),
            jax.ShapeDtypeStruct((rows, width), low),
            jax.ShapeDtypeStruct((2 * rows, 6 * HEAD_DIM), low),
            jax.ShapeDtypeStruct((rows, 6 * HEAD_DIM), low),
        ],
        in_specs=[smem] + [vmem] * 6 + [hbm] * 7,
        out_specs=[vmem] * 3 + [hbm] * 7,
        scratch_shapes=[
            pltpu.VMEM((BLOCK, width), f32),
            pltpu.VMEM((2, width), f32),
            pltpu.VMEM((8, 16, 256), low),
            pltpu.VMEM((rows, 4 * HEAD_DIM), f32),
            pltpu.VMEM((rows, HEAD_DIM), f32),
            pltpu.VMEM((rows, HEAD_DIM), f32),
            pltpu.VMEM((rows, width), low),
            pltpu.VMEM((rows, width), low),
            pltpu.VMEM((rows, width), low),
            pltpu.VMEM((hid, width), low),
            pltpu.VMEM((hid, width), low),
            pltpu.VMEM((hid, width), low),
            pltpu.VMEM((2 * rows, hid), low),
            pltpu.VMEM((rows, hid), low),
            pltpu.VMEM((rows, width), low),
            pltpu.VMEM((rows, width), low),
            pltpu.VMEM((rows, 2 * HEAD_DIM), low),
            pltpu.VMEM((rows, HEAD_DIM), f32),
            pltpu.VMEM((rows, HEAD_DIM), f32),
            pltpu.VMEM((rows, 4 * HEAD_DIM), low),
            pltpu.VMEM((hid // 2, width), low),
        ]
        + Scatter.scratch(width)
        + [
            pltpu.VMEM((BLOCK, 6 * HEAD_DIM), low),
            pltpu.VMEM((16, 3 * width), low),
            pltpu.VMEM((6,) + gain_shape, f32),
            pltpu.VMEM((15,) + gain_shape, f32),
            pltpu.SemaphoreType.DMA((2, 2, 11)),
            pltpu.SemaphoreType.DMA((3, 2)),
            pltpu.SemaphoreType.REGULAR,
            pltpu.SemaphoreType.REGULAR,
            pltpu.SemaphoreType.REGULAR,
            pltpu.SemaphoreType.DMA((6,)),
            pltpu.SemaphoreType.DMA((copies,)),
            pltpu.SemaphoreType.DMA((copies,)),
        ],
        compiler_params=pltpu.CompilerParams(
            collective_id=1, has_side_effects=True, vmem_limit_bytes=60 << 20
        ),
        cost_estimate=pl.CostEstimate(
            flops=36_000_000_000, bytes_accessed=60_000_000, transcendentals=4_000_000
        ),
    )(lengths, *args)


def widen_kernel(ffn, attn, *refs):
    outs, (narrow, narrow_attn, wide, wide_attn, load_sems, store_sems, attn_sems) = refs[:7], refs[7:]
    slots, tall, _ = wide.shape
    count = narrow.shape[0] // tall
    per = count // 3
    loads = []
    for i in range(count):
        rows = pl.ds(i % per * tall, tall)
        loads.append(
            pltpu.make_async_copy(
                ffn.at[i // per, rows], narrow.at[pl.ds(i * tall, tall)], load_sems.at[i]
            )
        )
    first = pltpu.make_async_copy(attn, narrow_attn, load_sems.at[count])
    first.start()
    for load in loads:
        load.start()
    first.wait()
    wide_attn[...] = narrow_attn[...].astype(f32)
    stores, at = [], 0
    for j, ref in enumerate(outs[3:]):
        size = ref.shape[1]
        stores.append(
            pltpu.make_async_copy(wide_attn.at[:, pl.ds(at, size)], ref, attn_sems.at[j])
        )
        stores[-1].start()
        at += size
    busy = [None] * slots
    for i in range(count):
        loads[i].wait()
        slot = i % slots
        if busy[slot] is not None:
            busy[slot].wait()
        wide[slot] = narrow[pl.ds(i * tall, tall), :].astype(f32)
        rows = pl.ds(i % per * tall, tall)
        busy[slot] = pltpu.make_async_copy(wide.at[slot], outs[i // per].at[rows], store_sems.at[slot])
        busy[slot].start()
    for copy in busy + stores:
        copy.wait()


def widen(ffn, attn):
    _, hid, width = ffn.shape
    rows = attn.shape[0]
    tall, slots = hid // 3, 6
    sizes = (width, width // 2, width // 2, width)
    hbm = pl.BlockSpec(memory_space=pltpu.HBM)
    return pl.pallas_call(
        widen_kernel,
        name="widen",
        out_shape=[jax.ShapeDtypeStruct((hid, width), f32)] * 3
        + [jax.ShapeDtypeStruct((rows, size), f32) for size in sizes],
        in_specs=[hbm, hbm],
        out_specs=[hbm] * 7,
        scratch_shapes=[
            pltpu.VMEM((3 * hid, width), low),
            pltpu.VMEM((rows, 3 * width), low),
            pltpu.VMEM((slots, tall, width), f32),
            pltpu.VMEM((rows, 3 * width), f32),
            pltpu.SemaphoreType.DMA((10,)),
            pltpu.SemaphoreType.DMA((slots,)),
            pltpu.SemaphoreType.DMA((4,)),
        ],
        compiler_params=pltpu.CompilerParams(vmem_limit_bytes=60 << 20),
    )(ffn, attn)


def per_device(
    tokens,
    cotangent,
    lengths,
    attn_gain,
    mlp_gain,
    query_gain,
    key_gain,
    w_query,
    w_key,
    w_value,
    w_out,
    w_gate,
    w_up,
    w_down,
):
    width = tokens.shape[1]
    shards = lax.axis_size("shard")
    feat = width // shards
    my_shard = lax.axis_index("shard")
    half = np.arange(HEAD_DIM, dtype=np.float64) % (HEAD_DIM // 2)
    frequency = jnp.asarray(theta_base ** (-half * (2.0 / HEAD_DIM)), f32)[None]
    result, grad_tokens, gains, attn_grads, ffn_grads, *_ = layer_call(
        lengths,
        tokens,
        cotangent,
        jnp.concatenate([attn_gain[None], mlp_gain[None], jnp.zeros((14, feat), low)]),
        query_gain[None],
        key_gain[None],
        frequency,
        w_query,
        w_key,
        w_value,
        w_out,
        w_gate,
        w_up,
        w_down,
    )
    grad_gate, grad_up, grad_down, grad_query, grad_key, grad_value, grad_out = widen(
        ffn_grads, attn_grads
    )
    gains = gains.reshape(-1)
    head_piece = HEAD_DIM // shards
    gains_first = lax.dynamic_slice_in_dim(gains, my_shard * feat, feat, 0)
    gains_second = lax.dynamic_slice_in_dim(gains, width + my_shard * feat, feat, 0)
    gains_query = lax.dynamic_slice_in_dim(gains, 2 * width + my_shard * head_piece, head_piece, 0)
    gains_key = lax.dynamic_slice_in_dim(
        gains, 2 * width + HEAD_DIM + my_shard * head_piece, head_piece, 0
    )
    return (
        result,
        grad_tokens,
        grad_query,
        grad_key,
        grad_value,
        grad_out,
        grad_gate,
        grad_up,
        grad_down,
        gains_first,
        gains_second,
        gains_query,
        gains_key,
    )


def solution(mesh):
    spread = P(("rep", "shard"), None)
    rowed = P("shard", None)
    return jax.shard_map(
        per_device,
        mesh=mesh,
        in_specs=(spread, spread, P("rep", None), P("shard"), P("shard"), P(), P()) + (rowed,) * 7,
        out_specs=(spread, spread) + (rowed,) * 7 + (P("shard"),) * 4,
        check_vma=False,
    )
```

```python
import functools
import math

import jax
import jax.numpy as jnp
import numpy as np
from jax import lax
from jax.experimental import pallas as pl
from jax.experimental.pallas import tpu as pltpu
from jax.sharding import PartitionSpec as P

HEADS = 16
KV_HEADS = 8
HEAD_DIM = 128

epsilon = 1e-06
theta_base = 1000000.0
masked_value = -1e30


MESH = pl.DeviceIdType.MESH
BLOCK = 128
HALF = 64
LINE = 512
low = jnp.bfloat16
f32 = jnp.float32


def mm(left, right):
    return lax.dot_general(left, right, (((1,), (0,)), ((), ())), preferred_element_type=f32)


def mm_nt(left, right):
    return lax.dot_general(left, right, (((1,), (1,)), ((), ())), preferred_element_type=f32)


def mm_tn(left, right):
    return lax.dot_general(left, right, (((0,), (0,)), ((), ())), preferred_element_type=f32)


class Place:
    def __init__(self):
        self.rep = lax.axis_index("rep")
        self.shard = lax.axis_index("shard")
        self.yl, self.z = self.shard // 4, self.shard % 4
        self.yh, self.x, self.core = self.rep // 8, (self.rep // 2) % 4, self.rep % 2

    def block(self, dy, dz):
        return ((self.yl + dy + 2) % 2) * 4 + (self.z + dz + 8) % 4

    def dev(self, dy, dz):
        return (self.rep, self.block(dy, dz))

    def x_at(self, dx):
        return (self.x + dx + 8) % 4

    def rep_dev(self, dyh, dx, dcore):
        rep = ((self.yh + dyh) % 2) * 8 + self.x_at(dx) * 2 + (self.core + dcore) % 2
        return (rep, self.shard)

    def rows(self, dy, dz, start=0, count=BLOCK):
        return pl.ds(pl.multiple_of(self.block(dy, dz) * BLOCK + start, 32), count)

    def line(self, dy):
        return pl.multiple_of(((self.yl + dy + 2) % 2) * LINE, LINE)

    def shard_peers(self):
        return [self.dev(dy, dz) for dy in range(2) for dz in range(4) if dy or dz]

    def rep_peers(self):
        return [
            self.rep_dev(*by) for by in ((0, 0, 1), (0, 1, 0), (0, 2, 0), (0, 3, 0), (1, 0, 0))
        ]

    def greet(self):
        barrier = pltpu.get_barrier_semaphore()
        peers = self.shard_peers() + self.rep_peers()
        for peer in peers:
            pl.semaphore_signal(barrier, inc=1, device_id=peer, device_id_type=MESH)
        pl.semaphore_wait(barrier, len(peers))


class Net:
    def __init__(self, send_sems, recv_sems):
        self.send_sems, self.recv_sems = send_sems, recv_sems
        self.started, self.coming = [], {}

    def send(self, tag, src, dst, dev, here):
        k = len(self.started)
        copy = pltpu.make_async_remote_copy(
            src_ref=src,
            dst_ref=dst,
            send_sem=self.send_sems.at[k],
            recv_sem=self.recv_sems.at[k],
            device_id=dev,
            device_id_type=MESH,
        )
        copy.start()
        self.started.append(copy)
        self.coming[tag] = (k, here, dev)

    def wait(self, tag):
        k, here, dev = self.coming.pop(tag)
        pltpu.make_async_remote_copy(
            src_ref=here,
            dst_ref=here,
            send_sem=self.send_sems.at[k],
            recv_sem=self.recv_sems.at[k],
            device_id=dev,
            device_id_type=MESH,
        ).wait_recv()

    def finish(self):
        for tag in list(self.coming):
            self.wait(tag)
        for copy in self.started:
            copy.wait_send()


class Gather:
    COPIES = 18

    def __init__(self, place, buf, send_sems, recv_sems):
        self.place, self.buf = place, buf
        self.net = Net(send_sems, recv_sems)

    def send(self, tag, block, start, count, to):
        rows = self.place.rows(*block, start, count)
        here = self.place.rows(block[0] - to[0], block[1] - to[1], start, count)
        self.net.send(
            tag, self.buf.at[rows], self.buf.at[rows], self.place.dev(*to), self.buf.at[here]
        )

    def start(self):
        self.send("y_up", (0, 0), 0, HALF, (1, 0))
        for d in (1, 3):
            self.send(f"z_low{d}", (0, 0), HALF, HALF, (0, d))
        self.send("y_low", (0, 0), HALF, HALF, (1, 0))

    def step_one(self):
        self.net.wait("y_up")
        for d in (1, 3):
            self.send(f"p_up{d}", (1, 0), 0, HALF, (0, d))

    def step_two(self):
        for e, d in enumerate((1, 3)):
            self.net.wait(f"z_low{d}")
            self.send(f"f_low{d}", (0, -d), HALF + 32 * e, 32, (0, d))
            self.send(f"q_low{d}", (0, -d), HALF, HALF, (1, 0))
        for d in (1, 3):
            self.send(f"z_up{d}", (0, 0), 0, HALF, (0, d))

    def step_three(self):
        for e, d in enumerate((1, 3)):
            self.net.wait(f"p_up{d}")
            self.send(f"f_p{d}", (1, -d), 32 * e, 32, (0, d))
        for e, d in enumerate((1, 3)):
            self.net.wait(f"f_low{d}")
            self.send(f"q_far{d}", (0, -2 * d), HALF + 32 * e, 32, (1, 0))

    def step_four(self):
        for e, d in enumerate((1, 3)):
            self.net.wait(f"z_up{d}")
            self.send(f"f_up{d}", (0, -d), 32 * e, 32, (0, d))

    def own_line(self):
        for d in (1, 3):
            self.net.wait(f"f_up{d}")

    def other_line(self):
        for tag in list(self.net.coming):
            self.net.wait(tag)

    def steps(self):
        return [self.start, self.step_one, self.step_two, self.step_three, self.step_four]

    def finish(self):
        self.net.finish()


class Slots:
    def __init__(self, ref, base, size):
        self.ref, self.base, self.size = ref, base, size

    @property
    def at(self):
        return self

    def __getitem__(self, i):
        i = i if isinstance(i, int) else 2 * i[0] + i[1]
        return self.ref.at[pl.ds(self.base + i * self.size, self.size)]


class Scatter:
    COPIES = 17

    @staticmethod
    def scratch(columns):
        return [
            pltpu.VMEM((4, HALF, columns), low),
            pltpu.VMEM((3, 2, 32, columns), low),
            pltpu.VMEM((3, 2, HALF, columns), low),
            pltpu.VMEM((HALF, columns), low),
        ]

    def __init__(self, place, part, across, near, far, last, send_sems, recv_sems):
        self.place, self.part = place, part
        self.across, self.near, self.far, self.last = across, near, far, last
        self.net = Net(send_sems, recv_sems)

    def add(self, rows, *refs):
        total = self.part[rows, :].astype(f32)
        for ref in refs:
            total = total + ref[...].astype(f32)
        self.part[rows, :] = total.astype(low)

    def first(self, kind):
        dy, start = ((1, 0), (0, 0), (0, HALF))[kind]
        for e, d in enumerate((1, 3)):
            src = self.part.at[self.place.rows(dy, 2, start + 32 * e, 32)]
            dst = self.near.at[kind, e]
            self.net.send(f"near{kind}{e}", src, dst, self.place.dev(0, d), dst)

    def second(self, kind):
        dy, start = ((1, 0), (0, 0), (0, HALF))[kind]
        for e, d in enumerate((1, 3)):
            self.net.wait(f"near{kind}{e}")
            self.add(self.place.rows(dy, d, start + 32 * e, 32), self.near.at[kind, e])
            src = self.part.at[self.place.rows(dy, d, start, HALF)]
            dst = self.far.at[kind, e]
            self.net.send(f"far{kind}{e}", src, dst, self.place.dev(0, d), dst)

    def send_other(self):
        for d in (2, 1, 3, 0):
            src = self.part.at[self.place.rows(1, d, HALF, HALF)]
            dst = self.across.at[d]
            self.net.send(f"across{d}", src, dst, self.place.dev(1, 0), dst)
        self.first(0)

    def send_own(self):
        self.first(1)

    def step_one(self):
        self.net.wait("across2")
        self.add(self.place.rows(0, 2, HALF, HALF), self.across.at[2])
        self.first(2)
        self.second(0)
        self.second(1)

    def step_two(self):
        for d in (1, 3):
            self.net.wait(f"across{d}")
            self.add(self.place.rows(0, d, HALF, HALF), self.across.at[d])
        self.second(2)

    def step_three(self):
        for e in range(2):
            self.net.wait(f"far0{e}")
        rows = self.place.rows(1, 0, 0, HALF)
        self.add(rows, self.far.at[0, 0], self.far.at[0, 1])
        self.net.send("last", self.part.at[rows], self.last, self.place.dev(1, 0), self.last)

    def total(self, half):
        if half == 0:
            tags, extra, kind = ("far10", "far11", "last"), self.last, 1
        else:
            tags, extra, kind = ("far20", "far21", "across0"), self.across.at[0], 2
        for tag in tags:
            self.net.wait(tag)
        out = self.part[self.place.rows(0, 0, half * HALF, HALF), :].astype(f32)
        for ref in (self.far.at[kind, 0], self.far.at[kind, 1], extra):
            out = out + ref[...].astype(f32)
        return out

    def finish(self):
        self.net.finish()


def add_rows(into, start, count, *refs):
    step = 64 if count % 64 == 0 else 48

    @pl.loop(0, count // step)
    def _(i):
        at = pl.multiple_of(i * step, 16)
        rows = pl.ds(pl.multiple_of(start + at, 16), step)
        total = into[rows, :].astype(f32)
        for ref in refs:
            total = total + ref[pl.ds(at, step), :].astype(f32)
        into[rows, :] = total.astype(low)


class RepSum:
    COPIES = 15

    def __init__(self, place, sems, own, other, landed, near, far, cross, out, unit, out_unit):
        self.place, self.net = place, Net(*sems)
        self.own, self.other, self.landed = own, other, landed
        self.near, self.far, self.cross = near, far, cross
        self.out, self.unit, self.out_unit = out, unit, out_unit

    def chunk(self, dx, start=0, count=None):
        at = self.place.x_at(dx) * 2 * self.unit + start
        return pl.ds(pl.multiple_of(at, 16), 2 * self.unit if count is None else count)

    def out_rows(self, dcore, dx, start=0, count=None):
        core = (self.place.core + dcore) % 2
        at = (core * 8 + self.place.x_at(dx) * 2 + start) * self.out_unit
        count = (2 if count is None else count) * self.out_unit
        return self.out.at[pl.ds(pl.multiple_of(at, 16), count)]

    def core_send(self):
        self.net.send("core", self.other, self.landed, self.place.rep_dev(0, 0, 1), self.landed)

    def x_first(self, load=None):
        self.net.wait("core")
        add_rows(self.own, 0, 8 * self.unit, self.landed if load is None else load())
        for e, d in enumerate((1, 3)):
            src = self.own.at[self.chunk(2, e * self.unit, self.unit)]
            dst = self.near[e]
            self.net.send(f"near{e}", src, dst, self.place.rep_dev(0, d, 0), dst)

    def x_second(self):
        for e, d in enumerate((1, 3)):
            self.net.wait(f"near{e}")
            add_rows(self.own, self.place.x_at(d) * 2 * self.unit + e * self.unit, self.unit, self.near[e])
            dst = self.far[e]
            self.net.send(
                f"far{e}", self.own.at[self.chunk(d)], dst, self.place.rep_dev(0, d, 0), dst
            )

    def y_send(self):
        for e in range(2):
            self.net.wait(f"far{e}")
        add_rows(self.own, self.place.x * 2 * self.unit, 2 * self.unit, *self.far)
        src = self.own.at[self.chunk(0, (1 - self.place.yh) * self.unit, self.unit)]
        self.net.send("cross", src, self.cross, self.place.rep_dev(1, 0, 0), self.cross)

    def piece(self):
        self.net.wait("cross")
        at = (self.place.x * 2 + self.place.yh) * self.unit
        add_rows(self.own, at, self.unit, self.cross)
        return self.own.at[pl.ds(pl.multiple_of(at, 16), self.unit)]

    def y_gather(self, piece, sem):
        mine = self.out_rows(0, 0, self.place.yh, 1)
        copy = pltpu.make_async_copy(piece, mine, sem)
        copy.start()
        self.net.send(
            "y", piece, mine, self.place.rep_dev(1, 0, 0), self.out_rows(0, 0, 1 - self.place.yh, 1)
        )
        copy.wait()

    def to_core(self, dx):
        rows = self.out_rows(0, dx)
        self.net.send(
            f"core{dx}", rows, rows, self.place.rep_dev(0, 0, 1), self.out_rows(1, dx)
        )

    def x_gather(self):
        self.net.wait("y")
        rows = self.out_rows(0, 0)
        for d in (1, 3):
            self.net.send(f"x{d}", rows, rows, self.place.rep_dev(0, d, 0), self.out_rows(0, -d))
        self.to_core(0)

    def x_forward(self):
        for e, d in enumerate((1, 3)):
            self.net.wait(f"x{d}")
            rows = self.out_rows(0, -d, e, 1)
            self.net.send(
                f"xx{d}", rows, rows, self.place.rep_dev(0, d, 0), self.out_rows(0, -2 * d, e, 1)
            )
            self.to_core(-d)

    def x_last(self):
        for d in (1, 3):
            self.net.wait(f"xx{d}")
        self.to_core(2)

    def finish(self):
        self.net.finish()


def rms_backward(value, gain, upstream):
    root = lax.rsqrt(jnp.mean(value * value, axis=-1, keepdims=True) + epsilon)
    pulled = upstream * gain
    back = root * pulled - value * (root * root * root) * jnp.mean(
        pulled * value, axis=-1, keepdims=True
    )
    return back, upstream * (value * root)


def swap_halves(value):
    return pltpu.roll(value, HEAD_DIM // 2, 1)


def layer_kernel(
    scale,
    lengths,
    tokens,
    cotangent,
    gain_shard,
    query_gain,
    key_gain,
    frequency,
    w_query_hbm,
    w_key_hbm,
    w_value_hbm,
    w_out_hbm,
    w_gate_hbm,
    w_up_hbm,
    w_down_hbm,
    result,
    grad_tokens,
    gains,
    attn_grads,
    ffn_grads,
    core_landed,
    head_core_landed,
    first_hbm,
    w_attn_hbm,
    heads_hbm,
    resid,
    gain_rows_all,
    gain_blocks,
    proj,
    cosine,
    sine,
    second,
    cot_all,
    branch,
    w_gate,
    w_up,
    w_down,
    pair,
    d_up,
    part_out,
    part_back,
    d_att,
    d_key,
    d_value,
    d_qkv,
    staged,
    across,
    near,
    far,
    last,
    swapped,
    assembled,
    gain_sums,
    gain_landed,
    swap_sems,
    sibling_sems,
    free_sem,
    landing_free,
    heads_free,
    local_sems,
    send_sems,
    recv_sems,
):
    place = Place()
    hidden = pair.at[pl.ds(0, 8 * BLOCK)]
    d_gate = pair.at[pl.ds(8 * BLOCK, 8 * BLOCK)]
    rows_all = 8 * BLOCK
    hid = w_gate.shape[0]
    width = second.shape[1]

    loads = [
        pltpu.make_async_copy(src, dst, local_sems.at[i])
        for i, (src, dst) in enumerate(
            ((w_gate_hbm, w_gate), (w_up_hbm, w_up), (w_down_hbm, w_down))
        )
    ]
    for load in loads:
        load.start()

    used = [0]

    def sems(count):
        at = used[0]
        used[0] += count
        return send_sems.at[pl.ds(at, count)], recv_sems.at[pl.ds(at, count)]

    own = place.rows(0, 0)
    gain_one = gain_rows_all.at[pl.ds(0, 1)]
    gain_two = gain_rows_all.at[pl.ds(1, 1)]
    cot_all[own, :] = cotangent[...].astype(low)
    branch[own, :] = tokens[...]
    feat = w_query_hbm.shape[0]
    gain_blocks[place.shard] = gain_shard[...]
    place.greet()

    gain_share = Net(*sems(7))
    peers = [(dy, dz) for dy in range(2) for dz in range(4) if dy or dz]
    for by in peers:
        gain_share.send(
            str(by),
            gain_blocks.at[place.shard],
            gain_blocks.at[place.shard],
            place.dev(*by),
            gain_blocks.at[place.block(-by[0], -by[1])],
        )
    qkv_parts = (
        (w_query_hbm, 0, 2 * HEAD_DIM),
        (w_key_hbm, 2 * HEAD_DIM, HEAD_DIM),
        (w_value_hbm, 3 * HEAD_DIM, HEAD_DIM),
    )
    out_parts = ((w_out_hbm, 4 * HEAD_DIM, 2 * HEAD_DIM),)
    few = feat // 8
    qkv_span = pl.ds(0, 4 * HEAD_DIM)
    out_span = pl.ds(4 * HEAD_DIM, 2 * HEAD_DIM)

    def swap_rows(block, dx=0, count=1):
        first = place.x_at(dx) if count == 1 else 0
        at = block * feat + (place.core * 4 + first) * few
        return pl.ds(pl.multiple_of(at, few), count * few)

    def swap_copy(src, dst, kind, i, dev):
        return pltpu.make_async_remote_copy(
            src_ref=src,
            dst_ref=dst,
            send_sem=swap_sems.at[0, kind, i],
            recv_sem=swap_sems.at[1, kind, i],
            device_id=dev,
            device_id_type=MESH,
        )

    def swap_send(parts, kind):
        own_rows = pl.ds(pl.multiple_of((place.core * 4 + place.x) * few, few), few)
        for i, by in enumerate(peers):
            to = place.block(*by)
            for whole, begin, size in parts:
                cols = pl.ds(pl.multiple_of(to * size, HEAD_DIM), size)
                src = whole.at[own_rows, cols]
                dst = pair.at[swap_rows(place.shard), pl.ds(begin, size)]
                swap_copy(src, dst, kind, i, place.dev(*by)).start()
        for whole, begin, size in parts:
            cols = pl.ds(pl.multiple_of(place.shard * size, HEAD_DIM), size)
            rows = pl.ds(pl.multiple_of(place.shard * feat, feat), feat)
            copy = pltpu.make_async_copy(
                whole.at[:, cols], pair.at[rows, pl.ds(begin, size)], sibling_sems.at[2, kind]
            )
            copy.start()

    def share_copy(ref, kind, i):
        return swap_copy(
            ref, ref, kind, 7 + i, place.rep_dev(0, i + 1, 0) if i < 3 else place.rep_dev(0, 0, 1)
        )

    def swap_relay(span, kind):
        for i, by in enumerate(peers):
            here = pair.at[swap_rows(place.block(-by[0], -by[1])), span]
            swap_copy(here, here, kind, i, place.dev(*by)).wait_recv()
            for d in range(3):
                share_copy(here, kind, d).start()

    def swap_share(span, kind):
        for d in range(3):
            share_copy(pair.at[pl.ds(0, 7 * few), span], kind, d).wait_recv()
        for by in peers:
            here = pair.at[swap_rows(place.block(-by[0], -by[1]), 0, 4), span]
            share_copy(here, kind, 3).start()

    def swap_done(span, kind):
        rows = pl.ds(pl.multiple_of(place.shard * feat, feat), feat)
        mine = pair.at[rows, span]
        pltpu.make_async_copy(mine, mine, sibling_sems.at[2, kind]).wait()
        share_copy(pair.at[pl.ds(0, 7 * 4 * few), span], kind, 3).wait()
        for d in range(3):
            share_copy(pair.at[pl.ds(0, 7 * few), span], kind, d).wait_send()
        for i, by in enumerate(peers):
            here = pair.at[swap_rows(place.block(-by[0], -by[1])), span]
            swap_copy(here, here, kind, i, place.dev(*by)).wait_send()

    swap_send(qkv_parts, 0)
    gather_tokens = Gather(place, branch, *sems(Gather.COPIES))
    gather_tokens.start()

    start_one = lengths[0, 0]
    start_two = lengths[0, 0] + lengths[0, 1]

    def begin_of(token):
        return jnp.where(
            token >= start_two, start_two, jnp.where(token >= start_one, start_one, 0)
        )

    token = lax.broadcasted_iota(jnp.int32, (rows_all, 1), 0)
    angles = (token - begin_of(token)).astype(f32) * frequency[...]
    lane = lax.broadcasted_iota(jnp.int32, (1, HEAD_DIM), 1)
    cosine[...] = jnp.cos(angles)
    sine[...] = jnp.sin(angles) * jnp.where(lane < HEAD_DIM // 2, -1.0, 1.0)

    gather_tokens.step_one()
    swap_relay(qkv_span, 0)
    gather_tokens.step_two()
    gain_share.finish()
    for j in range(8):
        span = slice(j * feat, (j + 1) * feat)
        gain_rows_all[0:2, span] = gain_blocks[j, 0:2, :].astype(f32)
    gather_tokens.step_three()
    swap_share(qkv_span, 0)
    swap_send(out_parts, 1)
    gather_tokens.step_four()

    def normalise(dy):
        line = place.line(dy)

        @pl.loop(0, LINE // BLOCK)
        def _(i):
            rows = pl.ds(pl.multiple_of(line + i * BLOCK, BLOCK), BLOCK)
            x = branch[rows, :].astype(f32)
            root = lax.rsqrt(jnp.mean(x * x, axis=-1, keepdims=True) + epsilon)
            second[rows, :] = (x * root * gain_one[...]).astype(low)

    gather_tokens.own_line()
    normalise(0)
    gather_tokens.other_line()
    normalise(1)
    gather_tokens.finish()
    keep_first = pltpu.make_async_copy(second, first_hbm, local_sems.at[3])
    keep_first.start()
    gather_cot = Gather(place, cot_all, *sems(Gather.COPIES))
    gather_cot.start()
    swap_relay(out_span, 1)
    swap_done(qkv_span, 0)
    heads = d_up
    gains_of_head = (query_gain, query_gain, key_gain)

    @pl.loop(0, rows_all // 256)
    def _(i):
        rows = pl.ds(pl.multiple_of(i * 256, 256), 256)
        proj[rows, :] = mm(second[rows, :], pair[:, 0 : 4 * HEAD_DIM])
        for g in range(3):
            lanes = pl.ds(g * HEAD_DIM, HEAD_DIM)
            u = proj[rows, lanes]
            root = lax.rsqrt(jnp.mean(u * u, axis=-1, keepdims=True) + epsilon)
            u = u * root * gains_of_head[g][...].astype(f32)
            heads[rows, lanes] = (u * cosine[rows, :] + swap_halves(u) * sine[rows, :]).astype(low)
        lanes = pl.ds(3 * HEAD_DIM, HEAD_DIM)
        heads[rows, lanes] = proj[rows, lanes].astype(low)

    swap_share(out_span, 1)
    chunk = 256
    for part in range(rows_all // chunk):
        rows = pl.ds(part * chunk, chunk)
        seen = (part + 1) * chunk
        token = part * chunk + lax.broadcasted_iota(jnp.int32, (chunk, 1), 0)
        source = lax.broadcasted_iota(jnp.int32, (1, seen), 1)
        visible = (source >= begin_of(token)) & (source <= token)
        for g in range(2):
            lanes = pl.ds(g * HEAD_DIM, HEAD_DIM)
            scores = mm_nt(heads[rows, lanes], heads[0:seen, 2 * HEAD_DIM : 3 * HEAD_DIM]) * scale
            scores = jnp.where(visible, scores, masked_value)
            top = jnp.max(scores, axis=-1, keepdims=True)
            raised = jnp.exp(scores - top)
            total = jnp.sum(raised, axis=-1, keepdims=True)
            probs = (raised * (1.0 / total)).astype(low)
            proj[rows, 3 * HEAD_DIM + g : 3 * HEAD_DIM + g + 1] = jnp.log(total) + top
            heads[rows, pl.ds((4 + g) * HEAD_DIM, HEAD_DIM)] = mm(
                probs, heads[0:seen, 3 * HEAD_DIM : 4 * HEAD_DIM]
            ).astype(low)
        if part == 2:
            gather_cot.step_one()
    keep_heads = pltpu.make_async_copy(heads, heads_hbm, local_sems.at[4])
    keep_heads.start()
    swap_done(out_span, 1)
    keep_weights = pltpu.make_async_copy(pair, w_attn_hbm, local_sems.at[5])
    keep_weights.start()
    landing = (across, near, far, last)
    scatter_attn = Scatter(place, part_back, *landing, *sems(Scatter.COPIES))

    def attention_out(dy):
        rows = pl.ds(place.line(dy), LINE)

        @pl.loop(0, width // 256)
        def _(i):
            cols = pl.ds(pl.multiple_of(i * 256, 256), 256)
            part_back[rows, cols] = mm_nt(
                heads[rows, 4 * HEAD_DIM :], pair[cols, 4 * HEAD_DIM :]
            ).astype(low)

    attention_out(1)
    keep_first.wait()
    scatter_attn.send_other()
    attention_out(0)
    scatter_attn.send_own()
    scatter_attn.step_one()
    scatter_attn.step_two()
    scatter_attn.step_three()
    keep_heads.wait()
    keep_weights.wait()
    for half in (1, 0):
        rows = pl.ds(half * HALF, HALF)
        x = tokens[rows, :].astype(f32) + scatter_attn.total(half)
        resid[rows, :] = x
        root = lax.rsqrt(jnp.mean(x * x, axis=-1, keepdims=True) + epsilon)
        at = place.rows(0, 0, half * HALF, HALF)
        second[at, :] = (x * root * gain_two[...]).astype(low)
    scatter_attn.finish()
    gather_second = Gather(place, second, *sems(Gather.COPIES))
    gather_branch = Gather(place, branch, *sems(Gather.COPIES))
    left, right = (pl.ds(side * (width // 2), width // 2) for side in range(2))
    scatter_left, scatter_right = (
        Scatter(
            place,
            part_out.at[:, cols],
            across.at[:, :, cols],
            near.at[:, :, :, cols],
            far.at[:, :, :, cols],
            last.at[:, cols],
            *sems(Scatter.COPIES),
        )
        for cols in (left, right)
    )
    scatter_back = Scatter(place, part_back, *landing, *sems(Scatter.COPIES))

    def feed_forward(rows):
        @pl.loop(0, hid // 256)
        def _(i):
            cols = pl.ds(pl.multiple_of(i * 256, 256), 256)
            gate = mm_nt(second[rows, :], w_gate[cols, :])
            up = mm_nt(second[rows, :], w_up[cols, :])
            sigma = 1.0 / (1.0 + jnp.exp(-gate))
            silu = gate * sigma
            hidden[rows, cols] = (silu * up).astype(low)
            d_gate[rows, cols] = (up * sigma * (1.0 + gate * (1.0 - sigma))).astype(low)
            d_up[rows, cols] = silu.astype(low)

    def project_out(dy):
        rows = pl.ds(place.line(dy), LINE)

        @pl.loop(0, width // 512)
        def _(i):
            cols = pl.ds(pl.multiple_of(i * 512, 512), 512)
            part_out[rows, cols] = mm(hidden[rows, :], w_down[:, cols]).astype(low)

    def feed_backward(dy):
        rows = pl.ds(place.line(dy), LINE)

        @pl.loop(0, hid // 256)
        def _(i):
            cols = pl.ds(pl.multiple_of(i * 256, 256), 256)
            d_hidden = mm_nt(cot_all[rows, :], w_down[cols, :])
            d_gate[rows, cols] = (d_hidden * d_gate[rows, cols].astype(f32)).astype(low)
            d_up[rows, cols] = (d_hidden * d_up[rows, cols].astype(f32)).astype(low)

        @pl.loop(0, width // 512)
        def _(i):
            cols = pl.ds(pl.multiple_of(i * 512, 512), 512)
            part_back[rows, cols] = (
                mm(d_gate[rows, :], w_gate[:, cols]) + mm(d_up[rows, :], w_up[:, cols])
            ).astype(low)

    def weight_grad(into, left, right):
        @pl.loop(0, hid // 256)
        def _(i):
            cols = pl.ds(pl.multiple_of(i * 256, 256), 256)
            into[cols, :] = mm_tn(left[:, cols], right[...]).astype(low)

    unit = hid // 16
    sums = []
    for i, whole in enumerate((w_gate, w_up, w_down)):
        base = i * 7 * unit

        def view(start, count, base=base):
            return second.at[pl.ds(base + start * unit, count * unit)]

        sums.append(
            RepSum(
                place,
                sems(RepSum.COPIES),
                whole.at[pl.ds(pl.multiple_of(place.core * 8 * unit, 16), 8 * unit)],
                whole.at[pl.ds(pl.multiple_of((1 - place.core) * 8 * unit, 16), 8 * unit)],
                core_landed.at[i],
                [view(0, 1), view(1, 1)],
                [view(2, 2), view(4, 2)],
                view(6, 1),
                ffn_grads.at[i],
                unit,
                unit,
            )
        )
    sum_gate, sum_up, sum_down = sums

    def load_landed(i):
        def load():
            here = staged.at[pl.ds(0, 8 * unit)]
            copy = pltpu.make_async_copy(core_landed.at[i], here, local_sems.at[3])
            copy.start()
            copy.wait()
            return here

        return load

    for step in gather_second.steps():
        step()
    gather_cot.step_two()
    for load in loads:
        load.wait()
    gather_second.own_line()
    gather_cot.step_three()
    feed_forward(pl.ds(place.line(0), LINE))
    gather_second.other_line()
    gather_cot.step_four()
    feed_forward(pl.ds(place.line(1), LINE))
    gather_cot.own_line()
    gather_cot.other_line()
    feed_backward(1)
    scatter_back.send_other()
    feed_backward(0)
    scatter_back.send_own()
    project_out(1)
    project_out(0)
    weight_grad(w_gate, d_gate, second)
    sum_gate.core_send()
    scatter_back.step_one()
    weight_grad(w_up, d_up, second)
    sum_up.core_send()
    gather_second.finish()
    for by in ((0, 1, 0), (0, 3, 0), (1, 0, 0)):
        pl.semaphore_signal(
            free_sem, inc=1, device_id=place.rep_dev(*by), device_id_type=MESH
        )
    scatter_back.step_two()
    weight_grad(w_down, hidden, cot_all)
    sum_down.core_send()
    pl.semaphore_wait(free_sem, 3)
    sum_gate.x_first(load_landed(0))
    sum_up.x_first(load_landed(1))
    gather_cot.finish()
    q_cols = 2 * HEAD_DIM
    query = heads.at[:, pl.ds(0, q_cols)]
    key = heads.at[:, pl.ds(q_cols, HEAD_DIM)]
    value = heads.at[:, pl.ds(q_cols + HEAD_DIM, HEAD_DIM)]
    attended = heads.at[:, pl.ds(q_cols + 2 * HEAD_DIM, q_cols)]
    w_attn = cot_all
    attn_cols = heads.shape[1]
    loads = [
        pltpu.make_async_copy(heads_hbm, heads, local_sems.at[0]),
        pltpu.make_async_copy(
            w_attn_hbm.at[pl.ds(0, rows_all)],
            w_attn.at[:, pl.ds(0, attn_cols)],
            local_sems.at[1],
        ),
        pltpu.make_async_copy(
            w_attn_hbm.at[pl.ds(rows_all, rows_all)],
            w_attn.at[:, pl.ds(attn_cols, attn_cols)],
            local_sems.at[2],
        ),
    ]
    for load in loads:
        load.start()
    scatter_back.step_three()
    gain_rows = None
    for half in (1, 0):
        rows = pl.ds(half * HALF, HALF)
        d_second = scatter_back.total(half)
        back, gain_part = rms_backward(resid[rows, :], gain_two[...], d_second)
        grad_tokens[rows, :] = cotangent[rows, :] + back
        gain_part = jnp.sum(gain_part, axis=0, keepdims=True)
        gain_rows = gain_part if gain_rows is None else gain_rows + gain_part
    gain_sums[0] = jnp.zeros_like(gain_sums[0])

    def keep_gain(first_row, value):
        for i in range(value.shape[1] // HEAD_DIM):
            gain_sums[0, first_row + i : first_row + i + 1, :] = value[
                :, i * HEAD_DIM : (i + 1) * HEAD_DIM
            ]

    gain_slots = width // HEAD_DIM
    keep_gain(gain_slots, gain_rows)
    branch[own, :] = grad_tokens[...].astype(low)
    gather_branch.start()
    sum_down.x_first(load_landed(2))
    gather_branch.step_one()
    sum_gate.x_second()
    gather_branch.step_two()
    sum_up.x_second()
    gather_branch.step_three()
    sum_down.x_second()
    sum_gate.y_send()
    gather_branch.step_four()
    sum_up.y_send()
    gather_branch.own_line()
    for load in loads:
        load.wait()

    def into_attention(dy):
        rows = pl.ds(place.line(dy), LINE)
        d_att[rows, :] = (
            mm(branch[rows, 0:rows_all], w_attn[:, 4 * HEAD_DIM : attn_cols])
            + mm(branch[rows, rows_all:], w_attn[:, attn_cols + 4 * HEAD_DIM : 2 * attn_cols])
        ).astype(low)

    into_attention(0)
    gather_branch.other_line()
    into_attention(1)
    sum_down.y_send()
    scatter_back.finish()
    load = pltpu.make_async_copy(first_hbm, part_back, local_sems.at[0])
    load.start()

    def unrotate(rows, upstream, projected, gain):
        turned = upstream * cosine[rows, :] - swap_halves(upstream) * sine[rows, :]
        return rms_backward(projected, gain, turned)

    gain_rows = jnp.zeros((1, HEAD_DIM), f32)
    d_key[...] = jnp.zeros_like(d_key)
    d_value[...] = jnp.zeros_like(d_value)
    for part in range(rows_all // chunk):
        rows = pl.ds(part * chunk, chunk)
        seen = (part + 1) * chunk
        token = part * chunk + lax.broadcasted_iota(jnp.int32, (chunk, 1), 0)
        source = lax.broadcasted_iota(jnp.int32, (1, seen), 1)
        visible = (source >= begin_of(token)) & (source <= token)
        for g in range(2):
            lanes = pl.ds(g * HEAD_DIM, HEAD_DIM)
            scores = mm_nt(query[rows, lanes], key[0:seen, :]) * scale
            weights = jnp.where(visible, jnp.exp(scores - proj[rows, 3 * HEAD_DIM + g : 3 * HEAD_DIM + g + 1]), 0.0)
            d_probs = mm_nt(d_att[rows, lanes], value[0:seen, :])
            inner = jnp.sum(weights * d_probs, axis=-1, keepdims=True)
            d_scores = (weights * (d_probs - inner)).astype(low)
            back, gain_part = unrotate(
                rows, mm(d_scores, key[0:seen, :]) * scale, proj[rows, lanes], query_gain[...].astype(f32)
            )
            d_qkv[rows, lanes] = back.astype(low)
            gain_rows = gain_rows + jnp.sum(gain_part, axis=0, keepdims=True)
            d_key[0:seen, :] += mm_tn(d_scores, query[rows, lanes])
            d_value[0:seen, :] += mm_tn(weights.astype(low), d_att[rows, lanes])
        if part == 1:
            sum_gate.y_gather(sum_gate.piece(), local_sems.at[3])
            scatter_left.send_other()
            scatter_left.send_own()
        if part == 3:
            sum_up.y_gather(sum_up.piece(), local_sems.at[3])
    d_qkv[:, 3 * HEAD_DIM :] = d_value[...].astype(low)

    keep_gain(2 * gain_slots, gain_rows)
    lanes = pl.ds(2 * HEAD_DIM, HEAD_DIM)
    back, gain_part = unrotate(pl.ds(0, rows_all), d_key[...] * scale, proj[:, lanes], key_gain[...].astype(f32))
    d_qkv[:, lanes] = back.astype(low)
    keep_gain(2 * gain_slots + 1, jnp.sum(gain_part, axis=0, keepdims=True))

    head_landed = cot_all.at[:, pl.ds(0, 6 * HEAD_DIM)]
    sum_attn = RepSum(
        place,
        sems(RepSum.COPIES),
        pair.at[pl.ds(pl.multiple_of(place.core * rows_all, BLOCK), rows_all)],
        pair.at[pl.ds(pl.multiple_of((1 - place.core) * rows_all, BLOCK), rows_all)],
        head_core_landed,
        [head_landed.at[pl.ds(e * BLOCK, BLOCK)] for e in range(2)],
        [head_landed.at[pl.ds((1 + e) * 2 * BLOCK, 2 * BLOCK)] for e in range(2)],
        head_landed.at[pl.ds(6 * BLOCK, BLOCK)],
        attn_grads,
        BLOCK,
        16,
    )

    load.wait()

    @pl.loop(0, width // 256)
    def _(i):
        cols = pl.ds(pl.multiple_of(i * 256, 256), 256)
        from_first = mm_tn(part_back[:, cols], d_qkv[...]).astype(low)
        from_branch = mm_tn(branch[:, cols], attended[...]).astype(low)
        for piece in range(16):
            rows = pl.ds(pl.multiple_of(piece * BLOCK + i * 16, 16), 16)
            pair[rows, 0 : 4 * HEAD_DIM] = from_first[piece * 16 : piece * 16 + 16, :]
            pair[rows, 4 * HEAD_DIM :] = from_branch[piece * 16 : piece * 16 + 16, :]

    gather_branch.finish()
    for by in ((1, 0), (0, 1), (0, 3)):
        pl.semaphore_signal(landing_free, inc=1, device_id=place.dev(*by), device_id_type=MESH)
    sum_attn.core_send()
    sum_gate.x_gather()
    scatter_left.step_one()
    scatter_first = Scatter(
        place,
        part_back,
        Slots(branch, 0, HALF),
        Slots(branch, 4 * HALF, 32),
        Slots(branch, 7 * HALF, HALF),
        branch.at[pl.ds(13 * HALF, HALF)],
        *sems(Scatter.COPIES),
    )

    def load_heads():
        copy = pltpu.make_async_copy(head_core_landed, d_up, local_sems.at[3])
        copy.start()
        copy.wait()
        return d_up

    def into_first(dy):
        rows = pl.ds(place.line(dy), LINE)

        for side in range(2):

            @pl.loop(0, rows_all // 256)
            def _(i):
                feats = pl.ds(pl.multiple_of(i * 256, 256), 256)
                cols = pl.ds(pl.multiple_of(side * rows_all + i * 256, 256), 256)
                part_back[rows, cols] = mm_nt(
                    d_qkv[rows, :], w_attn[feats, pl.ds(side * attn_cols, 4 * HEAD_DIM)]
                ).astype(low)

    into_first(1)
    pl.semaphore_wait(landing_free, 3)
    scatter_first.send_other()
    into_first(0)
    scatter_first.send_own()
    for by in ((0, 1, 0), (0, 3, 0), (1, 0, 0)):
        pl.semaphore_signal(
            heads_free, inc=1, device_id=place.rep_dev(*by), device_id_type=MESH
        )
    sum_down.y_gather(sum_down.piece(), local_sems.at[3])
    pl.semaphore_wait(heads_free, 3)
    sum_attn.x_first(load_heads)
    scatter_first.step_one()
    scatter_left.step_two()
    sum_attn.x_second()
    sum_gate.x_forward()
    sum_up.x_gather()
    scatter_left.step_three()
    scatter_first.step_two()
    scatter_first.step_three()
    sum_attn.y_send()
    piece = sum_attn.piece()
    swap_net = Net(*sems(7))
    for dy in range(2):
        for dz in range(4):
            if dy or dz:
                to = place.block(dy, dz)
                src = piece.at[pl.ds(pl.multiple_of(to * 16, 16), 16)]
                dst = swapped.at[pl.ds(pl.multiple_of(place.shard * 16, 16), 16)]
                here = place.block(-dy, -dz)
                here = swapped.at[pl.ds(pl.multiple_of(here * 16, 16), 16)]
                swap_net.send(f"{dy}{dz}", src, dst, place.dev(dy, dz), here)
    own_rows = pl.ds(pl.multiple_of(place.shard * 16, 16), 16)
    swapped[own_rows, :] = piece[own_rows, :]
    sum_up.x_forward()
    sum_down.x_gather()
    swap_net.finish()
    kv = 8 * HEAD_DIM
    for j in range(8):
        rows = pl.ds(j * 16, 16)
        at = 0
        for begin, size in ((0, 2), (2, 1), (3, 1), (4, 2)):
            assembled[:, at + j * size * HEAD_DIM : at + (j + 1) * size * HEAD_DIM] = swapped[
                rows, begin * HEAD_DIM : (begin + size) * HEAD_DIM
            ]
            at += size * kv
    sum_attn.y_gather(assembled, local_sems.at[3])
    gain_rows = None
    for half in (1, 0):
        rows = pl.ds(half * HALF, HALF)
        d_first = scatter_first.total(half)
        back, gain_part = rms_backward(tokens[rows, :].astype(f32), gain_one[...], d_first)
        grad_tokens[rows, :] += back
        gain_part = jnp.sum(gain_part, axis=0, keepdims=True)
        gain_rows = gain_part if gain_rows is None else gain_rows + gain_part
    keep_gain(0, gain_rows)

    gain_net = Net(*sems(9))
    stages = (
        [place.dev(0, d) for d in (1, 2, 3)],
        [place.dev(1, 0)],
        [place.rep_dev(1, 0, 0)],
        [place.rep_dev(0, 0, 1)],
        [place.rep_dev(0, d, 0) for d in (1, 2, 3)],
    )

    def gain_send(stage):
        for i, dev in enumerate(stages[stage]):
            dst = gain_landed.at[3 * stage + i]
            gain_net.send(f"{stage}.{i}", gain_sums.at[stage], dst, dev, dst)

    def gain_add(stage):
        total = gain_sums[stage]
        for i in range(len(stages[stage])):
            gain_net.wait(f"{stage}.{i}")
            total = total + gain_landed[3 * stage + i]
        gain_sums[stage + 1] = total

    gain_send(0)
    gain_add(0)
    gain_send(1)
    sum_attn.x_gather()
    gain_add(1)
    gain_send(2)
    scatter_right.send_other()
    scatter_right.send_own()
    for half in (0, 1):
        rows = pl.ds(half * HALF, HALF)
        result[rows, left] = resid[rows, left] + scatter_left.total(half)
    sum_gate.x_last()
    gain_add(2)
    gain_send(3)
    sum_down.x_forward()
    scatter_right.step_one()
    sum_up.x_last()
    sum_attn.x_forward()
    gain_add(3)
    gain_send(4)
    scatter_right.step_two()
    sum_down.x_last()
    scatter_right.step_three()
    sum_attn.x_last()
    gain_add(4)
    for half in (0, 1):
        rows = pl.ds(half * HALF, HALF)
        result[rows, right] = resid[rows, right] + scatter_right.total(half)
    gains[...] = gain_sums[5]

    for one in (scatter_first, scatter_left, scatter_right):
        one.finish()
    for one in sums:
        one.finish()
    sum_attn.finish()
    gain_net.finish()


def layer_call(lengths, *args):
    tokens, cotangent = args[:2]
    width = tokens.shape[1]
    hid = args[-1].shape[0]
    rows = 8 * BLOCK
    vmem = pl.BlockSpec(memory_space=pltpu.VMEM)
    smem = pl.BlockSpec(memory_space=pltpu.SMEM)
    hbm = pl.BlockSpec(memory_space=pltpu.HBM)
    copies = 4 * Gather.COPIES + 5 * Scatter.COPIES + 4 * RepSum.COPIES + 9 + 7 + 7
    gain_shape = (2 * width // HEAD_DIM + 8, HEAD_DIM)
    return pl.pallas_call(
        functools.partial(layer_kernel, 1.0 / math.sqrt(HEAD_DIM)),
        name="layer",
        out_shape=[
            jax.ShapeDtypeStruct((BLOCK, width), f32),
            jax.ShapeDtypeStruct((BLOCK, width), f32),
            jax.ShapeDtypeStruct(gain_shape, f32),
            jax.ShapeDtypeStruct((256, 3 * width), low),
            jax.ShapeDtypeStruct((3, hid, width), low),
            jax.ShapeDtypeStruct((3, hid // 2, width), low),
            jax.ShapeDtypeStruct((rows, 6 * HEAD_DIM), low),
            jax.ShapeDtypeStruct((rows, width), low),
            jax.ShapeDtypeStruct((2 * rows, 6 * HEAD_DIM), low),
            jax.ShapeDtypeStruct((rows, 6 * HEAD_DIM), low),
        ],
        in_specs=[smem] + [vmem] * 6 + [hbm] * 7,
        out_specs=[vmem] * 3 + [hbm] * 7,
        scratch_shapes=[
            pltpu.VMEM((BLOCK, width), f32),
            pltpu.VMEM((2, width), f32),
            pltpu.VMEM((8, 16, 256), low),
            pltpu.VMEM((rows, 4 * HEAD_DIM), f32),
            pltpu.VMEM((rows, HEAD_DIM), f32),
            pltpu.VMEM((rows, HEAD_DIM), f32),
            pltpu.VMEM((rows, width), low),
            pltpu.VMEM((rows, width), low),
            pltpu.VMEM((rows, width), low),
            pltpu.VMEM((hid, width), low),
            pltpu.VMEM((hid, width), low),
            pltpu.VMEM((hid, width), low),
            pltpu.VMEM((2 * rows, hid), low),
            pltpu.VMEM((rows, hid), low),
            pltpu.VMEM((rows, width), low),
            pltpu.VMEM((rows, width), low),
            pltpu.VMEM((rows, 2 * HEAD_DIM), low),
            pltpu.VMEM((rows, HEAD_DIM), f32),
            pltpu.VMEM((rows, HEAD_DIM), f32),
            pltpu.VMEM((rows, 4 * HEAD_DIM), low),
            pltpu.VMEM((hid // 2, width), low),
        ]
        + Scatter.scratch(width)
        + [
            pltpu.VMEM((BLOCK, 6 * HEAD_DIM), low),
            pltpu.VMEM((16, 3 * width), low),
            pltpu.VMEM((6,) + gain_shape, f32),
            pltpu.VMEM((15,) + gain_shape, f32),
            pltpu.SemaphoreType.DMA((2, 2, 11)),
            pltpu.SemaphoreType.DMA((3, 2)),
            pltpu.SemaphoreType.REGULAR,
            pltpu.SemaphoreType.REGULAR,
            pltpu.SemaphoreType.REGULAR,
            pltpu.SemaphoreType.DMA((6,)),
            pltpu.SemaphoreType.DMA((copies,)),
            pltpu.SemaphoreType.DMA((copies,)),
        ],
        compiler_params=pltpu.CompilerParams(
            collective_id=1, has_side_effects=True, vmem_limit_bytes=60 << 20
        ),
        cost_estimate=pl.CostEstimate(
            flops=36_000_000_000, bytes_accessed=60_000_000, transcendentals=4_000_000
        ),
    )(lengths, *args)


def widen_kernel(ffn, attn, *refs):
    outs, (narrow, narrow_attn, wide, wide_attn, load_sems, store_sems, attn_sems) = refs[:7], refs[7:]
    slots, tall, _ = wide.shape
    count = narrow.shape[0] // tall
    per = count // 3
    loads = []
    for i in range(count):
        rows = pl.ds(i % per * tall, tall)
        loads.append(
            pltpu.make_async_copy(
                ffn.at[i // per, rows], narrow.at[pl.ds(i * tall, tall)], load_sems.at[i]
            )
        )
    first = pltpu.make_async_copy(attn, narrow_attn, load_sems.at[count])
    first.start()
    for load in loads:
        load.start()
    first.wait()
    wide_attn[...] = narrow_attn[...].astype(f32)
    stores, at = [], 0
    for j, ref in enumerate(outs[3:]):
        size = ref.shape[1]
        stores.append(
            pltpu.make_async_copy(wide_attn.at[:, pl.ds(at, size)], ref, attn_sems.at[j])
        )
        stores[-1].start()
        at += size
    busy = [None] * slots
    for i in range(count):
        loads[i].wait()
        slot = i % slots
        if busy[slot] is not None:
            busy[slot].wait()
        wide[slot] = narrow[pl.ds(i * tall, tall), :].astype(f32)
        rows = pl.ds(i % per * tall, tall)
        busy[slot] = pltpu.make_async_copy(wide.at[slot], outs[i // per].at[rows], store_sems.at[slot])
        busy[slot].start()
    for copy in busy + stores:
        copy.wait()


def widen(ffn, attn):
    _, hid, width = ffn.shape
    rows = attn.shape[0]
    tall, slots = hid // 3, 6
    sizes = (width, width // 2, width // 2, width)
    hbm = pl.BlockSpec(memory_space=pltpu.HBM)
    return pl.pallas_call(
        widen_kernel,
        name="widen",
        out_shape=[jax.ShapeDtypeStruct((hid, width), f32)] * 3
        + [jax.ShapeDtypeStruct((rows, size), f32) for size in sizes],
        in_specs=[hbm, hbm],
        out_specs=[hbm] * 7,
        scratch_shapes=[
            pltpu.VMEM((3 * hid, width), low),
            pltpu.VMEM((rows, 3 * width), low),
            pltpu.VMEM((slots, tall, width), f32),
            pltpu.VMEM((rows, 3 * width), f32),
            pltpu.SemaphoreType.DMA((10,)),
            pltpu.SemaphoreType.DMA((slots,)),
            pltpu.SemaphoreType.DMA((4,)),
        ],
        compiler_params=pltpu.CompilerParams(vmem_limit_bytes=60 << 20),
    )(ffn, attn)


def per_device(
    tokens,
    cotangent,
    lengths,
    attn_gain,
    mlp_gain,
    query_gain,
    key_gain,
    w_query,
    w_key,
    w_value,
    w_out,
    w_gate,
    w_up,
    w_down,
):
    width = tokens.shape[1]
    shards = lax.axis_size("shard")
    feat = width // shards
    my_shard = lax.axis_index("shard")
    half = np.arange(HEAD_DIM, dtype=np.float64) % (HEAD_DIM // 2)
    frequency = jnp.asarray(theta_base ** (-half * (2.0 / HEAD_DIM)), f32)[None]
    result, grad_tokens, gains, attn_grads, ffn_grads, *_ = layer_call(
        lengths,
        tokens,
        cotangent,
        jnp.concatenate([attn_gain[None], mlp_gain[None], jnp.zeros((14, feat), low)]),
        query_gain[None],
        key_gain[None],
        frequency,
        w_query,
        w_key,
        w_value,
        w_out,
        w_gate,
        w_up,
        w_down,
    )
    grad_gate, grad_up, grad_down, grad_query, grad_key, grad_value, grad_out = widen(
        ffn_grads, attn_grads
    )
    gains = gains.reshape(-1)
    head_piece = HEAD_DIM // shards
    gains_first = lax.dynamic_slice_in_dim(gains, my_shard * feat, feat, 0)
    gains_second = lax.dynamic_slice_in_dim(gains, width + my_shard * feat, feat, 0)
    gains_query = lax.dynamic_slice_in_dim(gains, 2 * width + my_shard * head_piece, head_piece, 0)
    gains_key = lax.dynamic_slice_in_dim(
        gains, 2 * width + HEAD_DIM + my_shard * head_piece, head_piece, 0
    )
    return (
        result,
        grad_tokens,
        grad_query,
        grad_key,
        grad_value,
        grad_out,
        grad_gate,
        grad_up,
        grad_down,
        gains_first,
        gains_second,
        gains_query,
        gains_key,
    )


def solution(mesh):
    spread = P(("rep", "shard"), None)
    rowed = P("shard", None)
    return jax.shard_map(
        per_device,
        mesh=mesh,
        in_specs=(spread, spread, P("rep", None), P("shard"), P("shard"), P(), P()) + (rowed,) * 7,
        out_specs=(spread, spread) + (rowed,) * 7 + (P("shard"),) * 4,
        check_vma=False,
    )
```

```python
import functools
import math

import jax
import jax.numpy as jnp
import numpy as np
from jax import lax
from jax.experimental import pallas as pl
from jax.experimental.pallas import tpu as pltpu
from jax.sharding import PartitionSpec as P

HEADS = 16
KV_HEADS = 8
HEAD_DIM = 128

epsilon = 1e-06
theta_base = 1000000.0
masked_value = -1e30


MESH = pl.DeviceIdType.MESH
BLOCK = 128
HALF = 64
LINE = 512
low = jnp.bfloat16
f32 = jnp.float32


def mm(left, right):
    return lax.dot_general(left, right, (((1,), (0,)), ((), ())), preferred_element_type=f32)


def mm_nt(left, right):
    return lax.dot_general(left, right, (((1,), (1,)), ((), ())), preferred_element_type=f32)


def mm_tn(left, right):
    return lax.dot_general(left, right, (((0,), (0,)), ((), ())), preferred_element_type=f32)


class Place:
    def __init__(self):
        self.rep = lax.axis_index("rep")
        self.shard = lax.axis_index("shard")
        self.yl, self.z = self.shard // 4, self.shard % 4
        self.yh, self.x, self.core = self.rep // 8, (self.rep // 2) % 4, self.rep % 2

    def block(self, dy, dz):
        return ((self.yl + dy + 2) % 2) * 4 + (self.z + dz + 8) % 4

    def dev(self, dy, dz):
        return (self.rep, self.block(dy, dz))

    def x_at(self, dx):
        return (self.x + dx + 8) % 4

    def rep_dev(self, dyh, dx, dcore):
        rep = ((self.yh + dyh) % 2) * 8 + self.x_at(dx) * 2 + (self.core + dcore) % 2
        return (rep, self.shard)

    def rows(self, dy, dz, start=0, count=BLOCK):
        return pl.ds(pl.multiple_of(self.block(dy, dz) * BLOCK + start, 32), count)

    def line(self, dy):
        return pl.multiple_of(((self.yl + dy + 2) % 2) * LINE, LINE)

    def shard_peers(self):
        return [self.dev(dy, dz) for dy in range(2) for dz in range(4) if dy or dz]

    def rep_peers(self):
        return [
            self.rep_dev(*by) for by in ((0, 0, 1), (0, 1, 0), (0, 2, 0), (0, 3, 0), (1, 0, 0))
        ]

    def greet(self):
        barrier = pltpu.get_barrier_semaphore()
        peers = self.shard_peers() + self.rep_peers()
        for peer in peers:
            pl.semaphore_signal(barrier, inc=1, device_id=peer, device_id_type=MESH)
        pl.semaphore_wait(barrier, len(peers))


class Net:
    def __init__(self, send_sems, recv_sems):
        self.send_sems, self.recv_sems = send_sems, recv_sems
        self.started, self.coming = [], {}

    def send(self, tag, src, dst, dev, here):
        k = len(self.started)
        copy = pltpu.make_async_remote_copy(
            src_ref=src,
            dst_ref=dst,
            send_sem=self.send_sems.at[k],
            recv_sem=self.recv_sems.at[k],
            device_id=dev,
            device_id_type=MESH,
        )
        copy.start()
        self.started.append(copy)
        self.coming[tag] = (k, here, dev)

    def wait(self, tag):
        k, here, dev = self.coming.pop(tag)
        pltpu.make_async_remote_copy(
            src_ref=here,
            dst_ref=here,
            send_sem=self.send_sems.at[k],
            recv_sem=self.recv_sems.at[k],
            device_id=dev,
            device_id_type=MESH,
        ).wait_recv()

    def finish(self):
        for tag in list(self.coming):
            self.wait(tag)
        for copy in self.started:
            copy.wait_send()


class Gather:
    COPIES = 18

    def __init__(self, place, buf, send_sems, recv_sems):
        self.place, self.buf = place, buf
        self.net = Net(send_sems, recv_sems)

    def send(self, tag, block, start, count, to):
        rows = self.place.rows(*block, start, count)
        here = self.place.rows(block[0] - to[0], block[1] - to[1], start, count)
        self.net.send(
            tag, self.buf.at[rows], self.buf.at[rows], self.place.dev(*to), self.buf.at[here]
        )

    def start(self):
        self.send("y_up", (0, 0), 0, HALF, (1, 0))
        for d in (1, 3):
            self.send(f"z_low{d}", (0, 0), HALF, HALF, (0, d))
        self.send("y_low", (0, 0), HALF, HALF, (1, 0))

    def step_one(self):
        self.net.wait("y_up")
        for d in (1, 3):
            self.send(f"p_up{d}", (1, 0), 0, HALF, (0, d))

    def step_two(self):
        for e, d in enumerate((1, 3)):
            self.net.wait(f"z_low{d}")
            self.send(f"f_low{d}", (0, -d), HALF + 32 * e, 32, (0, d))
            self.send(f"q_low{d}", (0, -d), HALF, HALF, (1, 0))
        for d in (1, 3):
            self.send(f"z_up{d}", (0, 0), 0, HALF, (0, d))

    def step_three(self):
        for e, d in enumerate((1, 3)):
            self.net.wait(f"p_up{d}")
            self.send(f"f_p{d}", (1, -d), 32 * e, 32, (0, d))
        for e, d in enumerate((1, 3)):
            self.net.wait(f"f_low{d}")
            self.send(f"q_far{d}", (0, -2 * d), HALF + 32 * e, 32, (1, 0))

    def step_four(self):
        for e, d in enumerate((1, 3)):
            self.net.wait(f"z_up{d}")
            self.send(f"f_up{d}", (0, -d), 32 * e, 32, (0, d))

    def own_line(self):
        for d in (1, 3):
            self.net.wait(f"f_up{d}")

    def other_line(self):
        for tag in list(self.net.coming):
            self.net.wait(tag)

    def steps(self):
        return [self.start, self.step_one, self.step_two, self.step_three, self.step_four]

    def finish(self):
        self.net.finish()


class Slots:
    def __init__(self, ref, base, size):
        self.ref, self.base, self.size = ref, base, size

    @property
    def at(self):
        return self

    def __getitem__(self, i):
        i = i if isinstance(i, int) else 2 * i[0] + i[1]
        return self.ref.at[pl.ds(self.base + i * self.size, self.size)]


class Scatter:
    COPIES = 17

    @staticmethod
    def scratch(columns):
        return [
            pltpu.VMEM((4, HALF, columns), low),
            pltpu.VMEM((3, 2, 32, columns), low),
            pltpu.VMEM((3, 2, HALF, columns), low),
            pltpu.VMEM((HALF, columns), low),
        ]

    def __init__(self, place, part, across, near, far, last, send_sems, recv_sems):
        self.place, self.part = place, part
        self.across, self.near, self.far, self.last = across, near, far, last
        self.net = Net(send_sems, recv_sems)

    def add(self, rows, *refs):
        total = self.part[rows, :].astype(f32)
        for ref in refs:
            total = total + ref[...].astype(f32)
        self.part[rows, :] = total.astype(low)

    def first(self, kind):
        dy, start = ((1, 0), (0, 0), (0, HALF))[kind]
        for e, d in enumerate((1, 3)):
            src = self.part.at[self.place.rows(dy, 2, start + 32 * e, 32)]
            dst = self.near.at[kind, e]
            self.net.send(f"near{kind}{e}", src, dst, self.place.dev(0, d), dst)

    def second(self, kind):
        dy, start = ((1, 0), (0, 0), (0, HALF))[kind]
        for e, d in enumerate((1, 3)):
            self.net.wait(f"near{kind}{e}")
            self.add(self.place.rows(dy, d, start + 32 * e, 32), self.near.at[kind, e])
            src = self.part.at[self.place.rows(dy, d, start, HALF)]
            dst = self.far.at[kind, e]
            self.net.send(f"far{kind}{e}", src, dst, self.place.dev(0, d), dst)

    def send_other(self):
        for d in (2, 1, 3, 0):
            src = self.part.at[self.place.rows(1, d, HALF, HALF)]
            dst = self.across.at[d]
            self.net.send(f"across{d}", src, dst, self.place.dev(1, 0), dst)
        self.first(0)

    def send_own(self):
        self.first(1)

    def step_one(self):
        self.net.wait("across2")
        self.add(self.place.rows(0, 2, HALF, HALF), self.across.at[2])
        self.first(2)
        self.second(0)
        self.second(1)

    def step_two(self):
        for d in (1, 3):
            self.net.wait(f"across{d}")
            self.add(self.place.rows(0, d, HALF, HALF), self.across.at[d])
        self.second(2)

    def step_three(self):
        for e in range(2):
            self.net.wait(f"far0{e}")
        rows = self.place.rows(1, 0, 0, HALF)
        self.add(rows, self.far.at[0, 0], self.far.at[0, 1])
        self.net.send("last", self.part.at[rows], self.last, self.place.dev(1, 0), self.last)

    def total(self, half):
        if half == 0:
            tags, extra, kind = ("far10", "far11", "last"), self.last, 1
        else:
            tags, extra, kind = ("far20", "far21", "across0"), self.across.at[0], 2
        for tag in tags:
            self.net.wait(tag)
        out = self.part[self.place.rows(0, 0, half * HALF, HALF), :].astype(f32)
        for ref in (self.far.at[kind, 0], self.far.at[kind, 1], extra):
            out = out + ref[...].astype(f32)
        return out

    def finish(self):
        self.net.finish()


def add_rows(into, start, count, *refs):
    step = 64 if count % 64 == 0 else 48

    @pl.loop(0, count // step)
    def _(i):
        at = pl.multiple_of(i * step, 16)
        rows = pl.ds(pl.multiple_of(start + at, 16), step)
        total = into[rows, :].astype(f32)
        for ref in refs:
            total = total + ref[pl.ds(at, step), :].astype(f32)
        into[rows, :] = total.astype(low)


class RepSum:
    COPIES = 15

    def __init__(self, place, sems, own, other, landed, near, far, cross, out, unit, out_unit):
        self.place, self.net = place, Net(*sems)
        self.own, self.other, self.landed = own, other, landed
        self.near, self.far, self.cross = near, far, cross
        self.out, self.unit, self.out_unit = out, unit, out_unit

    def chunk(self, dx, start=0, count=None):
        at = self.place.x_at(dx) * 2 * self.unit + start
        return pl.ds(pl.multiple_of(at, 16), 2 * self.unit if count is None else count)

    def out_rows(self, dcore, dx, start=0, count=None):
        core = (self.place.core + dcore) % 2
        at = (core * 8 + self.place.x_at(dx) * 2 + start) * self.out_unit
        count = (2 if count is None else count) * self.out_unit
        return self.out.at[pl.ds(pl.multiple_of(at, 16), count)]

    def core_send(self):
        self.net.send("core", self.other, self.landed, self.place.rep_dev(0, 0, 1), self.landed)

    def x_first(self, load=None):
        self.net.wait("core")
        add_rows(self.own, 0, 8 * self.unit, self.landed if load is None else load())
        for e, d in enumerate((1, 3)):
            src = self.own.at[self.chunk(2, e * self.unit, self.unit)]
            dst = self.near[e]
            self.net.send(f"near{e}", src, dst, self.place.rep_dev(0, d, 0), dst)

    def x_second(self):
        for e, d in enumerate((1, 3)):
            self.net.wait(f"near{e}")
            add_rows(self.own, self.place.x_at(d) * 2 * self.unit + e * self.unit, self.unit, self.near[e])
            dst = self.far[e]
            self.net.send(
                f"far{e}", self.own.at[self.chunk(d)], dst, self.place.rep_dev(0, d, 0), dst
            )

    def y_send(self):
        for e in range(2):
            self.net.wait(f"far{e}")
        add_rows(self.own, self.place.x * 2 * self.unit, 2 * self.unit, *self.far)
        src = self.own.at[self.chunk(0, (1 - self.place.yh) * self.unit, self.unit)]
        self.net.send("cross", src, self.cross, self.place.rep_dev(1, 0, 0), self.cross)

    def piece(self):
        self.net.wait("cross")
        at = (self.place.x * 2 + self.place.yh) * self.unit
        add_rows(self.own, at, self.unit, self.cross)
        return self.own.at[pl.ds(pl.multiple_of(at, 16), self.unit)]

    def y_gather(self, piece, sem):
        mine = self.out_rows(0, 0, self.place.yh, 1)
        copy = pltpu.make_async_copy(piece, mine, sem)
        copy.start()
        self.net.send(
            "y", piece, mine, self.place.rep_dev(1, 0, 0), self.out_rows(0, 0, 1 - self.place.yh, 1)
        )
        copy.wait()

    def to_core(self, dx):
        rows = self.out_rows(0, dx)
        self.net.send(
            f"core{dx}", rows, rows, self.place.rep_dev(0, 0, 1), self.out_rows(1, dx)
        )

    def x_gather(self):
        self.net.wait("y")
        rows = self.out_rows(0, 0)
        for d in (1, 3):
            self.net.send(f"x{d}", rows, rows, self.place.rep_dev(0, d, 0), self.out_rows(0, -d))
        self.to_core(0)

    def x_forward(self):
        for e, d in enumerate((1, 3)):
            self.net.wait(f"x{d}")
            rows = self.out_rows(0, -d, e, 1)
            self.net.send(
                f"xx{d}", rows, rows, self.place.rep_dev(0, d, 0), self.out_rows(0, -2 * d, e, 1)
            )
            self.to_core(-d)

    def x_last(self):
        for d in (1, 3):
            self.net.wait(f"xx{d}")
        self.to_core(2)

    def finish(self):
        self.net.finish()


def rms_backward(value, gain, upstream):
    root = lax.rsqrt(jnp.mean(value * value, axis=-1, keepdims=True) + epsilon)
    pulled = upstream * gain
    back = root * pulled - value * (root * root * root) * jnp.mean(
        pulled * value, axis=-1, keepdims=True
    )
    return back, upstream * (value * root)


def swap_halves(value):
    return pltpu.roll(value, HEAD_DIM // 2, 1)


def layer_kernel(
    scale,
    lengths,
    tokens,
    cotangent,
    gain_shard,
    query_gain,
    key_gain,
    frequency,
    w_query_hbm,
    w_key_hbm,
    w_value_hbm,
    w_out_hbm,
    w_gate_hbm,
    w_up_hbm,
    w_down_hbm,
    result,
    grad_tokens,
    gains,
    attn_grads,
    ffn_grads,
    core_landed,
    head_core_landed,
    first_hbm,
    w_attn_hbm,
    heads_hbm,
    resid,
    gain_rows_all,
    gain_blocks,
    proj,
    cosine,
    sine,
    second,
    cot_all,
    branch,
    w_gate,
    w_up,
    w_down,
    pair,
    d_up,
    part_out,
    part_back,
    d_att,
    d_key,
    d_value,
    d_qkv,
    staged,
    across,
    near,
    far,
    last,
    swapped,
    assembled,
    gain_sums,
    gain_landed,
    swap_sems,
    sibling_sems,
    free_sem,
    landing_free,
    heads_free,
    local_sems,
    send_sems,
    recv_sems,
):
    place = Place()
    hidden = pair.at[pl.ds(0, 8 * BLOCK)]
    d_gate = pair.at[pl.ds(8 * BLOCK, 8 * BLOCK)]
    rows_all = 8 * BLOCK
    hid = w_gate.shape[0]
    width = second.shape[1]

    loads = [
        pltpu.make_async_copy(src, dst, local_sems.at[i])
        for i, (src, dst) in enumerate(
            ((w_gate_hbm, w_gate), (w_up_hbm, w_up), (w_down_hbm, w_down))
        )
    ]
    for load in loads:
        load.start()

    used = [0]

    def sems(count):
        at = used[0]
        used[0] += count
        return send_sems.at[pl.ds(at, count)], recv_sems.at[pl.ds(at, count)]

    own = place.rows(0, 0)
    gain_one = gain_rows_all.at[pl.ds(0, 1)]
    gain_two = gain_rows_all.at[pl.ds(1, 1)]
    cot_all[own, :] = cotangent[...].astype(low)
    branch[own, :] = tokens[...]
    feat = w_query_hbm.shape[0]
    gain_blocks[place.shard] = gain_shard[...]
    place.greet()

    gain_share = Net(*sems(7))
    peers = [(dy, dz) for dy in range(2) for dz in range(4) if dy or dz]
    for by in peers:
        gain_share.send(
            str(by),
            gain_blocks.at[place.shard],
            gain_blocks.at[place.shard],
            place.dev(*by),
            gain_blocks.at[place.block(-by[0], -by[1])],
        )
    qkv_parts = (
        (w_query_hbm, 0, 2 * HEAD_DIM),
        (w_key_hbm, 2 * HEAD_DIM, HEAD_DIM),
        (w_value_hbm, 3 * HEAD_DIM, HEAD_DIM),
    )
    out_parts = ((w_out_hbm, 4 * HEAD_DIM, 2 * HEAD_DIM),)
    few = feat // 8
    qkv_span = pl.ds(0, 4 * HEAD_DIM)
    out_span = pl.ds(4 * HEAD_DIM, 2 * HEAD_DIM)

    def swap_rows(block, dx=0, count=1):
        first = place.x_at(dx) if count == 1 else 0
        at = block * feat + (place.core * 4 + first) * few
        return pl.ds(pl.multiple_of(at, few), count * few)

    def swap_copy(src, dst, kind, i, dev):
        return pltpu.make_async_remote_copy(
            src_ref=src,
            dst_ref=dst,
            send_sem=swap_sems.at[0, kind, i],
            recv_sem=swap_sems.at[1, kind, i],
            device_id=dev,
            device_id_type=MESH,
        )

    def swap_send(parts, kind):
        own_rows = pl.ds(pl.multiple_of((place.core * 4 + place.x) * few, few), few)
        for i, by in enumerate(peers):
            to = place.block(*by)
            for whole, begin, size in parts:
                cols = pl.ds(pl.multiple_of(to * size, HEAD_DIM), size)
                src = whole.at[own_rows, cols]
                dst = pair.at[swap_rows(place.shard), pl.ds(begin, size)]
                swap_copy(src, dst, kind, i, place.dev(*by)).start()
        for whole, begin, size in parts:
            cols = pl.ds(pl.multiple_of(place.shard * size, HEAD_DIM), size)
            rows = pl.ds(pl.multiple_of(place.shard * feat, feat), feat)
            copy = pltpu.make_async_copy(
                whole.at[:, cols], pair.at[rows, pl.ds(begin, size)], sibling_sems.at[2, kind]
            )
            copy.start()

    def share_copy(ref, kind, i):
        return swap_copy(
            ref, ref, kind, 7 + i, place.rep_dev(0, i + 1, 0) if i < 3 else place.rep_dev(0, 0, 1)
        )

    def swap_relay(span, kind):
        for i, by in enumerate(peers):
            here = pair.at[swap_rows(place.block(-by[0], -by[1])), span]
            swap_copy(here, here, kind, i, place.dev(*by)).wait_recv()
            for d in range(3):
                share_copy(here, kind, d).start()

    def swap_share(span, kind):
        for d in range(3):
            share_copy(pair.at[pl.ds(0, 7 * few), span], kind, d).wait_recv()
        for by in peers:
            here = pair.at[swap_rows(place.block(-by[0], -by[1]), 0, 4), span]
            share_copy(here, kind, 3).start()

    def swap_done(span, kind):
        rows = pl.ds(pl.multiple_of(place.shard * feat, feat), feat)
        mine = pair.at[rows, span]
        pltpu.make_async_copy(mine, mine, sibling_sems.at[2, kind]).wait()
        share_copy(pair.at[pl.ds(0, 7 * 4 * few), span], kind, 3).wait()
        for d in range(3):
            share_copy(pair.at[pl.ds(0, 7 * few), span], kind, d).wait_send()
        for i, by in enumerate(peers):
            here = pair.at[swap_rows(place.block(-by[0], -by[1])), span]
            swap_copy(here, here, kind, i, place.dev(*by)).wait_send()

    swap_send(qkv_parts, 0)
    gather_tokens = Gather(place, branch, *sems(Gather.COPIES))
    gather_tokens.start()

    start_one = lengths[0, 0]
    start_two = lengths[0, 0] + lengths[0, 1]

    def begin_of(token):
        return jnp.where(
            token >= start_two, start_two, jnp.where(token >= start_one, start_one, 0)
        )

    token = lax.broadcasted_iota(jnp.int32, (rows_all, 1), 0)
    angles = (token - begin_of(token)).astype(f32) * frequency[...]
    lane = lax.broadcasted_iota(jnp.int32, (1, HEAD_DIM), 1)
    cosine[...] = jnp.cos(angles)
    sine[...] = jnp.sin(angles) * jnp.where(lane < HEAD_DIM // 2, -1.0, 1.0)

    gather_tokens.step_one()
    swap_relay(qkv_span, 0)
    gather_tokens.step_two()
    gain_share.finish()
    for j in range(8):
        span = slice(j * feat, (j + 1) * feat)
        gain_rows_all[0:2, span] = gain_blocks[j, 0:2, :].astype(f32)
    gather_tokens.step_three()
    swap_share(qkv_span, 0)
    swap_send(out_parts, 1)
    gather_tokens.step_four()

    def normalise(dy):
        line = place.line(dy)

        @pl.loop(0, LINE // BLOCK)
        def _(i):
            rows = pl.ds(pl.multiple_of(line + i * BLOCK, BLOCK), BLOCK)
            x = branch[rows, :].astype(f32)
            root = lax.rsqrt(jnp.mean(x * x, axis=-1, keepdims=True) + epsilon)
            second[rows, :] = (x * root * gain_one[...]).astype(low)

    gather_tokens.own_line()
    normalise(0)
    gather_tokens.other_line()
    normalise(1)
    gather_tokens.finish()
    keep_first = pltpu.make_async_copy(second, first_hbm, local_sems.at[3])
    keep_first.start()
    gather_cot = Gather(place, cot_all, *sems(Gather.COPIES))
    gather_cot.start()
    swap_relay(out_span, 1)
    swap_done(qkv_span, 0)
    heads = d_up
    gains_of_head = (query_gain, query_gain, key_gain)

    @pl.loop(0, rows_all // 256)
    def _(i):
        rows = pl.ds(pl.multiple_of(i * 256, 256), 256)
        proj[rows, :] = mm(second[rows, :], pair[:, 0 : 4 * HEAD_DIM])
        for g in range(3):
            lanes = pl.ds(g * HEAD_DIM, HEAD_DIM)
            u = proj[rows, lanes]
            root = lax.rsqrt(jnp.mean(u * u, axis=-1, keepdims=True) + epsilon)
            u = u * root * gains_of_head[g][...].astype(f32)
            heads[rows, lanes] = (u * cosine[rows, :] + swap_halves(u) * sine[rows, :]).astype(low)
        lanes = pl.ds(3 * HEAD_DIM, HEAD_DIM)
        heads[rows, lanes] = proj[rows, lanes].astype(low)

    swap_share(out_span, 1)
    chunk = 256
    for part in range(rows_all // chunk):
        rows = pl.ds(part * chunk, chunk)
        seen = (part + 1) * chunk
        token = part * chunk + lax.broadcasted_iota(jnp.int32, (chunk, 1), 0)
        source = lax.broadcasted_iota(jnp.int32, (1, seen), 1)
        visible = (source >= begin_of(token)) & (source <= token)
        for g in range(2):
            lanes = pl.ds(g * HEAD_DIM, HEAD_DIM)
            scores = mm_nt(heads[rows, lanes], heads[0:seen, 2 * HEAD_DIM : 3 * HEAD_DIM]) * scale
            scores = jnp.where(visible, scores, masked_value)
            top = jnp.max(scores, axis=-1, keepdims=True)
            raised = jnp.exp(scores - top)
            total = jnp.sum(raised, axis=-1, keepdims=True)
            probs = (raised * (1.0 / total)).astype(low)
            proj[rows, 3 * HEAD_DIM + g : 3 * HEAD_DIM + g + 1] = jnp.log(total) + top
            heads[rows, pl.ds((4 + g) * HEAD_DIM, HEAD_DIM)] = mm(
                probs, heads[0:seen, 3 * HEAD_DIM : 4 * HEAD_DIM]
            ).astype(low)
        if part == 2:
            gather_cot.step_one()
    keep_heads = pltpu.make_async_copy(heads, heads_hbm, local_sems.at[4])
    keep_heads.start()
    swap_done(out_span, 1)
    keep_weights = pltpu.make_async_copy(pair, w_attn_hbm, local_sems.at[5])
    keep_weights.start()
    landing = (across, near, far, last)
    scatter_attn = Scatter(place, part_back, *landing, *sems(Scatter.COPIES))

    def attention_out(dy):
        rows = pl.ds(place.line(dy), LINE)

        @pl.loop(0, width // 256)
        def _(i):
            cols = pl.ds(pl.multiple_of(i * 256, 256), 256)
            part_back[rows, cols] = mm_nt(
                heads[rows, 4 * HEAD_DIM :], pair[cols, 4 * HEAD_DIM :]
            ).astype(low)

    attention_out(1)
    keep_first.wait()
    scatter_attn.send_other()
    attention_out(0)
    scatter_attn.send_own()
    scatter_attn.step_one()
    scatter_attn.step_two()
    scatter_attn.step_three()
    keep_heads.wait()
    keep_weights.wait()
    for half in (1, 0):
        rows = pl.ds(half * HALF, HALF)
        x = tokens[rows, :].astype(f32) + scatter_attn.total(half)
        resid[rows, :] = x
        root = lax.rsqrt(jnp.mean(x * x, axis=-1, keepdims=True) + epsilon)
        at = place.rows(0, 0, half * HALF, HALF)
        second[at, :] = (x * root * gain_two[...]).astype(low)
    scatter_attn.finish()
    gather_second = Gather(place, second, *sems(Gather.COPIES))
    gather_branch = Gather(place, branch, *sems(Gather.COPIES))
    left, right = (pl.ds(side * (width // 2), width // 2) for side in range(2))
    scatter_left, scatter_right = (
        Scatter(
            place,
            part_out.at[:, cols],
            across.at[:, :, cols],
            near.at[:, :, :, cols],
            far.at[:, :, :, cols],
            last.at[:, cols],
            *sems(Scatter.COPIES),
        )
        for cols in (left, right)
    )
    scatter_back = Scatter(place, part_back, *landing, *sems(Scatter.COPIES))

    def feed_forward(rows):
        @pl.loop(0, hid // 256)
        def _(i):
            cols = pl.ds(pl.multiple_of(i * 256, 256), 256)
            gate = mm_nt(second[rows, :], w_gate[cols, :])
            up = mm_nt(second[rows, :], w_up[cols, :])
            sigma = 1.0 / (1.0 + jnp.exp(-gate))
            silu = gate * sigma
            hidden[rows, cols] = (silu * up).astype(low)
            d_gate[rows, cols] = (up * sigma * (1.0 + gate * (1.0 - sigma))).astype(low)
            d_up[rows, cols] = silu.astype(low)

    def project_out(dy):
        rows = pl.ds(place.line(dy), LINE)

        @pl.loop(0, width // 512)
        def _(i):
            cols = pl.ds(pl.multiple_of(i * 512, 512), 512)
            part_out[rows, cols] = mm(hidden[rows, :], w_down[:, cols]).astype(low)

    def feed_backward(dy):
        rows = pl.ds(place.line(dy), LINE)

        @pl.loop(0, hid // 256)
        def _(i):
            cols = pl.ds(pl.multiple_of(i * 256, 256), 256)
            d_hidden = mm_nt(cot_all[rows, :], w_down[cols, :])
            d_gate[rows, cols] = (d_hidden * d_gate[rows, cols].astype(f32)).astype(low)
            d_up[rows, cols] = (d_hidden * d_up[rows, cols].astype(f32)).astype(low)

        @pl.loop(0, width // 512)
        def _(i):
            cols = pl.ds(pl.multiple_of(i * 512, 512), 512)
            part_back[rows, cols] = (
                mm(d_gate[rows, :], w_gate[:, cols]) + mm(d_up[rows, :], w_up[:, cols])
            ).astype(low)

    def weight_grad(into, left, right):
        @pl.loop(0, hid // 256)
        def _(i):
            cols = pl.ds(pl.multiple_of(i * 256, 256), 256)
            into[cols, :] = mm_tn(left[:, cols], right[...]).astype(low)

    unit = hid // 16
    sums = []
    for i, whole in enumerate((w_gate, w_up, w_down)):
        base = i * 7 * unit

        def view(start, count, base=base):
            return second.at[pl.ds(base + start * unit, count * unit)]

        sums.append(
            RepSum(
                place,
                sems(RepSum.COPIES),
                whole.at[pl.ds(pl.multiple_of(place.core * 8 * unit, 16), 8 * unit)],
                whole.at[pl.ds(pl.multiple_of((1 - place.core) * 8 * unit, 16), 8 * unit)],
                core_landed.at[i],
                [view(0, 1), view(1, 1)],
                [view(2, 2), view(4, 2)],
                view(6, 1),
                ffn_grads.at[i],
                unit,
                unit,
            )
        )
    sum_gate, sum_up, sum_down = sums

    def load_landed(i):
        def load():
            here = staged.at[pl.ds(0, 8 * unit)]
            copy = pltpu.make_async_copy(core_landed.at[i], here, local_sems.at[3])
            copy.start()
            copy.wait()
            return here

        return load

    for step in gather_second.steps():
        step()
    gather_cot.step_two()
    for load in loads:
        load.wait()
    gather_second.own_line()
    gather_cot.step_three()
    feed_forward(pl.ds(place.line(0), LINE))
    gather_second.other_line()
    gather_cot.step_four()
    feed_forward(pl.ds(place.line(1), LINE))
    gather_cot.own_line()
    gather_cot.other_line()
    feed_backward(1)
    scatter_back.send_other()
    feed_backward(0)
    scatter_back.send_own()
    project_out(1)
    project_out(0)
    weight_grad(w_gate, d_gate, second)
    sum_gate.core_send()
    scatter_back.step_one()
    weight_grad(w_up, d_up, second)
    sum_up.core_send()
    gather_second.finish()
    for by in ((0, 1, 0), (0, 3, 0), (1, 0, 0)):
        pl.semaphore_signal(
            free_sem, inc=1, device_id=place.rep_dev(*by), device_id_type=MESH
        )
    scatter_back.step_two()
    weight_grad(w_down, hidden, cot_all)
    sum_down.core_send()
    pl.semaphore_wait(free_sem, 3)
    sum_gate.x_first(load_landed(0))
    sum_up.x_first(load_landed(1))
    gather_cot.finish()
    q_cols = 2 * HEAD_DIM
    query = heads.at[:, pl.ds(0, q_cols)]
    key = heads.at[:, pl.ds(q_cols, HEAD_DIM)]
    value = heads.at[:, pl.ds(q_cols + HEAD_DIM, HEAD_DIM)]
    attended = heads.at[:, pl.ds(q_cols + 2 * HEAD_DIM, q_cols)]
    w_attn = cot_all
    attn_cols = heads.shape[1]
    loads = [
        pltpu.make_async_copy(heads_hbm, heads, local_sems.at[0]),
        pltpu.make_async_copy(
            w_attn_hbm.at[pl.ds(0, rows_all)],
            w_attn.at[:, pl.ds(0, attn_cols)],
            local_sems.at[1],
        ),
        pltpu.make_async_copy(
            w_attn_hbm.at[pl.ds(rows_all, rows_all)],
            w_attn.at[:, pl.ds(attn_cols, attn_cols)],
            local_sems.at[2],
        ),
    ]
    for load in loads:
        load.start()
    scatter_back.step_three()
    gain_rows = None
    for half in (1, 0):
        rows = pl.ds(half * HALF, HALF)
        d_second = scatter_back.total(half)
        back, gain_part = rms_backward(resid[rows, :], gain_two[...], d_second)
        grad_tokens[rows, :] = cotangent[rows, :] + back
        gain_part = jnp.sum(gain_part, axis=0, keepdims=True)
        gain_rows = gain_part if gain_rows is None else gain_rows + gain_part
    gain_sums[0] = jnp.zeros_like(gain_sums[0])

    def keep_gain(first_row, value):
        for i in range(value.shape[1] // HEAD_DIM):
            gain_sums[0, first_row + i : first_row + i + 1, :] = value[
                :, i * HEAD_DIM : (i + 1) * HEAD_DIM
            ]

    gain_slots = width // HEAD_DIM
    keep_gain(gain_slots, gain_rows)
    branch[own, :] = grad_tokens[...].astype(low)
    gather_branch.start()
    sum_down.x_first(load_landed(2))
    gather_branch.step_one()
    sum_gate.x_second()
    gather_branch.step_two()
    sum_up.x_second()
    gather_branch.step_three()
    sum_down.x_second()
    sum_gate.y_send()
    gather_branch.step_four()
    sum_up.y_send()
    gather_branch.own_line()
    for load in loads:
        load.wait()

    def into_attention(dy):
        rows = pl.ds(place.line(dy), LINE)
        d_att[rows, :] = (
            mm(branch[rows, 0:rows_all], w_attn[:, 4 * HEAD_DIM : attn_cols])
            + mm(branch[rows, rows_all:], w_attn[:, attn_cols + 4 * HEAD_DIM : 2 * attn_cols])
        ).astype(low)

    into_attention(0)
    gather_branch.other_line()
    into_attention(1)
    sum_down.y_send()
    scatter_back.finish()
    load = pltpu.make_async_copy(first_hbm, part_back, local_sems.at[0])
    load.start()

    def unrotate(rows, upstream, projected, gain):
        turned = upstream * cosine[rows, :] - swap_halves(upstream) * sine[rows, :]
        return rms_backward(projected, gain, turned)

    gain_rows = jnp.zeros((1, HEAD_DIM), f32)
    d_key[...] = jnp.zeros_like(d_key)
    d_value[...] = jnp.zeros_like(d_value)
    for part in range(rows_all // chunk):
        rows = pl.ds(part * chunk, chunk)
        seen = (part + 1) * chunk
        token = part * chunk + lax.broadcasted_iota(jnp.int32, (chunk, 1), 0)
        source = lax.broadcasted_iota(jnp.int32, (1, seen), 1)
        visible = (source >= begin_of(token)) & (source <= token)
        for g in range(2):
            lanes = pl.ds(g * HEAD_DIM, HEAD_DIM)
            scores = mm_nt(query[rows, lanes], key[0:seen, :]) * scale
            weights = jnp.where(visible, jnp.exp(scores - proj[rows, 3 * HEAD_DIM + g : 3 * HEAD_DIM + g + 1]), 0.0)
            d_probs = mm_nt(d_att[rows, lanes], value[0:seen, :])
            inner = jnp.sum(weights * d_probs, axis=-1, keepdims=True)
            d_scores = (weights * (d_probs - inner)).astype(low)
            back, gain_part = unrotate(
                rows, mm(d_scores, key[0:seen, :]) * scale, proj[rows, lanes], query_gain[...].astype(f32)
            )
            d_qkv[rows, lanes] = back.astype(low)
            gain_rows = gain_rows + jnp.sum(gain_part, axis=0, keepdims=True)
            d_key[0:seen, :] += mm_tn(d_scores, query[rows, lanes])
            d_value[0:seen, :] += mm_tn(weights.astype(low), d_att[rows, lanes])
        if part == 1:
            sum_gate.y_gather(sum_gate.piece(), local_sems.at[3])
            scatter_left.send_other()
            scatter_left.send_own()
        if part == 3:
            sum_up.y_gather(sum_up.piece(), local_sems.at[3])
    d_qkv[:, 3 * HEAD_DIM :] = d_value[...].astype(low)

    keep_gain(2 * gain_slots, gain_rows)
    lanes = pl.ds(2 * HEAD_DIM, HEAD_DIM)
    back, gain_part = unrotate(pl.ds(0, rows_all), d_key[...] * scale, proj[:, lanes], key_gain[...].astype(f32))
    d_qkv[:, lanes] = back.astype(low)
    keep_gain(2 * gain_slots + 1, jnp.sum(gain_part, axis=0, keepdims=True))

    head_landed = cot_all.at[:, pl.ds(0, 6 * HEAD_DIM)]
    sum_attn = RepSum(
        place,
        sems(RepSum.COPIES),
        pair.at[pl.ds(pl.multiple_of(place.core * rows_all, BLOCK), rows_all)],
        pair.at[pl.ds(pl.multiple_of((1 - place.core) * rows_all, BLOCK), rows_all)],
        head_core_landed,
        [head_landed.at[pl.ds(e * BLOCK, BLOCK)] for e in range(2)],
        [head_landed.at[pl.ds((1 + e) * 2 * BLOCK, 2 * BLOCK)] for e in range(2)],
        head_landed.at[pl.ds(6 * BLOCK, BLOCK)],
        attn_grads,
        BLOCK,
        16,
    )

    load.wait()

    @pl.loop(0, width // 256)
    def _(i):
        cols = pl.ds(pl.multiple_of(i * 256, 256), 256)
        from_first = mm_tn(part_back[:, cols], d_qkv[...]).astype(low)
        from_branch = mm_tn(branch[:, cols], attended[...]).astype(low)
        for piece in range(16):
            rows = pl.ds(pl.multiple_of(piece * BLOCK + i * 16, 16), 16)
            pair[rows, 0 : 4 * HEAD_DIM] = from_first[piece * 16 : piece * 16 + 16, :]
            pair[rows, 4 * HEAD_DIM :] = from_branch[piece * 16 : piece * 16 + 16, :]

    gather_branch.finish()
    for by in ((1, 0), (0, 1), (0, 3)):
        pl.semaphore_signal(landing_free, inc=1, device_id=place.dev(*by), device_id_type=MESH)
    sum_attn.core_send()
    sum_gate.x_gather()
    scatter_left.step_one()
    scatter_first = Scatter(
        place,
        part_back,
        Slots(branch, 0, HALF),
        Slots(branch, 4 * HALF, 32),
        Slots(branch, 7 * HALF, HALF),
        branch.at[pl.ds(13 * HALF, HALF)],
        *sems(Scatter.COPIES),
    )

    def load_heads():
        copy = pltpu.make_async_copy(head_core_landed, d_up, local_sems.at[3])
        copy.start()
        copy.wait()
        return d_up

    def into_first(dy):
        rows = pl.ds(place.line(dy), LINE)

        for side in range(2):

            @pl.loop(0, rows_all // 256)
            def _(i):
                feats = pl.ds(pl.multiple_of(i * 256, 256), 256)
                cols = pl.ds(pl.multiple_of(side * rows_all + i * 256, 256), 256)
                part_back[rows, cols] = mm_nt(
                    d_qkv[rows, :], w_attn[feats, pl.ds(side * attn_cols, 4 * HEAD_DIM)]
                ).astype(low)

    into_first(1)
    pl.semaphore_wait(landing_free, 3)
    scatter_first.send_other()
    into_first(0)
    scatter_first.send_own()
    for by in ((0, 1, 0), (0, 3, 0), (1, 0, 0)):
        pl.semaphore_signal(
            heads_free, inc=1, device_id=place.rep_dev(*by), device_id_type=MESH
        )
    sum_down.y_gather(sum_down.piece(), local_sems.at[3])
    pl.semaphore_wait(heads_free, 3)
    sum_attn.x_first(load_heads)
    scatter_first.step_one()
    scatter_left.step_two()
    sum_attn.x_second()
    sum_gate.x_forward()
    sum_up.x_gather()
    scatter_left.step_three()
    scatter_first.step_two()
    scatter_first.step_three()
    sum_attn.y_send()
    sum_up.x_forward()
    sum_down.x_gather()
    piece = sum_attn.piece()
    swap_net = Net(*sems(7))
    for dy in range(2):
        for dz in range(4):
            if dy or dz:
                to = place.block(dy, dz)
                src = piece.at[pl.ds(pl.multiple_of(to * 16, 16), 16)]
                dst = swapped.at[pl.ds(pl.multiple_of(place.shard * 16, 16), 16)]
                here = place.block(-dy, -dz)
                here = swapped.at[pl.ds(pl.multiple_of(here * 16, 16), 16)]
                swap_net.send(f"{dy}{dz}", src, dst, place.dev(dy, dz), here)
    own_rows = pl.ds(pl.multiple_of(place.shard * 16, 16), 16)
    swapped[own_rows, :] = piece[own_rows, :]
    swap_net.finish()
    kv = 8 * HEAD_DIM
    for j in range(8):
        rows = pl.ds(j * 16, 16)
        at = 0
        for begin, size in ((0, 2), (2, 1), (3, 1), (4, 2)):
            assembled[:, at + j * size * HEAD_DIM : at + (j + 1) * size * HEAD_DIM] = swapped[
                rows, begin * HEAD_DIM : (begin + size) * HEAD_DIM
            ]
            at += size * kv
    sum_attn.y_gather(assembled, local_sems.at[3])
    gain_rows = None
    for half in (1, 0):
        rows = pl.ds(half * HALF, HALF)
        d_first = scatter_first.total(half)
        back, gain_part = rms_backward(tokens[rows, :].astype(f32), gain_one[...], d_first)
        grad_tokens[rows, :] += back
        gain_part = jnp.sum(gain_part, axis=0, keepdims=True)
        gain_rows = gain_part if gain_rows is None else gain_rows + gain_part
    keep_gain(0, gain_rows)

    gain_net = Net(*sems(9))
    stages = (
        [place.dev(0, d) for d in (1, 2, 3)],
        [place.dev(1, 0)],
        [place.rep_dev(1, 0, 0)],
        [place.rep_dev(0, 0, 1)],
        [place.rep_dev(0, d, 0) for d in (1, 2, 3)],
    )

    def gain_send(stage):
        for i, dev in enumerate(stages[stage]):
            dst = gain_landed.at[3 * stage + i]
            gain_net.send(f"{stage}.{i}", gain_sums.at[stage], dst, dev, dst)

    def gain_add(stage):
        total = gain_sums[stage]
        for i in range(len(stages[stage])):
            gain_net.wait(f"{stage}.{i}")
            total = total + gain_landed[3 * stage + i]
        gain_sums[stage + 1] = total

    gain_send(0)
    gain_add(0)
    gain_send(1)
    sum_attn.x_gather()
    gain_add(1)
    gain_send(2)
    scatter_right.send_other()
    scatter_right.send_own()
    for half in (0, 1):
        rows = pl.ds(half * HALF, HALF)
        result[rows, left] = resid[rows, left] + scatter_left.total(half)
    sum_gate.x_last()
    gain_add(2)
    gain_send(3)
    sum_down.x_forward()
    scatter_right.step_one()
    sum_up.x_last()
    sum_attn.x_forward()
    gain_add(3)
    gain_send(4)
    scatter_right.step_two()
    sum_down.x_last()
    scatter_right.step_three()
    sum_attn.x_last()
    gain_add(4)
    for half in (0, 1):
        rows = pl.ds(half * HALF, HALF)
        result[rows, right] = resid[rows, right] + scatter_right.total(half)
    gains[...] = gain_sums[5]

    for one in (scatter_first, scatter_left, scatter_right):
        one.finish()
    for one in sums:
        one.finish()
    sum_attn.finish()
    gain_net.finish()


def layer_call(lengths, *args):
    tokens, cotangent = args[:2]
    width = tokens.shape[1]
    hid = args[-1].shape[0]
    rows = 8 * BLOCK
    vmem = pl.BlockSpec(memory_space=pltpu.VMEM)
    smem = pl.BlockSpec(memory_space=pltpu.SMEM)
    hbm = pl.BlockSpec(memory_space=pltpu.HBM)
    copies = 4 * Gather.COPIES + 5 * Scatter.COPIES + 4 * RepSum.COPIES + 9 + 7 + 7
    gain_shape = (2 * width // HEAD_DIM + 8, HEAD_DIM)
    return pl.pallas_call(
        functools.partial(layer_kernel, 1.0 / math.sqrt(HEAD_DIM)),
        name="layer",
        out_shape=[
            jax.ShapeDtypeStruct((BLOCK, width), f32),
            jax.ShapeDtypeStruct((BLOCK, width), f32),
            jax.ShapeDtypeStruct(gain_shape, f32),
            jax.ShapeDtypeStruct((256, 3 * width), low),
            jax.ShapeDtypeStruct((3, hid, width), low),
            jax.ShapeDtypeStruct((3, hid // 2, width), low),
            jax.ShapeDtypeStruct((rows, 6 * HEAD_DIM), low),
            jax.ShapeDtypeStruct((rows, width), low),
            jax.ShapeDtypeStruct((2 * rows, 6 * HEAD_DIM), low),
            jax.ShapeDtypeStruct((rows, 6 * HEAD_DIM), low),
        ],
        in_specs=[smem] + [vmem] * 6 + [hbm] * 7,
        out_specs=[vmem] * 3 + [hbm] * 7,
        scratch_shapes=[
            pltpu.VMEM((BLOCK, width), f32),
            pltpu.VMEM((2, width), f32),
            pltpu.VMEM((8, 16, 256), low),
            pltpu.VMEM((rows, 4 * HEAD_DIM), f32),
            pltpu.VMEM((rows, HEAD_DIM), f32),
            pltpu.VMEM((rows, HEAD_DIM), f32),
            pltpu.VMEM((rows, width), low),
            pltpu.VMEM((rows, width), low),
            pltpu.VMEM((rows, width), low),
            pltpu.VMEM((hid, width), low),
            pltpu.VMEM((hid, width), low),
            pltpu.VMEM((hid, width), low),
            pltpu.VMEM((2 * rows, hid), low),
            pltpu.VMEM((rows, hid), low),
            pltpu.VMEM((rows, width), low),
            pltpu.VMEM((rows, width), low),
            pltpu.VMEM((rows, 2 * HEAD_DIM), low),
            pltpu.VMEM((rows, HEAD_DIM), f32),
            pltpu.VMEM((rows, HEAD_DIM), f32),
            pltpu.VMEM((rows, 4 * HEAD_DIM), low),
            pltpu.VMEM((hid // 2, width), low),
        ]
        + Scatter.scratch(width)
        + [
            pltpu.VMEM((BLOCK, 6 * HEAD_DIM), low),
            pltpu.VMEM((16, 3 * width), low),
            pltpu.VMEM((6,) + gain_shape, f32),
            pltpu.VMEM((15,) + gain_shape, f32),
            pltpu.SemaphoreType.DMA((2, 2, 11)),
            pltpu.SemaphoreType.DMA((3, 2)),
            pltpu.SemaphoreType.REGULAR,
            pltpu.SemaphoreType.REGULAR,
            pltpu.SemaphoreType.REGULAR,
            pltpu.SemaphoreType.DMA((6,)),
            pltpu.SemaphoreType.DMA((copies,)),
            pltpu.SemaphoreType.DMA((copies,)),
        ],
        compiler_params=pltpu.CompilerParams(
            collective_id=1, has_side_effects=True, vmem_limit_bytes=60 << 20
        ),
        cost_estimate=pl.CostEstimate(
            flops=36_000_000_000, bytes_accessed=60_000_000, transcendentals=4_000_000
        ),
    )(lengths, *args)


def widen_kernel(ffn, attn, *refs):
    outs, (narrow, narrow_attn, wide, wide_attn, load_sems, store_sems, attn_sems) = refs[:7], refs[7:]
    slots, tall, _ = wide.shape
    count = narrow.shape[0] // tall
    per = count // 3
    loads = []
    for i in range(count):
        rows = pl.ds(i % per * tall, tall)
        loads.append(
            pltpu.make_async_copy(
                ffn.at[i // per, rows], narrow.at[pl.ds(i * tall, tall)], load_sems.at[i]
            )
        )
    first = pltpu.make_async_copy(attn, narrow_attn, load_sems.at[count])
    first.start()
    for load in loads:
        load.start()
    first.wait()
    wide_attn[...] = narrow_attn[...].astype(f32)
    stores, at = [], 0
    for j, ref in enumerate(outs[3:]):
        size = ref.shape[1]
        stores.append(
            pltpu.make_async_copy(wide_attn.at[:, pl.ds(at, size)], ref, attn_sems.at[j])
        )
        stores[-1].start()
        at += size
    busy = [None] * slots
    for i in range(count):
        loads[i].wait()
        slot = i % slots
        if busy[slot] is not None:
            busy[slot].wait()
        wide[slot] = narrow[pl.ds(i * tall, tall), :].astype(f32)
        rows = pl.ds(i % per * tall, tall)
        busy[slot] = pltpu.make_async_copy(wide.at[slot], outs[i // per].at[rows], store_sems.at[slot])
        busy[slot].start()
    for copy in busy + stores:
        copy.wait()


def widen(ffn, attn):
    _, hid, width = ffn.shape
    rows = attn.shape[0]
    tall, slots = hid // 3, 6
    sizes = (width, width // 2, width // 2, width)
    hbm = pl.BlockSpec(memory_space=pltpu.HBM)
    return pl.pallas_call(
        widen_kernel,
        name="widen",
        out_shape=[jax.ShapeDtypeStruct((hid, width), f32)] * 3
        + [jax.ShapeDtypeStruct((rows, size), f32) for size in sizes],
        in_specs=[hbm, hbm],
        out_specs=[hbm] * 7,
        scratch_shapes=[
            pltpu.VMEM((3 * hid, width), low),
            pltpu.VMEM((rows, 3 * width), low),
            pltpu.VMEM((slots, tall, width), f32),
            pltpu.VMEM((rows, 3 * width), f32),
            pltpu.SemaphoreType.DMA((10,)),
            pltpu.SemaphoreType.DMA((slots,)),
            pltpu.SemaphoreType.DMA((4,)),
        ],
        compiler_params=pltpu.CompilerParams(vmem_limit_bytes=60 << 20),
    )(ffn, attn)


def per_device(
    tokens,
    cotangent,
    lengths,
    attn_gain,
    mlp_gain,
    query_gain,
    key_gain,
    w_query,
    w_key,
    w_value,
    w_out,
    w_gate,
    w_up,
    w_down,
):
    width = tokens.shape[1]
    shards = lax.axis_size("shard")
    feat = width // shards
    my_shard = lax.axis_index("shard")
    half = np.arange(HEAD_DIM, dtype=np.float64) % (HEAD_DIM // 2)
    frequency = jnp.asarray(theta_base ** (-half * (2.0 / HEAD_DIM)), f32)[None]
    result, grad_tokens, gains, attn_grads, ffn_grads, *_ = layer_call(
        lengths,
        tokens,
        cotangent,
        jnp.concatenate([attn_gain[None], mlp_gain[None], jnp.zeros((14, feat), low)]),
        query_gain[None],
        key_gain[None],
        frequency,
        w_query,
        w_key,
        w_value,
        w_out,
        w_gate,
        w_up,
        w_down,
    )
    grad_gate, grad_up, grad_down, grad_query, grad_key, grad_value, grad_out = widen(
        ffn_grads, attn_grads
    )
    gains = gains.reshape(-1)
    head_piece = HEAD_DIM // shards
    gains_first = lax.dynamic_slice_in_dim(gains, my_shard * feat, feat, 0)
    gains_second = lax.dynamic_slice_in_dim(gains, width + my_shard * feat, feat, 0)
    gains_query = lax.dynamic_slice_in_dim(gains, 2 * width + my_shard * head_piece, head_piece, 0)
    gains_key = lax.dynamic_slice_in_dim(
        gains, 2 * width + HEAD_DIM + my_shard * head_piece, head_piece, 0
    )
    return (
        result,
        grad_tokens,
        grad_query,
        grad_key,
        grad_value,
        grad_out,
        grad_gate,
        grad_up,
        grad_down,
        gains_first,
        gains_second,
        gains_query,
        gains_key,
    )


def solution(mesh):
    spread = P(("rep", "shard"), None)
    rowed = P("shard", None)
    return jax.shard_map(
        per_device,
        mesh=mesh,
        in_specs=(spread, spread, P("rep", None), P("shard"), P("shard"), P(), P()) + (rowed,) * 7,
        out_specs=(spread, spread) + (rowed,) * 7 + (P("shard"),) * 4,
        check_vma=False,
    )
```
